32 devices in a mesh: node: 4 (over y, core), zero: 8 (over z, x).
Axes of the slice: x: 2, y: 2, z: 4, core: 2. Of those that a mesh axis runs over, the one named last changes fastest.
Arguments:
- grid_in: bfloat16 [8, 16, 360, 261], P('zero', 'node'), may hold values from -6 to 6
- target: float32 [8, 16, 360, 83], P('zero', 'node'), may hold values from -6 to 6
- noise_level: int32 [8], P('zero'), may hold values from 0 to 15
- land_mask: int32 [16, 360], P('node'), may hold values 0 or 1
- neighbours: int32 [3072, 16], P('node'), may hold values from 0 to 959
- halo_send: int32 [384], P('node'), may hold values from 0 to 767
- g2m: int32 [3072, 4], P('node'), may hold values from 0 to 1439
- m2g: int32 [5760, 3], P('node'), may hold values from 0 to 767
- legendre: float32 [16, 181, 181], P('node'), may hold values from -0.078125 to 0.078125
- w_attn: float32 [2048, 512], P(('node', 'zero')), may hold values from -0.25 to 0.25
- w_mlp: float32 [4096, 512], P(('node', 'zero')), may hold values from -0.25 to 0.25
- w_small: float32 [512, 512], P(('node', 'zero')), may hold values from -0.74278135 to 0.74278135
- mom_attn: float32 [2048, 512], P(('node', 'zero')), may hold values from -0.0078125 to 0.0078125
- mom_mlp: float32 [4096, 512], P(('node', 'zero')), may hold values from -0.0078125 to 0.0078125
- m_small: float32 [512, 512], P(('node', 'zero')), may hold values from -0.0008544922 to 0.0008544922
- v_small: float32 [512, 512], P(('node', 'zero')), may hold values from 1.5434852e-08 to 6.162203e-08
- ema_attn: float32 [2048, 512], P(('node', 'zero')), may hold values from -0.25 to 0.25
- ema_mlp: float32 [4096, 512], P(('node', 'zero')), may hold values from -0.25 to 0.25
- ema_small: float32 [512, 512], P(('node', 'zero')), may hold values from -0.375 to 0.375
Outputs:
- loss: float32 [], replicated
- clip_norm: float32 [], replicated
- new_attn: float32 [2048, 512], P(('node', 'zero'))
- new_mlp: float32 [4096, 512], P(('node', 'zero'))
- new_small: float32 [512, 512], P(('node', 'zero'))
- new_mom_attn: float32 [2048, 512], P(('node', 'zero'))
- new_mom_mlp: float32 [4096, 512], P(('node', 'zero'))
- new_m_small: float32 [512, 512], P(('node', 'zero'))
- new_v_small: float32 [512, 512], P(('node', 'zero'))
- new_ema_attn: float32 [2048, 512], P(('node', 'zero'))
- new_ema_mlp: float32 [4096, 512], P(('node', 'zero'))
- new_ema_small: float32 [512, 512], P(('node', 'zero'))
The draws below stay inside these ranges and needn't reach their ends.
Inputs may be any that keep to these rules, and one draw needn't show every extreme that they name: `neighbours`: in the neighbour lists of node block b, a value below 768 names a node of block b, 768 + i the i-th halo_send entry of block b-1, 864 + i that of block b+1 (cyclic); g2m names pixels of the same block, m2g nodes of the same block.
All inputs are finite; a program needn't handle non-finite values. No bound on the sum of `land_mask` on one device may be relied on, other than what follows from the above.
Results may differ from the reference program's by a relative error of at most 0.0068.
The reference program's roundings to bfloat16 on the way count: a program that leaves them out, or rounds other values in their place, can miss the bound.
Values may be sent and summed in bfloat16 or wider, within the bound.
A program may use at most 384 MiB of HBM per device.

```python
import math
from functools import partial
import jax
import jax.numpy as jnp
from jax import lax

D = 512
HEAD_COUNT = 4
HEAD_WIDTH = 128
FF = 2048
CH = 83
CIN = 261
NOISE_FEATS = 42
NLON = 360
MODES = 181
DEGREES = 181
ATT_NBRS = 16
ENC_EDGES = 4
DEC_EDGES = 3
LEVELS = 16
NS_ITERS = 3
STEP = 10
MESH_PER_DEVICE = 768
LAT_DEV = 4
HALO = 96
DATES = 8
NMESH = 3072
NLAT = 16
NPIX = 5760
SENDS = 384
SMALL_ROWS = 512
N_NODE = 4


def draw_w_small(key, part):
    key = jax.random.fold_in(key, 11)
    values = jax.random.truncated_normal(key, -4.0, 4.0, (SMALL_ROWS, D), jnp.float32)
    row_ids = jnp.arange(SMALL_ROWS)
    decoder_rows = (row_ids >= CIN) & (row_ids < CIN + CH)
    row_scale = jnp.where(decoder_rows, 3.0, 1.0) / math.sqrt(CIN)
    return values * row_scale[:, None]


def touch_ends(result, key, smallest, top_value):
    extent = result.shape
    spot = [jax.random.randint(jax.random.fold_in(key, axis), (), 0, extent[axis]) for axis in range(len(extent))]
    result = result.at[tuple(spot)].set(smallest)
    longest = extent.index(max(extent))
    spot[longest] = (spot[longest] + 1) % extent[longest]
    return result.at[tuple(spot)].set(top_value)


def block_scale(rng, shape, shards, least, top_value):
    factor_of = 1.0
    for position, shards_of in shards:
        draws = jax.random.uniform(jax.random.fold_in(jax.random.fold_in(rng, 6), position), (shards_of,), jnp.float32, least / len(shards), top_value / len(shards))
        factor_of = factor_of * jnp.repeat(jnp.exp(draws), shape[position] // shards_of).reshape((-1,) + (1,) * (len(shape) - 1 - position))
    return factor_of


def bell_draw(key, extent, scale, reach, pieces=(), kind=jnp.bfloat16):
    gain = block_scale(key, extent, pieces, -0.22, 0.18) if pieces else 1.0
    result = jax.random.normal(key, extent, jnp.float32) * scale * gain
    return jnp.minimum(jnp.maximum(result, -reach), reach).astype(kind)


def setup_inputs(seed: int = 0) -> dict:
    streams_of = jax.random.split(jax.random.key(seed), 20)
    grid_in = bell_draw(streams_of[0], (DATES, NLAT, NLON, CIN), 1.0, 6.0, ((0, 8), (1, 4)))
    target = bell_draw(streams_of[1], (DATES, NLAT, NLON, CH), 1.0, 6.0, ((0, 8), (1, 4)), jnp.float32)
    noise_level = touch_ends(jax.random.randint(streams_of[2], (DATES,), 0, LEVELS), jax.random.fold_in(streams_of[2], 1), 0, LEVELS - 1).astype(jnp.int32)
    land_mask = touch_ends((jax.random.randint(streams_of[3], (NLAT, NLON), 0, 10) < 3).astype(jnp.int32), jax.random.fold_in(streams_of[3], 1), 0, 1)
    neighbours = touch_ends(jax.random.randint(streams_of[4], (NMESH, ATT_NBRS), 0, MESH_PER_DEVICE + 2 * HALO), jax.random.fold_in(streams_of[4], 1), 0, (MESH_PER_DEVICE + 2 * HALO) - 1).astype(jnp.int32)
    halo_send = touch_ends(jax.random.randint(streams_of[5], (SENDS,), 0, MESH_PER_DEVICE), jax.random.fold_in(streams_of[5], 1), 0, MESH_PER_DEVICE - 1).astype(jnp.int32)
    g2m = touch_ends(jax.random.randint(streams_of[6], (NMESH, ENC_EDGES), 0, LAT_DEV * NLON), jax.random.fold_in(streams_of[6], 1), 0, (LAT_DEV * NLON) - 1).astype(jnp.int32)
    m2g = touch_ends(jax.random.randint(streams_of[7], (NPIX, DEC_EDGES), 0, MESH_PER_DEVICE), jax.random.fold_in(streams_of[7], 1), 0, MESH_PER_DEVICE - 1).astype(jnp.int32)
    legendre = bell_draw(streams_of[8], (NLAT, MODES, DEGREES), (NLAT * NLON) ** -0.5, 0.078125, ((0, 4),), jnp.float32)
    w_attn = bell_draw(streams_of[9], (4 * D, D), D ** -0.5, 0.25, ((0, 32),), jnp.float32)
    w_mlp = bell_draw(streams_of[10], (2 * FF, D), D ** -0.5, 0.25, ((0, 32),), jnp.float32)
    w_small = draw_w_small(jax.random.fold_in(streams_of[19], 71), 0)
    mom_attn = bell_draw(streams_of[12], (4 * D, D), (((4 * D + 2 * FF + SMALL_ROWS) * D) ** -0.5), 0.0078125, ((0, 32),), jnp.float32)
    mom_mlp = bell_draw(streams_of[13], (2 * FF, D), (((4 * D + 2 * FF + SMALL_ROWS) * D) ** -0.5), 0.0078125, ((0, 32),), jnp.float32)
    m_small = bell_draw(streams_of[14], (SMALL_ROWS, D), (0.111 * ((4 * D + 2 * FF + SMALL_ROWS) * D) ** -0.5), 0.0008544922, ((0, 32),), jnp.float32)
    v_small = jnp.clip(jnp.exp(math.log(6.162203192161542e-08) - 1.3843914 * jax.random.uniform(streams_of[15], (SMALL_ROWS, D), jnp.float32) ** block_scale(streams_of[15], (SMALL_ROWS, D), ((0, 32),), -0.2, 0.2)), 1.5434851619033907e-08, 6.162203192161542e-08)
    ema_attn = bell_draw(streams_of[16], (4 * D, D), D ** -0.5, 0.25, ((0, 32),), jnp.float32)
    ema_mlp = bell_draw(streams_of[17], (2 * FF, D), D ** -0.5, 0.25, ((0, 32),), jnp.float32)
    ema_small = bell_draw(streams_of[18], (SMALL_ROWS, D), CIN ** -0.5, 0.375, ((0, 32),), jnp.float32)
    return dict(grid_in=grid_in, target=target, noise_level=noise_level, land_mask=land_mask, neighbours=neighbours, halo_send=halo_send, g2m=g2m, m2g=m2g, legendre=legendre, w_attn=w_attn, w_mlp=w_mlp, w_small=w_small, mom_attn=mom_attn, mom_mlp=mom_mlp, m_small=m_small, v_small=v_small, ema_attn=ema_attn, ema_mlp=ema_mlp, ema_small=ema_small)


@jax.custom_vjp
def bfloat_inputs(v):
    return lax.optimization_barrier(v.astype(jnp.bfloat16)).astype(jnp.float32)

@jax.custom_vjp
def low_back(v):
    return v

def low_keep(v):
    return (bfloat_inputs(v), None)

def low_pass(kept, grad):
    return (grad,)

def back_keep(v):
    return (v, None)

def back_low(kept, grad):
    return (bfloat_inputs(grad),)
bfloat_inputs.defvjp(low_keep, low_pass)
low_back.defvjp(back_keep, back_low)
top_precision = lax.Precision.HIGHEST
norm_epsilon = 1e-05
trace_epsilon = 1e-12
clip_limit = 1.0
moment_decay = 0.95
orthogonal_rate = 0.1
adam_first = 0.9
adam_second = 0.95
adam_rate = 0.02
adam_epsilon = 1e-08
average_decay = 0.9
newton_first = 3.4445
newton_second = -4.775
newton_third = 2.0315
sigma_lowest = 0.1
sigma_highest = 20.0

def noise_scalars(level):
    sigma = sigma_lowest * (sigma_highest / sigma_lowest) ** (level.astype(jnp.float32) / (LEVELS - 1))
    total = sigma * sigma + 1.0
    return (sigma, lax.rsqrt(total), 1.0 / total, sigma * lax.rsqrt(total), total / (sigma * sigma))

def noise_features(sigma):
    half_count = NOISE_FEATS // 2
    frequency = jnp.exp(jnp.arange(half_count).astype(jnp.float32) * (3.0 / half_count))
    phases = 0.25 * jnp.log(sigma) * frequency
    return jnp.concatenate([jnp.sin(phases), jnp.cos(phases)])

def cond_norm(value_rows, gain_shift, bias_shift):
    centred = value_rows - lax.optimization_barrier(jnp.mean(value_rows, axis=-1, keepdims=True))
    spread = lax.optimization_barrier(jnp.mean(centred * centred, axis=-1, keepdims=True))
    return centred * lax.rsqrt(spread + norm_epsilon) * (1.0 + gain_shift) + bias_shift

def ns_basis(gram_matrix):
    score_scale = lax.rsqrt(jnp.trace(gram_matrix) + trace_epsilon)
    current = gram_matrix * (score_scale * score_scale)
    identity = jnp.eye(gram_matrix.shape[0], dtype=jnp.float32)
    basis = identity
    for iteration in range(NS_ITERS):
        squared = jnp.dot(current, current, precision=top_precision)
        polynomial = newton_first * identity + newton_second * current + newton_third * squared
        basis = jnp.dot(basis, polynomial, precision=top_precision)
        if iteration + 1 < NS_ITERS:
            current = jnp.dot(polynomial, jnp.dot(current, polynomial, precision=top_precision), precision=top_precision)
    return (basis, score_scale)

def attend(block):
    query_rows, extended, indices = block
    picked = extended[indices]
    key_rows = picked[:, :, :D].reshape(MESH_PER_DEVICE, ATT_NBRS, HEAD_COUNT, HEAD_WIDTH)
    value_rows = picked[:, :, D:].reshape(MESH_PER_DEVICE, ATT_NBRS, HEAD_COUNT, HEAD_WIDTH)
    attention_logits = jnp.einsum('out,ovut->ouv', query_rows.reshape(MESH_PER_DEVICE, HEAD_COUNT, HEAD_WIDTH), key_rows, precision=top_precision) * HEAD_WIDTH ** (-0.5)
    attention_probabilities = jax.nn.softmax(low_back(attention_logits), axis=-1)
    blended_values = jnp.einsum('iqa,iaqz->iqz', bfloat_inputs(attention_probabilities), value_rows, precision=top_precision)
    return blended_values.reshape(MESH_PER_DEVICE, D)

def sample_loss(lowered, graph, keep_mask, legendre, grid_values, target_values, level):
    attn_weights, mlp_weights, small_weights = lowered
    neighbour_ids, send_ids, enc_ids, dec_ids = graph
    w_query = attn_weights[:3 * D]
    w_output = attn_weights[3 * D:]
    w_upper = mlp_weights[:FF]
    w_down = mlp_weights[FF:]
    w_enc = small_weights[:CIN]
    w_dec = small_weights[CIN:CIN + CH]
    w_cond = small_weights[CIN + CH:].reshape(4, NOISE_FEATS, D)
    sigma, c_input, c_skip, c_output, loss_weight = noise_scalars(level)
    scale_input = jnp.where(jnp.arange(CIN) < CH, c_input, 1.0)
    inputs = bfloat_inputs(grid_values * scale_input).reshape(N_NODE, LAT_DEV * NLON, CIN)
    embedded = low_back(jnp.einsum('npc,cd->npd', inputs, w_enc, precision=top_precision))
    stream_in = jax.vmap(lambda table, index: lax.optimization_barrier(jnp.mean(table[index], axis=1)))(embedded, enc_ids)
    features = bfloat_inputs(noise_features(sigma))
    modulation = jnp.einsum('f,jfd->jd', features, w_cond, precision=top_precision)
    first = bfloat_inputs(cond_norm(stream_in, modulation[0], modulation[1]))
    packed = bfloat_inputs(low_back(jnp.einsum('nmd,rd->nmr', first, w_query, precision=top_precision)))
    query_rows = packed[..., :D]
    pairs = packed[..., D:]
    lent = jax.vmap(lambda table, index: table[index])(pairs, send_ids)
    extended = jnp.concatenate([pairs, jnp.roll(lent, 1, axis=0), jnp.roll(lent, -1, axis=0)], axis=1)
    blended_values = lax.map(jax.checkpoint(attend), (query_rows, extended, neighbour_ids))
    blended_values = bfloat_inputs(low_back(blended_values))
    stream_mid = stream_in + low_back(jnp.einsum('nmd,rd->nmr', blended_values, w_output, precision=top_precision))
    second = bfloat_inputs(cond_norm(stream_mid, modulation[2], modulation[3]))
    upper = low_back(jnp.einsum('nmd,fd->nmf', second, w_upper, precision=top_precision))
    activ = bfloat_inputs(jax.nn.gelu(upper))
    stream_out = stream_mid + low_back(jnp.einsum('nmf,fd->nmd', activ, w_down, precision=top_precision))
    latent = bfloat_inputs(jax.vmap(lambda table, index: lax.optimization_barrier(jnp.mean(table[index], axis=1)))(stream_out, dec_ids))
    network = low_back(jnp.einsum('npd,cd->npc', latent, w_dec, precision=top_precision)).reshape(NLAT, NLON, CH)
    predicted = c_skip * grid_values[..., :CH] + c_output * network
    error = (predicted - target_values) * keep_mask
    spectrum = jnp.fft.rfft(error, axis=1)[:, :MODES, :]
    parts = jnp.stack([jnp.real(spectrum), jnp.imag(spectrum)])
    coeffs = jnp.einsum('tml,rtmc->rmlc', legendre, parts, precision=top_precision)
    return loss_weight / (2 * MODES * DEGREES * CH) * jnp.sum(coeffs * coeffs)

def orthogonal_step(weight, moment, start, stop):
    block = moment[start:stop]
    basis, score_scale = ns_basis(jnp.dot(block.T, block, precision=top_precision))
    update = jnp.dot(block * score_scale, basis, precision=top_precision)
    return weight[start:stop] - orthogonal_rate * 0.2 * math.sqrt(max(stop - start, D)) * update

def reference(grid_in, target, noise_level, land_mask, neighbours, halo_send, g2m, m2g, legendre, w_attn, w_mlp, w_small, mom_attn, mom_mlp, m_small, v_small, ema_attn, ema_mlp, ema_small):
    graph = (neighbours.reshape(N_NODE, MESH_PER_DEVICE, ATT_NBRS), halo_send.reshape(N_NODE, HALO), g2m.reshape(N_NODE, MESH_PER_DEVICE, ENC_EDGES), m2g.reshape(N_NODE, LAT_DEV * NLON, DEC_EDGES))
    keep_mask = 1.0 - land_mask.astype(jnp.float32)[:, :, None] * (jnp.arange(CH) == CH - 1).astype(jnp.float32)
    grid_values = grid_in.astype(jnp.float32)

    def total_loss(params):
        lowered = tuple((bfloat_inputs(item) for item in params))
        one_date = jax.checkpoint(partial(sample_loss, lowered, graph, keep_mask, legendre))

        def accumulate(running, sample):
            return (running + one_date(*sample), None)
        summed, unused = lax.scan(accumulate, jnp.zeros((), jnp.float32), (grid_values, target, noise_level))
        return summed
    loss, pullback = jax.vjp(total_loss, (w_attn, w_mlp, w_small))
    g_attn, g_mlp, g_small = pullback(jnp.ones((), jnp.float32))[0]
    total_sq = jnp.sum(g_attn * g_attn) + jnp.sum(g_mlp * g_mlp) + jnp.sum(g_small * g_small)
    clip_norm = jnp.sqrt(total_sq)
    factor = jnp.minimum(1.0, clip_limit / clip_norm)
    new_mom_attn = moment_decay * mom_attn + factor * g_attn
    new_mom_mlp = moment_decay * mom_mlp + factor * g_mlp
    new_attn = jnp.concatenate([orthogonal_step(w_attn, new_mom_attn, 0, 3 * D), orthogonal_step(w_attn, new_mom_attn, 3 * D, 4 * D)])
    new_mlp = jnp.concatenate([orthogonal_step(w_mlp, new_mom_mlp, 0, FF), orthogonal_step(w_mlp, new_mom_mlp, FF, 2 * FF)])
    clipped = factor * g_small
    new_m_small = adam_first * m_small + (1.0 - adam_first) * clipped
    new_v_small = adam_second * v_small + (1.0 - adam_second) * clipped * clipped
    new_small = w_small - adam_rate * (new_m_small / (1.0 - adam_first ** STEP)) / (jnp.sqrt(new_v_small / (1.0 - adam_second ** STEP)) + adam_epsilon)
    new_ema_attn = average_decay * ema_attn + (1.0 - average_decay) * new_attn
    new_ema_mlp = average_decay * ema_mlp + (1.0 - average_decay) * new_mlp
    new_ema_small = average_decay * ema_small + (1.0 - average_decay) * new_small
    return (loss, clip_norm, new_attn, new_mlp, new_small, new_mom_attn, new_mom_mlp, new_m_small, new_v_small, new_ema_attn, new_ema_mlp, new_ema_small)
```

```python
import math

import jax
import jax.numpy as jnp
import numpy as np
from jax import lax
from jax.sharding import PartitionSpec as P

HEAD_COUNT = 4
NOISE_FEATS = 42
LEVELS = 16
NS_ITERS = 3
STEP = 10

top_precision = lax.Precision.HIGHEST
mid_precision = lax.Precision.HIGH
norm_epsilon = 1e-05
trace_epsilon = 1e-12
clip_limit = 1.0
moment_decay = 0.95
orthogonal_rate = 0.1
adam_first = 0.9
adam_second = 0.95
adam_rate = 0.02
adam_epsilon = 1e-08
average_decay = 0.9
newton_first = 3.4445
newton_second = -4.775
newton_third = 2.0315
sigma_lowest = 0.1
sigma_highest = 20.0
f32 = jnp.float32
bf16 = jnp.bfloat16


def noise_scalars(level):
    sigma = sigma_lowest * (sigma_highest / sigma_lowest) ** (level.astype(f32) / (LEVELS - 1))
    total = sigma * sigma + 1.0
    return (sigma, lax.rsqrt(total), 1.0 / total, sigma * lax.rsqrt(total), total / (sigma * sigma))


def noise_features(sigma):
    half_count = NOISE_FEATS // 2
    frequency = jnp.exp(jnp.arange(half_count).astype(f32) * (3.0 / half_count))
    phases = 0.25 * jnp.log(sigma) * frequency
    return jnp.concatenate([jnp.sin(phases), jnp.cos(phases)])


def normed(rows):
    centred = rows - jnp.mean(rows, axis=-1, keepdims=True)
    spread = jnp.mean(centred * centred, axis=-1, keepdims=True)
    inverse = lax.rsqrt(spread + norm_epsilon)
    return centred * inverse, inverse


def normed_back(grad, unit, inverse, gain):
    scaled = grad * (1.0 + gain)
    back = inverse * (
        scaled
        - jnp.mean(scaled, axis=-1, keepdims=True)
        - unit * jnp.mean(scaled * unit, axis=-1, keepdims=True)
    )
    return back, jnp.sum(grad * unit, axis=0), jnp.sum(grad, axis=0)


def dot(left, right, contract):
    return lax.dot_general(left, right, (contract, ((), ())), preferred_element_type=f32)


def dot_nn(left, right):
    return dot(left, right, ((1,), (0,)))


def dot_nt(left, right):
    return dot(left, right, ((1,), (1,)))


def dot_tn(left, right):
    return dot(left, right, ((0,), (0,)))


def split(value):
    high = value.astype(bf16)
    return high, (value - high.astype(f32)).astype(bf16)


def counted(index, size):
    hits = index[:, :, None] == jnp.arange(size, dtype=index.dtype)
    return jnp.sum(hits.astype(f32), axis=1)


def passed_along(value, axis, steps):
    count = lax.axis_size(axis)
    pairs = [(source, (source + steps) % count) for source in range(count)]
    return lax.ppermute(value, axis, pairs)


def turn_tables(lon_count, modes):
    turns = np.arange(lon_count)[:, None] * np.arange(modes)[None, :] % lon_count
    phases = turns * (2.0 * np.pi / lon_count)
    return np.cos(phases).astype(np.float32), -np.sin(phases).astype(np.float32)


def heads_of(rows):
    return [rows[:, i * 128 : (i + 1) * 128] for i in range(HEAD_COUNT)]


def ns_apply(gram_matrix, moment):
    score_scale = lax.rsqrt(jnp.trace(gram_matrix) + trace_epsilon)
    current = gram_matrix * (score_scale * score_scale)
    identity = jnp.eye(gram_matrix.shape[0], dtype=f32)
    result = moment * score_scale
    for iteration in range(NS_ITERS):
        squared = jnp.dot(current, current, precision=mid_precision)
        polynomial = newton_first * identity + newton_second * current + newton_third * squared
        result = jnp.dot(result, polynomial, precision=mid_precision)
        if iteration + 1 < NS_ITERS:
            current = jnp.dot(
                jnp.dot(polynomial, current, precision=mid_precision),
                polynomial,
                precision=mid_precision,
            )
    return result


def gram_of(left):
    return jnp.dot(left.T, left, precision=mid_precision)


def on_device(
    grid_in,
    target,
    noise_level,
    land_mask,
    neighbours,
    halo_send,
    g2m,
    m2g,
    legendre,
    w_attn,
    w_mlp,
    w_small,
    mom_attn,
    mom_mlp,
    m_small,
    v_small,
    ema_attn,
    ema_mlp,
    ema_small,
):
    cin = grid_in.shape[-1]
    lat_rows, lon_count, channels = target.shape[1:]
    modes, degrees = legendre.shape[1:]
    rows = neighbours.shape[0]
    halo_rows = halo_send.shape[0]
    pixels = m2g.shape[0]
    width = w_attn.shape[1]
    both = ("node", "zero")

    attn_full = lax.all_gather(w_attn.astype(bf16), both, axis=0, tiled=True)
    mlp_full = lax.all_gather(w_mlp.astype(bf16), both, axis=0, tiled=True)
    small_full = lax.all_gather(w_small.astype(bf16), both, axis=0, tiled=True)
    half = mlp_full.shape[0] // 2
    w_query, w_output = attn_full[: 3 * width], attn_full[3 * width :]
    w_upper, w_down = mlp_full[:half], mlp_full[half:]
    w_enc = small_full[:cin]
    w_dec = small_full[cin : cin + channels]
    w_cond = small_full[cin + channels :].reshape(4, -1, width)

    enc_count = (counted(g2m, pixels) * (1.0 / g2m.shape[1])).astype(bf16)
    dec_count = counted(m2g, rows).astype(bf16)
    near_count = counted(neighbours, rows + 2 * halo_rows)
    near_low = near_count.astype(bf16)
    lend = (halo_send[:, None] == jnp.arange(rows, dtype=halo_send.dtype)).astype(bf16)

    sigma, c_input, c_skip, c_output, loss_weight = noise_scalars(noise_level[0])
    scale_input = jnp.where(jnp.arange(cin) < channels, c_input, 1.0)
    inputs = (grid_in[0].reshape(-1, cin).astype(f32) * scale_input).astype(bf16)
    mixed_high, mixed_low = split(dot_nn(enc_count, inputs))
    stream_in = dot_nn(mixed_high, w_enc) + dot_nn(mixed_low, w_enc)
    features = noise_features(sigma).astype(bf16)
    modulation = jnp.einsum("f,jfd->jd", features, w_cond, preferred_element_type=f32)

    unit_one, inverse_one = normed(stream_in)
    first = (unit_one * (1.0 + modulation[0]) + modulation[1]).astype(bf16)
    packed = dot_nt(first, w_query).astype(bf16)
    queries, pairs = packed[:, :width], packed[:, width:]
    lent = dot_nn(lend, pairs).astype(bf16)
    extended = jnp.concatenate(
        [pairs, passed_along(lent, "node", 1), passed_along(lent, "node", -1)], axis=0
    )
    keys, values = heads_of(extended[:, :width]), heads_of(extended[:, width:])
    query_heads = heads_of(queries)
    score_scale = query_heads[0].shape[-1] ** (-0.5)
    present = near_count > 0.0
    probs, probs_low, blended = [], [], []
    for head in range(HEAD_COUNT):
        logits = jnp.where(present, dot_nt(query_heads[head], keys[head]) * score_scale, -jnp.inf)
        raised = jnp.exp(logits - jnp.max(logits, axis=-1, keepdims=True))
        prob = raised / jnp.sum(raised * near_count, axis=-1, keepdims=True)
        low = (prob.astype(bf16).astype(f32) * near_count).astype(bf16)
        probs.append(prob)
        probs_low.append(low)
        blended.append(dot_nn(low, values[head]))
    blended = jnp.concatenate(blended, axis=1).astype(bf16)
    stream_mid = stream_in + dot_nt(blended, w_output)

    unit_two, inverse_two = normed(stream_mid)
    second = (unit_two * (1.0 + modulation[2]) + modulation[3]).astype(bf16)
    upper = dot_nt(second, w_upper)
    activ = jax.nn.gelu(upper).astype(bf16)
    stream_out = stream_mid + dot_nn(activ, w_down)

    out_high, out_low = split(stream_out)
    node_high, node_low = split(dot_nt(out_high, w_dec) + dot_nt(out_low, w_dec))
    third = 1.0 / m2g.shape[1]
    network = (dot_nn(dec_count, node_high) + dot_nn(dec_count, node_low)) * third

    keep_mask = 1.0 - land_mask.astype(f32)[:, :, None] * (
        jnp.arange(channels) == channels - 1
    ).astype(f32)
    predicted = c_skip * grid_in[0, :, :, :channels].astype(f32) + c_output * network.reshape(
        lat_rows, lon_count, channels
    )
    error = (predicted - target[0]) * keep_mask
    cosine, sine = turn_tables(lon_count, modes)
    tables = jnp.stack([jnp.asarray(cosine), jnp.asarray(sine)])
    parts = jnp.einsum("tnc,rnm->rtcm", error, tables, precision=mid_precision)
    weight = loss_weight / (2 * modes * degrees * channels)
    all_parts = lax.all_gather(parts.astype(bf16), "node", axis=1, tiled=True)
    all_legendre = lax.all_gather(legendre, "node", axis=0, tiled=True)
    kernel = jnp.einsum("tml,uml->tum", legendre, all_legendre, precision=top_precision)
    grad_parts = jnp.sum(kernel[None, :, :, None, :] * all_parts[:, None].astype(f32), axis=2)
    loss_here = weight * jnp.sum(grad_parts * parts)
    grad_error = jnp.einsum(
        "rtcm,rnm->tnc", grad_parts * (2.0 * weight), tables, precision=mid_precision
    )
    grad_network = (
        (grad_error * keep_mask * c_output).reshape(lat_rows * lon_count, channels).astype(bf16)
    )

    grad_nodes = dot_tn(dec_count, grad_network) * third
    grad_nodes_high, grad_nodes_low = split(grad_nodes)
    g_dec = dot_tn(grad_nodes_high, out_high)
    grad_out = dot_nn(grad_nodes_high, w_dec) + dot_nn(grad_nodes_low, w_dec)
    grad_branch = grad_out.astype(bf16)
    g_down = dot_tn(activ, grad_branch)
    grad_activ = dot_nt(grad_branch, w_down)
    gelu_value, gelu_back = jax.vjp(jax.nn.gelu, upper)
    grad_upper = gelu_back(grad_activ)[0].astype(bf16)
    g_upper = dot_tn(grad_upper, second)
    grad_second = dot_nn(grad_upper, w_upper)
    back_two, gain_two, bias_two = normed_back(grad_second, unit_two, inverse_two, modulation[2])
    grad_mid = grad_out + back_two
    grad_attn = grad_mid.astype(bf16)
    g_output = dot_tn(grad_attn, blended)
    grad_blended = heads_of(dot_nn(grad_attn, w_output).astype(bf16))
    grad_q, grad_k, grad_v = [], [], []
    for head in range(HEAD_COUNT):
        grad_prob = dot_nt(grad_blended[head], values[head])
        prob = probs[head]
        mean = jnp.sum(prob * near_count * grad_prob, axis=-1, keepdims=True)
        grad_logit = (prob * (grad_prob - mean)).astype(bf16).astype(f32)
        grad_logit = (grad_logit * near_count).astype(bf16)
        grad_q.append(dot_nn(grad_logit, keys[head]) * score_scale)
        grad_k.append(dot_tn(grad_logit, query_heads[head]) * score_scale)
        grad_v.append(dot_tn(probs_low[head], grad_blended[head]))
    grad_queries = jnp.concatenate(grad_q, axis=1)
    grad_extended = jnp.concatenate(grad_k + grad_v, axis=1)
    from_upper = passed_along(grad_extended[rows : rows + halo_rows].astype(bf16), "node", -1)
    from_lower = passed_along(grad_extended[rows + halo_rows :].astype(bf16), "node", 1)
    grad_pairs = grad_extended[:rows] + dot_tn(lend, from_upper) + dot_tn(lend, from_lower)
    grad_packed = jnp.concatenate([grad_queries, grad_pairs], axis=-1).astype(bf16)
    g_query = dot_tn(grad_packed, first)
    grad_first = dot_nn(grad_packed, w_query)
    back_one, gain_one, bias_one = normed_back(grad_first, unit_one, inverse_one, modulation[0])
    grad_in = (grad_mid + back_one).astype(bf16)
    grad_modulation = jnp.stack([gain_one, bias_one, gain_two, bias_two])
    g_cond = jnp.einsum("f,jd->jfd", features.astype(f32), grad_modulation).reshape(-1, width)
    g_enc = dot_tn(mixed_high, grad_in) + dot_tn(mixed_low, grad_in)

    local = (
        jnp.concatenate([g_query, g_output], axis=0),
        jnp.concatenate([g_upper, g_down], axis=0),
        jnp.concatenate([g_enc, g_dec, g_cond], axis=0),
    )
    g_attn, g_mlp = [
        lax.psum_scatter(item.astype(bf16), both, scatter_dimension=0, tiled=True).astype(f32)
        for item in local[:2]
    ]
    g_small = lax.psum_scatter(local[2], both, scatter_dimension=0, tiled=True)

    squares = jnp.sum(g_attn * g_attn) + jnp.sum(g_mlp * g_mlp) + jnp.sum(g_small * g_small)
    total_sq, loss = lax.psum((squares, loss_here), both)
    clip_norm = jnp.sqrt(total_sq)
    factor = jnp.minimum(1.0, clip_limit / clip_norm)
    moment_attn = moment_decay * mom_attn + factor * g_attn
    moment_mlp = moment_decay * mom_mlp + factor * g_mlp

    flat_index = lax.axis_index(both)
    full_rows = lax.axis_size(both)
    attn_upper = (flat_index * w_attn.shape[0] >= 3 * width).astype(f32)
    mlp_upper = (flat_index * w_mlp.shape[0] >= half).astype(f32)
    attn_all = lax.all_gather(moment_attn.astype(bf16), both, axis=0, tiled=True)
    mlp_all = lax.all_gather(moment_mlp.astype(bf16), both, axis=0, tiled=True)
    gram_attn = jnp.where(
        attn_upper > 0.5,
        dot_tn(attn_all[3 * width :], attn_all[3 * width :]),
        dot_tn(attn_all[: 3 * width], attn_all[: 3 * width]),
    )
    mlp_mine = jnp.where(mlp_upper > 0.5, mlp_all[half:], mlp_all[:half])
    gram_mlp = dot_tn(mlp_mine, mlp_mine)
    attn_factor = jnp.where(attn_upper > 0.5, 0.2 * math.sqrt(width), 0.2 * math.sqrt(3 * width))
    mlp_factor = 0.2 * math.sqrt(max(half, width))
    new_attn = w_attn - orthogonal_rate * attn_factor * ns_apply(gram_attn, moment_attn)
    new_mlp = w_mlp - orthogonal_rate * mlp_factor * ns_apply(gram_mlp, moment_mlp)
    clipped = factor * g_small
    first_small = adam_first * m_small + (1.0 - adam_first) * clipped
    second_small = adam_second * v_small + (1.0 - adam_second) * clipped * clipped
    new_small = w_small - adam_rate * (first_small / (1.0 - adam_first**STEP)) / (
        jnp.sqrt(second_small / (1.0 - adam_second**STEP)) + adam_epsilon
    )
    return (
        loss,
        clip_norm,
        new_attn,
        new_mlp,
        new_small,
        moment_attn,
        moment_mlp,
        first_small,
        second_small,
        average_decay * ema_attn + (1.0 - average_decay) * new_attn,
        average_decay * ema_mlp + (1.0 - average_decay) * new_mlp,
        average_decay * ema_small + (1.0 - average_decay) * new_small,
    )


def solution(mesh):
    split_rows = P(("node", "zero"), None)
    return jax.shard_map(
        on_device,
        mesh=mesh,
        in_specs=(
            P("zero", "node", None, None),
            P("zero", "node", None, None),
            P("zero"),
            P("node", None),
            P("node", None),
            P("node"),
            P("node", None),
            P("node", None),
            P("node", None, None),
        )
        + (split_rows,) * 10,
        out_specs=(P(), P()) + (split_rows,) * 10,
        check_vma=False,
    )
```

```python
import math

import jax
import jax.numpy as jnp
import numpy as np
from jax import lax
from jax.experimental import pallas as pl
from jax.experimental.pallas import tpu as pltpu
from jax.sharding import PartitionSpec as P

HEAD_COUNT = 4
NOISE_FEATS = 42
LEVELS = 16
NS_ITERS = 3
STEP = 10

top_precision = lax.Precision.HIGHEST
mid_precision = lax.Precision.HIGH
norm_epsilon = 1e-05
trace_epsilon = 1e-12
clip_limit = 1.0
moment_decay = 0.95
orthogonal_rate = 0.1
adam_first = 0.9
adam_second = 0.95
adam_rate = 0.02
adam_epsilon = 1e-08
average_decay = 0.9
newton_first = 3.4445
newton_second = -4.775
newton_third = 2.0315
sigma_lowest = 0.1
sigma_highest = 20.0
f32 = jnp.float32
bf16 = jnp.bfloat16


MESH = pl.DeviceIdType.MESH
ROW_CHUNK = 16


class Place:
    def __init__(self, nodes, zeros):
        self.uppers, self.cores = nodes // 2, 2
        self.nears = 2 if zeros < 16 else 4
        self.fars = zeros // self.nears
        self.mates = max(self.uppers // 2, 1)
        self.zeros = zeros

    def locate(self):
        node, zero = lax.axis_index("node"), lax.axis_index("zero")
        self.upper, self.core = node // 2, node % 2
        self.far, self.near = zero // self.nears, zero % self.nears

    def moved(self, upper=0, core=0, far=0, near=0, mate=0):
        row = lax.rem(self.upper + upper, self.uppers) if upper else self.upper
        if mate:
            group = self.upper // self.mates * self.mates
            row = group + lax.rem(self.upper - group + mate, self.mates)
        return (
            row,
            1 - self.core if core else self.core,
            lax.rem(self.far + far, self.fars) if far else self.far,
            lax.rem(self.near + near, self.nears) if near else self.near,
        )

    def device(self, **steps):
        upper, core, far, near = self.moved(**steps)
        return (upper * 2 + core, far * self.nears + near)

    def slot(self, upper, core, far, near):
        return (upper * 2 + core) * self.zeros + far * self.nears + near

    def peers(self):
        return (
            [dict(far=k) for k in range(1, self.fars)]
            + [dict(near=j) for j in range(1, self.nears)]
            + [dict(upper=i) for i in range(1, self.uppers)]
            + [dict(core=1)]
        )

    def greet(self):
        barrier = pltpu.get_barrier_semaphore()
        for steps in self.peers():
            pl.semaphore_signal(barrier, 1, device_id=self.device(**steps), device_id_type=MESH)
        pl.semaphore_wait(barrier, len(self.peers()))


def half_rows(rows):
    return (rows // 2 + 15) // 16 * 16


def gather_body(place, shard, out, own_sem, far_sem, near_sem, upper_sem, over_sem, under_sem, core_sem):
    rows = shard.shape[0]
    head = half_rows(rows)
    parts = (pl.ds(0, head), pl.ds(head, rows - head))
    fars, nears, uppers = place.fars, place.nears, place.uppers
    here = place.slot(*place.moved())
    kept = pltpu.make_async_copy(shard, out.at[here], own_sem)
    kept.start()
    started = []

    def send(source, target, sems, **steps):
        copy = pltpu.make_async_remote_copy(
            src_ref=source,
            dst_ref=target,
            send_sem=sems.at[0],
            recv_sem=sems.at[1],
            device_id=place.device(**steps),
            device_id_type=MESH,
        )
        copy.start()
        started.append(copy)
        return copy

    def block(upper=0, far=0, near=0):
        return out.at[place.slot(*place.moved(upper=upper, far=far, near=near))]

    def back(steps, size):
        return (size - steps) % size

    far_copies = {}
    for k in range(1, fars):
        far_copies[k] = send(shard, out.at[here], far_sem.at[k], far=k)
    near_copies, upper_copies, over, under, cores = {}, {}, {}, {}, []

    def first(k):
        if k:
            far_copies[k].wait_recv()
        target = block(far=back(k, fars))
        source = target if k else shard
        for j in range(1, nears):
            near_copies[k, j] = send(source, target, near_sem.at[k, j], near=j)
        for i in range(1, uppers):
            upper_copies[k, i] = send(source, target, upper_sem.at[k, i], upper=i)
        cores.append(send(source, target, core_sem.at[k, 0, 0], core=1))

    def second(k):
        for j in range(1, nears):
            near_copies[k, j].wait_recv()
            item = block(far=back(k, fars), near=back(j, nears))
            for i in range(1, uppers):
                over[k, j, i] = send(
                    item.at[parts[0]], item.at[parts[0]], over_sem.at[k, j, i], upper=i
                )
            cores.append(send(item, item, core_sem.at[k, j, 0], core=1))
        for i in range(1, uppers):
            upper_copies[k, i].wait_recv()
            item = block(far=back(k, fars), upper=back(i, uppers))
            for j in range(1, nears):
                under[k, j, i] = send(
                    item.at[parts[1]], item.at[parts[1]], under_sem.at[k, j, i], near=j
                )
            cores.append(send(item, item, core_sem.at[k, 0, i], core=1))

    def third(k):
        for j in range(1, nears):
            for i in range(1, uppers):
                over[k, j, i].wait_recv()
                under[k, j, i].wait_recv()
                item = block(far=back(k, fars), near=back(j, nears), upper=back(i, uppers))
                cores.append(send(item, item, core_sem.at[k, j, i], core=1))

    for k in range(fars + 2):
        if k < fars:
            first(k)
        if 1 <= k <= fars:
            second(k - 1)
        if k >= 2:
            third(k - 2)
    kept.wait()
    for copy in cores:
        copy.wait_recv()
    for copy in started:
        copy.wait_send()


def gather_sems(place):
    dma = pltpu.SemaphoreType.DMA
    fars, nears, uppers = place.fars, place.nears, place.uppers
    return [
        dma,
        dma((fars, 2)),
        dma((fars, nears, 2)),
        dma((fars, uppers, 2)),
        dma((fars, nears, uppers, 2)),
        dma((fars, nears, uppers, 2)),
        dma((fars, nears, uppers, 2)),
    ]


def gather_weights(nodes, zeros, w_attn, w_mlp, w_small, collective):
    place = Place(nodes, zeros)
    sizes = [w.shape[0] for w in (w_attn, w_mlp, w_small)]
    rows = -(-sum(sizes) // 16) * 16
    width = w_attn.shape[1]

    def kernel(attn_ref, mlp_ref, small_ref, out_ref, shard, *sems):
        place.locate()
        start = 0
        for ref, size in zip((attn_ref, mlp_ref, small_ref), sizes):
            shard[pl.ds(start, size)] = ref[...].astype(bf16)
            start += size
        place.greet()
        gather_body(place, shard, out_ref, *sems)

    return pl.pallas_call(
        kernel,
        out_shape=jax.ShapeDtypeStruct((nodes * zeros, rows, width), bf16),
        in_specs=[pl.BlockSpec(memory_space=pltpu.VMEM)] * 3,
        out_specs=pl.BlockSpec(memory_space=pl.ANY),
        scratch_shapes=[pltpu.VMEM((rows, width), bf16)] + gather_sems(place),
        compiler_params=pltpu.CompilerParams(
            collective_id=collective, has_side_effects=True, vmem_limit_bytes=48 << 20
        ),
    )(w_attn, w_mlp, w_small)


def scatter_body(place, grads, own, bufs, sems):
    (core_in, over_out, over_in, under_out, under_in, over_out2, over_in2, under_out2, under_in2, far_out, far_in) = bufs
    (core_sem, over_sem, under_sem, over_sem2, under_sem2, far_sem) = sems
    rows = grads.shape[1]
    head = half_rows(rows)
    tail = rows - head
    fars, nears, uppers = place.fars, place.nears, place.uppers
    started = []

    def send(source, target, sem, **steps):
        copy = pltpu.make_async_remote_copy(
            src_ref=source,
            dst_ref=target,
            send_sem=sem.at[0],
            recv_sem=sem.at[1],
            device_id=place.device(**steps),
            device_id_type=MESH,
        )
        copy.start()
        started.append(copy)
        return copy

    def add(target, sources, count):
        @pl.loop(0, count // ROW_CHUNK)
        def _(index):
            spot = pl.ds(pl.multiple_of(index * ROW_CHUNK, ROW_CHUNK), ROW_CHUNK)
            total = sources[0][spot].astype(f32)
            for source in sources[1:]:
                total += source[spot].astype(f32)
            target[spot] = total.astype(target.dtype)

    order = list(range(1, fars)) + [0]
    core_copies = {}
    other = 1 - place.core
    for k in order:
        far = place.moved(far=k)[2]
        for i in range(uppers):
            first = place.slot(i, other, far, 0)
            core_copies[k, i] = send(
                grads.at[pl.ds(first, nears)], core_in.at[k, i], core_sem.at[k, i], core=1
            )

    over, under, over2, under2, far_copies = {}, {}, {}, {}, {}

    def pair(k, upper, near, part):
        far = place.moved(far=k)[2]
        return [
            grads.at[place.slot(upper, place.core, far, near), part],
            core_in.at[k, upper, near, part],
        ]

    top, low = pl.ds(0, head), pl.ds(head, tail)

    def one(k):
        for i in range(uppers):
            core_copies[k, i].wait_recv()
        for i in range(1, uppers):
            for near in range(nears):
                add(over_out.at[k, i, near], pair(k, place.moved(upper=i)[0], near, top), head)
            over[k, i] = send(over_out.at[k, i], over_in.at[k, i], over_sem.at[k, i], upper=i)
        for j in range(1, nears):
            for upper in range(uppers):
                add(under_out.at[k, j, upper], pair(k, upper, place.moved(near=j)[3], low), tail)
            under[k, j] = send(under_out.at[k, j], under_in.at[k, j], under_sem.at[k, j], near=j)

    def top_sum(k, near):
        return pair(k, place.upper, near, top) + [
            over_in.at[k, i, near] for i in range(1, uppers)
        ]

    def low_sum(k, upper):
        return pair(k, upper, place.near, low) + [
            under_in.at[k, j, upper] for j in range(1, nears)
        ]

    def two(k):
        for i in range(1, uppers):
            over[k, i].wait_recv()
        for j in range(1, nears):
            add(over_out2.at[k, j], top_sum(k, place.moved(near=j)[3]), head)
            over2[k, j] = send(over_out2.at[k, j], over_in2.at[k, j], over_sem2.at[k, j], near=j)
        for j in range(1, nears):
            under[k, j].wait_recv()
        for i in range(1, uppers):
            add(under_out2.at[k, i], low_sum(k, place.moved(upper=i)[0]), tail)
            under2[k, i] = send(
                under_out2.at[k, i], under_in2.at[k, i], under_sem2.at[k, i], upper=i
            )

    def ready(k):
        for j in range(1, nears):
            over2[k, j].wait_recv()
        for i in range(1, uppers):
            under2[k, i].wait_recv()
        return (
            top_sum(k, place.near) + [over_in2.at[k, j] for j in range(1, nears)],
            low_sum(k, place.upper) + [under_in2.at[k, i] for i in range(1, uppers)],
        )

    def three(k):
        tops, lows = ready(k)
        add(far_out.at[k, top], tops, head)
        add(far_out.at[k, low], lows, tail)
        far_copies[k] = send(far_out.at[k], far_in.at[k], far_sem.at[k], far=k)

    for step in range(fars + 2):
        if step < fars:
            one(order[step])
        if 1 <= step <= fars:
            two(order[step - 1])
        if 2 <= step and order[step - 2]:
            three(order[step - 2])
    tops, lows = ready(0)
    for k in range(1, fars):
        far_copies[k].wait_recv()
    add(own.at[top], tops + [far_in.at[k, top] for k in range(1, fars)], head)
    add(own.at[low], lows + [far_in.at[k, low] for k in range(1, fars)], tail)
    for copy in started:
        copy.wait_send()


def scatter_scratch(place, rows, width):
    fars, nears, uppers = place.fars, place.nears, place.uppers
    head = half_rows(rows)
    tail = rows - head
    vmem = lambda *shape: pltpu.VMEM(shape + (width,), bf16)
    dma = pltpu.SemaphoreType.DMA
    bufs = [vmem(fars, uppers, nears, rows)]
    bufs += [vmem(fars, uppers, nears, head)] * 2
    bufs += [vmem(fars, nears, uppers, tail)] * 2
    bufs += [vmem(fars, nears, head)] * 2
    bufs += [vmem(fars, uppers, tail)] * 2
    bufs += [vmem(fars, rows)] * 2
    sems = [
        dma((fars, uppers, 2)),
        dma((fars, uppers, 2)),
        dma((fars, nears, 2)),
        dma((fars, nears, 2)),
        dma((fars, uppers, 2)),
        dma((fars, 2)),
    ]
    return bufs, sems


def sixteens(rows):
    return -(-rows // 16) * 16


def moment_gather_body(place, shard, out, low, own_sem, far_sem, near_sem, upper_sem, mate_sem, core_sem):
    rows = shard.shape[0]
    fars, nears, uppers, mates = place.fars, place.nears, place.uppers, place.mates
    base, rest = pl.ds(0, low), pl.ds(low, rows - low)
    here = place.slot(*place.moved())
    kept = pltpu.make_async_copy(shard, out.at[here], own_sem)
    kept.start()
    started, cores = [], []

    def send(source, target, sems, **steps):
        copy = pltpu.make_async_remote_copy(
            src_ref=source,
            dst_ref=target,
            send_sem=sems.at[0],
            recv_sem=sems.at[1],
            device_id=place.device(**steps),
            device_id_type=MESH,
        )
        copy.start()
        started.append(copy)
        return copy

    def block(**steps):
        return out.at[place.slot(*place.moved(**steps))]

    far_copies, near_copies, upper_copies, mate_copies = {}, {}, {}, {}
    for k in range(1, fars):
        far_copies[k] = send(shard, out.at[here], far_sem.at[k], far=k)

    def spread(k, j, source, target):
        for i in range(1, uppers):
            upper_copies[k, j, i] = send(
                source.at[base], target.at[base], upper_sem.at[k, j, i], upper=i
            )
        for i in range(1, mates):
            mate_copies[k, j, i] = send(
                source.at[rest], target.at[rest], mate_sem.at[k, j, i], mate=i
            )
        cores.append(send(source, target, core_sem.at[k, j, 0, 0], core=1))

    def first(k):
        if k:
            far_copies[k].wait_recv()
        target = block(far=(fars - k) % fars)
        source = target if k else shard
        for j in range(1, nears):
            near_copies[k, j] = send(source, target, near_sem.at[k, j], near=j)
        spread(k, 0, source, target)

    def second(k):
        for j in range(1, nears):
            near_copies[k, j].wait_recv()
            item = block(far=(fars - k) % fars, near=nears - j)
            spread(k, j, item, item)

    def third(k):
        for j in range(nears):
            steps = dict(far=(fars - k) % fars, near=(nears - j) % nears)
            for i in range(1, uppers):
                upper_copies[k, j, i].wait_recv()
                item = block(upper=uppers - i, **steps).at[base]
                cores.append(send(item, item, core_sem.at[k, j, i, 0], core=1))
            for i in range(1, mates):
                mate_copies[k, j, i].wait_recv()
                item = block(mate=mates - i, **steps).at[rest]
                cores.append(send(item, item, core_sem.at[k, j, i, 1], core=1))

    for k in range(fars + 2):
        if k < fars:
            first(k)
        if 1 <= k <= fars:
            second(k - 1)
        if k >= 2:
            third(k - 2)
    kept.wait()
    for copy in cores:
        copy.wait_recv()
    for copy in started:
        copy.wait_send()


def moment_gather_sems(place):
    dma = pltpu.SemaphoreType.DMA
    fars, nears, uppers, mates = place.fars, place.nears, place.uppers, place.mates
    return [
        dma,
        dma((fars, 2)),
        dma((fars, nears, 2)),
        dma((fars, nears, uppers, 2)),
        dma((fars, nears, max(mates, 2), 2)),
        dma((fars, nears, uppers, 2, 2)),
    ]


def total_body(place, tile, slots, sems):
    value = tile
    upper, core, far, near = place.moved()
    stages = (
        (dict(core=1), 2, core),
        (dict(near=1), place.nears, near),
        (dict(upper=1), place.uppers, upper),
        (dict(far=1), place.fars, far),
    )
    for stage, (axis, size, mine) in enumerate(stages):
        name = list(axis)[0]
        slots[stage, mine] = value
        copies = []
        for step in range(1, size):
            copy = pltpu.make_async_remote_copy(
                src_ref=slots.at[stage, mine],
                dst_ref=slots.at[stage, mine],
                send_sem=sems.at[stage, step, 0],
                recv_sem=sems.at[stage, step, 1],
                device_id=place.device(**{name: step}),
                device_id_type=MESH,
            )
            copy.start()
            copies.append(copy)
        for copy in copies:
            copy.wait()
        value = slots[stage, 0]
        for other in range(1, size):
            value = value + slots[stage, other]
    return value


def reduce_and_gather(nodes, zeros, grads, loss_tile, mom_attn, mom_mlp, small_rows, collective):
    place = Place(nodes, zeros)
    devices, rows, width = grads.shape
    attn_rows, mlp_rows = mom_attn.shape[0], mom_mlp.shape[0]
    low = sixteens(attn_rows)
    moment_rows = low + sixteens(mlp_rows)
    bufs, sems = scatter_scratch(place, rows, width)
    total_sems = [
        pltpu.VMEM((4, max(place.fars, place.uppers, place.nears, 2), 8, 128), f32),
        pltpu.SemaphoreType.DMA((4, max(place.fars, place.uppers, place.nears, 2), 2)),
    ]
    moment_sems = moment_gather_sems(place)

    def kernel(
        grads_ref, loss_ref, attn_ref, mlp_ref, small_out, attn_out, mlp_out, total_out, all_out,
        own, shard, *scratch,
    ):
        place.locate()
        place.greet()
        first = len(bufs)
        second = first + len(sems)
        scatter_body(place, grads_ref, own, scratch[:first], scratch[first:second])
        g_attn = own[pl.ds(0, attn_rows)]
        g_mlp = own[pl.ds(attn_rows, mlp_rows)]
        start = attn_rows + mlp_rows
        g_small = own[pl.ds(start, small_rows)] + own[pl.ds(start + small_rows, small_rows)]
        small_out[...] = g_small
        squares = jnp.sum(g_attn * g_attn) + jnp.sum(g_mlp * g_mlp) + jnp.sum(g_small * g_small)
        row = lax.broadcasted_iota(jnp.int32, (8, 128), 0)
        tile = jnp.where(row < 4, squares, loss_ref[...])
        slots, slot_sems = scratch[second : second + 2]
        total = total_body(place, tile, slots, slot_sems)
        total_out[...] = total
        factor = jnp.minimum(1.0, clip_limit * lax.rsqrt(total[0:1, 0:1]))
        new_attn = moment_decay * attn_ref[...] + factor * g_attn
        new_mlp = moment_decay * mlp_ref[...] + factor * g_mlp
        attn_out[...] = new_attn
        mlp_out[...] = new_mlp
        shard[pl.ds(0, attn_rows)] = new_attn.astype(bf16)
        shard[pl.ds(low, mlp_rows)] = new_mlp.astype(bf16)
        moment_gather_body(place, shard, all_out, low, *scratch[second + 2 :])

    vmem = pl.BlockSpec(memory_space=pltpu.VMEM)
    return pl.pallas_call(
        kernel,
        out_shape=(
            jax.ShapeDtypeStruct((small_rows, width), f32),
            jax.ShapeDtypeStruct((attn_rows, width), f32),
            jax.ShapeDtypeStruct((mlp_rows, width), f32),
            jax.ShapeDtypeStruct((8, 128), f32),
            jax.ShapeDtypeStruct((devices, moment_rows, width), bf16),
        ),
        in_specs=[vmem] * 4,
        out_specs=(vmem, vmem, vmem, vmem, pl.BlockSpec(memory_space=pl.ANY)),
        scratch_shapes=[pltpu.VMEM((rows, width), f32), pltpu.VMEM((moment_rows, width), bf16)]
        + bufs
        + sems
        + total_sems
        + moment_sems,
        compiler_params=pltpu.CompilerParams(
            collective_id=collective, has_side_effects=True, vmem_limit_bytes=56 << 20
        ),
    )(grads, loss_tile, mom_attn, mom_mlp)


def noise_scalars(level):
    sigma = sigma_lowest * (sigma_highest / sigma_lowest) ** (level.astype(f32) / (LEVELS - 1))
    total = sigma * sigma + 1.0
    return (sigma, lax.rsqrt(total), 1.0 / total, sigma * lax.rsqrt(total), total / (sigma * sigma))


def noise_features(sigma):
    half_count = NOISE_FEATS // 2
    frequency = jnp.exp(jnp.arange(half_count).astype(f32) * (3.0 / half_count))
    phases = 0.25 * jnp.log(sigma) * frequency
    return jnp.concatenate([jnp.sin(phases), jnp.cos(phases)])


def normed(rows):
    centred = rows - jnp.mean(rows, axis=-1, keepdims=True)
    spread = jnp.mean(centred * centred, axis=-1, keepdims=True)
    inverse = lax.rsqrt(spread + norm_epsilon)
    return centred * inverse, inverse


def normed_back(grad, unit, inverse, gain):
    scaled = grad * (1.0 + gain)
    back = inverse * (
        scaled
        - jnp.mean(scaled, axis=-1, keepdims=True)
        - unit * jnp.mean(scaled * unit, axis=-1, keepdims=True)
    )
    return back, jnp.sum(grad * unit, axis=0), jnp.sum(grad, axis=0)


def dot(left, right, contract):
    return lax.dot_general(left, right, (contract, ((), ())), preferred_element_type=f32)


def dot_nn(left, right):
    return dot(left, right, ((1,), (0,)))


def dot_nt(left, right):
    return dot(left, right, ((1,), (1,)))


def dot_tn(left, right):
    return dot(left, right, ((0,), (0,)))


def split(value):
    high = value.astype(bf16)
    return high, (value - high.astype(f32)).astype(bf16)


def counted(index, size):
    hits = index[:, :, None] == jnp.arange(size, dtype=index.dtype)
    return jnp.sum(hits.astype(f32), axis=1)


def passed_along(value, axis, steps):
    count = lax.axis_size(axis)
    pairs = [(source, (source + steps) % count) for source in range(count)]
    return lax.ppermute(value, axis, pairs)


def turn_tables(lon_count, modes):
    turns = np.arange(lon_count)[:, None] * np.arange(modes)[None, :] % lon_count
    phases = turns * (2.0 * np.pi / lon_count)
    return np.cos(phases).astype(np.float32), -np.sin(phases).astype(np.float32)


def heads_of(rows):
    return [rows[:, i * 128 : (i + 1) * 128] for i in range(HEAD_COUNT)]


def ns_apply(gram_matrix, moment):
    score_scale = lax.rsqrt(jnp.trace(gram_matrix) + trace_epsilon)
    current = gram_matrix * (score_scale * score_scale)
    identity = jnp.eye(gram_matrix.shape[0], dtype=f32)
    result = moment * score_scale
    for iteration in range(NS_ITERS):
        squared = jnp.dot(current, current, precision=mid_precision)
        polynomial = newton_first * identity + newton_second * current + newton_third * squared
        result = jnp.dot(result, polynomial, precision=mid_precision)
        if iteration + 1 < NS_ITERS:
            current = jnp.dot(
                jnp.dot(polynomial, current, precision=mid_precision),
                polynomial,
                precision=mid_precision,
            )
    return result


def gram_of(left):
    return jnp.dot(left.T, left, precision=mid_precision)


def on_device(
    grid_in,
    target,
    noise_level,
    land_mask,
    neighbours,
    halo_send,
    g2m,
    m2g,
    legendre,
    w_attn,
    w_mlp,
    w_small,
    mom_attn,
    mom_mlp,
    m_small,
    v_small,
    ema_attn,
    ema_mlp,
    ema_small,
):
    cin = grid_in.shape[-1]
    lat_rows, lon_count, channels = target.shape[1:]
    modes, degrees = legendre.shape[1:]
    rows = neighbours.shape[0]
    halo_rows = halo_send.shape[0]
    pixels = m2g.shape[0]
    width = w_attn.shape[1]
    both = ("node", "zero")

    nodes, zeros = lax.axis_size("node"), lax.axis_size("zero")
    devices = nodes * zeros
    attn_rows, mlp_rows, small_rows = w_attn.shape[0], w_mlp.shape[0], w_small.shape[0]
    gathered = gather_weights(nodes, zeros, w_attn, w_mlp, w_small, 1)
    start = attn_rows + mlp_rows
    attn_full = gathered[:, :attn_rows].reshape(-1, width)
    mlp_full = gathered[:, attn_rows:start].reshape(-1, width)
    small_full = gathered[:, start : start + small_rows].reshape(-1, width)
    half = mlp_full.shape[0] // 2
    w_query, w_output = attn_full[: 3 * width], attn_full[3 * width :]
    w_upper, w_down = mlp_full[:half], mlp_full[half:]
    w_enc = small_full[:cin]
    w_dec = small_full[cin : cin + channels]
    w_cond = small_full[cin + channels :].reshape(4, -1, width)

    enc_count = (counted(g2m, pixels) * (1.0 / g2m.shape[1])).astype(bf16)
    dec_count = counted(m2g, rows).astype(bf16)
    near_count = counted(neighbours, rows + 2 * halo_rows)
    near_low = near_count.astype(bf16)
    lend = (halo_send[:, None] == jnp.arange(rows, dtype=halo_send.dtype)).astype(bf16)

    sigma, c_input, c_skip, c_output, loss_weight = noise_scalars(noise_level[0])
    scale_input = jnp.where(jnp.arange(cin) < channels, c_input, 1.0)
    inputs = (grid_in[0].reshape(-1, cin).astype(f32) * scale_input).astype(bf16)
    mixed_high, mixed_low = split(dot_nn(enc_count, inputs))
    stream_in = dot_nn(mixed_high, w_enc) + dot_nn(mixed_low, w_enc)
    features = noise_features(sigma).astype(bf16)
    modulation = jnp.einsum("f,jfd->jd", features, w_cond, preferred_element_type=f32)

    unit_one, inverse_one = normed(stream_in)
    first = (unit_one * (1.0 + modulation[0]) + modulation[1]).astype(bf16)
    packed = dot_nt(first, w_query).astype(bf16)
    queries, pairs = packed[:, :width], packed[:, width:]
    lent = dot_nn(lend, pairs).astype(bf16)
    extended = jnp.concatenate(
        [pairs, passed_along(lent, "node", 1), passed_along(lent, "node", -1)], axis=0
    )
    keys, values = heads_of(extended[:, :width]), heads_of(extended[:, width:])
    query_heads = heads_of(queries)
    score_scale = query_heads[0].shape[-1] ** (-0.5)
    present = near_count > 0.0
    probs, probs_low, blended = [], [], []
    for head in range(HEAD_COUNT):
        logits = jnp.where(present, dot_nt(query_heads[head], keys[head]) * score_scale, -jnp.inf)
        raised = jnp.exp(logits - jnp.max(logits, axis=-1, keepdims=True))
        prob = raised / jnp.sum(raised * near_count, axis=-1, keepdims=True)
        low = (prob.astype(bf16).astype(f32) * near_count).astype(bf16)
        probs.append(prob)
        probs_low.append(low)
        blended.append(dot_nn(low, values[head]))
    blended = jnp.concatenate(blended, axis=1).astype(bf16)
    stream_mid = stream_in + dot_nt(blended, w_output)

    unit_two, inverse_two = normed(stream_mid)
    second = (unit_two * (1.0 + modulation[2]) + modulation[3]).astype(bf16)
    upper = dot_nt(second, w_upper)
    activ = jax.nn.gelu(upper).astype(bf16)
    stream_out = stream_mid + dot_nn(activ, w_down)

    out_high, out_low = split(stream_out)
    node_high, node_low = split(dot_nt(out_high, w_dec) + dot_nt(out_low, w_dec))
    third = 1.0 / m2g.shape[1]
    network = (dot_nn(dec_count, node_high) + dot_nn(dec_count, node_low)) * third

    keep_mask = 1.0 - land_mask.astype(f32)[:, :, None] * (
        jnp.arange(channels) == channels - 1
    ).astype(f32)
    predicted = c_skip * grid_in[0, :, :, :channels].astype(f32) + c_output * network.reshape(
        lat_rows, lon_count, channels
    )
    error = (predicted - target[0]) * keep_mask
    cosine, sine = turn_tables(lon_count, modes)
    tables = jnp.stack([jnp.asarray(cosine), jnp.asarray(sine)])
    parts = jnp.einsum("tnc,rnm->rtcm", error, tables, precision=mid_precision)
    weight = loss_weight / (2 * modes * degrees * channels)
    all_parts = lax.all_gather(parts.astype(bf16), "node", axis=1, tiled=True)
    all_legendre = lax.all_gather(legendre, "node", axis=0, tiled=True)
    kernel = jnp.einsum("tml,uml->tum", legendre, all_legendre, precision=top_precision)
    grad_parts = jnp.sum(kernel[None, :, :, None, :] * all_parts[:, None].astype(f32), axis=2)
    loss_here = weight * jnp.sum(grad_parts * parts)
    grad_error = jnp.einsum(
        "rtcm,rnm->tnc", grad_parts * (2.0 * weight), tables, precision=mid_precision
    )
    grad_network = (
        (grad_error * keep_mask * c_output).reshape(lat_rows * lon_count, channels).astype(bf16)
    )

    grad_nodes = dot_tn(dec_count, grad_network) * third
    grad_nodes_high, grad_nodes_low = split(grad_nodes)
    g_dec = dot_tn(grad_nodes_high, out_high)
    grad_out = dot_nn(grad_nodes_high, w_dec) + dot_nn(grad_nodes_low, w_dec)
    grad_branch = grad_out.astype(bf16)
    g_down = dot_tn(activ, grad_branch)
    grad_activ = dot_nt(grad_branch, w_down)
    gelu_value, gelu_back = jax.vjp(jax.nn.gelu, upper)
    grad_upper = gelu_back(grad_activ)[0].astype(bf16)
    g_upper = dot_tn(grad_upper, second)
    grad_second = dot_nn(grad_upper, w_upper)
    back_two, gain_two, bias_two = normed_back(grad_second, unit_two, inverse_two, modulation[2])
    grad_mid = grad_out + back_two
    grad_attn = grad_mid.astype(bf16)
    g_output = dot_tn(grad_attn, blended)
    grad_blended = heads_of(dot_nn(grad_attn, w_output).astype(bf16))
    grad_q, grad_k, grad_v = [], [], []
    for head in range(HEAD_COUNT):
        grad_prob = dot_nt(grad_blended[head], values[head])
        prob = probs[head]
        mean = jnp.sum(prob * near_count * grad_prob, axis=-1, keepdims=True)
        grad_logit = (prob * (grad_prob - mean)).astype(bf16).astype(f32)
        grad_logit = (grad_logit * near_count).astype(bf16)
        grad_q.append(dot_nn(grad_logit, keys[head]) * score_scale)
        grad_k.append(dot_tn(grad_logit, query_heads[head]) * score_scale)
        grad_v.append(dot_tn(probs_low[head], grad_blended[head]))
    grad_queries = jnp.concatenate(grad_q, axis=1)
    grad_extended = jnp.concatenate(grad_k + grad_v, axis=1)
    from_upper = passed_along(grad_extended[rows : rows + halo_rows].astype(bf16), "node", -1)
    from_lower = passed_along(grad_extended[rows + halo_rows :].astype(bf16), "node", 1)
    grad_pairs = grad_extended[:rows] + dot_tn(lend, from_upper) + dot_tn(lend, from_lower)
    grad_packed = jnp.concatenate([grad_queries, grad_pairs], axis=-1).astype(bf16)
    g_query = dot_tn(grad_packed, first)
    grad_first = dot_nn(grad_packed, w_query)
    back_one, gain_one, bias_one = normed_back(grad_first, unit_one, inverse_one, modulation[0])
    grad_in = (grad_mid + back_one).astype(bf16)
    grad_modulation = jnp.stack([gain_one, bias_one, gain_two, bias_two])
    g_cond = jnp.einsum("f,jd->jfd", features.astype(f32), grad_modulation).reshape(-1, width)
    g_enc = dot_tn(mixed_high, grad_in) + dot_tn(mixed_low, grad_in)

    small_local = split(jnp.concatenate([g_enc, g_dec, g_cond], axis=0))
    packed_grads = [
        jnp.concatenate([g_query, g_output], axis=0).astype(bf16).reshape(devices, attn_rows, width),
        jnp.concatenate([g_upper, g_down], axis=0).astype(bf16).reshape(devices, mlp_rows, width),
        small_local[0].reshape(devices, small_rows, width),
        small_local[1].reshape(devices, small_rows, width),
    ]
    packed_rows = start + 2 * small_rows
    packed_grads.append(jnp.zeros((devices, -packed_rows % 16, width), bf16))
    local = jnp.concatenate(packed_grads, axis=1)

    g_small, moment_attn, moment_mlp, totals, moments = reduce_and_gather(
        nodes,
        zeros,
        local,
        jnp.full((8, 128), loss_here),
        mom_attn,
        mom_mlp,
        small_rows,
        2,
    )
    loss = totals[4, 0]
    clip_norm = jnp.sqrt(totals[0, 0])
    factor = jnp.minimum(1.0, clip_limit / clip_norm)

    flat_index = lax.axis_index(both)
    attn_upper = (flat_index * w_attn.shape[0] >= 3 * width).astype(f32)
    mlp_upper = (flat_index * w_mlp.shape[0] >= half).astype(f32)
    attn_all = moments[:, :attn_rows].reshape(-1, width)
    mlp_half = lax.dynamic_slice_in_dim(
        moments, jnp.where(mlp_upper > 0.5, devices // 2, 0), devices // 2, axis=0
    )
    low = sixteens(attn_rows)
    mlp_mine = mlp_half[:, low : low + mlp_rows].reshape(-1, width)
    gram_attn = jnp.where(
        attn_upper > 0.5,
        dot_tn(attn_all[3 * width :], attn_all[3 * width :]),
        dot_tn(attn_all[: 3 * width], attn_all[: 3 * width]),
    )
    gram_mlp = dot_tn(mlp_mine, mlp_mine)
    attn_factor = jnp.where(attn_upper > 0.5, 0.2 * math.sqrt(width), 0.2 * math.sqrt(3 * width))
    mlp_factor = 0.2 * math.sqrt(max(half, width))
    new_attn = w_attn - orthogonal_rate * attn_factor * ns_apply(gram_attn, moment_attn)
    new_mlp = w_mlp - orthogonal_rate * mlp_factor * ns_apply(gram_mlp, moment_mlp)
    clipped = factor * g_small
    first_small = adam_first * m_small + (1.0 - adam_first) * clipped
    second_small = adam_second * v_small + (1.0 - adam_second) * clipped * clipped
    new_small = w_small - adam_rate * (first_small / (1.0 - adam_first**STEP)) / (
        jnp.sqrt(second_small / (1.0 - adam_second**STEP)) + adam_epsilon
    )
    return (
        loss,
        clip_norm,
        new_attn,
        new_mlp,
        new_small,
        moment_attn,
        moment_mlp,
        first_small,
        second_small,
        average_decay * ema_attn + (1.0 - average_decay) * new_attn,
        average_decay * ema_mlp + (1.0 - average_decay) * new_mlp,
        average_decay * ema_small + (1.0 - average_decay) * new_small,
    )


def solution(mesh):
    split_rows = P(("node", "zero"), None)
    return jax.shard_map(
        on_device,
        mesh=mesh,
        in_specs=(
            P("zero", "node", None, None),
            P("zero", "node", None, None),
            P("zero"),
            P("node", None),
            P("node", None),
            P("node"),
            P("node", None),
            P("node", None),
            P("node", None, None),
        )
        + (split_rows,) * 10,
        out_specs=(P(), P()) + (split_rows,) * 10,
        check_vma=False,
    )
```

```python
import math

import jax
import jax.numpy as jnp
import ml_dtypes
import numpy as np
from jax import lax
from jax.experimental import pallas as pl
from jax.experimental.pallas import tpu as pltpu
from jax.sharding import PartitionSpec as P

HEAD_COUNT = 4
NOISE_FEATS = 42
LEVELS = 16
NS_ITERS = 3
STEP = 10

top_precision = lax.Precision.HIGHEST
mid_precision = lax.Precision.HIGH
norm_epsilon = 1e-05
trace_epsilon = 1e-12
clip_limit = 1.0
moment_decay = 0.95
orthogonal_rate = 0.1
adam_first = 0.9
adam_second = 0.95
adam_rate = 0.02
adam_epsilon = 1e-08
average_decay = 0.9
newton_first = 3.4445
newton_second = -4.775
newton_third = 2.0315
sigma_lowest = 0.1
sigma_highest = 20.0
gelu_scale = math.sqrt(2.0 / math.pi)
gelu_cubic = 0.044715
f32 = jnp.float32
bf16 = jnp.bfloat16


def noise_scalars(level):
    sigma = sigma_lowest * (sigma_highest / sigma_lowest) ** (level.astype(f32) / (LEVELS - 1))
    total = sigma * sigma + 1.0
    return (sigma, lax.rsqrt(total), 1.0 / total, sigma * lax.rsqrt(total), total / (sigma * sigma))


def noise_features(sigma):
    half_count = NOISE_FEATS // 2
    frequency = jnp.exp(jnp.arange(half_count).astype(f32) * (3.0 / half_count))
    phases = 0.25 * jnp.log(sigma) * frequency
    return jnp.concatenate([jnp.sin(phases), jnp.cos(phases)])


def dot(left, right, contract):
    return lax.dot_general(left, right, (contract, ((), ())), preferred_element_type=f32)


def dot_nn(left, right):
    return dot(left, right, ((1,), (0,)))


def dot_nt(left, right):
    return dot(left, right, ((1,), (1,)))


def dot_tn(left, right):
    return dot(left, right, ((0,), (0,)))


def ns_apply(gram_matrix, moment):
    score_scale = lax.rsqrt(jnp.trace(gram_matrix) + trace_epsilon)
    current = gram_matrix * (score_scale * score_scale)
    identity = jnp.eye(gram_matrix.shape[0], dtype=f32)
    result = moment * score_scale
    for iteration in range(NS_ITERS):
        squared = jnp.dot(current, current, precision=mid_precision)
        polynomial = newton_first * identity + newton_second * current + newton_third * squared
        result = jnp.dot(result, polynomial, precision=mid_precision)
        if iteration + 1 < NS_ITERS:
            current = jnp.dot(
                jnp.dot(polynomial, current, precision=mid_precision),
                polynomial,
                precision=mid_precision,
            )
    return result


MESH = pl.DeviceIdType.MESH
ROW_CHUNK = 16


class Place:
    def __init__(self, nodes, zeros):
        self.uppers, self.cores = nodes // 2, 2
        self.nears = 2 if zeros < 16 else 4
        self.fars = zeros // self.nears
        self.mates = max(self.uppers // 2, 1)
        self.zeros = zeros

    def locate(self):
        node, zero = lax.axis_index("node"), lax.axis_index("zero")
        self.upper, self.core = node // 2, node % 2
        self.far, self.near = zero // self.nears, zero % self.nears

    def moved(self, upper=0, core=0, far=0, near=0, mate=0):
        row = lax.rem(self.upper + upper, self.uppers) if upper else self.upper
        if mate:
            group = self.upper // self.mates * self.mates
            row = group + lax.rem(self.upper - group + mate, self.mates)
        return (
            row,
            1 - self.core if core else self.core,
            lax.rem(self.far + far, self.fars) if far else self.far,
            lax.rem(self.near + near, self.nears) if near else self.near,
        )

    def device(self, **steps):
        upper, core, far, near = self.moved(**steps)
        return (upper * 2 + core, far * self.nears + near)

    def slot(self, upper, core, far, near):
        return (upper * 2 + core) * self.zeros + far * self.nears + near

    def peers(self):
        return (
            [dict(far=k) for k in range(1, self.fars)]
            + [dict(near=j) for j in range(1, self.nears)]
            + [dict(upper=i) for i in range(1, self.uppers)]
            + [dict(core=1)]
        )

    def greet(self, nodes=0):
        barrier = pltpu.get_barrier_semaphore()
        peers = [self.device(**steps) for steps in self.peers() if not nodes or set(steps) <= {"far", "near"}]
        if nodes:
            node, zero = lax.axis_index("node"), lax.axis_index("zero")
            peers += [(lax.rem(node + step, nodes), zero) for step in range(1, nodes)]
        for device in peers:
            pl.semaphore_signal(barrier, 1, device_id=device, device_id_type=MESH)
        pl.semaphore_wait(barrier, len(peers))


def half_rows(rows):
    return (rows // 2 + 15) // 16 * 16


def start_copy(started, place, source, target, sems, **steps):
    copy = pltpu.make_async_remote_copy(
        src_ref=source,
        dst_ref=target,
        send_sem=sems.at[0],
        recv_sem=sems.at[1],
        device_id=place.device(**steps),
        device_id_type=MESH,
    )
    copy.start()
    started.append(copy)
    return copy


def sixteens(rows):
    return -(-rows // 16) * 16


class Pieces:
    def __init__(self, sizes, first):
        self.sizes = sizes
        total = sum(sizes)
        cut = min(half_rows(total), sizes[first])
        self.whole = [(i, 0, size) for i, size in enumerate(sizes)]
        self.head = [(first, 0, cut)]
        self.tail = [(first, cut, sizes[first] - cut)] if cut < sizes[first] else []
        self.tail += [(i, 0, size) for i, size in enumerate(sizes) if i != first]


def send_pieces(started, place, pieces, sources, targets, sems, **steps):
    copies = []
    for index, (array, start, rows) in enumerate(pieces):
        part = pl.ds(start, rows)
        copies.append(
            start_copy(
                started, place, sources[array].at[part], targets[array].at[part], sems.at[index], **steps
            )
        )
    return copies


def wait_all(copies):
    for copy in copies:
        copy.wait_recv()


class Gather:
    def __init__(self, place, pieces, shards, outs, sems):
        self.place, self.pieces, self.shards, self.outs = place, pieces, shards, outs
        (self.own_sem, self.far_sem, self.near_sem, self.upper_sem, self.over_sem, self.under_sem, self.core_sem) = sems
        self.started, self.cores = [], []
        self.far, self.near, self.upper, self.over, self.under = {}, {}, {}, {}, {}

    def block(self, **steps):
        slot = self.place.slot(*self.place.moved(**steps))
        return [out.at[slot] for out in self.outs]

    def send(self, pieces, source, target, sems, **steps):
        return send_pieces(self.started, self.place, pieces, source, target, sems, **steps)

    def begin(self):
        here = self.block()
        self.kept = []
        for index, (shard, target) in enumerate(zip(self.shards, here)):
            copy = pltpu.make_async_copy(shard, target, self.own_sem.at[index])
            copy.start()
            self.kept.append(copy)
        for k in range(1, self.place.fars):
            self.far[k] = self.send(self.pieces.whole, self.shards, here, self.far_sem.at[k], far=k)

    def first(self, k):
        place, whole = self.place, self.pieces.whole
        if k:
            wait_all(self.far[k])
        target = self.block(far=(place.fars - k) % place.fars)
        source = target if k else self.shards
        for j in range(1, place.nears):
            self.near[k, j] = self.send(whole, source, target, self.near_sem.at[k, j], near=j)
        for i in range(1, place.uppers):
            self.upper[k, i] = self.send(whole, source, target, self.upper_sem.at[k, i], upper=i)
        self.cores += self.send(whole, source, target, self.core_sem.at[k, 0, 0], core=1)

    def second(self, k):
        place, whole = self.place, self.pieces.whole
        far = (place.fars - k) % place.fars
        for j in range(1, place.nears):
            wait_all(self.near[k, j])
            item = self.block(far=far, near=place.nears - j)
            for i in range(1, place.uppers):
                self.over[k, j, i] = self.send(
                    self.pieces.head, item, item, self.over_sem.at[k, j, i], upper=i
                )
            self.cores += self.send(whole, item, item, self.core_sem.at[k, j, 0], core=1)
        for i in range(1, place.uppers):
            wait_all(self.upper[k, i])
            item = self.block(far=far, upper=place.uppers - i)
            for j in range(1, place.nears):
                self.under[k, j, i] = self.send(
                    self.pieces.tail, item, item, self.under_sem.at[k, j, i], near=j
                )
            self.cores += self.send(whole, item, item, self.core_sem.at[k, 0, i], core=1)

    def third(self, k):
        place, whole = self.place, self.pieces.whole
        far = (place.fars - k) % place.fars
        for j in range(1, place.nears):
            for i in range(1, place.uppers):
                wait_all(self.over[k, j, i])
                wait_all(self.under[k, j, i])
                item = self.block(far=far, near=place.nears - j, upper=place.uppers - i)
                self.cores += self.send(whole, item, item, self.core_sem.at[k, j, i], core=1)

    def step(self, k):
        fars = self.place.fars
        if k < fars:
            self.first(k)
        if 1 <= k <= fars:
            self.second(k - 1)
        if k >= 2:
            self.third(k - 2)

    def end(self):
        for copy in self.kept:
            copy.wait()
        wait_all(self.cores)
        for copy in self.started:
            copy.wait_send()

    @staticmethod
    def sems(place, pieces):
        dma = pltpu.SemaphoreType.DMA
        fars, nears, uppers = place.fars, place.nears, place.uppers
        whole, head, tail = len(pieces.whole), len(pieces.head), len(pieces.tail)
        return [
            dma((whole,)),
            dma((fars, whole, 2)),
            dma((fars, nears, whole, 2)),
            dma((fars, uppers, whole, 2)),
            dma((fars, nears, uppers, head, 2)),
            dma((fars, nears, uppers, tail, 2)),
            dma((fars, nears, uppers, whole, 2)),
        ]


def iota(shape, axis):
    return lax.broadcasted_iota(jnp.int32, shape, axis)


def gather_and_count(nodes, zeros, weights, grid, scale, g2m, m2g, m2g_turned, neighbours, lent, lent_row, legendre, collective):
    place = Place(nodes, zeros)
    width = weights[0].shape[1]
    sizes = [sixteens(w.shape[0]) for w in weights]
    pieces = Pieces(sizes, 1)
    devices = nodes * zeros
    pixels, cin = grid.shape
    wide = -(-cin // 128) * 128
    rows, fanout = neighbours.shape
    halo = lent.shape[0]
    ext = rows + 2 * halo
    bands, lons, dec_edges = m2g.shape
    lats, lows, lanes = legendre.shape
    enc_edges = g2m.shape[1]
    tile = 128

    def kernel(
        attn_ref, mlp_ref, small_ref, grid_ref, scale_ref, g2m_ref, m2g_ref, turned_ref, near_ref, lent_ref,
        row_ref, leg_ref,
        attn_out, mlp_out, small_out, near_out, dec_out, turned_out, mixed_out, lend_out, lendt_out, kern_out,
        attn_shard, mlp_shard, small_shard, inputs, legs, parts, sums, leg_sem, part_sem, sum_sem, *sems,
    ):
        place.locate()
        node = lax.axis_index("node")
        shards = (attn_shard, mlp_shard, small_shard)
        for ref, shard, size in zip((attn_ref, mlp_ref, small_ref), shards, sizes):
            if ref.shape[0] < size:
                shard[...] = jnp.zeros_like(shard)
            shard[pl.ds(0, ref.shape[0])] = ref[...].astype(bf16)
        legs[node] = leg_ref[...]
        place.greet(nodes)
        gather = Gather(place, pieces, shards, (attn_out, mlp_out, small_out), sems)
        gather.begin()
        started = []
        leg_copies = []
        for step in range(1, nodes):
            target = (lax.rem(node + step, nodes), lax.axis_index("zero"))
            copy = pltpu.make_async_remote_copy(
                src_ref=leg_ref,
                dst_ref=legs.at[node],
                send_sem=leg_sem.at[step, 0],
                recv_sem=leg_sem.at[step, 1],
                device_id=target,
                device_id_type=MESH,
            )
            copy.start()
            leg_copies.append(copy)

        def count_near():
            @pl.loop(0, rows // tile)
            def _(index):
                spot = pl.ds(pl.multiple_of(index * tile, tile), tile)
                lists = near_ref[spot]
                place_of = iota((tile, ext), 1)
                total = jnp.zeros((tile, ext), f32)
                for j in range(fanout):
                    total += jnp.where(lists[:, j : j + 1] == place_of, 1.0, 0.0)
                near_out[spot] = total.astype(bf16)

        def count_dec():
            @pl.loop(0, bands)
            def _(band):
                lists = m2g_ref[band]
                place_of = iota((lons, rows), 1)
                total = jnp.zeros((lons, rows), f32)
                for j in range(dec_edges):
                    total += jnp.where(lists[:, j : j + 1] == place_of, 1.0, 0.0)
                dec_out[band] = total.astype(bf16)
                lists = turned_ref[band]
                place_of = iota((rows, lons), 0)
                total = jnp.zeros((rows, lons), f32)
                for j in range(dec_edges):
                    total += jnp.where(lists[j : j + 1] == place_of, 1.0, 0.0)
                turned_out[band] = total.astype(bf16)

        def mix():
            inputs[...] = (grid_ref[...].astype(f32) * scale_ref[...]).astype(bf16)
            mixed_out[...] = jnp.zeros_like(mixed_out)

            @pl.loop(0, rows // tile)
            def _(index):
                spot = pl.ds(pl.multiple_of(index * tile, tile), tile)
                lists = g2m_ref[spot]
                place_of = iota((tile, pixels), 1)
                total = jnp.zeros((tile, pixels), f32)
                for j in range(enc_edges):
                    total += jnp.where(lists[:, j : j + 1] == place_of, 1.0 / enc_edges, 0.0)
                mean = dot_nn(total.astype(bf16), inputs[...])
                high = mean.astype(bf16)
                mixed_out[0, spot, pl.ds(0, cin)] = high
                mixed_out[1, spot, pl.ds(0, cin)] = (mean - high.astype(f32)).astype(bf16)

        def lend():
            lend_out[...] = jnp.where(lent_ref[...] == iota((halo, rows), 1), 1.0, 0.0).astype(bf16)
            lendt_out[...] = jnp.where(row_ref[...] == iota((rows, 2 * halo), 0), 1.0, 0.0).astype(bf16)

        def gram():
            for copy in leg_copies:
                copy.wait()

            @pl.loop(0, nodes * lats)
            def _(index):
                other = legs[index // lats, lax.rem(index, lats)]
                for t in range(lats):
                    product = leg_ref[t] * other
                    parts[place.near, t, pl.ds(index, 1)] = jnp.sum(product, axis=0, keepdims=True)

            for j in range(1, place.nears):
                near_parts.append(
                    start_copy(
                        started, place, parts.at[place.near], parts.at[place.near], part_sem.at[j], near=j
                    )
                )

        near_parts, far_sums = [], []

        def gram_near():
            wait_all(near_parts)
            total = parts[0]
            for j in range(1, place.nears):
                total = total + parts[j]
            sums[place.far] = total
            for k in range(1, place.fars):
                far_sums.append(
                    start_copy(
                        started, place, sums.at[place.far], sums.at[place.far], sum_sem.at[k], far=k
                    )
                )

        def gram_far():
            wait_all(far_sums)
            total = sums[0]
            for k in range(1, place.fars):
                total = total + sums[k]
            kern_out[...] = total

        work = [lend, mix, gram, count_dec, gram_near, count_near, gram_far]
        steps = place.fars + 2
        for k in range(steps):
            gather.step(k)
            share = -(-len(work) // (steps - k))
            for part in work[:share]:
                part()
            work = work[share:]
        gather.end()
        for copy in started:
            copy.wait_send()

    vmem = pl.BlockSpec(memory_space=pltpu.VMEM)
    hbm = pl.BlockSpec(memory_space=pl.ANY)
    dma = pltpu.SemaphoreType.DMA
    struct = jax.ShapeDtypeStruct
    return pl.pallas_call(
        kernel,
        out_shape=tuple(struct((devices, size, width), bf16) for size in sizes)
        + (
            struct((rows, ext), bf16),
            struct((bands, lons, rows), bf16),
            struct((bands, rows, lons), bf16),
            struct((2, rows, wide), bf16),
            struct((halo, rows), bf16),
            struct((rows, 2 * halo), bf16),
            struct((lats, nodes * lats, lanes), f32),
        ),
        in_specs=[vmem] * 12,
        out_specs=(hbm,) * 3 + (vmem,) * 7,
        scratch_shapes=[pltpu.VMEM((size, width), bf16) for size in sizes]
        + [
            pltpu.VMEM((pixels, cin), bf16),
            pltpu.VMEM((nodes, lats, lows, lanes), f32),
            pltpu.VMEM((place.nears, lats, nodes * lats, lanes), f32),
            pltpu.VMEM((place.fars, lats, nodes * lats, lanes), f32),
            dma((nodes, 2)),
            dma((place.nears, 2)),
            dma((place.fars, 2)),
        ]
        + Gather.sems(place, pieces),
        compiler_params=pltpu.CompilerParams(
            collective_id=collective, has_side_effects=True, vmem_limit_bytes=56 << 20
        ),
    )(*weights, grid, scale, g2m, m2g, m2g_turned, neighbours, lent, lent_row, legendre)


def norm_parts(rows):
    centred = rows - jnp.mean(rows, axis=-1, keepdims=True)
    inverse = lax.rsqrt(jnp.mean(centred * centred, axis=-1, keepdims=True) + norm_epsilon)
    return centred * inverse, inverse


def model_step(
    nodes, zeros, weights, graph, kern, feats, base, keep, tables, scalars, first_channel, channels, dec_edges, collective
):
    place = Place(nodes, zeros)
    attn, mlp, small = weights
    near, dec, dec_turned, mixed, lend, lendt = graph
    width = attn.shape[1]
    hidden = mlp.shape[0] // 2
    rows, ext_rows = near.shape
    halo = lend.shape[0]
    bands, lons, _ = dec.shape
    wide = mixed.shape[2]
    lats, all_lats, lanes = kern.shape
    start = first_channel // 128 * 128
    shift = first_channel - start
    sent = sixteens(shift + channels)
    big, tile = 256, 128
    head_width = width // HEAD_COUNT
    score_scale = head_width ** (-0.5)
    third = 1.0 / dec_edges

    def kernel(
        attn_hbm, mlp_hbm, small_ref, near_hbm, dec_hbm, turned_hbm, mixed_ref, lend_ref, lendt_ref, kern_ref,
        feats_ref, base_ref, keep_ref, table_ref, scalar_ref,
        attn_out, mlp_out, high_out, low_out, loss_out,
        attn_ref, mlp_ref, near_ref, dec_ref, turned_ref, h0_ref, h1_ref, first_ref, q_ref, ext_ref, lent_ref,
        prob_ref, blend_ref, second_ref, activ_ref, slope_ref, out_ref, node_ref, f_ref, all_ref, gf_ref, gnet_ref,
        gb_ref, gattn_ref, gblend_ref, gext_ref, back_ref, lost_ref, sums_ref,
        load_sem, lend_sem, f_sem, pass_sem, back_sem,
    ):
        place.locate()
        node = lax.axis_index("node")
        zero = lax.axis_index("zero")
        loads = []
        for index, (source, target) in enumerate(
            (
                (attn_hbm, attn_ref),
                (near_hbm, near_ref),
                (mlp_hbm, mlp_ref),
                (dec_hbm, dec_ref),
                (turned_hbm, turned_ref),
            )
        ):
            copy = pltpu.make_async_copy(source, target, load_sem.at[index])
            copy.start()
            loads.append(copy)
        barrier = pltpu.get_barrier_semaphore()
        for step in range(1, nodes):
            pl.semaphore_signal(
                barrier, 1, device_id=(lax.rem(node + step, nodes), zero), device_id_type=MESH
            )
        started = []

        def to_node(step, source, target, sems):
            copy = pltpu.make_async_remote_copy(
                src_ref=source,
                dst_ref=target,
                send_sem=sems.at[0],
                recv_sem=sems.at[1],
                device_id=(lax.rem(node + step, nodes), zero),
                device_id_type=MESH,
            )
            copy.start()
            started.append(copy)
            return copy

        def row_loop(size, body):
            @pl.loop(0, rows // size)
            def _(index):
                body(pl.ds(pl.multiple_of(index * size, size), size))

        mods = dot_tn(feats_ref[...].astype(bf16), small_ref[...])
        mod = [mods[j : j + 1] for j in range(4)]
        enc = small_ref[pl.ds(0, wide)]
        loads[0].wait()

        def encode(spot):
            h0 = dot_nn(mixed_ref[0, spot], enc) + dot_nn(mixed_ref[1, spot], enc)
            h0_ref[spot] = h0
            unit, inverse = norm_parts(h0)
            first = (unit * (1.0 + mod[0]) + mod[1]).astype(bf16)
            first_ref[spot] = first
            ext_ref[spot] = dot_nt(first, attn_ref[pl.ds(width, 2 * width)]).astype(bf16)
            q_ref[spot] = dot_nt(first, attn_ref[pl.ds(0, width)]).astype(bf16)

        row_loop(big, encode)
        lent_ref[...] = dot_nn(lend_ref[...], ext_ref[pl.ds(0, rows)]).astype(bf16)
        pl.semaphore_wait(barrier, nodes - 1)
        up = to_node(1, lent_ref, ext_ref.at[pl.ds(rows, halo)], lend_sem.at[0])
        down = to_node(nodes - 1, lent_ref, ext_ref.at[pl.ds(rows + halo, halo)], lend_sem.at[1])
        loads[1].wait()
        up.wait_recv()
        down.wait_recv()

        def attend(spot):
            count = near_ref[spot].astype(f32)
            for head in range(HEAD_COUNT):
                part = pl.ds(head * head_width, head_width)
                values = pl.ds(width + head * head_width, head_width)
                logits = dot_nt(q_ref[spot, part], ext_ref[:, part]) * score_scale
                logits = jnp.where(count > 0.0, logits, -jnp.inf)
                raised = jnp.exp(logits - jnp.max(logits, axis=-1, keepdims=True))
                prob = raised * (1.0 / jnp.sum(raised * count, axis=-1, keepdims=True))
                prob = prob.astype(bf16)
                prob_ref[head, spot] = prob
                low = (prob.astype(f32) * count).astype(bf16)
                blend_ref[spot, part] = dot_nn(low, ext_ref[:, values]).astype(bf16)

        row_loop(tile, attend)
        loads[2].wait()
        dec_rows = small_ref[pl.ds(start, 128)]
        lane = iota((1, 128), 1)
        live = jnp.where((lane >= shift) & (lane < shift + channels), 1.0, 0.0)

        def feed(spot):
            h1 = h0_ref[spot] + dot_nt(blend_ref[spot], attn_ref[pl.ds(3 * width, width)])
            h1_ref[spot] = h1
            unit, inverse = norm_parts(h1)
            second = (unit * (1.0 + mod[2]) + mod[3]).astype(bf16)
            second_ref[spot] = second
            upper = dot_nt(second, mlp_ref[pl.ds(0, hidden)])
            square = upper * upper
            bend = jnp.tanh(gelu_scale * upper * (1.0 + gelu_cubic * square))
            half = 0.5 + 0.5 * bend
            activ = (upper * half).astype(bf16)
            activ_ref[spot] = activ
            slope = half + (0.5 * gelu_scale) * upper * (1.0 - bend * bend) * (
                1.0 + 3.0 * gelu_cubic * square
            )
            slope_ref[spot] = slope.astype(bf16)
            h2 = h1 + dot_nn(activ, mlp_ref[pl.ds(hidden, hidden)])
            high = h2.astype(bf16)
            out_ref[spot] = high
            low = (h2 - high.astype(f32)).astype(bf16)
            projected = (dot_nt(high, dec_rows) + dot_nt(low, dec_rows)) * live
            top = projected.astype(bf16)
            node_ref[spot, pl.ds(0, 128)] = top
            node_ref[spot, pl.ds(128, 128)] = (projected - top.astype(f32)).astype(bf16)

        row_loop(tile, feed)

        c_output, weight = scalar_ref[0], scalar_ref[1]
        loads[3].wait()
        cores, uppers = {}, {}
        for band in range(bands):
            net = dot_nn(dec_ref[band], node_ref[...])
            net = (net[:, :128] + net[:, 128:]) * (c_output * third)
            error = (base_ref[band] + net) * keep_ref[band]
            high = error.astype(bf16)
            low = (error - high.astype(f32)).astype(bf16)
            turned = dot_tn(high, table_ref[0]) + dot_tn(low, table_ref[0]) + dot_tn(high, table_ref[1])
            f_ref[band] = turned[:sent]
            all_ref[node, band] = turned[:sent].astype(bf16)
            piece = all_ref.at[node, band]
            cores[0, band] = start_copy(started, place, piece, piece, f_sem.at[0, band], core=1)
            for i in range(1, place.uppers):
                uppers[i, band] = start_copy(started, place, piece, piece, f_sem.at[i, band], upper=i)
        gf_ref[...] = jnp.zeros_like(gf_ref)
        for band in range(bands):
            for i in range(1, place.uppers):
                uppers[i, band].wait_recv()
                source = lax.rem(place.upper + place.uppers - i, place.uppers) * 2 + place.core
                piece = all_ref.at[source, band]
                cores[i, band] = start_copy(started, place, piece, piece, pass_sem.at[i, band], core=1)
        for key in cores:
            cores[key].wait_recv()
        loss_rows = jnp.zeros((8, 128), f32)
        loads[4].wait()
        for band in range(bands):

            def add_lat(index, total):
                return total + kern_ref[band, pl.ds(index, 1)] * all_ref[
                    index // lats, lax.rem(index, lats)
                ].astype(f32)

            total = lax.fori_loop(0, all_lats, add_lat, jnp.zeros((sent, lanes), f32), unroll=4)
            loss_rows = loss_rows + jnp.sum(total * f_ref[band])
            gf_ref[pl.ds(0, sent)] = total * (2.0 * weight)
            grad = gf_ref[...]
            high = grad.astype(bf16)
            low = (grad - high.astype(f32)).astype(bf16)
            back = dot_nt(table_ref[0], high) + dot_nt(table_ref[0], low) + dot_nt(table_ref[1], high)
            gnet_ref[band] = (back * keep_ref[band] * c_output).astype(bf16)
        loss_out[...] = loss_rows * weight

        sums_ref[...] = jnp.zeros_like(sums_ref)

        def back_feed(spot):
            grad_node = dot_nn(turned_ref[0, spot], gnet_ref[0])
            for band in range(1, bands):
                grad_node += dot_nn(turned_ref[band, spot], gnet_ref[band])
            grad_node = grad_node * third
            high = grad_node.astype(bf16)
            low = (grad_node - high.astype(f32)).astype(bf16)
            node_ref[spot, pl.ds(0, 128)] = high
            grad_out = dot_nn(high, dec_rows) + dot_nn(low, dec_rows)
            branch = grad_out.astype(bf16)
            gb_ref[spot] = branch
            grad_activ = dot_nt(branch, mlp_ref[pl.ds(hidden, hidden)])
            grad_upper = (grad_activ * slope_ref[spot].astype(f32)).astype(bf16)
            slope_ref[spot] = grad_upper
            grad_second = dot_nn(grad_upper, mlp_ref[pl.ds(0, hidden)])
            unit, inverse = norm_parts(h1_ref[spot])
            scaled = grad_second * (1.0 + mod[2])
            grad_mid = grad_out + inverse * (
                scaled
                - jnp.mean(scaled, axis=-1, keepdims=True)
                - unit * jnp.mean(scaled * unit, axis=-1, keepdims=True)
            )
            sums_ref[2:3] += jnp.sum(grad_second * unit, axis=0, keepdims=True)
            sums_ref[3:4] += jnp.sum(grad_second, axis=0, keepdims=True)
            h1_ref[spot] = grad_mid
            grad_attn = grad_mid.astype(bf16)
            gattn_ref[spot] = grad_attn
            gblend_ref[spot] = dot_nn(grad_attn, attn_ref[pl.ds(3 * width, width)]).astype(bf16)

        row_loop(tile, back_feed)

        def outer_loop(target, offset, left, right, columns):
            @pl.loop(0, columns // big)
            def _(index):
                part = pl.multiple_of(index * big, big)
                product = dot_tn(left[:, pl.ds(part, big)], right[...])
                target[pl.ds(pl.multiple_of(offset + part, big), big)] = product.astype(bf16)

        gext_ref[...] = jnp.zeros_like(gext_ref)

        def back_attend(spot):
            count = near_ref[spot].astype(f32)
            for head in range(HEAD_COUNT):
                part = pl.ds(head * head_width, head_width)
                values = pl.ds(width + head * head_width, head_width)
                prob = prob_ref[head, spot].astype(f32)
                counted_prob = prob * count
                grad_blend = gblend_ref[spot, part]
                grad_prob = dot_nt(grad_blend, ext_ref[:, values])
                mean = jnp.sum(counted_prob * grad_prob, axis=-1, keepdims=True)
                grad_logit = (counted_prob * (grad_prob - mean)).astype(bf16)
                gext_ref[:, part] += dot_tn(grad_logit, q_ref[spot, part])
                q_ref[spot, part] = (dot_nn(grad_logit, ext_ref[:, part]) * score_scale).astype(bf16)
                gext_ref[:, values] += dot_tn(counted_prob.astype(bf16), grad_blend)

        row_loop(tile, back_attend)
        gext_ref[:, pl.ds(0, width)] = gext_ref[:, pl.ds(0, width)] * score_scale
        lost_ref[0] = gext_ref[pl.ds(rows, halo)].astype(bf16)
        lost_ref[1] = gext_ref[pl.ds(rows + halo, halo)].astype(bf16)
        from_upper = to_node(nodes - 1, lost_ref.at[0], back_ref.at[pl.ds(0, halo)], back_sem.at[0])
        from_lower = to_node(1, lost_ref.at[1], back_ref.at[pl.ds(halo, halo)], back_sem.at[1])

        outer_loop(mlp_out, hidden, activ_ref, gb_ref, hidden)
        outer_loop(mlp_out, 0, slope_ref, second_ref, hidden)
        outer_loop(attn_out, 3 * width, gattn_ref, blend_ref, width)
        outer_loop(attn_out, 0, q_ref, first_ref, width)
        from_upper.wait_recv()
        from_lower.wait_recv()

        def back_encode(spot):
            grad_pairs = gext_ref[spot] + dot_nn(lendt_ref[spot], back_ref[...])
            grad_pairs = grad_pairs.astype(bf16)
            ext_ref[spot] = grad_pairs
            grad_first = dot_nn(q_ref[spot], attn_ref[pl.ds(0, width)]) + dot_nn(
                grad_pairs, attn_ref[pl.ds(width, 2 * width)]
            )
            unit, inverse = norm_parts(h0_ref[spot])
            scaled = grad_first * (1.0 + mod[0])
            grad_in = h1_ref[spot] + inverse * (
                scaled
                - jnp.mean(scaled, axis=-1, keepdims=True)
                - unit * jnp.mean(scaled * unit, axis=-1, keepdims=True)
            )
            sums_ref[0:1] += jnp.sum(grad_first * unit, axis=0, keepdims=True)
            sums_ref[1:2] += jnp.sum(grad_first, axis=0, keepdims=True)
            gb_ref[spot] = grad_in.astype(bf16)

        row_loop(big, back_encode)
        outer_loop(attn_out, width, ext_ref.at[pl.ds(0, rows)], first_ref, 2 * width)

        feats_value = feats_ref[...]
        small_rows = small_ref.shape[0]
        cond = feats_value[:, 0:1] * sums_ref[0:1]
        for j in range(1, 4):
            cond += feats_value[:, j : j + 1] * sums_ref[j : j + 1]
        for low_row in range(0, small_rows, 128):
            total = cond[low_row : low_row + 128]
            if low_row < wide:
                total += dot_tn(mixed_ref[0, :, pl.ds(low_row, 128)], gb_ref[...])
            if low_row == start:
                total += dot_tn(node_ref[:, pl.ds(0, 128)], out_ref[...])
            high = total.astype(bf16)
            high_out[pl.ds(low_row, 128)] = high
            low_out[pl.ds(low_row, 128)] = (total - high.astype(f32)).astype(bf16)
        for copy in started:
            copy.wait_send()

    vmem = pl.BlockSpec(memory_space=pltpu.VMEM)
    hbm = pl.BlockSpec(memory_space=pl.ANY)
    dma = pltpu.SemaphoreType.DMA
    struct = jax.ShapeDtypeStruct
    low = lambda *shape: pltpu.VMEM(shape, bf16)
    full = lambda *shape: pltpu.VMEM(shape, f32)
    return pl.pallas_call(
        kernel,
        out_shape=(
            struct(attn.shape, bf16),
            struct(mlp.shape, bf16),
            struct(small.shape, bf16),
            struct(small.shape, bf16),
            struct((8, 128), f32),
        ),
        in_specs=[hbm, hbm, vmem, hbm, hbm, hbm] + [vmem] * 8 + [pl.BlockSpec(memory_space=pltpu.SMEM)],
        out_specs=(vmem,) * 5,
        scratch_shapes=[
            low(*attn.shape),
            low(*mlp.shape),
            low(*near.shape),
            low(*dec.shape),
            low(*dec_turned.shape),
            full(rows, width),
            full(rows, width),
            low(rows, width),
            low(rows, width),
            low(ext_rows, 2 * width),
            low(halo, 2 * width),
            low(HEAD_COUNT, rows, ext_rows),
            low(rows, width),
            low(rows, width),
            low(rows, hidden),
            low(rows, hidden),
            low(rows, width),
            low(rows, 256),
            full(lats, sent, lanes),
            low(nodes, lats, sent, lanes),
            full(128, lanes),
            low(bands, lons, 128),
            low(rows, width),
            low(rows, width),
            low(rows, width),
            full(ext_rows, 2 * width),
            low(2 * halo, 2 * width),
            low(2, halo, 2 * width),
            full(8, width),
            dma((5,)),
            dma((2, 2)),
            dma((place.uppers, lats, 2)),
            dma((place.uppers, lats, 2)),
            dma((2, 2)),
        ],
        compiler_params=pltpu.CompilerParams(
            collective_id=collective, has_side_effects=True, vmem_limit_bytes=62 << 20
        ),
    )(attn, mlp, small, near, dec, dec_turned, mixed, lend, lendt, kern, feats, base, keep, tables, scalars)


class Scatter:
    def __init__(self, place, pieces, grads, bufs, sems):
        self.place, self.pieces, self.grads = place, pieces, grads
        count = len(grads)
        self.core_in = bufs[:count]
        (self.over_out, self.over_in, self.under_out, self.under_in, self.over_out2, self.over_in2,
         self.under_out2, self.under_in2, self.far_out, self.far_in) = bufs[count:]
        (self.core_sem, self.over_sem, self.under_sem, self.over_sem2, self.under_sem2, self.far_sem) = sems
        self.started = []
        self.order = list(range(1, place.fars)) + [0]
        self.core, self.over, self.under, self.over2, self.under2, self.far = {}, {}, {}, {}, {}, {}
        self.head_rows = sum(rows for _, _, rows in pieces.head)
        self.tail_rows = sum(rows for _, _, rows in pieces.tail)

    def send(self, source, target, sem, **steps):
        return start_copy(self.started, self.place, source, target, sem, **steps)

    def begin(self, arrays):
        place = self.place
        other = 1 - place.core
        for k in self.order:
            far = place.moved(far=k)[2]
            for upper in range(place.uppers):
                spot = pl.ds(place.slot(upper, other, far, 0), place.nears)
                for a in arrays:
                    self.core[k, upper, a] = self.send(
                        self.grads[a].at[spot], self.core_in[a].at[k, upper], self.core_sem.at[k, upper, a], core=1
                    )

    def add(self, target, k, upper, near, pieces, others):
        far = self.place.moved(far=k)[2]
        slot = self.place.slot(upper, self.place.core, far, near)
        offset = 0
        for array, start, rows in pieces:
            mine = self.grads[array].at[slot]
            theirs = self.core_in[array].at[k, upper, near]

            @pl.loop(0, rows // ROW_CHUNK)
            def _(index, start=start, offset=offset, mine=mine, theirs=theirs):
                step = index * ROW_CHUNK
                here = pl.ds(pl.multiple_of(start + step, ROW_CHUNK), ROW_CHUNK)
                there = pl.ds(pl.multiple_of(offset + step, ROW_CHUNK), ROW_CHUNK)
                total = mine[here].astype(f32) + theirs[here].astype(f32)
                for other in others:
                    total += other[there].astype(f32)
                target[there] = total.astype(target.dtype)

            offset += rows

    def one(self, k):
        place, pieces = self.place, self.pieces
        for key in self.core:
            if key[0] == k:
                self.core[key].wait_recv()
        for i in range(1, place.uppers):
            for near in range(place.nears):
                self.add(self.over_out.at[k, i, near], k, place.moved(upper=i)[0], near, pieces.head, [])
            self.over[k, i] = self.send(
                self.over_out.at[k, i], self.over_in.at[k, i], self.over_sem.at[k, i], upper=i
            )
        for j in range(1, place.nears):
            for upper in range(place.uppers):
                self.add(self.under_out.at[k, j, upper], k, upper, place.moved(near=j)[3], pieces.tail, [])
            self.under[k, j] = self.send(
                self.under_out.at[k, j], self.under_in.at[k, j], self.under_sem.at[k, j], near=j
            )

    def overs(self, k, near):
        return [self.over_in.at[k, i, near] for i in range(1, self.place.uppers)]

    def unders(self, k, upper):
        return [self.under_in.at[k, j, upper] for j in range(1, self.place.nears)]

    def two(self, k):
        place, pieces = self.place, self.pieces
        for i in range(1, place.uppers):
            self.over[k, i].wait_recv()
        for j in range(1, place.nears):
            near = place.moved(near=j)[3]
            self.add(self.over_out2.at[k, j], k, place.upper, near, pieces.head, self.overs(k, near))
            self.over2[k, j] = self.send(
                self.over_out2.at[k, j], self.over_in2.at[k, j], self.over_sem2.at[k, j], near=j
            )
        for j in range(1, place.nears):
            self.under[k, j].wait_recv()
        for i in range(1, place.uppers):
            upper = place.moved(upper=i)[0]
            self.add(self.under_out2.at[k, i], k, upper, place.near, pieces.tail, self.unders(k, upper))
            self.under2[k, i] = self.send(
                self.under_out2.at[k, i], self.under_in2.at[k, i], self.under_sem2.at[k, i], upper=i
            )

    def three(self, k, target, extra):
        place, pieces = self.place, self.pieces
        for j in range(1, place.nears):
            self.over2[k, j].wait_recv()
        for i in range(1, place.uppers):
            self.under2[k, i].wait_recv()
        head, tail = pl.ds(0, self.head_rows), pl.ds(self.head_rows, self.tail_rows)
        self.add(
            target.at[head], k, place.upper, place.near, pieces.head,
            self.overs(k, place.near)
            + [self.over_in2.at[k, j] for j in range(1, place.nears)]
            + [item.at[head] for item in extra],
        )
        self.add(
            target.at[tail], k, place.upper, place.near, pieces.tail,
            self.unders(k, place.upper)
            + [self.under_in2.at[k, i] for i in range(1, place.uppers)]
            + [item.at[tail] for item in extra],
        )

    def run(self, own):
        fars, order = self.place.fars, self.order
        for step in range(fars + 2):
            if step < fars:
                self.one(order[step])
            if 1 <= step <= fars:
                self.two(order[step - 1])
            if step >= 2 and order[step - 2]:
                k = order[step - 2]
                self.three(k, self.far_out.at[k], [])
                self.far[k] = self.send(self.far_out.at[k], self.far_in.at[k], self.far_sem.at[k], far=k)
        for k in range(1, fars):
            self.far[k].wait_recv()
        self.three(0, own, [self.far_in.at[k] for k in range(1, fars)])

    def end(self):
        for copy in self.started:
            copy.wait_send()

    @staticmethod
    def scratch(place, pieces, width):
        fars, nears, uppers = place.fars, place.nears, place.uppers
        head = sum(rows for _, _, rows in pieces.head)
        tail = sum(rows for _, _, rows in pieces.tail)
        vmem = lambda *shape: pltpu.VMEM(shape + (width,), bf16)
        dma = pltpu.SemaphoreType.DMA
        bufs = [vmem(fars, uppers, nears, size) for size in pieces.sizes]
        bufs += [vmem(fars, uppers, nears, head)] * 2
        bufs += [vmem(fars, nears, uppers, tail)] * 2
        bufs += [vmem(fars, nears, head)] * 2
        bufs += [vmem(fars, uppers, tail)] * 2
        bufs += [vmem(fars, head + tail)] * 2
        sems = [
            dma((fars, uppers, len(pieces.sizes), 2)),
            dma((fars, uppers, 2)),
            dma((fars, nears, 2)),
            dma((fars, nears, 2)),
            dma((fars, uppers, 2)),
            dma((fars, 2)),
        ]
        return bufs, sems


class MomentGather:
    def __init__(self, place, shards, outs, sems):
        self.place, self.shards, self.outs = place, shards, outs
        (self.own_sem, self.far_sem, self.near_sem, self.spread_sem, self.core_sem) = sems
        self.started, self.cores = [], []
        self.far, self.near, self.spread_copies = {}, {}, {}

    def block(self, **steps):
        slot = self.place.slot(*self.place.moved(**steps))
        return [out.at[slot] for out in self.outs]

    def send(self, source, target, sem, **steps):
        return start_copy(self.started, self.place, source, target, sem, **steps)

    def both(self, source, target, sems, **steps):
        return [self.send(source[a], target[a], sems.at[a], **steps) for a in range(2)]

    def spread(self, k, j, source, target):
        place = self.place
        for i in range(1, place.uppers):
            self.spread_copies[k, j, i, 0] = self.send(
                source[0], target[0], self.spread_sem.at[k, j, i, 0], upper=i
            )
        for i in range(1, place.mates):
            self.spread_copies[k, j, i, 1] = self.send(
                source[1], target[1], self.spread_sem.at[k, j, i, 1], mate=i
            )
        self.cores += self.both(source, target, self.core_sem.at[k, j, 0], core=1)

    def run(self):
        place = self.place
        fars, nears = place.fars, place.nears
        here = self.block()
        kept = [
            pltpu.make_async_copy(shard, target, self.own_sem.at[a])
            for a, (shard, target) in enumerate(zip(self.shards, here))
        ]
        for copy in kept:
            copy.start()
        for k in range(1, fars):
            self.far[k] = self.both(self.shards, here, self.far_sem.at[k], far=k)
        for step in range(fars + 2):
            if step < fars:
                k = step
                if k:
                    wait_all(self.far[k])
                target = self.block(far=(fars - k) % fars)
                source = target if k else self.shards
                for j in range(1, nears):
                    self.near[k, j] = self.both(source, target, self.near_sem.at[k, j], near=j)
                self.spread(k, 0, source, target)
            if 1 <= step <= fars:
                k = step - 1
                for j in range(1, nears):
                    wait_all(self.near[k, j])
                    item = self.block(far=(fars - k) % fars, near=nears - j)
                    self.spread(k, j, item, item)
            if step >= 2:
                k = step - 2
                for j in range(nears):
                    steps = dict(far=(fars - k) % fars, near=(nears - j) % nears)
                    for key in self.spread_copies:
                        if key[:2] != (k, j):
                            continue
                        i, a = key[2:]
                        self.spread_copies[key].wait_recv()
                        if a:
                            item = self.block(mate=place.mates - i, **steps)[1]
                        else:
                            item = self.block(upper=place.uppers - i, **steps)[0]
                        self.cores.append(self.send(item, item, self.core_sem.at[k, j, i, a], core=1))
        for copy in kept:
            copy.wait()
        wait_all(self.cores)
        for copy in self.started:
            copy.wait_send()

    @staticmethod
    def sems(place):
        dma = pltpu.SemaphoreType.DMA
        fars, nears, uppers = place.fars, place.nears, place.uppers
        return [
            dma((2,)),
            dma((fars, 2, 2)),
            dma((fars, nears, 2, 2)),
            dma((fars, nears, uppers, 2, 2)),
            dma((fars, nears, uppers, 2, 2)),
        ]


def total_body(place, tile, slots, sems):
    value = tile
    upper, core, far, near = place.moved()
    stages = (
        ("core", 2, core),
        ("near", place.nears, near),
        ("upper", place.uppers, upper),
        ("far", place.fars, far),
    )
    for stage, (name, size, mine) in enumerate(stages):
        slots[stage, mine] = value
        copies = []
        for step in range(1, size):
            piece = slots.at[stage, mine]
            start_copy(copies, place, piece, piece, sems.at[stage, step], **{name: step})
        for copy in copies:
            copy.wait()
        value = slots[stage, 0]
        for other in range(1, size):
            value = value + slots[stage, other]
    return value


def reduce_and_gather(nodes, zeros, grads, loss_tile, mom_attn, mom_mlp, small_rows, collective):
    place = Place(nodes, zeros)
    devices, _, width = grads[0].shape
    attn_rows, mlp_rows = mom_attn.shape[0], mom_mlp.shape[0]
    pieces = Pieces([item.shape[1] for item in grads], 1)
    moment_sizes = (sixteens(attn_rows), sixteens(mlp_rows))
    bufs, sems = Scatter.scratch(place, pieces, width)
    deepest = max(place.fars, place.uppers, place.nears, 2)
    count = len(grads)

    def kernel(*refs):
        grad_refs = refs[:count]
        loss_ref, attn_ref, mlp_ref = refs[count : count + 3]
        small_out, attn_out, mlp_out, total_out, attn_all, mlp_all = refs[count + 3 : count + 9]
        own, attn_shard, mlp_shard, slots, slot_sems = refs[count + 9 : count + 14]
        rest = refs[count + 14 :]
        place.locate()
        place.greet()
        scatter = Scatter(
            place, pieces, grad_refs, rest[: len(bufs)], rest[len(bufs) : len(bufs) + len(sems)]
        )
        scatter.begin((1, 0, 2, 3))
        scatter.run(own)
        starts = [0] * count
        starts[0] = pieces.sizes[1]
        starts[2] = starts[0] + pieces.sizes[0]
        starts[3] = starts[2] + pieces.sizes[2]
        g_attn = own[pl.ds(starts[0], attn_rows)]
        g_mlp = own[pl.ds(starts[1], mlp_rows)]
        g_small = own[pl.ds(starts[2], small_rows)] + own[pl.ds(starts[3], small_rows)]
        small_out[...] = g_small
        squares = jnp.sum(g_attn * g_attn) + jnp.sum(g_mlp * g_mlp) + jnp.sum(g_small * g_small)
        tile = jnp.where(iota((8, 128), 0) < 4, squares, loss_ref[...])
        total = total_body(place, tile, slots, slot_sems)
        total_out[...] = total
        factor = jnp.minimum(1.0, clip_limit * lax.rsqrt(total[0:1, 0:1]))
        for ref, out, shard, grad, size in (
            (attn_ref, attn_out, attn_shard, g_attn, attn_rows),
            (mlp_ref, mlp_out, mlp_shard, g_mlp, mlp_rows),
        ):
            moment = moment_decay * ref[...] + factor * grad
            out[...] = moment
            if size < shard.shape[0]:
                shard[...] = jnp.zeros_like(shard)
            shard[pl.ds(0, size)] = moment.astype(bf16)
        moments = MomentGather(
            place, (attn_shard, mlp_shard), (attn_all, mlp_all), rest[len(bufs) + len(sems) :]
        )
        moments.run()
        scatter.end()

    vmem = pl.BlockSpec(memory_space=pltpu.VMEM)
    hbm = pl.BlockSpec(memory_space=pl.ANY)
    struct = jax.ShapeDtypeStruct
    return pl.pallas_call(
        kernel,
        out_shape=(
            struct((small_rows, width), f32),
            struct((attn_rows, width), f32),
            struct((mlp_rows, width), f32),
            struct((8, 128), f32),
            struct((devices, moment_sizes[0], width), bf16),
            struct((devices, moment_sizes[1], width), bf16),
        ),
        in_specs=[vmem] * (count + 3),
        out_specs=(vmem,) * 4 + (hbm,) * 2,
        scratch_shapes=[
            pltpu.VMEM((sum(pieces.sizes), width), f32),
            pltpu.VMEM((moment_sizes[0], width), bf16),
            pltpu.VMEM((moment_sizes[1], width), bf16),
            pltpu.VMEM((4, deepest, 8, 128), f32),
            pltpu.SemaphoreType.DMA((4, deepest, 2)),
        ]
        + bufs
        + sems
        + MomentGather.sems(place),
        compiler_params=pltpu.CompilerParams(
            collective_id=collective, has_side_effects=True, vmem_limit_bytes=56 << 20
        ),
    )(*grads, loss_tile, mom_attn, mom_mlp)


def turn_tables(lon_count, modes):
    turns = np.arange(lon_count)[:, None] * np.arange(modes)[None, :] % lon_count
    phases = turns * (2.0 * np.pi / lon_count)
    waves = [m for m in range(modes) if (2 * m) % lon_count]
    picks = list(range(modes)) + waves
    lanes = -(-len(picks) // 128) * 128
    table = np.zeros((lon_count, lanes), np.float32)
    table[:, :modes] = np.cos(phases)
    table[:, modes : len(picks)] = -np.sin(phases[:, waves])
    high = table.astype(ml_dtypes.bfloat16)
    low = (table - high.astype(np.float32)).astype(ml_dtypes.bfloat16)
    return np.stack([high, low]), (waves[0], waves[-1] + 1, lanes - len(picks))


def to_sixteens(blocks):
    return jnp.pad(blocks, ((0, 0), (0, sixteens(blocks.shape[1]) - blocks.shape[1]), (0, 0)))


def on_device(
    grid_in,
    target,
    noise_level,
    land_mask,
    neighbours,
    halo_send,
    g2m,
    m2g,
    legendre,
    w_attn,
    w_mlp,
    w_small,
    mom_attn,
    mom_mlp,
    m_small,
    v_small,
    ema_attn,
    ema_mlp,
    ema_small,
):
    cin = grid_in.shape[-1]
    lat_rows, lon_count, channels = target.shape[1:]
    modes, degrees = legendre.shape[1:]
    halo_rows = halo_send.shape[0]
    width = w_attn.shape[1]
    both = ("node", "zero")
    nodes, zeros = lax.axis_size("node"), lax.axis_size("zero")
    devices = nodes * zeros
    attn_rows, mlp_rows, small_rows = w_attn.shape[0], w_mlp.shape[0], w_small.shape[0]
    half = mlp_rows * devices // 2

    sigma, c_input, c_skip, c_output, loss_weight = noise_scalars(noise_level[0])
    scale_input = jnp.where(jnp.arange(cin) < channels, c_input, 1.0)[None]
    features = noise_features(sigma).astype(bf16).astype(f32)
    cond_rows = jnp.where(
        jnp.arange(128)[None, None] == jnp.arange(4)[:, None, None], features[None, :, None], 0.0
    ).reshape(-1, 128)
    feats = jnp.pad(cond_rows, ((cin + channels, 0), (0, 0)))
    shift = cin % 128
    sides = ((0, 0), (0, 0), (shift, 128 - shift - channels))
    keep_mask = 1.0 - land_mask.astype(f32)[:, :, None] * (
        jnp.arange(channels) == channels - 1
    ).astype(f32)
    base = jnp.pad(c_skip * grid_in[0, :, :, :channels].astype(f32) - target[0], sides)
    keep = jnp.pad(keep_mask, sides)
    tables, (wave_first, wave_end, wave_pad) = turn_tables(lon_count, modes)
    lows = -(-degrees // (8 * zeros)) * 8
    leg = jnp.pad(legendre, ((0, 0), (0, 0), (0, lows * zeros - degrees)))
    leg = lax.dynamic_slice_in_dim(leg, lax.axis_index("zero") * lows, lows, axis=2)
    leg = jnp.transpose(leg, (0, 2, 1))
    leg = jnp.concatenate(
        [leg, leg[:, :, wave_first:wave_end], jnp.zeros(leg.shape[:2] + (wave_pad,), f32)], axis=2
    )
    m2g_bands = m2g.reshape(lat_rows, lon_count, -1)

    attn, mlp, small, near, dec, dec_turned, mixed, lend, lendt, kern = gather_and_count(
        nodes,
        zeros,
        (w_attn, w_mlp, w_small),
        grid_in[0].reshape(-1, cin),
        scale_input,
        g2m,
        m2g_bands,
        jnp.transpose(m2g_bands, (0, 2, 1)),
        neighbours,
        halo_send[:, None],
        jnp.concatenate([halo_send, halo_send])[None],
        leg,
        1,
    )
    full = [
        item[:, :size].reshape(-1, width)
        for item, size in ((attn, attn_rows), (mlp, mlp_rows), (small, small_rows))
    ]
    weight = loss_weight / (2 * modes * degrees * channels)
    *local, loss_tile = model_step(
        nodes,
        zeros,
        full,
        (near, dec, dec_turned, mixed, lend, lendt),
        kern,
        feats,
        base,
        keep,
        jnp.asarray(tables),
        jnp.stack([c_output, weight]),
        cin,
        channels,
        m2g.shape[1],
        2,
    )

    g_small, moment_attn, moment_mlp, totals, attn_all, mlp_all = reduce_and_gather(
        nodes,
        zeros,
        [to_sixteens(item.reshape(devices, -1, width)) for item in local],
        loss_tile,
        mom_attn,
        mom_mlp,
        small_rows,
        3,
    )
    loss = totals[4, 0]
    clip_norm = jnp.sqrt(totals[0, 0])
    factor = jnp.minimum(1.0, clip_limit / clip_norm)
    flat_index = lax.axis_index(both)
    attn_upper = flat_index * attn_rows >= 3 * width
    mlp_upper = flat_index * mlp_rows >= half
    attn_all = attn_all[:, :attn_rows].reshape(-1, width)
    mlp_half = lax.dynamic_slice_in_dim(
        mlp_all, jnp.where(mlp_upper, devices // 2, 0), devices // 2, axis=0
    )
    mlp_mine = mlp_half[:, :mlp_rows].reshape(-1, width)
    gram_attn = jnp.where(
        attn_upper,
        dot_tn(attn_all[3 * width :], attn_all[3 * width :]),
        dot_tn(attn_all[: 3 * width], attn_all[: 3 * width]),
    )
    gram_mlp = dot_tn(mlp_mine, mlp_mine)
    attn_factor = jnp.where(attn_upper, 0.2 * math.sqrt(width), 0.2 * math.sqrt(3 * width))
    mlp_factor = 0.2 * math.sqrt(max(half, width))
    new_attn = w_attn - orthogonal_rate * attn_factor * ns_apply(gram_attn, moment_attn)
    new_mlp = w_mlp - orthogonal_rate * mlp_factor * ns_apply(gram_mlp, moment_mlp)
    clipped = factor * g_small
    first_small = adam_first * m_small + (1.0 - adam_first) * clipped
    second_small = adam_second * v_small + (1.0 - adam_second) * clipped * clipped
    new_small = w_small - adam_rate * (first_small / (1.0 - adam_first**STEP)) / (
        jnp.sqrt(second_small / (1.0 - adam_second**STEP)) + adam_epsilon
    )
    return (
        loss,
        clip_norm,
        new_attn,
        new_mlp,
        new_small,
        moment_attn,
        moment_mlp,
        first_small,
        second_small,
        average_decay * ema_attn + (1.0 - average_decay) * new_attn,
        average_decay * ema_mlp + (1.0 - average_decay) * new_mlp,
        average_decay * ema_small + (1.0 - average_decay) * new_small,
    )


def solution(mesh):
    split_rows = P(("node", "zero"), None)
    return jax.shard_map(
        on_device,
        mesh=mesh,
        in_specs=(
            P("zero", "node", None, None),
            P("zero", "node", None, None),
            P("zero"),
            P("node", None),
            P("node", None),
            P("node"),
            P("node", None),
            P("node", None),
            P("node", None, None),
        )
        + (split_rows,) * 10,
        out_specs=(P(), P()) + (split_rows,) * 10,
        check_vma=False,
    )
```

```python
import math

import jax
import jax.numpy as jnp
import ml_dtypes
import numpy as np
from jax import lax
from jax.experimental import pallas as pl
from jax.experimental.pallas import tpu as pltpu
from jax.sharding import PartitionSpec as P

HEAD_COUNT = 4
NOISE_FEATS = 42
LEVELS = 16
NS_ITERS = 3
STEP = 10

top_precision = lax.Precision.HIGHEST
mid_precision = lax.Precision.HIGH
norm_epsilon = 1e-05
trace_epsilon = 1e-12
clip_limit = 1.0
moment_decay = 0.95
orthogonal_rate = 0.1
adam_first = 0.9
adam_second = 0.95
adam_rate = 0.02
adam_epsilon = 1e-08
average_decay = 0.9
newton_first = 3.4445
newton_second = -4.775
newton_third = 2.0315
sigma_lowest = 0.1
sigma_highest = 20.0
c_input_lane = 64
c_skip_lane = 65
c_output_lane = 66
weight_lane = 67
gelu_scale = math.sqrt(2.0 / math.pi)
gelu_cubic = 0.044715
f32 = jnp.float32
bf16 = jnp.bfloat16


def noise_scalars(level):
    sigma = sigma_lowest * (sigma_highest / sigma_lowest) ** (level.astype(f32) / (LEVELS - 1))
    total = sigma * sigma + 1.0
    return (sigma, lax.rsqrt(total), 1.0 / total, sigma * lax.rsqrt(total), total / (sigma * sigma))


def noise_features(sigma):
    half_count = NOISE_FEATS // 2
    frequency = jnp.exp(jnp.arange(half_count).astype(f32) * (3.0 / half_count))
    phases = 0.25 * jnp.log(sigma) * frequency
    return jnp.concatenate([jnp.sin(phases), jnp.cos(phases)])


def dot(left, right, contract):
    return lax.dot_general(left, right, (contract, ((), ())), preferred_element_type=f32)


def dot_nn(left, right):
    return dot(left, right, ((1,), (0,)))


def dot_nt(left, right):
    return dot(left, right, ((1,), (1,)))


def dot_tn(left, right):
    return dot(left, right, ((0,), (0,)))


MESH = pl.DeviceIdType.MESH
ROW_CHUNK = 16


class Place:
    def __init__(self, nodes, zeros):
        self.uppers, self.cores = nodes // 2, 2
        self.nears = 2 if zeros < 16 else 4
        self.fars = zeros // self.nears
        self.mates = max(self.uppers // 2, 1)
        self.zeros = zeros

    def locate(self):
        node, zero = lax.axis_index("node"), lax.axis_index("zero")
        self.upper, self.core = node // 2, node % 2
        self.far, self.near = zero // self.nears, zero % self.nears

    def moved(self, upper=0, core=0, far=0, near=0, mate=0):
        row = lax.rem(self.upper + upper, self.uppers) if upper else self.upper
        if mate:
            group = self.upper // self.mates * self.mates
            row = group + lax.rem(self.upper - group + mate, self.mates)
        return (
            row,
            1 - self.core if core else self.core,
            lax.rem(self.far + far, self.fars) if far else self.far,
            lax.rem(self.near + near, self.nears) if near else self.near,
        )

    def device(self, **steps):
        upper, core, far, near = self.moved(**steps)
        return (upper * 2 + core, far * self.nears + near)

    def slot(self, upper, core, far, near):
        return (upper * 2 + core) * self.zeros + far * self.nears + near

    def peers(self):
        return (
            [dict(far=k) for k in range(1, self.fars)]
            + [dict(near=j) for j in range(1, self.nears)]
            + [dict(upper=i) for i in range(1, self.uppers)]
            + [dict(core=1)]
        )

    def greet(self, nodes=0):
        barrier = pltpu.get_barrier_semaphore()
        peers = [self.device(**steps) for steps in self.peers() if not nodes or set(steps) <= {"far", "near"}]
        if nodes:
            node, zero = lax.axis_index("node"), lax.axis_index("zero")
            peers += [(lax.rem(node + step, nodes), zero) for step in range(1, nodes)]
        for device in peers:
            pl.semaphore_signal(barrier, 1, device_id=device, device_id_type=MESH)
        pl.semaphore_wait(barrier, len(peers))


def half_rows(rows):
    return (rows // 2 + 15) // 16 * 16


def start_copy(started, place, source, target, sems, **steps):
    copy = pltpu.make_async_remote_copy(
        src_ref=source,
        dst_ref=target,
        send_sem=sems.at[0],
        recv_sem=sems.at[1],
        device_id=place.device(**steps),
        device_id_type=MESH,
    )
    copy.start()
    started.append(copy)
    return copy


def sixteens(rows):
    return -(-rows // 16) * 16


class Pieces:
    def __init__(self, sizes, first):
        self.sizes = sizes
        total = sum(sizes)
        cut = min(half_rows(total), sizes[first])
        self.whole = [(i, 0, size) for i, size in enumerate(sizes)]
        self.head = [(first, 0, cut)]
        self.tail = [(first, cut, sizes[first] - cut)] if cut < sizes[first] else []
        self.tail += [(i, 0, size) for i, size in enumerate(sizes) if i != first]


def send_pieces(started, place, pieces, sources, targets, sems, **steps):
    copies = []
    for index, (array, start, rows) in enumerate(pieces):
        part = pl.ds(start, rows)
        copies.append(
            start_copy(
                started, place, sources[array].at[part], targets[array].at[part], sems.at[index], **steps
            )
        )
    return copies


def wait_all(copies):
    for copy in copies:
        copy.wait_recv()


class Gather:
    def __init__(self, place, pieces, shards, outs, sems):
        self.place, self.pieces, self.shards, self.outs = place, pieces, shards, outs
        (self.own_sem, self.far_sem, self.near_sem, self.upper_sem, self.over_sem, self.under_sem, self.core_sem) = sems
        self.started, self.cores = [], []
        self.far, self.near, self.upper, self.over, self.under = {}, {}, {}, {}, {}

    def block(self, **steps):
        slot = self.place.slot(*self.place.moved(**steps))
        return [out.at[slot] for out in self.outs]

    def send(self, pieces, source, target, sems, **steps):
        return send_pieces(self.started, self.place, pieces, source, target, sems, **steps)

    def begin(self):
        here = self.block()
        self.kept = []
        for index, (shard, target) in enumerate(zip(self.shards, here)):
            copy = pltpu.make_async_copy(shard, target, self.own_sem.at[index])
            copy.start()
            self.kept.append(copy)
        for k in range(1, self.place.fars):
            self.far[k] = self.send(self.pieces.whole, self.shards, here, self.far_sem.at[k], far=k)

    def first(self, k):
        place, whole = self.place, self.pieces.whole
        if k:
            wait_all(self.far[k])
        target = self.block(far=(place.fars - k) % place.fars)
        source = target if k else self.shards
        for j in range(1, place.nears):
            self.near[k, j] = self.send(whole, source, target, self.near_sem.at[k, j], near=j)
        for i in range(1, place.uppers):
            self.upper[k, i] = self.send(whole, source, target, self.upper_sem.at[k, i], upper=i)
        self.cores += self.send(whole, source, target, self.core_sem.at[k, 0, 0], core=1)

    def second(self, k):
        place, whole = self.place, self.pieces.whole
        far = (place.fars - k) % place.fars
        for j in range(1, place.nears):
            wait_all(self.near[k, j])
            item = self.block(far=far, near=place.nears - j)
            for i in range(1, place.uppers):
                self.over[k, j, i] = self.send(
                    self.pieces.head, item, item, self.over_sem.at[k, j, i], upper=i
                )
            self.cores += self.send(whole, item, item, self.core_sem.at[k, j, 0], core=1)
        for i in range(1, place.uppers):
            wait_all(self.upper[k, i])
            item = self.block(far=far, upper=place.uppers - i)
            for j in range(1, place.nears):
                self.under[k, j, i] = self.send(
                    self.pieces.tail, item, item, self.under_sem.at[k, j, i], near=j
                )
            self.cores += self.send(whole, item, item, self.core_sem.at[k, 0, i], core=1)

    def third(self, k):
        place, whole = self.place, self.pieces.whole
        far = (place.fars - k) % place.fars
        for j in range(1, place.nears):
            for i in range(1, place.uppers):
                wait_all(self.over[k, j, i])
                wait_all(self.under[k, j, i])
                item = self.block(far=far, near=place.nears - j, upper=place.uppers - i)
                self.cores += self.send(whole, item, item, self.core_sem.at[k, j, i], core=1)

    def step(self, k):
        fars = self.place.fars
        if k < fars:
            self.first(k)
        if 1 <= k <= fars:
            self.second(k - 1)
        if k >= 2:
            self.third(k - 2)

    def end(self):
        for copy in self.kept:
            copy.wait()
        wait_all(self.cores)
        for copy in self.started:
            copy.wait_send()

    @staticmethod
    def sems(place, pieces):
        dma = pltpu.SemaphoreType.DMA
        fars, nears, uppers = place.fars, place.nears, place.uppers
        whole, head, tail = len(pieces.whole), len(pieces.head), len(pieces.tail)
        return [
            dma((whole,)),
            dma((fars, whole, 2)),
            dma((fars, nears, whole, 2)),
            dma((fars, uppers, whole, 2)),
            dma((fars, nears, uppers, head, 2)),
            dma((fars, nears, uppers, tail, 2)),
            dma((fars, nears, uppers, whole, 2)),
        ]


def iota(shape, axis):
    return lax.broadcasted_iota(jnp.int32, shape, axis)


def gather_and_count(nodes, zeros, weights, grid, scale, g2m, m2g, m2g_turned, neighbours, lent, lent_row, legendre, collective):
    place = Place(nodes, zeros)
    width = weights[0].shape[1]
    sizes = [sixteens(w.shape[0]) for w in weights]
    pieces = Pieces(sizes, 1)
    devices = nodes * zeros
    pixels, cin = grid.shape
    wide = -(-cin // 128) * 128
    rows, fanout = neighbours.shape
    halo = lent.shape[0]
    ext = rows + 2 * halo
    bands, lons, dec_edges = m2g.shape
    lats, lows, lanes = legendre.shape
    enc_edges = g2m.shape[1]
    tile = 128

    def kernel(
        attn_ref, mlp_ref, small_ref, grid_ref, scale_ref, g2m_ref, m2g_ref, turned_ref, near_ref, lent_ref,
        row_ref, leg_ref,
        attn_out, mlp_out, small_out, near_out, dec_out, turned_out, mixed_out, lend_out, lendt_out, kern_out,
        attn_shard, mlp_shard, small_shard, inputs, legs, parts, sums, leg_sem, part_sem, sum_sem, *sems,
    ):
        place.locate()
        node = lax.axis_index("node")
        shards = (attn_shard, mlp_shard, small_shard)
        for ref, shard, size in zip((attn_ref, mlp_ref, small_ref), shards, sizes):
            if ref.shape[0] < size:
                shard[...] = jnp.zeros_like(shard)
            shard[pl.ds(0, ref.shape[0])] = ref[...].astype(bf16)
        legs[node] = leg_ref[...]
        place.greet(nodes)
        gather = Gather(place, pieces, shards, (attn_out, mlp_out, small_out), sems)
        gather.begin()
        started = []
        leg_copies = []
        for step in range(1, nodes):
            target = (lax.rem(node + step, nodes), lax.axis_index("zero"))
            copy = pltpu.make_async_remote_copy(
                src_ref=leg_ref,
                dst_ref=legs.at[node],
                send_sem=leg_sem.at[step, 0],
                recv_sem=leg_sem.at[step, 1],
                device_id=target,
                device_id_type=MESH,
            )
            copy.start()
            leg_copies.append(copy)

        def count_near():
            @pl.loop(0, rows // tile)
            def _(index):
                spot = pl.ds(pl.multiple_of(index * tile, tile), tile)
                lists = near_ref[spot]
                place_of = iota((tile, ext), 1)
                total = jnp.zeros((tile, ext), f32)
                for j in range(fanout):
                    total += jnp.where(lists[:, j : j + 1] == place_of, 1.0, 0.0)
                near_out[spot] = total.astype(bf16)

        def count_dec():
            @pl.loop(0, bands)
            def _(band):
                lists = m2g_ref[band]
                place_of = iota((lons, rows), 1)
                total = jnp.zeros((lons, rows), f32)
                for j in range(dec_edges):
                    total += jnp.where(lists[:, j : j + 1] == place_of, 1.0, 0.0)
                dec_out[band] = total.astype(bf16)
                lists = turned_ref[band]
                place_of = iota((rows, lons), 0)
                total = jnp.zeros((rows, lons), f32)
                for j in range(dec_edges):
                    total += jnp.where(lists[j : j + 1] == place_of, 1.0, 0.0)
                turned_out[band] = total.astype(bf16)

        def mix():
            inputs[...] = (grid_ref[...].astype(f32) * scale_ref[...]).astype(bf16)
            mixed_out[...] = jnp.zeros_like(mixed_out)

            @pl.loop(0, rows // tile)
            def _(index):
                spot = pl.ds(pl.multiple_of(index * tile, tile), tile)
                lists = g2m_ref[spot]
                place_of = iota((tile, pixels), 1)
                total = jnp.zeros((tile, pixels), f32)
                for j in range(enc_edges):
                    total += jnp.where(lists[:, j : j + 1] == place_of, 1.0 / enc_edges, 0.0)
                mean = dot_nn(total.astype(bf16), inputs[...])
                high = mean.astype(bf16)
                mixed_out[0, spot, pl.ds(0, cin)] = high
                mixed_out[1, spot, pl.ds(0, cin)] = (mean - high.astype(f32)).astype(bf16)

        def lend():
            lend_out[...] = jnp.where(lent_ref[...] == iota((halo, rows), 1), 1.0, 0.0).astype(bf16)
            lendt_out[...] = jnp.where(row_ref[...] == iota((rows, 2 * halo), 0), 1.0, 0.0).astype(bf16)

        def gram():
            for copy in leg_copies:
                copy.wait()

            @pl.loop(0, nodes * lats)
            def _(index):
                other = legs[index // lats, lax.rem(index, lats)]
                for t in range(lats):
                    product = leg_ref[t] * other
                    parts[place.near, t, pl.ds(index, 1)] = jnp.sum(product, axis=0, keepdims=True)

            for j in range(1, place.nears):
                near_parts.append(
                    start_copy(
                        started, place, parts.at[place.near], parts.at[place.near], part_sem.at[j], near=j
                    )
                )

        near_parts, far_sums = [], []

        def gram_near():
            wait_all(near_parts)
            total = parts[0]
            for j in range(1, place.nears):
                total = total + parts[j]
            sums[place.far] = total
            for k in range(1, place.fars):
                far_sums.append(
                    start_copy(
                        started, place, sums.at[place.far], sums.at[place.far], sum_sem.at[k], far=k
                    )
                )

        def gram_far():
            wait_all(far_sums)
            total = sums[0]
            for k in range(1, place.fars):
                total = total + sums[k]
            kern_out[...] = total

        work = [lend, mix, gram, count_dec, gram_near, count_near, gram_far]
        steps = place.fars + 2
        for k in range(steps):
            gather.step(k)
            share = -(-len(work) // (steps - k))
            for part in work[:share]:
                part()
            work = work[share:]
        gather.end()
        for copy in started:
            copy.wait_send()

    vmem = pl.BlockSpec(memory_space=pltpu.VMEM)
    hbm = pl.BlockSpec(memory_space=pl.ANY)
    dma = pltpu.SemaphoreType.DMA
    struct = jax.ShapeDtypeStruct
    return pl.pallas_call(
        kernel,
        out_shape=tuple(struct((devices, size, width), bf16) for size in sizes)
        + (
            struct((rows, ext), bf16),
            struct((bands, lons, rows), bf16),
            struct((bands, rows, lons), bf16),
            struct((2, rows, wide), bf16),
            struct((halo, rows), bf16),
            struct((rows, 2 * halo), bf16),
            struct((lats, nodes * lats, lanes), f32),
        ),
        in_specs=[vmem] * 12,
        out_specs=(hbm,) * 3 + (vmem,) * 7,
        scratch_shapes=[pltpu.VMEM((size, width), bf16) for size in sizes]
        + [
            pltpu.VMEM((pixels, cin), bf16),
            pltpu.VMEM((nodes, lats, lows, lanes), f32),
            pltpu.VMEM((place.nears, lats, nodes * lats, lanes), f32),
            pltpu.VMEM((place.fars, lats, nodes * lats, lanes), f32),
            dma((nodes, 2)),
            dma((place.nears, 2)),
            dma((place.fars, 2)),
        ]
        + Gather.sems(place, pieces),
        compiler_params=pltpu.CompilerParams(
            collective_id=collective, has_side_effects=True, vmem_limit_bytes=56 << 20
        ),
    )(*weights, grid, scale, g2m, m2g, m2g_turned, neighbours, lent, lent_row, legendre)


def norm_parts(rows):
    centred = rows - jnp.mean(rows, axis=-1, keepdims=True)
    inverse = lax.rsqrt(jnp.mean(centred * centred, axis=-1, keepdims=True) + norm_epsilon)
    return centred * inverse, inverse


def model_step(
    nodes, zeros, weights, graph, kern, feats, base, keep, tables, scalars, first_channel, channels, dec_edges, collective
):
    place = Place(nodes, zeros)
    attn, mlp, small = weights
    near, dec, dec_turned, mixed, lend, lendt = graph
    width = attn.shape[1]
    hidden = mlp.shape[0] // 2
    rows, ext_rows = near.shape
    halo = lend.shape[0]
    bands, lons, _ = dec.shape
    wide = mixed.shape[2]
    lats, all_lats, lanes = kern.shape
    start = first_channel // 128 * 128
    shift = first_channel - start
    sent = sixteens(shift + channels)
    big, tile = 256, 128
    head_width = width // HEAD_COUNT
    score_scale = head_width ** (-0.5)
    third = 1.0 / dec_edges

    def kernel(
        attn_hbm, mlp_hbm, small_ref, near_hbm, dec_hbm, turned_hbm, mixed_ref, lend_ref, lendt_ref, kern_ref,
        feats_ref, base_ref, keep_ref, table_ref, scalar_ref,
        attn_out, mlp_out, high_out, low_out, loss_out,
        attn_ref, mlp_ref, near_ref, dec_ref, turned_ref, h0_ref, h1_ref, first_ref, q_ref, ext_ref, lent_ref,
        prob_ref, blend_ref, second_ref, activ_ref, slope_ref, out_ref, node_ref, f_ref, all_ref, gf_ref, gnet_ref,
        gb_ref, gattn_ref, gblend_ref, gext_ref, back_ref, lost_ref, sums_ref,
        load_sem, lend_sem, f_sem, pass_sem, back_sem,
    ):
        place.locate()
        node = lax.axis_index("node")
        zero = lax.axis_index("zero")
        loads = []
        for index, (source, target) in enumerate(
            (
                (attn_hbm, attn_ref),
                (near_hbm, near_ref),
                (mlp_hbm, mlp_ref),
                (dec_hbm, dec_ref),
                (turned_hbm, turned_ref),
            )
        ):
            copy = pltpu.make_async_copy(source, target, load_sem.at[index])
            copy.start()
            loads.append(copy)
        barrier = pltpu.get_barrier_semaphore()
        for step in range(1, nodes):
            pl.semaphore_signal(
                barrier, 1, device_id=(lax.rem(node + step, nodes), zero), device_id_type=MESH
            )
        started = []

        def to_node(step, source, target, sems):
            copy = pltpu.make_async_remote_copy(
                src_ref=source,
                dst_ref=target,
                send_sem=sems.at[0],
                recv_sem=sems.at[1],
                device_id=(lax.rem(node + step, nodes), zero),
                device_id_type=MESH,
            )
            copy.start()
            started.append(copy)
            return copy

        def row_loop(size, body):
            @pl.loop(0, rows // size)
            def _(index):
                body(pl.ds(pl.multiple_of(index * size, size), size))

        mods = dot_tn(feats_ref[...].astype(bf16), small_ref[...])
        mod = [mods[j : j + 1] for j in range(4)]
        enc = small_ref[pl.ds(0, wide)]
        loads[0].wait()

        def encode(spot):
            h0 = dot_nn(mixed_ref[0, spot], enc) + dot_nn(mixed_ref[1, spot], enc)
            h0_ref[spot] = h0
            unit, inverse = norm_parts(h0)
            first = (unit * (1.0 + mod[0]) + mod[1]).astype(bf16)
            first_ref[spot] = first
            ext_ref[spot] = dot_nt(first, attn_ref[pl.ds(width, 2 * width)]).astype(bf16)
            q_ref[spot] = dot_nt(first, attn_ref[pl.ds(0, width)]).astype(bf16)

        row_loop(big, encode)
        lent_ref[...] = dot_nn(lend_ref[...], ext_ref[pl.ds(0, rows)]).astype(bf16)
        pl.semaphore_wait(barrier, nodes - 1)
        up = to_node(1, lent_ref, ext_ref.at[pl.ds(rows, halo)], lend_sem.at[0])
        down = to_node(nodes - 1, lent_ref, ext_ref.at[pl.ds(rows + halo, halo)], lend_sem.at[1])
        loads[1].wait()
        up.wait_recv()
        down.wait_recv()

        def attend(spot):
            count = near_ref[spot].astype(f32)
            for head in range(HEAD_COUNT):
                part = pl.ds(head * head_width, head_width)
                values = pl.ds(width + head * head_width, head_width)
                logits = dot_nt(q_ref[spot, part], ext_ref[:, part]) * score_scale
                logits = jnp.where(count > 0.0, logits, -jnp.inf)
                raised = jnp.exp(logits - jnp.max(logits, axis=-1, keepdims=True))
                prob = raised * (1.0 / jnp.sum(raised * count, axis=-1, keepdims=True))
                prob = prob.astype(bf16)
                prob_ref[head, spot] = prob
                low = (prob.astype(f32) * count).astype(bf16)
                blend_ref[spot, part] = dot_nn(low, ext_ref[:, values]).astype(bf16)

        row_loop(tile, attend)
        loads[2].wait()
        dec_rows = small_ref[pl.ds(start, 128)]
        lane = iota((1, 128), 1)
        live = jnp.where((lane >= shift) & (lane < shift + channels), 1.0, 0.0)

        def feed(spot):
            h1 = h0_ref[spot] + dot_nt(blend_ref[spot], attn_ref[pl.ds(3 * width, width)])
            h1_ref[spot] = h1
            unit, inverse = norm_parts(h1)
            second = (unit * (1.0 + mod[2]) + mod[3]).astype(bf16)
            second_ref[spot] = second
            upper = dot_nt(second, mlp_ref[pl.ds(0, hidden)])
            square = upper * upper
            bend = jnp.tanh(gelu_scale * upper * (1.0 + gelu_cubic * square))
            half = 0.5 + 0.5 * bend
            activ = (upper * half).astype(bf16)
            activ_ref[spot] = activ
            slope = half + (0.5 * gelu_scale) * upper * (1.0 - bend * bend) * (
                1.0 + 3.0 * gelu_cubic * square
            )
            slope_ref[spot] = slope.astype(bf16)
            h2 = h1 + dot_nn(activ, mlp_ref[pl.ds(hidden, hidden)])
            high = h2.astype(bf16)
            out_ref[spot] = high
            low = (h2 - high.astype(f32)).astype(bf16)
            projected = (dot_nt(high, dec_rows) + dot_nt(low, dec_rows)) * live
            top = projected.astype(bf16)
            node_ref[spot, pl.ds(0, 128)] = top
            node_ref[spot, pl.ds(128, 128)] = (projected - top.astype(f32)).astype(bf16)

        row_loop(tile, feed)

        c_output, weight = scalar_ref[0], scalar_ref[1]
        loads[3].wait()
        cores, uppers = {}, {}
        for band in range(bands):
            net = dot_nn(dec_ref[band], node_ref[...])
            net = (net[:, :128] + net[:, 128:]) * (c_output * third)
            error = (base_ref[band] + net) * keep_ref[band]
            high = error.astype(bf16)
            low = (error - high.astype(f32)).astype(bf16)
            turned = dot_tn(high, table_ref[0]) + dot_tn(low, table_ref[0]) + dot_tn(high, table_ref[1])
            f_ref[band] = turned[:sent]
            all_ref[node, band] = turned[:sent].astype(bf16)
            piece = all_ref.at[node, band]
            cores[0, band] = start_copy(started, place, piece, piece, f_sem.at[0, band], core=1)
            for i in range(1, place.uppers):
                uppers[i, band] = start_copy(started, place, piece, piece, f_sem.at[i, band], upper=i)
        gf_ref[...] = jnp.zeros_like(gf_ref)
        for band in range(bands):
            for i in range(1, place.uppers):
                uppers[i, band].wait_recv()
                source = lax.rem(place.upper + place.uppers - i, place.uppers) * 2 + place.core
                piece = all_ref.at[source, band]
                cores[i, band] = start_copy(started, place, piece, piece, pass_sem.at[i, band], core=1)
        for key in cores:
            cores[key].wait_recv()
        loss_rows = jnp.zeros((8, 128), f32)
        loads[4].wait()
        for band in range(bands):

            def add_lat(index, total):
                return total + kern_ref[band, pl.ds(index, 1)] * all_ref[
                    index // lats, lax.rem(index, lats)
                ].astype(f32)

            total = lax.fori_loop(0, all_lats, add_lat, jnp.zeros((sent, lanes), f32), unroll=4)
            loss_rows = loss_rows + jnp.sum(total * f_ref[band])
            gf_ref[pl.ds(0, sent)] = total * (2.0 * weight)
            grad = gf_ref[...]
            high = grad.astype(bf16)
            low = (grad - high.astype(f32)).astype(bf16)
            back = dot_nt(table_ref[0], high) + dot_nt(table_ref[0], low) + dot_nt(table_ref[1], high)
            gnet_ref[band] = (back * keep_ref[band] * c_output).astype(bf16)
        loss_out[...] = loss_rows * weight

        sums_ref[...] = jnp.zeros_like(sums_ref)

        def back_feed(spot):
            grad_node = dot_nn(turned_ref[0, spot], gnet_ref[0])
            for band in range(1, bands):
                grad_node += dot_nn(turned_ref[band, spot], gnet_ref[band])
            grad_node = grad_node * third
            high = grad_node.astype(bf16)
            low = (grad_node - high.astype(f32)).astype(bf16)
            node_ref[spot, pl.ds(0, 128)] = high
            grad_out = dot_nn(high, dec_rows) + dot_nn(low, dec_rows)
            branch = grad_out.astype(bf16)
            gb_ref[spot] = branch
            grad_activ = dot_nt(branch, mlp_ref[pl.ds(hidden, hidden)])
            grad_upper = (grad_activ * slope_ref[spot].astype(f32)).astype(bf16)
            slope_ref[spot] = grad_upper
            grad_second = dot_nn(grad_upper, mlp_ref[pl.ds(0, hidden)])
            unit, inverse = norm_parts(h1_ref[spot])
            scaled = grad_second * (1.0 + mod[2])
            grad_mid = grad_out + inverse * (
                scaled
                - jnp.mean(scaled, axis=-1, keepdims=True)
                - unit * jnp.mean(scaled * unit, axis=-1, keepdims=True)
            )
            sums_ref[2:3] += jnp.sum(grad_second * unit, axis=0, keepdims=True)
            sums_ref[3:4] += jnp.sum(grad_second, axis=0, keepdims=True)
            h1_ref[spot] = grad_mid
            grad_attn = grad_mid.astype(bf16)
            gattn_ref[spot] = grad_attn
            gblend_ref[spot] = dot_nn(grad_attn, attn_ref[pl.ds(3 * width, width)]).astype(bf16)

        row_loop(tile, back_feed)

        def outer_loop(target, offset, left, right, columns):
            @pl.loop(0, columns // big)
            def _(index):
                part = pl.multiple_of(index * big, big)
                product = dot_tn(left[:, pl.ds(part, big)], right[...])
                target[pl.ds(pl.multiple_of(offset + part, big), big)] = product.astype(bf16)

        gext_ref[...] = jnp.zeros_like(gext_ref)

        def back_attend(spot):
            count = near_ref[spot].astype(f32)
            for head in range(HEAD_COUNT):
                part = pl.ds(head * head_width, head_width)
                values = pl.ds(width + head * head_width, head_width)
                prob = prob_ref[head, spot].astype(f32)
                counted_prob = prob * count
                grad_blend = gblend_ref[spot, part]
                grad_prob = dot_nt(grad_blend, ext_ref[:, values])
                mean = jnp.sum(counted_prob * grad_prob, axis=-1, keepdims=True)
                grad_logit = (counted_prob * (grad_prob - mean)).astype(bf16)
                gext_ref[:, part] += dot_tn(grad_logit, q_ref[spot, part])
                q_ref[spot, part] = (dot_nn(grad_logit, ext_ref[:, part]) * score_scale).astype(bf16)
                gext_ref[:, values] += dot_tn(counted_prob.astype(bf16), grad_blend)

        row_loop(tile, back_attend)
        gext_ref[:, pl.ds(0, width)] = gext_ref[:, pl.ds(0, width)] * score_scale
        lost_ref[0] = gext_ref[pl.ds(rows, halo)].astype(bf16)
        lost_ref[1] = gext_ref[pl.ds(rows + halo, halo)].astype(bf16)
        from_upper = to_node(nodes - 1, lost_ref.at[0], back_ref.at[pl.ds(0, halo)], back_sem.at[0])
        from_lower = to_node(1, lost_ref.at[1], back_ref.at[pl.ds(halo, halo)], back_sem.at[1])

        outer_loop(mlp_out, hidden, activ_ref, gb_ref, hidden)
        outer_loop(mlp_out, 0, slope_ref, second_ref, hidden)
        outer_loop(attn_out, 3 * width, gattn_ref, blend_ref, width)
        outer_loop(attn_out, 0, q_ref, first_ref, width)
        from_upper.wait_recv()
        from_lower.wait_recv()

        def back_encode(spot):
            grad_pairs = gext_ref[spot] + dot_nn(lendt_ref[spot], back_ref[...])
            grad_pairs = grad_pairs.astype(bf16)
            ext_ref[spot] = grad_pairs
            grad_first = dot_nn(q_ref[spot], attn_ref[pl.ds(0, width)]) + dot_nn(
                grad_pairs, attn_ref[pl.ds(width, 2 * width)]
            )
            unit, inverse = norm_parts(h0_ref[spot])
            scaled = grad_first * (1.0 + mod[0])
            grad_in = h1_ref[spot] + inverse * (
                scaled
                - jnp.mean(scaled, axis=-1, keepdims=True)
                - unit * jnp.mean(scaled * unit, axis=-1, keepdims=True)
            )
            sums_ref[0:1] += jnp.sum(grad_first * unit, axis=0, keepdims=True)
            sums_ref[1:2] += jnp.sum(grad_first, axis=0, keepdims=True)
            gb_ref[spot] = grad_in.astype(bf16)

        row_loop(big, back_encode)
        outer_loop(attn_out, width, ext_ref.at[pl.ds(0, rows)], first_ref, 2 * width)

        feats_value = feats_ref[...]
        small_rows = small_ref.shape[0]
        cond = feats_value[:, 0:1] * sums_ref[0:1]
        for j in range(1, 4):
            cond += feats_value[:, j : j + 1] * sums_ref[j : j + 1]
        for low_row in range(0, small_rows, 128):
            total = cond[low_row : low_row + 128]
            if low_row < wide:
                total += dot_tn(mixed_ref[0, :, pl.ds(low_row, 128)], gb_ref[...])
            if low_row == start:
                total += dot_tn(node_ref[:, pl.ds(0, 128)], out_ref[...])
            high = total.astype(bf16)
            high_out[pl.ds(low_row, 128)] = high
            low_out[pl.ds(low_row, 128)] = (total - high.astype(f32)).astype(bf16)
        for copy in started:
            copy.wait_send()

    vmem = pl.BlockSpec(memory_space=pltpu.VMEM)
    hbm = pl.BlockSpec(memory_space=pl.ANY)
    dma = pltpu.SemaphoreType.DMA
    struct = jax.ShapeDtypeStruct
    low = lambda *shape: pltpu.VMEM(shape, bf16)
    full = lambda *shape: pltpu.VMEM(shape, f32)
    return pl.pallas_call(
        kernel,
        out_shape=(
            struct(attn.shape, bf16),
            struct(mlp.shape, bf16),
            struct(small.shape, bf16),
            struct(small.shape, bf16),
            struct((8, 128), f32),
        ),
        in_specs=[hbm, hbm, vmem, hbm, hbm, hbm] + [vmem] * 8 + [pl.BlockSpec(memory_space=pltpu.SMEM)],
        out_specs=(vmem,) * 5,
        scratch_shapes=[
            low(*attn.shape),
            low(*mlp.shape),
            low(*near.shape),
            low(*dec.shape),
            low(*dec_turned.shape),
            full(rows, width),
            full(rows, width),
            low(rows, width),
            low(rows, width),
            low(ext_rows, 2 * width),
            low(halo, 2 * width),
            low(HEAD_COUNT, rows, ext_rows),
            low(rows, width),
            low(rows, width),
            low(rows, hidden),
            low(rows, hidden),
            low(rows, width),
            low(rows, 256),
            full(lats, sent, lanes),
            low(nodes, lats, sent, lanes),
            full(128, lanes),
            low(bands, lons, 128),
            low(rows, width),
            low(rows, width),
            low(rows, width),
            full(ext_rows, 2 * width),
            low(2 * halo, 2 * width),
            low(2, halo, 2 * width),
            full(8, width),
            dma((5,)),
            dma((2, 2)),
            dma((place.uppers, lats, 2)),
            dma((place.uppers, lats, 2)),
            dma((2, 2)),
        ],
        compiler_params=pltpu.CompilerParams(
            collective_id=collective, has_side_effects=True, vmem_limit_bytes=62 << 20
        ),
    )(attn, mlp, small, near, dec, dec_turned, mixed, lend, lendt, kern, feats, base, keep, tables, scalars)


class Scatter:
    def __init__(self, place, pieces, grads, bufs, sems):
        self.place, self.pieces, self.grads = place, pieces, grads
        count = len(grads)
        self.core_in = bufs[:count]
        (self.over_out, self.over_in, self.under_out, self.under_in, self.over_out2, self.over_in2,
         self.under_out2, self.under_in2, self.far_out, self.far_in) = bufs[count:]
        (self.core_sem, self.over_sem, self.under_sem, self.over_sem2, self.under_sem2, self.far_sem) = sems
        self.started = []
        self.order = list(range(1, place.fars)) + [0]
        self.core, self.over, self.under, self.over2, self.under2, self.far = {}, {}, {}, {}, {}, {}
        self.head_rows = sum(rows for _, _, rows in pieces.head)
        self.tail_rows = sum(rows for _, _, rows in pieces.tail)

    def send(self, source, target, sem, **steps):
        return start_copy(self.started, self.place, source, target, sem, **steps)

    def begin(self, arrays):
        place = self.place
        other = 1 - place.core
        for k in self.order:
            far = place.moved(far=k)[2]
            for upper in range(place.uppers):
                spot = pl.ds(place.slot(upper, other, far, 0), place.nears)
                for a in arrays:
                    self.core[k, upper, a] = self.send(
                        self.grads[a].at[spot], self.core_in[a].at[k, upper], self.core_sem.at[k, upper, a], core=1
                    )

    def add(self, target, k, upper, near, pieces, others):
        far = self.place.moved(far=k)[2]
        slot = self.place.slot(upper, self.place.core, far, near)
        offset = 0
        for array, start, rows in pieces:
            mine = self.grads[array].at[slot]
            theirs = self.core_in[array].at[k, upper, near]

            @pl.loop(0, rows // ROW_CHUNK)
            def _(index, start=start, offset=offset, mine=mine, theirs=theirs):
                step = index * ROW_CHUNK
                here = pl.ds(pl.multiple_of(start + step, ROW_CHUNK), ROW_CHUNK)
                there = pl.ds(pl.multiple_of(offset + step, ROW_CHUNK), ROW_CHUNK)
                total = mine[here].astype(f32) + theirs[here].astype(f32)
                for other in others:
                    total += other[there].astype(f32)
                target[there] = total.astype(target.dtype)

            offset += rows

    def one(self, k):
        place, pieces = self.place, self.pieces
        for key in self.core:
            if key[0] == k:
                self.core[key].wait_recv()
        for i in range(1, place.uppers):
            for near in range(place.nears):
                self.add(self.over_out.at[k, i - 1, near], k, place.moved(upper=i)[0], near, pieces.head, [])
            self.over[k, i] = self.send(
                self.over_out.at[k, i - 1], self.over_in.at[k, i - 1], self.over_sem.at[k, i], upper=i
            )
        for j in range(1, place.nears):
            for upper in range(place.uppers):
                self.add(self.under_out.at[k, j - 1, upper], k, upper, place.moved(near=j)[3], pieces.tail, [])
            self.under[k, j] = self.send(
                self.under_out.at[k, j - 1], self.under_in.at[k, j - 1], self.under_sem.at[k, j], near=j
            )

    def overs(self, k, near):
        return [self.over_in.at[k, i - 1, near] for i in range(1, self.place.uppers)]

    def unders(self, k, upper):
        return [self.under_in.at[k, j - 1, upper] for j in range(1, self.place.nears)]

    def two(self, k):
        place, pieces = self.place, self.pieces
        for i in range(1, place.uppers):
            self.over[k, i].wait_recv()
        for j in range(1, place.nears):
            near = place.moved(near=j)[3]
            self.add(self.over_out2.at[k, j - 1], k, place.upper, near, pieces.head, self.overs(k, near))
            self.over2[k, j] = self.send(
                self.over_out2.at[k, j - 1], self.over_in2.at[k, j - 1], self.over_sem2.at[k, j], near=j
            )
        for j in range(1, place.nears):
            self.under[k, j].wait_recv()
        for i in range(1, place.uppers):
            upper = place.moved(upper=i)[0]
            self.add(self.under_out2.at[k, i - 1], k, upper, place.near, pieces.tail, self.unders(k, upper))
            self.under2[k, i] = self.send(
                self.under_out2.at[k, i - 1], self.under_in2.at[k, i - 1], self.under_sem2.at[k, i], upper=i
            )

    def three(self, k, target, extra):
        place, pieces = self.place, self.pieces
        for j in range(1, place.nears):
            self.over2[k, j].wait_recv()
        for i in range(1, place.uppers):
            self.under2[k, i].wait_recv()
        head, tail = pl.ds(0, self.head_rows), pl.ds(self.head_rows, self.tail_rows)
        self.add(
            target.at[head], k, place.upper, place.near, pieces.head,
            self.overs(k, place.near)
            + [self.over_in2.at[k, j - 1] for j in range(1, place.nears)]
            + [item.at[head] for item in extra],
        )
        self.add(
            target.at[tail], k, place.upper, place.near, pieces.tail,
            self.unders(k, place.upper)
            + [self.under_in2.at[k, i - 1] for i in range(1, place.uppers)]
            + [item.at[tail] for item in extra],
        )

    def step(self, step):
        fars, order = self.place.fars, self.order
        if step < fars:
            self.one(order[step])
        if 1 <= step <= fars:
            self.two(order[step - 1])
        if step >= 2 and order[step - 2]:
            k = order[step - 2]
            self.three(k, self.far_out.at[k - 1], [])
            self.far[k] = self.send(self.far_out.at[k - 1], self.far_in.at[k - 1], self.far_sem.at[k], far=k)

    def steps(self):
        return self.place.fars + 2

    def finish(self, own):
        fars = self.place.fars
        for k in range(1, fars):
            self.far[k].wait_recv()
        self.three(0, own, [self.far_in.at[k - 1] for k in range(1, fars)])

    def end(self):
        for copy in self.started:
            copy.wait_send()

    @staticmethod
    def scratch(place, pieces, width):
        fars, nears, uppers = place.fars, place.nears, place.uppers
        head = sum(rows for _, _, rows in pieces.head)
        tail = sum(rows for _, _, rows in pieces.tail)
        vmem = lambda *shape: pltpu.VMEM(shape + (width,), bf16)
        dma = pltpu.SemaphoreType.DMA
        bufs = [vmem(fars, uppers, nears, size) for size in pieces.sizes]
        bufs += [vmem(fars, uppers - 1, nears, head)] * 2
        bufs += [vmem(fars, nears - 1, uppers, tail)] * 2
        bufs += [vmem(fars, nears - 1, head)] * 2
        bufs += [vmem(fars, uppers - 1, tail)] * 2
        bufs += [vmem(fars - 1, head + tail)] * 2
        sems = [
            dma((fars, uppers, len(pieces.sizes), 2)),
            dma((fars, uppers, 2)),
            dma((fars, nears, 2)),
            dma((fars, nears, 2)),
            dma((fars, uppers, 2)),
            dma((fars, 2)),
        ]
        return bufs, sems


class MomentGather:
    def __init__(self, place, shards, outs, sems):
        self.place, self.shards, self.outs = place, shards, outs
        (self.own_sem, self.far_sem, self.near_sem, self.spread_sem, self.core_sem) = sems
        self.started, self.cores = [], []
        self.far, self.near, self.spread_copies = {}, {}, {}

    def block(self, **steps):
        slot = self.place.slot(*self.place.moved(**steps))
        return [out.at[slot] for out in self.outs]

    def send(self, source, target, sem, **steps):
        return start_copy(self.started, self.place, source, target, sem, **steps)

    def both(self, source, target, sems, **steps):
        return [self.send(source[a], target[a], sems.at[a], **steps) for a in range(2)]

    def spread(self, k, j, source, target):
        place = self.place
        for i in range(1, place.uppers):
            self.spread_copies[k, j, i, 0] = self.send(
                source[0], target[0], self.spread_sem.at[k, j, i, 0], upper=i
            )
        for i in range(1, place.mates):
            self.spread_copies[k, j, i, 1] = self.send(
                source[1], target[1], self.spread_sem.at[k, j, i, 1], mate=i
            )
        self.cores += self.both(source, target, self.core_sem.at[k, j, 0], core=1)

    def run(self):
        place = self.place
        fars, nears = place.fars, place.nears
        here = self.block()
        kept = [
            pltpu.make_async_copy(shard, target, self.own_sem.at[a])
            for a, (shard, target) in enumerate(zip(self.shards, here))
        ]
        for copy in kept:
            copy.start()
        for k in range(1, fars):
            self.far[k] = self.both(self.shards, here, self.far_sem.at[k], far=k)
        for step in range(fars + 2):
            if step < fars:
                k = step
                if k:
                    wait_all(self.far[k])
                target = self.block(far=(fars - k) % fars)
                source = target if k else self.shards
                for j in range(1, nears):
                    self.near[k, j] = self.both(source, target, self.near_sem.at[k, j], near=j)
                self.spread(k, 0, source, target)
            if 1 <= step <= fars:
                k = step - 1
                for j in range(1, nears):
                    wait_all(self.near[k, j])
                    item = self.block(far=(fars - k) % fars, near=nears - j)
                    self.spread(k, j, item, item)
            if step >= 2:
                k = step - 2
                for j in range(nears):
                    steps = dict(far=(fars - k) % fars, near=(nears - j) % nears)
                    for key in self.spread_copies:
                        if key[:2] != (k, j):
                            continue
                        i, a = key[2:]
                        self.spread_copies[key].wait_recv()
                        if a:
                            item = self.block(mate=place.mates - i, **steps)[1]
                        else:
                            item = self.block(upper=place.uppers - i, **steps)[0]
                        self.cores.append(self.send(item, item, self.core_sem.at[k, j, i, a], core=1))
        for copy in kept:
            copy.wait()
        wait_all(self.cores)
        for copy in self.started:
            copy.wait_send()

    @staticmethod
    def sems(place):
        dma = pltpu.SemaphoreType.DMA
        fars, nears, uppers = place.fars, place.nears, place.uppers
        return [
            dma((2,)),
            dma((fars, 2, 2)),
            dma((fars, nears, 2, 2)),
            dma((fars, nears, uppers, 2, 2)),
            dma((fars, nears, uppers, 2, 2)),
        ]


def total_body(place, tile, slots, sems):
    value = tile
    upper, core, far, near = place.moved()
    stages = (
        ("core", 2, core),
        ("near", place.nears, near),
        ("upper", place.uppers, upper),
        ("far", place.fars, far),
    )
    for stage, (name, size, mine) in enumerate(stages):
        slots[stage, mine] = value
        copies = []
        for step in range(1, size):
            piece = slots.at[stage, mine]
            start_copy(copies, place, piece, piece, sems.at[stage, step], **{name: step})
        for copy in copies:
            copy.wait()
        value = slots[stage, 0]
        for other in range(1, size):
            value = value + slots[stage, other]
    return value


def reduce_and_gather(nodes, zeros, names, grads, mlp_sum, loss_tile, mom_attn, mom_mlp, small_rows, collective):
    place = Place(nodes, zeros)
    devices, _, width = grads[0].shape
    attn_rows, mlp_rows = mom_attn.shape[0], mom_mlp.shape[0]
    lead = names.index("mlp") if "mlp" in names else 0
    pieces = Pieces([item.shape[1] for item in grads], lead)
    moment_sizes = (sixteens(attn_rows), sixteens(mlp_rows))
    bufs, sems = Scatter.scratch(place, pieces, width)
    deepest = max(place.fars, place.uppers, place.nears, 2)
    summed = [] if mlp_sum is None else [mlp_sum]
    count = len(grads)
    starts, offset = {}, 0
    for array in [lead] + [i for i in range(count) if i != lead]:
        starts[names[array]] = offset
        offset += pieces.sizes[array]

    def kernel(*refs):
        grad_refs = refs[:count]
        refs = refs[count:]
        if summed:
            sum_ref, *refs = refs
        loss_ref, attn_ref, mlp_ref = refs[:3]
        small_out, attn_out, mlp_out, total_out, attn_all, mlp_all = refs[3:9]
        own, attn_shard, mlp_shard, slots, slot_sems = refs[9:14]
        rest = refs[14:]
        place.locate()
        place.greet()
        scatter = Scatter(
            place, pieces, grad_refs, rest[: len(bufs)], rest[len(bufs) : len(bufs) + len(sems)]
        )
        scatter.begin([lead] + [i for i in range(count) if i != lead])
        for step in range(scatter.steps()):
            scatter.step(step)
        scatter.finish(own)
        g_attn = own[pl.ds(starts["attn"], attn_rows)]
        g_mlp = sum_ref[...] if summed else own[pl.ds(starts["mlp"], mlp_rows)]
        g_small = own[pl.ds(starts["high"], small_rows)] + own[pl.ds(starts["low"], small_rows)]
        small_out[...] = g_small
        squares = jnp.sum(g_attn * g_attn) + jnp.sum(g_mlp * g_mlp) + jnp.sum(g_small * g_small)
        tile = jnp.where(iota((8, 128), 0) < 4, squares, loss_ref[...])
        total = total_body(place, tile, slots, slot_sems)
        total_out[...] = total
        factor = jnp.minimum(1.0, clip_limit * lax.rsqrt(total[0:1, 0:1]))
        for ref, out, shard, grad, size in (
            (attn_ref, attn_out, attn_shard, g_attn, attn_rows),
            (mlp_ref, mlp_out, mlp_shard, g_mlp, mlp_rows),
        ):
            moment = moment_decay * ref[...] + factor * grad
            out[...] = moment
            if size < shard.shape[0]:
                shard[...] = jnp.zeros_like(shard)
            shard[pl.ds(0, size)] = moment.astype(bf16)
        moments = MomentGather(
            place, (attn_shard, mlp_shard), (attn_all, mlp_all), rest[len(bufs) + len(sems) :]
        )
        moments.run()
        scatter.end()

    vmem = pl.BlockSpec(memory_space=pltpu.VMEM)
    hbm = pl.BlockSpec(memory_space=pl.ANY)
    struct = jax.ShapeDtypeStruct
    return pl.pallas_call(
        kernel,
        out_shape=(
            struct((small_rows, width), f32),
            struct((attn_rows, width), f32),
            struct((mlp_rows, width), f32),
            struct((8, 128), f32),
            struct((devices, moment_sizes[0], width), bf16),
            struct((devices, moment_sizes[1], width), bf16),
        ),
        in_specs=[vmem] * (count + len(summed) + 3),
        out_specs=(vmem,) * 4 + (hbm,) * 2,
        scratch_shapes=[
            pltpu.VMEM((sum(pieces.sizes), width), f32),
            pltpu.VMEM((moment_sizes[0], width), bf16),
            pltpu.VMEM((moment_sizes[1], width), bf16),
            pltpu.VMEM((4, deepest, 8, 128), f32),
            pltpu.SemaphoreType.DMA((4, deepest, 2)),
        ]
        + bufs
        + sems
        + MomentGather.sems(place),
        compiler_params=pltpu.CompilerParams(
            collective_id=collective, has_side_effects=True, vmem_limit_bytes=56 << 20
        ),
    )(*grads, *summed, loss_tile, mom_attn, mom_mlp)


def basis_apply(gram, moment):
    size = gram.shape[0]
    eye = jnp.where(iota((size, size), 0) == iota((size, size), 1), 1.0, 0.0)
    trace = jnp.sum(jnp.sum(gram * eye, axis=1, keepdims=True), axis=0, keepdims=True)
    scale = lax.rsqrt(trace + trace_epsilon)
    current = gram * (scale * scale)
    result = moment * scale
    for iteration in range(NS_ITERS):
        low = current.astype(bf16)
        rest = newton_second * current + newton_third * dot_nn(low, low)
        rest_low = rest.astype(bf16)
        result = newton_first * result + dot_nn(result.astype(bf16), rest_low)
        if iteration + 1 < NS_ITERS:
            once = dot_nn(rest_low, low)
            current = (
                (newton_first * newton_first) * current
                + (2.0 * newton_first) * once
                + dot_nn(once.astype(bf16), rest_low)
            )
    return result


def update_weights(nodes, zeros, attn_all, mlp_all, totals, g_small, moments, weights, averages, small_moments):
    width = attn_all.shape[1]
    attn_rows, mlp_rows, small_rows = [w.shape[0] for w in weights]
    half = mlp_all.shape[0] // 2
    block = width
    inputs = (g_small, *moments, *weights, *averages, *small_moments)
    count = len(inputs)

    def kernel(attn_hbm, mlp_hbm, total_ref, *refs):
        sources, refs = refs[:count], refs[count:]
        loss_out, clip_out, new_attn, new_mlp, new_small, new_m, new_v, new_e_attn, new_e_mlp, new_e_small = refs[:10]
        attn_ref, mlp_ref, gram_attn, gram_mlp, attn_sem, mlp_sem, row_sem = refs[10:17]
        rows = refs[17:]
        g_small_ref, mom_attn, mom_mlp, w_attn, w_mlp, w_small, e_attn, e_mlp, e_small, m_ref, v_ref = rows
        flat = lax.axis_index("node") * zeros + lax.axis_index("zero")
        attn_upper = flat * attn_rows >= 3 * width
        mlp_upper = flat * mlp_rows >= half
        copy_mlp = pltpu.make_async_copy(
            mlp_hbm.at[pl.ds(pl.multiple_of(jnp.where(mlp_upper, half, 0), half), half)], mlp_ref, mlp_sem
        )
        copy_attn = pltpu.make_async_copy(attn_hbm, attn_ref, attn_sem)
        copy_mlp.start()
        copy_attn.start()
        copies = [
            pltpu.make_async_copy(source, target, row_sem.at[index])
            for index, (source, target) in enumerate(zip(sources, rows))
        ]
        for copy in copies:
            copy.start()
        loss_out[...] = total_ref[4:5, 0:1]
        clip_out[...] = jnp.sqrt(total_ref[0:1, 0:1])
        copy_mlp.wait()
        gram_mlp[...] = jnp.zeros_like(gram_mlp)

        @pl.loop(0, half // block)
        def _(index):
            part = mlp_ref[pl.ds(pl.multiple_of(index * block, block), block)]
            gram_mlp[...] += dot_tn(part, part)

        copy_attn.wait()
        gram_attn[...] = jnp.zeros_like(gram_attn)
        start = jnp.where(attn_upper, 3, 0)

        @pl.loop(start, jnp.where(attn_upper, 4, 3))
        def _(index):
            part = attn_ref[pl.ds(pl.multiple_of(index * block, block), block)]
            gram_attn[...] += dot_tn(part, part)

        for copy in copies:
            copy.wait()

        factor = jnp.minimum(1.0, clip_limit * lax.rsqrt(total_ref[0:1, 0:1]))
        clipped = factor * g_small_ref[...]
        first = adam_first * m_ref[...] + (1.0 - adam_first) * clipped
        second = adam_second * v_ref[...] + (1.0 - adam_second) * clipped * clipped
        new_m[...] = first
        new_v[...] = second
        small = w_small[...] - adam_rate * (first / (1.0 - adam_first**STEP)) / (
            jnp.sqrt(second / (1.0 - adam_second**STEP)) + adam_epsilon
        )
        new_small[...] = small
        new_e_small[...] = average_decay * e_small[...] + (1.0 - average_decay) * small

        attn_step = basis_apply(gram_attn[...], mom_attn[...])
        mlp_step = basis_apply(gram_mlp[...], mom_mlp[...])
        attn_factor = jnp.where(attn_upper, 0.2 * math.sqrt(width), 0.2 * math.sqrt(3 * width))
        mlp_factor = 0.2 * math.sqrt(max(half, width))
        for step, rate, old, new, mean, new_mean in (
            (attn_step, orthogonal_rate * attn_factor, w_attn, new_attn, e_attn, new_e_attn),
            (mlp_step, orthogonal_rate * mlp_factor, w_mlp, new_mlp, e_mlp, new_e_mlp),
        ):
            value = old[...] - rate * step
            new[...] = value
            new_mean[...] = average_decay * mean[...] + (1.0 - average_decay) * value

    vmem = pl.BlockSpec(memory_space=pltpu.VMEM)
    hbm = pl.BlockSpec(memory_space=pl.ANY)
    one = jnp.zeros((1, 1), f32)
    outs = [one, one, weights[0], weights[1], weights[2], weights[2], weights[2], weights[0], weights[1], weights[2]]
    return pl.pallas_call(
        kernel,
        out_shape=tuple(jax.ShapeDtypeStruct(item.shape, f32) for item in outs),
        in_specs=[hbm, hbm, vmem] + [hbm] * count,
        out_specs=(vmem,) * 10,
        scratch_shapes=[
            pltpu.VMEM(attn_all.shape, bf16),
            pltpu.VMEM((half, width), bf16),
            pltpu.VMEM((width, width), f32),
            pltpu.VMEM((width, width), f32),
            pltpu.SemaphoreType.DMA,
            pltpu.SemaphoreType.DMA,
            pltpu.SemaphoreType.DMA((count,)),
        ]
        + [pltpu.VMEM(item.shape, f32) for item in inputs],
        compiler_params=pltpu.CompilerParams(vmem_limit_bytes=48 << 20),
    )(attn_all, mlp_all, totals, *inputs)


def train_step(nodes, zeros, weights, grid, target, land, near_turned, enc_turned, dec_turned, lent, legendre, vector, tables, cin, collective):
    place = Place(nodes, zeros)
    devices = nodes * zeros
    attn_rows, mlp_rows, small_rows = [w.shape[0] for w in weights]
    width = weights[0].shape[1]
    hidden = devices * mlp_rows // 2
    bands, lons, channels = target.shape
    fanout, rows = near_turned.shape
    enc_edges, dec_edges = enc_turned.shape[0], dec_turned.shape[0]
    halo = lent.shape[1]
    ext_rows = rows + 2 * halo
    lats, lows, lanes = legendre.shape
    all_lats = nodes * lats
    wide = -(-cin // 128) * 128
    start = cin // 128 * 128
    shift = cin - start
    sent = sixteens(channels)
    flat_lons = -(-lons // 128) * 128
    flat_pixels = -(-bands * lons // 128) * 128
    all_small = devices * small_rows
    cond_start = cin + channels
    big, tile = 256, 128
    head_width = width // HEAD_COUNT
    score_scale = head_width ** (-0.5)
    third = 1.0 / dec_edges
    first_pieces = Pieces([attn_rows, small_rows], 0)
    mlp_pieces = Pieces([mlp_rows], 0)
    scatter_bufs, scatter_sems = Scatter.scratch(place, mlp_pieces, width)
    gather_sems_a, gather_sems_b = Gather.sems(place, first_pieces), Gather.sems(place, mlp_pieces)

    def kernel(
        attn_in, mlp_in, small_in, grid_ref, target_ref, land_ref, near_in, enc_in, dec_in, lent_ref, leg_ref,
        vector_ref, table_ref,
        attn_out, mlp_sum, high_out, low_out, loss_out,
        attn_shard, mlp_shard, small_shard, legs, parts, sums, kern_ref,
        attn_ref, mlp_ref, small_ref, near_ref, dec_ref, mixed_ref, lendt_ref, h0_ref, h1_ref, first_ref, q_ref,
        ext_ref, lent_rows, prob_ref, blend_ref, second_ref, activ_ref, slope_ref, out_ref, node_ref, f_ref, all_ref,
        gf_ref, gnet_ref, gnode_ref, gb_ref, gattn_ref, gblend_ref, gext_ref, back_ref, lost_ref, sums_ref,
        error_ref, column_ref, lists_ref, input_ref, dec_rows_ref, feats_ref, total_ref,
        leg_sem, part_sem, sum_sem, lend_sem, f_sem, pass_sem, back_sem,
        *rest,
    ):
        sems_a, rest = rest[: len(gather_sems_a)], rest[len(gather_sems_a) :]
        sems_b, rest = rest[: len(gather_sems_b)], rest[len(gather_sems_b) :]
        bufs, sems_c = rest[: len(scatter_bufs)], rest[len(scatter_bufs) :]
        place.locate()
        node = lax.axis_index("node")
        zero = lax.axis_index("zero")
        attn_shard[...] = attn_in[...].astype(bf16)
        small_shard[...] = small_in[...].astype(bf16)
        legs[node] = leg_ref[...]
        place.greet(nodes)
        gather = Gather(place, first_pieces, (attn_shard, small_shard), (attn_ref, small_ref), sems_a)
        gather_mlp = Gather(place, mlp_pieces, (mlp_shard,), (mlp_ref,), sems_b)
        gather.begin()
        started = []

        def to_node(step, source, target, sems):
            copy = pltpu.make_async_remote_copy(
                src_ref=source,
                dst_ref=target,
                send_sem=sems.at[0],
                recv_sem=sems.at[1],
                device_id=(lax.rem(node + step, nodes), zero),
                device_id_type=MESH,
            )
            copy.start()
            started.append(copy)
            return copy

        gather.step(0)
        leg_copies = [
            to_node(step, leg_ref, legs.at[node], leg_sem.at[step]) for step in range(1, nodes)
        ]
        mlp_shard[...] = mlp_in[...].astype(bf16)
        gather_mlp.begin()

        def row_loop(size, body, hooks=()):
            count = rows // size
            cuts = [count * i // (len(hooks) + 1) for i in range(len(hooks) + 2)]
            for i in range(len(hooks) + 1):

                @pl.loop(cuts[i], cuts[i + 1])
                def _(index):
                    body(pl.ds(pl.multiple_of(index * size, size), size))

                if i < len(hooks):
                    hooks[i]()

        def mix():
            column_ref[pl.ds(0, enc_edges), pl.ds(0, rows)] = enc_in[...]
            lists_ref[pl.ds(0, rows), pl.ds(0, 8)] = jnp.transpose(column_ref[pl.ds(0, 8), pl.ds(0, rows)])
            lane = iota((1, cin), 1)
            scale = jnp.where(lane < channels, vector_ref[0:1, c_input_lane : c_input_lane + 1], 1.0)

            @pl.loop(0, bands)
            def _(band):
                input_ref[band] = (grid_ref[band].astype(f32) * scale).astype(bf16)

            mixed_ref[...] = jnp.zeros_like(mixed_ref)

            def mix_rows(spot):
                lists = lists_ref[spot]
                mean = jnp.zeros((tile, cin), f32)
                for band in range(bands):
                    place_of = iota((tile, lons), 1) + band * lons
                    total = jnp.zeros((tile, lons), f32)
                    for j in range(enc_edges):
                        total += jnp.where(lists[:, j : j + 1] == place_of, 1.0 / enc_edges, 0.0)
                    mean += dot_nn(total.astype(bf16), input_ref[band])
                high = mean.astype(bf16)
                mixed_ref[0, spot, pl.ds(0, cin)] = high
                mixed_ref[1, spot, pl.ds(0, cin)] = (mean - high.astype(f32)).astype(bf16)

            row_loop(tile, mix_rows)

        def count_near():
            lists_ref[pl.ds(0, rows), pl.ds(0, fanout)] = jnp.transpose(near_in[...])

            def count_rows(spot):
                lists = lists_ref[spot]
                place_of = iota((tile, ext_rows), 1)
                total = jnp.zeros((tile, ext_rows), f32)
                for j in range(fanout):
                    total += jnp.where(lists[:, j : j + 1] == place_of, 1.0, 0.0)
                near_ref[spot] = total.astype(bf16)

            row_loop(tile, count_rows)

        def count_dec():
            column_ref[pl.ds(0, dec_edges), pl.ds(0, bands * lons)] = dec_in[...]
            lists_ref[:, pl.ds(0, 8)] = jnp.transpose(column_ref[...])

            @pl.loop(0, bands)
            def _(band):
                lists = lists_ref[pl.ds(pl.multiple_of(band * lons, 8), lons)]
                place_of = iota((lons, rows), 1)
                total = jnp.zeros((lons, rows), f32)
                for j in range(dec_edges):
                    total += jnp.where(lists[:, j : j + 1] == place_of, 1.0, 0.0)
                dec_ref[band] = total.astype(bf16)

        near_parts, far_sums = [], []

        def gram():
            for copy in leg_copies:
                copy.wait_recv()

            @pl.loop(0, all_lats)
            def _(index):
                other = legs[index // lats, lax.rem(index, lats)]
                for t in range(lats):
                    parts[place.near, t, pl.ds(index, 1)] = jnp.sum(leg_ref[t] * other, axis=0, keepdims=True)

            for j in range(1, place.nears):
                piece = parts.at[place.near]
                near_parts.append(start_copy(started, place, piece, piece, part_sem.at[j], near=j))

        def gram_near():
            wait_all(near_parts)
            total = parts[0]
            for j in range(1, place.nears):
                total = total + parts[j]
            sums[place.far] = total
            for k in range(1, place.fars):
                piece = sums.at[place.far]
                far_sums.append(start_copy(started, place, piece, piece, sum_sem.at[k], far=k))

        def gram_far():
            wait_all(far_sums)
            total = sums[0]
            for k in range(1, place.fars):
                total = total + sums[k]
            kern_ref[...] = total

        lendt_ref[...] = jnp.where(lent_ref[...] == iota((rows, halo), 0), 1.0, 0.0).astype(bf16)
        work = [mix, gram, count_dec, gram_near]
        for k in range(1, place.fars + 2):
            gather.step(k)
            if k == 1:
                gather_mlp.step(0)
            if work:
                work.pop(0)()
        while work:
            work.pop(0)()
        gather.end()
        gather_mlp.step(1)

        def small_part(low, size):
            return small_ref[pl.ds(low // small_rows, size // small_rows)].reshape(size, width)

        row = iota((all_small, 128), 0) - cond_start
        lane = iota((all_small, 128), 1)
        feature = vector_ref[0:1]
        block = jnp.where(row >= 0, row // NOISE_FEATS, 4)
        picked = jnp.where((row - block * NOISE_FEATS == lane) & (block < 4) & (lane < NOISE_FEATS), feature, 0.0)
        column = jnp.sum(picked, axis=1, keepdims=True)
        feats_ref[...] = jnp.where(lane == block, column, 0.0)
        mods = dot_tn(feats_ref[...].astype(bf16), small_part(0, all_small))
        mod = [mods[j : j + 1] for j in range(4)]

        def attn_part(low, size):
            return attn_ref[pl.ds(low // attn_rows, size // attn_rows)].reshape(size, width)

        def mlp_part(low):
            return mlp_ref[pl.ds(low // mlp_rows, hidden // mlp_rows)].reshape(hidden, width)

        def encode(spot):
            enc = small_part(0, wide)
            h0 = dot_nn(mixed_ref[0, spot], enc) + dot_nn(mixed_ref[1, spot], enc)
            h0_ref[spot] = h0
            unit, inverse = norm_parts(h0)
            first = (unit * (1.0 + mod[0]) + mod[1]).astype(bf16)
            first_ref[spot] = first
            ext_ref[spot] = dot_nt(first, attn_part(width, 2 * width)).astype(bf16)
            q_ref[spot] = dot_nt(first, attn_part(0, width)).astype(bf16)

        row_loop(big, encode)
        lent_rows[...] = dot_tn(lendt_ref[...], ext_ref[pl.ds(0, rows)]).astype(bf16)
        up = to_node(1, lent_rows, ext_ref.at[pl.ds(rows, halo)], lend_sem.at[0])
        down = to_node(nodes - 1, lent_rows, ext_ref.at[pl.ds(rows + halo, halo)], lend_sem.at[1])
        gather_mlp.step(2)
        count_near()
        gram_far()
        gather_mlp.step(3)
        up.wait_recv()
        down.wait_recv()

        def attend(spot):
            count = near_ref[spot].astype(f32)
            for head in range(HEAD_COUNT):
                part = pl.ds(head * head_width, head_width)
                values = pl.ds(width + head * head_width, head_width)
                logits = dot_nt(q_ref[spot, part], ext_ref[:, part]) * score_scale
                logits = jnp.where(count > 0.0, logits, -jnp.inf)
                raised = jnp.exp(logits - jnp.max(logits, axis=-1, keepdims=True))
                prob = raised * (1.0 / jnp.sum(raised * count, axis=-1, keepdims=True))
                prob = prob.astype(bf16)
                prob_ref[head, spot] = prob
                low = (prob.astype(f32) * count).astype(bf16)
                blend_ref[spot, part] = dot_nn(low, ext_ref[:, values]).astype(bf16)

        row_loop(tile, attend, [lambda: gather_mlp.step(4), lambda: gather_mlp.step(5)])
        for k in range(6, place.fars + 2):
            gather_mlp.step(k)
        gather_mlp.end()
        lane = iota((1, 128), 1)
        live = jnp.where(lane < channels, 1.0, 0.0)
        dec_rows_ref[...] = pltpu.roll(small_part(start, 128).astype(f32), 128 - shift, 0).astype(bf16)

        def feed(spot):
            h1 = h0_ref[spot] + dot_nt(blend_ref[spot], attn_part(3 * width, width))
            h1_ref[spot] = h1
            unit, inverse = norm_parts(h1)
            second = (unit * (1.0 + mod[2]) + mod[3]).astype(bf16)
            second_ref[spot] = second
            upper = dot_nt(second, mlp_part(0))
            square = upper * upper
            bend = jnp.tanh(gelu_scale * upper * (1.0 + gelu_cubic * square))
            half = 0.5 + 0.5 * bend
            activ = (upper * half).astype(bf16)
            activ_ref[spot] = activ
            slope = half + (0.5 * gelu_scale) * upper * (1.0 - bend * bend) * (
                1.0 + 3.0 * gelu_cubic * square
            )
            slope_ref[spot] = slope.astype(bf16)
            h2 = h1 + dot_nn(activ, mlp_part(hidden))
            high = h2.astype(bf16)
            out_ref[spot] = high
            low = (h2 - high.astype(f32)).astype(bf16)
            dec_rows = dec_rows_ref[...]
            projected = (dot_nt(high, dec_rows) + dot_nt(low, dec_rows)) * live
            top = projected.astype(bf16)
            node_ref[spot, pl.ds(0, 128)] = top
            node_ref[spot, pl.ds(128, 128)] = (projected - top.astype(f32)).astype(bf16)

        row_loop(tile, feed)

        c_skip = vector_ref[0:1, c_skip_lane : c_skip_lane + 1]
        c_output = vector_ref[0:1, c_output_lane : c_output_lane + 1]
        weight = vector_ref[0:1, weight_lane : weight_lane + 1]
        column_ref[pl.ds(0, bands), pl.ds(0, lons)] = land_ref[...]
        masks = jnp.transpose(column_ref[pl.ds(0, 8), pl.ds(0, flat_lons)].astype(f32))
        last = jnp.where(lane == channels - 1, 1.0, 0.0)

        def keep(band):
            return live * (1.0 - masks[:lons, band : band + 1] * last)

        error_ref[...] = jnp.zeros_like(error_ref)
        cores, uppers = {}, {}
        for band in range(bands):
            net = dot_nn(dec_ref[band], node_ref[...])
            net = (net[:, :128] + net[:, 128:]) * (c_output * third)
            noisy = grid_ref[band, :, pl.ds(0, 128)].astype(f32)
            error_ref[:, pl.ds(0, channels)] = target_ref[band]
            error = (c_skip * noisy + net - error_ref[...]) * keep(band)
            high = error.astype(bf16)
            low = (error - high.astype(f32)).astype(bf16)
            turned = dot_tn(high, table_ref[0]) + dot_tn(low, table_ref[0]) + dot_tn(high, table_ref[1])
            f_ref[band] = turned[:sent]
            all_ref[node, band] = turned[:sent].astype(bf16)
            piece = all_ref.at[node, band]
            for i in range(1, place.uppers):
                uppers[i, band] = start_copy(started, place, piece, piece, f_sem.at[i, band], upper=i)
            cores[0, band] = start_copy(started, place, piece, piece, f_sem.at[0, band], core=1)
        gf_ref[...] = jnp.zeros_like(gf_ref)

        def add_nodes(base, total, band):
            def add_lat(index, value):
                source = base + index // lats
                return value + kern_ref[band, pl.ds(source * lats + lax.rem(index, lats), 1)] * all_ref[
                    source, lax.rem(index, lats)
                ].astype(f32)

            return lax.fori_loop(0, 2 * lats, add_lat, total, unroll=8)

        for band in range(bands):
            cores[0, band].wait_recv()
        for band in range(bands):
            total_ref[band] = add_nodes(place.upper * 2, jnp.zeros((sent, lanes), f32), band)
            for i in range(1, place.uppers):
                uppers[i, band].wait_recv()
                source = lax.rem(place.upper + place.uppers - i, place.uppers) * 2 + place.core
                piece = all_ref.at[source, band]
                cores[i, band] = start_copy(started, place, piece, piece, pass_sem.at[i, band], core=1)
        for i in range(1, place.uppers):
            for band in range(bands):
                cores[i, band].wait_recv()
        loss_rows = jnp.zeros((8, 128), f32)
        for band in range(bands):
            total = total_ref[band]
            for i in range(1, place.uppers):
                total = add_nodes(lax.rem(place.upper + i, place.uppers) * 2, total, band)
            loss_rows = loss_rows + jnp.sum(total * f_ref[band])
            gf_ref[pl.ds(0, sent)] = total * (2.0 * weight)
            grad = gf_ref[...]
            high = grad.astype(bf16)
            low = (grad - high.astype(f32)).astype(bf16)
            back = dot_nt(table_ref[0], high) + dot_nt(table_ref[0], low) + dot_nt(table_ref[1], high)
            gnet_ref[band] = (back * keep(band) * c_output).astype(bf16)
        loss_out[...] = loss_rows * weight

        sums_ref[...] = jnp.zeros_like(sums_ref)
        grad_node = dot_tn(gnet_ref[0], dec_ref[0])
        for band in range(1, bands):
            grad_node += dot_tn(gnet_ref[band], dec_ref[band])
        gnode_ref[...] = jnp.transpose(grad_node * third)

        def back_feed(spot):
            grad_node = gnode_ref[spot]
            high = grad_node.astype(bf16)
            low = (grad_node - high.astype(f32)).astype(bf16)
            node_ref[spot, pl.ds(0, 128)] = high
            dec_rows = dec_rows_ref[...]
            grad_out = dot_nn(high, dec_rows) + dot_nn(low, dec_rows)
            branch = grad_out.astype(bf16)
            gb_ref[spot] = branch
            grad_activ = dot_nt(branch, mlp_part(hidden))
            grad_upper = (grad_activ * slope_ref[spot].astype(f32)).astype(bf16)
            slope_ref[spot] = grad_upper
            grad_second = dot_nn(grad_upper, mlp_part(0))
            unit, inverse = norm_parts(h1_ref[spot])
            scaled = grad_second * (1.0 + mod[2])
            grad_mid = grad_out + inverse * (
                scaled
                - jnp.mean(scaled, axis=-1, keepdims=True)
                - unit * jnp.mean(scaled * unit, axis=-1, keepdims=True)
            )
            sums_ref[2:3] += jnp.sum(grad_second * unit, axis=0, keepdims=True)
            sums_ref[3:4] += jnp.sum(grad_second, axis=0, keepdims=True)
            h1_ref[spot] = grad_mid
            grad_attn = grad_mid.astype(bf16)
            gattn_ref[spot] = grad_attn
            gblend_ref[spot] = dot_nn(grad_attn, attn_part(3 * width, width)).astype(bf16)

        row_loop(tile, back_feed)

        def outer_loop(target, block, offset, left, right, columns):
            @pl.loop(0, columns // big)
            def _(index):
                part = pl.multiple_of(index * big, big)
                product = dot_tn(left[:, pl.ds(part, big)], right[...]).astype(bf16)
                target[pl.ds((offset + part) // block, big // block)] = product.reshape(
                    big // block, block, width
                )

        outer_loop(mlp_ref, mlp_rows, hidden, activ_ref, gb_ref, hidden)
        outer_loop(mlp_ref, mlp_rows, 0, slope_ref, second_ref, hidden)
        scatter = Scatter(place, mlp_pieces, (mlp_ref,), bufs, sems_c)
        scatter.begin([0])

        gext_ref[...] = jnp.zeros_like(gext_ref)

        def back_attend(spot):
            count = near_ref[spot].astype(f32)
            for head in range(HEAD_COUNT):
                part = pl.ds(head * head_width, head_width)
                values = pl.ds(width + head * head_width, head_width)
                prob = prob_ref[head, spot].astype(f32)
                counted_prob = prob * count
                grad_blend = gblend_ref[spot, part]
                grad_prob = dot_nt(grad_blend, ext_ref[:, values])
                mean = jnp.sum(counted_prob * grad_prob, axis=-1, keepdims=True)
                grad_logit = (counted_prob * (grad_prob - mean)).astype(bf16)
                gext_ref[:, part] += dot_tn(grad_logit, q_ref[spot, part])
                q_ref[spot, part] = (dot_nn(grad_logit, ext_ref[:, part]) * score_scale).astype(bf16)
                gext_ref[:, values] += dot_tn(counted_prob.astype(bf16), grad_blend)

        row_loop(tile, back_attend, [lambda: scatter.step(0), lambda: scatter.step(1)])
        key_scale = jnp.where(iota((1, 2 * width), 1) < width, score_scale, 1.0)
        lost_ref[0] = (gext_ref[pl.ds(rows, halo)] * key_scale).astype(bf16)
        lost_ref[1] = (gext_ref[pl.ds(rows + halo, halo)] * key_scale).astype(bf16)
        from_upper = to_node(nodes - 1, lost_ref.at[0], back_ref.at[0], back_sem.at[0])
        from_lower = to_node(1, lost_ref.at[1], back_ref.at[1], back_sem.at[1])
        scatter.step(2)
        outer_loop(attn_out, attn_rows, 3 * width, gattn_ref, blend_ref, width)
        outer_loop(attn_out, attn_rows, 0, q_ref, first_ref, width)
        scatter.step(3)
        from_upper.wait_recv()
        from_lower.wait_recv()

        def back_encode(spot):
            grad_pairs = gext_ref[spot] * key_scale + dot_nn(lendt_ref[spot], back_ref[0]) + dot_nn(
                lendt_ref[spot], back_ref[1]
            )
            grad_pairs = grad_pairs.astype(bf16)
            ext_ref[spot] = grad_pairs
            grad_first = dot_nn(q_ref[spot], attn_part(0, width)) + dot_nn(
                grad_pairs, attn_part(width, 2 * width)
            )
            unit, inverse = norm_parts(h0_ref[spot])
            scaled = grad_first * (1.0 + mod[0])
            grad_in = h1_ref[spot] + inverse * (
                scaled
                - jnp.mean(scaled, axis=-1, keepdims=True)
                - unit * jnp.mean(scaled * unit, axis=-1, keepdims=True)
            )
            sums_ref[0:1] += jnp.sum(grad_first * unit, axis=0, keepdims=True)
            sums_ref[1:2] += jnp.sum(grad_first, axis=0, keepdims=True)
            gb_ref[spot] = grad_in.astype(bf16)

        row_loop(big, back_encode)
        scatter.step(4)
        outer_loop(attn_out, attn_rows, width, ext_ref.at[pl.ds(0, rows)], first_ref, 2 * width)
        for k in range(5, scatter.steps()):
            scatter.step(k)

        for low_row in range(0, all_small, 128):
            part = feats_ref[pl.ds(low_row, 128)]
            total = part[:, 0:1] * sums_ref[0:1]
            for j in range(1, 4):
                total += part[:, j : j + 1] * sums_ref[j : j + 1]
            if low_row < wide:
                total += dot_tn(mixed_ref[0, :, pl.ds(low_row, 128)], gb_ref[...])
            if low_row == start:
                total += pltpu.roll(dot_tn(node_ref[:, pl.ds(0, 128)], out_ref[...]), shift, 0)
            high = total.astype(bf16)
            high_out[pl.ds(low_row, 128)] = high
            low_out[pl.ds(low_row, 128)] = (total - high.astype(f32)).astype(bf16)
        scatter.finish(mlp_sum)
        scatter.end()
        for copy in started:
            copy.wait_send()

    vmem = pl.BlockSpec(memory_space=pltpu.VMEM)
    dma = pltpu.SemaphoreType.DMA
    struct = jax.ShapeDtypeStruct
    low = lambda *shape: pltpu.VMEM(shape, bf16)
    full = lambda *shape: pltpu.VMEM(shape, f32)
    return pl.pallas_call(
        kernel,
        out_shape=(
            struct((devices, attn_rows, width), bf16),
            struct((mlp_rows, width), f32),
            struct((all_small, width), bf16),
            struct((all_small, width), bf16),
            struct((8, 128), f32),
        ),
        in_specs=[vmem] * 13,
        out_specs=(vmem,) * 5,
        scratch_shapes=[
            low(attn_rows, width),
            low(mlp_rows, width),
            low(small_rows, width),
            full(nodes, lats, lows, lanes),
            full(place.nears, lats, all_lats, lanes),
            full(place.fars, lats, all_lats, lanes),
            full(lats, all_lats, lanes),
            low(devices, attn_rows, width),
            low(devices, mlp_rows, width),
            low(devices, small_rows, width),
            low(rows, ext_rows),
            low(bands, lons, rows),
            low(2, rows, wide),
            low(rows, halo),
            full(rows, width),
            full(rows, width),
            low(rows, width),
            low(rows, width),
            low(ext_rows, 2 * width),
            low(halo, 2 * width),
            low(HEAD_COUNT, rows, ext_rows),
            low(rows, width),
            low(rows, width),
            low(rows, hidden),
            low(rows, hidden),
            low(rows, width),
            low(rows, 256),
            full(lats, sent, lanes),
            low(nodes, lats, sent, lanes),
            full(128, lanes),
            low(bands, lons, 128),
            full(rows, 128),
            low(rows, width),
            low(rows, width),
            low(rows, width),
            full(ext_rows, 2 * width),
            low(2, halo, 2 * width),
            low(2, halo, 2 * width),
            full(8, width),
            full(lons, 128),
            pltpu.VMEM((8, flat_pixels), jnp.int32),
            pltpu.VMEM((flat_pixels, 128), jnp.int32),
            low(bands, lons, cin),
            low(128, width),
            full(all_small, 128),
            full(lats, sent, lanes),
            dma((nodes, 2)),
            dma((place.nears, 2)),
            dma((place.fars, 2)),
            dma((2, 2)),
            dma((place.uppers, lats, 2)),
            dma((place.uppers, lats, 2)),
            dma((2, 2)),
        ]
        + gather_sems_a
        + gather_sems_b
        + scatter_bufs
        + scatter_sems,
        compiler_params=pltpu.CompilerParams(
            collective_id=collective, has_side_effects=True, vmem_limit_bytes=62 << 20
        ),
    )(*weights, grid, target, land, near_turned, enc_turned, dec_turned, lent, legendre, vector, tables)


def turn_tables(lon_count, modes):
    turns = np.arange(lon_count)[:, None] * np.arange(modes)[None, :] % lon_count
    phases = turns * (2.0 * np.pi / lon_count)
    waves = [m for m in range(modes) if (2 * m) % lon_count]
    picks = list(range(modes)) + waves
    lanes = -(-len(picks) // 128) * 128
    table = np.zeros((lon_count, lanes), np.float32)
    table[:, :modes] = np.cos(phases)
    table[:, modes : len(picks)] = -np.sin(phases[:, waves])
    high = table.astype(ml_dtypes.bfloat16)
    low = (table - high.astype(np.float32)).astype(ml_dtypes.bfloat16)
    return np.stack([high, low]), (waves[0], waves[-1] + 1, lanes - len(picks))


def to_sixteens(blocks):
    return jnp.pad(blocks, ((0, 0), (0, sixteens(blocks.shape[1]) - blocks.shape[1]), (0, 0)))


def on_device(
    grid_in,
    target,
    noise_level,
    land_mask,
    neighbours,
    halo_send,
    g2m,
    m2g,
    legendre,
    w_attn,
    w_mlp,
    w_small,
    mom_attn,
    mom_mlp,
    m_small,
    v_small,
    ema_attn,
    ema_mlp,
    ema_small,
):
    cin = grid_in.shape[-1]
    lat_rows, lon_count, channels = target.shape[1:]
    modes, degrees = legendre.shape[1:]
    halo_rows = halo_send.shape[0]
    width = w_attn.shape[1]
    nodes, zeros = lax.axis_size("node"), lax.axis_size("zero")
    devices = nodes * zeros
    attn_rows, mlp_rows, small_rows = w_attn.shape[0], w_mlp.shape[0], w_small.shape[0]

    sigma, c_input, c_skip, c_output, loss_weight = noise_scalars(noise_level[0])
    features = noise_features(sigma).astype(bf16).astype(f32)
    weight = loss_weight / (2 * modes * degrees * channels)
    tables, (wave_first, wave_end, wave_pad) = turn_tables(lon_count, modes)
    lows = -(-degrees // (8 * zeros)) * 8
    leg = jnp.pad(legendre, ((0, 0), (0, 0), (0, lows * zeros - degrees)))
    leg = lax.dynamic_slice_in_dim(leg, lax.axis_index("zero") * lows, lows, axis=2)
    leg = jnp.transpose(leg, (0, 2, 1))
    leg = jnp.concatenate(
        [leg, leg[:, :, wave_first:wave_end], jnp.zeros(leg.shape[:2] + (wave_pad,), f32)], axis=2
    )
    whole_tiles = all(size % 16 == 0 and 256 % size == 0 for size in (attn_rows, mlp_rows, small_rows))
    if whole_tiles:
        lane = jnp.arange(128)
        vector = jnp.where(lane < NOISE_FEATS, jnp.pad(features, (0, 128 - NOISE_FEATS)), 0.0)
        for spot, value in (
            (c_input_lane, c_input),
            (c_skip_lane, c_skip),
            (c_output_lane, c_output),
            (weight_lane, weight),
        ):
            vector = jnp.where(lane == spot, value, vector)
        g_attn, mlp_sum, g_high, g_low, loss_tile = train_step(
            nodes,
            zeros,
            (w_attn, w_mlp, w_small),
            grid_in[0],
            target[0],
            land_mask,
            neighbours.T,
            g2m.T,
            m2g.T,
            halo_send[None],
            leg,
            vector[None],
            jnp.asarray(tables),
            cin,
            1,
        )
        names = ["attn", "high", "low"]
        local = [g_attn, g_high, g_low]
    else:
        scale_input = jnp.where(jnp.arange(cin) < channels, c_input, 1.0)[None]
        cond_rows = jnp.where(
            jnp.arange(128)[None, None] == jnp.arange(4)[:, None, None], features[None, :, None], 0.0
        ).reshape(-1, 128)
        feats = jnp.pad(cond_rows, ((cin + channels, 0), (0, 0)))
        shift = cin % 128
        sides = ((0, 0), (0, 0), (shift, 128 - shift - channels))
        keep_mask = 1.0 - land_mask.astype(f32)[:, :, None] * (
            jnp.arange(channels) == channels - 1
        ).astype(f32)
        base = jnp.pad(c_skip * grid_in[0, :, :, :channels].astype(f32) - target[0], sides)
        keep = jnp.pad(keep_mask, sides)
        m2g_bands = m2g.reshape(lat_rows, lon_count, -1)

        attn, mlp, small, near, dec, dec_turned, mixed, lend, lendt, kern = gather_and_count(
            nodes,
            zeros,
            (w_attn, w_mlp, w_small),
            grid_in[0].reshape(-1, cin),
            scale_input,
            g2m,
            m2g_bands,
            jnp.transpose(m2g_bands, (0, 2, 1)),
            neighbours,
            halo_send[:, None],
            jnp.concatenate([halo_send, halo_send])[None],
            leg,
            1,
        )
        full = [
            item[:, :size].reshape(-1, width)
            for item, size in ((attn, attn_rows), (mlp, mlp_rows), (small, small_rows))
        ]
        *local, loss_tile = model_step(
            nodes,
            zeros,
            full,
            (near, dec, dec_turned, mixed, lend, lendt),
            kern,
            feats,
            base,
            keep,
            jnp.asarray(tables),
            jnp.stack([c_output, weight]),
            cin,
            channels,
            m2g.shape[1],
            2,
        )
        names = ["attn", "mlp", "high", "low"]
        mlp_sum = None

    g_small, moment_attn, moment_mlp, totals, attn_all, mlp_all = reduce_and_gather(
        nodes,
        zeros,
        names,
        [to_sixteens(item.reshape(devices, -1, width)) for item in local],
        mlp_sum,
        loss_tile,
        mom_attn,
        mom_mlp,
        small_rows,
        3,
    )
    loss, clip_norm, new_attn, new_mlp, new_small, new_m, new_v, *new_averages = update_weights(
        nodes,
        zeros,
        attn_all[:, :attn_rows].reshape(-1, width),
        mlp_all[:, :mlp_rows].reshape(-1, width),
        totals,
        g_small,
        (moment_attn, moment_mlp),
        (w_attn, w_mlp, w_small),
        (ema_attn, ema_mlp, ema_small),
        (m_small, v_small),
    )
    return (
        loss[0, 0], clip_norm[0, 0], new_attn, new_mlp, new_small, moment_attn, moment_mlp, new_m, new_v, *new_averages
    )


def solution(mesh):
    split_rows = P(("node", "zero"), None)
    return jax.shard_map(
        on_device,
        mesh=mesh,
        in_specs=(
            P("zero", "node", None, None),
            P("zero", "node", None, None),
            P("zero"),
            P("node", None),
            P("node", None),
            P("node"),
            P("node", None),
            P("node", None),
            P("node", None, None),
        )
        + (split_rows,) * 10,
        out_specs=(P(), P()) + (split_rows,) * 10,
        check_vma=False,
    )
```

```python
import math

import jax
import jax.numpy as jnp
import ml_dtypes
import numpy as np
from jax import lax
from jax.experimental import pallas as pl
from jax.experimental.pallas import tpu as pltpu
from jax.sharding import PartitionSpec as P

HEAD_COUNT = 4
NOISE_FEATS = 42
LEVELS = 16
NS_ITERS = 3
STEP = 10

top_precision = lax.Precision.HIGHEST
mid_precision = lax.Precision.HIGH
norm_epsilon = 1e-05
trace_epsilon = 1e-12
clip_limit = 1.0
moment_decay = 0.95
orthogonal_rate = 0.1
adam_first = 0.9
adam_second = 0.95
adam_rate = 0.02
adam_epsilon = 1e-08
average_decay = 0.9
newton_first = 3.4445
newton_second = -4.775
newton_third = 2.0315
sigma_lowest = 0.1
sigma_highest = 20.0
c_input_lane = 64
c_skip_lane = 65
c_output_lane = 66
weight_lane = 67
log2_e = math.log2(math.e)
absent = -1e30
gelu_scale = math.sqrt(2.0 / math.pi)
gelu_cubic = 0.044715
f32 = jnp.float32
bf16 = jnp.bfloat16


def noise_scalars(level):
    sigma = sigma_lowest * (sigma_highest / sigma_lowest) ** (level.astype(f32) / (LEVELS - 1))
    total = sigma * sigma + 1.0
    return (sigma, lax.rsqrt(total), 1.0 / total, sigma * lax.rsqrt(total), total / (sigma * sigma))


def noise_features(sigma):
    half_count = NOISE_FEATS // 2
    frequency = jnp.exp(jnp.arange(half_count).astype(f32) * (3.0 / half_count))
    phases = 0.25 * jnp.log(sigma) * frequency
    return jnp.concatenate([jnp.sin(phases), jnp.cos(phases)])


def dot(left, right, contract):
    return lax.dot_general(left, right, (contract, ((), ())), preferred_element_type=f32)


def dot_nn(left, right):
    return dot(left, right, ((1,), (0,)))


def dot_nt(left, right):
    return dot(left, right, ((1,), (1,)))


def dot_tn(left, right):
    return dot(left, right, ((0,), (0,)))


MESH = pl.DeviceIdType.MESH
ROW_CHUNK = 16


class Place:
    def __init__(self, nodes, zeros):
        self.uppers, self.cores = nodes // 2, 2
        self.nears = 2 if zeros < 16 else 4
        self.fars = zeros // self.nears
        self.mates = max(self.uppers // 2, 1)
        self.zeros = zeros

    def locate(self):
        node, zero = lax.axis_index("node"), lax.axis_index("zero")
        self.upper, self.core = node // 2, node % 2
        self.far, self.near = zero // self.nears, zero % self.nears

    def moved(self, upper=0, core=0, far=0, near=0, mate=0):
        row = lax.rem(self.upper + upper, self.uppers) if upper else self.upper
        if mate:
            group = self.upper // self.mates * self.mates
            row = group + lax.rem(self.upper - group + mate, self.mates)
        return (
            row,
            1 - self.core if core else self.core,
            lax.rem(self.far + far, self.fars) if far else self.far,
            lax.rem(self.near + near, self.nears) if near else self.near,
        )

    def device(self, **steps):
        upper, core, far, near = self.moved(**steps)
        return (upper * 2 + core, far * self.nears + near)

    def slot(self, upper, core, far, near):
        return (upper * 2 + core) * self.zeros + far * self.nears + near

    def peers(self):
        return (
            [dict(far=k) for k in range(1, self.fars)]
            + [dict(near=j) for j in range(1, self.nears)]
            + [dict(upper=i) for i in range(1, self.uppers)]
            + [dict(core=1)]
        )

    def greet(self, nodes=0):
        barrier = pltpu.get_barrier_semaphore()
        peers = [self.device(**steps) for steps in self.peers() if not nodes or set(steps) <= {"far", "near"}]
        if nodes:
            node, zero = lax.axis_index("node"), lax.axis_index("zero")
            peers += [(lax.rem(node + step, nodes), zero) for step in range(1, nodes)]
        for device in peers:
            pl.semaphore_signal(barrier, 1, device_id=device, device_id_type=MESH)
        pl.semaphore_wait(barrier, len(peers))


def half_rows(rows):
    return (rows // 2 + 15) // 16 * 16


def start_copy(started, place, source, target, sems, **steps):
    copy = pltpu.make_async_remote_copy(
        src_ref=source,
        dst_ref=target,
        send_sem=sems.at[0],
        recv_sem=sems.at[1],
        device_id=place.device(**steps),
        device_id_type=MESH,
    )
    copy.start()
    started.append(copy)
    return copy


def sixteens(rows):
    return -(-rows // 16) * 16


class Pieces:
    def __init__(self, sizes, first):
        self.sizes = sizes
        total = sum(sizes)
        cut = min(half_rows(total), sizes[first])
        self.whole = [(i, 0, size) for i, size in enumerate(sizes)]
        self.head = [(first, 0, cut)]
        self.tail = [(first, cut, sizes[first] - cut)] if cut < sizes[first] else []
        self.tail += [(i, 0, size) for i, size in enumerate(sizes) if i != first]


def send_pieces(started, place, pieces, sources, targets, sems, **steps):
    copies = []
    for index, (array, start, rows) in enumerate(pieces):
        part = pl.ds(start, rows)
        copies.append(
            start_copy(
                started, place, sources[array].at[part], targets[array].at[part], sems.at[index], **steps
            )
        )
    return copies


def wait_all(copies):
    for copy in copies:
        copy.wait_recv()


class Gather:
    def __init__(self, place, pieces, shards, outs, sems):
        self.place, self.pieces, self.shards, self.outs = place, pieces, shards, outs
        (self.own_sem, self.far_sem, self.near_sem, self.upper_sem, self.over_sem, self.under_sem, self.core_sem) = sems
        self.started, self.cores = [], []
        self.far, self.near, self.upper, self.over, self.under = {}, {}, {}, {}, {}

    def block(self, **steps):
        slot = self.place.slot(*self.place.moved(**steps))
        return [out.at[slot] for out in self.outs]

    def send(self, pieces, source, target, sems, **steps):
        return send_pieces(self.started, self.place, pieces, source, target, sems, **steps)

    def begin(self):
        here = self.block()
        self.kept = []
        for index, (shard, target) in enumerate(zip(self.shards, here)):
            copy = pltpu.make_async_copy(shard, target, self.own_sem.at[index])
            copy.start()
            self.kept.append(copy)
        for k in range(1, self.place.fars):
            self.far[k] = self.send(self.pieces.whole, self.shards, here, self.far_sem.at[k], far=k)

    def first(self, k):
        place, whole = self.place, self.pieces.whole
        if k:
            wait_all(self.far[k])
        target = self.block(far=(place.fars - k) % place.fars)
        source = target if k else self.shards
        for j in range(1, place.nears):
            self.near[k, j] = self.send(whole, source, target, self.near_sem.at[k, j], near=j)
        for i in range(1, place.uppers):
            self.upper[k, i] = self.send(whole, source, target, self.upper_sem.at[k, i], upper=i)
        self.cores += self.send(whole, source, target, self.core_sem.at[k, 0, 0], core=1)

    def second(self, k):
        place, whole = self.place, self.pieces.whole
        far = (place.fars - k) % place.fars
        for j in range(1, place.nears):
            wait_all(self.near[k, j])
            item = self.block(far=far, near=place.nears - j)
            for i in range(1, place.uppers):
                self.over[k, j, i] = self.send(
                    self.pieces.head, item, item, self.over_sem.at[k, j, i], upper=i
                )
            self.cores += self.send(whole, item, item, self.core_sem.at[k, j, 0], core=1)
        for i in range(1, place.uppers):
            wait_all(self.upper[k, i])
            item = self.block(far=far, upper=place.uppers - i)
            for j in range(1, place.nears):
                self.under[k, j, i] = self.send(
                    self.pieces.tail, item, item, self.under_sem.at[k, j, i], near=j
                )
            self.cores += self.send(whole, item, item, self.core_sem.at[k, 0, i], core=1)

    def third(self, k):
        place, whole = self.place, self.pieces.whole
        far = (place.fars - k) % place.fars
        for j in range(1, place.nears):
            for i in range(1, place.uppers):
                wait_all(self.over[k, j, i])
                wait_all(self.under[k, j, i])
                item = self.block(far=far, near=place.nears - j, upper=place.uppers - i)
                self.cores += self.send(whole, item, item, self.core_sem.at[k, j, i], core=1)

    def step(self, k):
        fars = self.place.fars
        if k < fars:
            self.first(k)
        if 1 <= k <= fars:
            self.second(k - 1)
        if k >= 2:
            self.third(k - 2)

    def end(self):
        for copy in self.kept:
            copy.wait()
        wait_all(self.cores)
        for copy in self.started:
            copy.wait_send()

    @staticmethod
    def sems(place, pieces):
        dma = pltpu.SemaphoreType.DMA
        fars, nears, uppers = place.fars, place.nears, place.uppers
        whole, head, tail = len(pieces.whole), len(pieces.head), len(pieces.tail)
        return [
            dma((whole,)),
            dma((fars, whole, 2)),
            dma((fars, nears, whole, 2)),
            dma((fars, uppers, whole, 2)),
            dma((fars, nears, uppers, head, 2)),
            dma((fars, nears, uppers, tail, 2)),
            dma((fars, nears, uppers, whole, 2)),
        ]


def iota(shape, axis):
    return lax.broadcasted_iota(jnp.int32, shape, axis)


def gather_and_count(nodes, zeros, weights, grid, scale, g2m, m2g, m2g_turned, neighbours, lent, lent_row, legendre, collective):
    place = Place(nodes, zeros)
    width = weights[0].shape[1]
    sizes = [sixteens(w.shape[0]) for w in weights]
    pieces = Pieces(sizes, 1)
    devices = nodes * zeros
    pixels, cin = grid.shape
    wide = -(-cin // 128) * 128
    rows, fanout = neighbours.shape
    halo = lent.shape[0]
    ext = rows + 2 * halo
    bands, lons, dec_edges = m2g.shape
    lats, lows, lanes = legendre.shape
    enc_edges = g2m.shape[1]
    tile = 128

    def kernel(
        attn_ref, mlp_ref, small_ref, grid_ref, scale_ref, g2m_ref, m2g_ref, turned_ref, near_ref, lent_ref,
        row_ref, leg_ref,
        attn_out, mlp_out, small_out, near_out, dec_out, turned_out, mixed_out, lend_out, lendt_out, kern_out,
        attn_shard, mlp_shard, small_shard, inputs, legs, parts, sums, leg_sem, part_sem, sum_sem, *sems,
    ):
        place.locate()
        node = lax.axis_index("node")
        shards = (attn_shard, mlp_shard, small_shard)
        for ref, shard, size in zip((attn_ref, mlp_ref, small_ref), shards, sizes):
            if ref.shape[0] < size:
                shard[...] = jnp.zeros_like(shard)
            shard[pl.ds(0, ref.shape[0])] = ref[...].astype(bf16)
        legs[node] = leg_ref[...]
        place.greet(nodes)
        gather = Gather(place, pieces, shards, (attn_out, mlp_out, small_out), sems)
        gather.begin()
        started = []
        leg_copies = []
        for step in range(1, nodes):
            target = (lax.rem(node + step, nodes), lax.axis_index("zero"))
            copy = pltpu.make_async_remote_copy(
                src_ref=leg_ref,
                dst_ref=legs.at[node],
                send_sem=leg_sem.at[step, 0],
                recv_sem=leg_sem.at[step, 1],
                device_id=target,
                device_id_type=MESH,
            )
            copy.start()
            leg_copies.append(copy)

        def count_near():
            @pl.loop(0, rows // tile)
            def _(index):
                spot = pl.ds(pl.multiple_of(index * tile, tile), tile)
                lists = near_ref[spot]
                place_of = iota((tile, ext), 1)
                total = jnp.zeros((tile, ext), f32)
                for j in range(fanout):
                    total += jnp.where(lists[:, j : j + 1] == place_of, 1.0, 0.0)
                near_out[spot] = total.astype(bf16)

        def count_dec():
            @pl.loop(0, bands)
            def _(band):
                lists = m2g_ref[band]
                place_of = iota((lons, rows), 1)
                total = jnp.zeros((lons, rows), f32)
                for j in range(dec_edges):
                    total += jnp.where(lists[:, j : j + 1] == place_of, 1.0, 0.0)
                dec_out[band] = total.astype(bf16)
                lists = turned_ref[band]
                place_of = iota((rows, lons), 0)
                total = jnp.zeros((rows, lons), f32)
                for j in range(dec_edges):
                    total += jnp.where(lists[j : j + 1] == place_of, 1.0, 0.0)
                turned_out[band] = total.astype(bf16)

        def mix():
            inputs[...] = (grid_ref[...].astype(f32) * scale_ref[...]).astype(bf16)
            mixed_out[...] = jnp.zeros_like(mixed_out)

            @pl.loop(0, rows // tile)
            def _(index):
                spot = pl.ds(pl.multiple_of(index * tile, tile), tile)
                lists = g2m_ref[spot]
                place_of = iota((tile, pixels), 1)
                total = jnp.zeros((tile, pixels), f32)
                for j in range(enc_edges):
                    total += jnp.where(lists[:, j : j + 1] == place_of, 1.0 / enc_edges, 0.0)
                mean = dot_nn(total.astype(bf16), inputs[...])
                high = mean.astype(bf16)
                mixed_out[0, spot, pl.ds(0, cin)] = high
                mixed_out[1, spot, pl.ds(0, cin)] = (mean - high.astype(f32)).astype(bf16)

        def lend():
            lend_out[...] = jnp.where(lent_ref[...] == iota((halo, rows), 1), 1.0, 0.0).astype(bf16)
            lendt_out[...] = jnp.where(row_ref[...] == iota((rows, 2 * halo), 0), 1.0, 0.0).astype(bf16)

        def gram():
            for copy in leg_copies:
                copy.wait()

            @pl.loop(0, nodes * lats)
            def _(index):
                other = legs[index // lats, lax.rem(index, lats)]
                for t in range(lats):
                    product = leg_ref[t] * other
                    parts[place.near, t, pl.ds(index, 1)] = jnp.sum(product, axis=0, keepdims=True)

            for j in range(1, place.nears):
                near_parts.append(
                    start_copy(
                        started, place, parts.at[place.near], parts.at[place.near], part_sem.at[j], near=j
                    )
                )

        near_parts, far_sums = [], []

        def gram_near():
            wait_all(near_parts)
            total = parts[0]
            for j in range(1, place.nears):
                total = total + parts[j]
            sums[place.far] = total
            for k in range(1, place.fars):
                far_sums.append(
                    start_copy(
                        started, place, sums.at[place.far], sums.at[place.far], sum_sem.at[k], far=k
                    )
                )

        def gram_far():
            wait_all(far_sums)
            total = sums[0]
            for k in range(1, place.fars):
                total = total + sums[k]
            kern_out[...] = total

        work = [lend, mix, gram, count_dec, gram_near, count_near, gram_far]
        steps = place.fars + 2
        for k in range(steps):
            gather.step(k)
            share = -(-len(work) // (steps - k))
            for part in work[:share]:
                part()
            work = work[share:]
        gather.end()
        for copy in started:
            copy.wait_send()

    vmem = pl.BlockSpec(memory_space=pltpu.VMEM)
    hbm = pl.BlockSpec(memory_space=pl.ANY)
    dma = pltpu.SemaphoreType.DMA
    struct = jax.ShapeDtypeStruct
    return pl.pallas_call(
        kernel,
        out_shape=tuple(struct((devices, size, width), bf16) for size in sizes)
        + (
            struct((rows, ext), bf16),
            struct((bands, lons, rows), bf16),
            struct((bands, rows, lons), bf16),
            struct((2, rows, wide), bf16),
            struct((halo, rows), bf16),
            struct((rows, 2 * halo), bf16),
            struct((lats, nodes * lats, lanes), f32),
        ),
        in_specs=[vmem] * 12,
        out_specs=(hbm,) * 3 + (vmem,) * 7,
        scratch_shapes=[pltpu.VMEM((size, width), bf16) for size in sizes]
        + [
            pltpu.VMEM((pixels, cin), bf16),
            pltpu.VMEM((nodes, lats, lows, lanes), f32),
            pltpu.VMEM((place.nears, lats, nodes * lats, lanes), f32),
            pltpu.VMEM((place.fars, lats, nodes * lats, lanes), f32),
            dma((nodes, 2)),
            dma((place.nears, 2)),
            dma((place.fars, 2)),
        ]
        + Gather.sems(place, pieces),
        compiler_params=pltpu.CompilerParams(
            collective_id=collective, has_side_effects=True, vmem_limit_bytes=56 << 20
        ),
    )(*weights, grid, scale, g2m, m2g, m2g_turned, neighbours, lent, lent_row, legendre)


def norm_parts(rows):
    centred = rows - jnp.mean(rows, axis=-1, keepdims=True)
    inverse = lax.rsqrt(jnp.mean(centred * centred, axis=-1, keepdims=True) + norm_epsilon)
    return centred * inverse, inverse


def model_step(
    nodes, zeros, weights, graph, kern, feats, base, keep, tables, scalars, first_channel, channels, dec_edges, collective
):
    place = Place(nodes, zeros)
    attn, mlp, small = weights
    near, dec, dec_turned, mixed, lend, lendt = graph
    width = attn.shape[1]
    hidden = mlp.shape[0] // 2
    rows, ext_rows = near.shape
    halo = lend.shape[0]
    bands, lons, _ = dec.shape
    wide = mixed.shape[2]
    lats, all_lats, lanes = kern.shape
    start = first_channel // 128 * 128
    shift = first_channel - start
    sent = sixteens(shift + channels)
    big, tile = 256, 128
    head_width = width // HEAD_COUNT
    score_scale = head_width ** (-0.5)
    third = 1.0 / dec_edges

    def kernel(
        attn_hbm, mlp_hbm, small_ref, near_hbm, dec_hbm, turned_hbm, mixed_ref, lend_ref, lendt_ref, kern_ref,
        feats_ref, base_ref, keep_ref, table_ref, scalar_ref,
        attn_out, mlp_out, high_out, low_out, loss_out,
        attn_ref, mlp_ref, near_ref, dec_ref, turned_ref, h0_ref, h1_ref, first_ref, q_ref, ext_ref, lent_ref,
        prob_ref, blend_ref, second_ref, activ_ref, slope_ref, out_ref, node_ref, f_ref, all_ref, gf_ref, gnet_ref,
        gb_ref, gattn_ref, gblend_ref, gext_ref, back_ref, lost_ref, sums_ref,
        load_sem, lend_sem, f_sem, pass_sem, back_sem,
    ):
        place.locate()
        node = lax.axis_index("node")
        zero = lax.axis_index("zero")
        loads = []
        for index, (source, target) in enumerate(
            (
                (attn_hbm, attn_ref),
                (near_hbm, near_ref),
                (mlp_hbm, mlp_ref),
                (dec_hbm, dec_ref),
                (turned_hbm, turned_ref),
            )
        ):
            copy = pltpu.make_async_copy(source, target, load_sem.at[index])
            copy.start()
            loads.append(copy)
        barrier = pltpu.get_barrier_semaphore()
        for step in range(1, nodes):
            pl.semaphore_signal(
                barrier, 1, device_id=(lax.rem(node + step, nodes), zero), device_id_type=MESH
            )
        started = []

        def to_node(step, source, target, sems):
            copy = pltpu.make_async_remote_copy(
                src_ref=source,
                dst_ref=target,
                send_sem=sems.at[0],
                recv_sem=sems.at[1],
                device_id=(lax.rem(node + step, nodes), zero),
                device_id_type=MESH,
            )
            copy.start()
            started.append(copy)
            return copy

        def row_loop(size, body):
            @pl.loop(0, rows // size)
            def _(index):
                body(pl.ds(pl.multiple_of(index * size, size), size))

        mods = dot_tn(feats_ref[...].astype(bf16), small_ref[...])
        mod = [mods[j : j + 1] for j in range(4)]
        enc = small_ref[pl.ds(0, wide)]
        loads[0].wait()

        def encode(spot):
            h0 = dot_nn(mixed_ref[0, spot], enc) + dot_nn(mixed_ref[1, spot], enc)
            h0_ref[spot] = h0
            unit, inverse = norm_parts(h0)
            first = (unit * (1.0 + mod[0]) + mod[1]).astype(bf16)
            first_ref[spot] = first
            ext_ref[spot] = dot_nt(first, attn_ref[pl.ds(width, 2 * width)]).astype(bf16)
            q_ref[spot] = dot_nt(first, attn_ref[pl.ds(0, width)]).astype(bf16)

        row_loop(big, encode)
        lent_ref[...] = dot_nn(lend_ref[...], ext_ref[pl.ds(0, rows)]).astype(bf16)
        pl.semaphore_wait(barrier, nodes - 1)
        up = to_node(1, lent_ref, ext_ref.at[pl.ds(rows, halo)], lend_sem.at[0])
        down = to_node(nodes - 1, lent_ref, ext_ref.at[pl.ds(rows + halo, halo)], lend_sem.at[1])
        loads[1].wait()
        up.wait_recv()
        down.wait_recv()

        def attend(spot):
            count = near_ref[spot].astype(f32)
            for head in range(HEAD_COUNT):
                part = pl.ds(head * head_width, head_width)
                values = pl.ds(width + head * head_width, head_width)
                logits = dot_nt(q_ref[spot, part], ext_ref[:, part]) * score_scale
                logits = jnp.where(count > 0.0, logits, -jnp.inf)
                raised = jnp.exp(logits - jnp.max(logits, axis=-1, keepdims=True))
                prob = raised * (1.0 / jnp.sum(raised * count, axis=-1, keepdims=True))
                prob = prob.astype(bf16)
                prob_ref[head, spot] = prob
                low = (prob.astype(f32) * count).astype(bf16)
                blend_ref[spot, part] = dot_nn(low, ext_ref[:, values]).astype(bf16)

        row_loop(tile, attend)
        loads[2].wait()
        dec_rows = small_ref[pl.ds(start, 128)]
        lane = iota((1, 128), 1)
        live = jnp.where((lane >= shift) & (lane < shift + channels), 1.0, 0.0)

        def feed(spot):
            h1 = h0_ref[spot] + dot_nt(blend_ref[spot], attn_ref[pl.ds(3 * width, width)])
            h1_ref[spot] = h1
            unit, inverse = norm_parts(h1)
            second = (unit * (1.0 + mod[2]) + mod[3]).astype(bf16)
            second_ref[spot] = second
            upper = dot_nt(second, mlp_ref[pl.ds(0, hidden)])
            square = upper * upper
            bend = jnp.tanh(gelu_scale * upper * (1.0 + gelu_cubic * square))
            half = 0.5 + 0.5 * bend
            activ = (upper * half).astype(bf16)
            activ_ref[spot] = activ
            slope = half + (0.5 * gelu_scale) * upper * (1.0 - bend * bend) * (
                1.0 + 3.0 * gelu_cubic * square
            )
            slope_ref[spot] = slope.astype(bf16)
            h2 = h1 + dot_nn(activ, mlp_ref[pl.ds(hidden, hidden)])
            high = h2.astype(bf16)
            out_ref[spot] = high
            low = (h2 - high.astype(f32)).astype(bf16)
            projected = (dot_nt(high, dec_rows) + dot_nt(low, dec_rows)) * live
            top = projected.astype(bf16)
            node_ref[spot, pl.ds(0, 128)] = top
            node_ref[spot, pl.ds(128, 128)] = (projected - top.astype(f32)).astype(bf16)

        row_loop(tile, feed)

        c_output, weight = scalar_ref[0], scalar_ref[1]
        loads[3].wait()
        cores, uppers = {}, {}
        for band in range(bands):
            net = dot_nn(dec_ref[band], node_ref[...])
            net = (net[:, :128] + net[:, 128:]) * (c_output * third)
            error = (base_ref[band] + net) * keep_ref[band]
            high = error.astype(bf16)
            low = (error - high.astype(f32)).astype(bf16)
            turned = dot_tn(high, table_ref[0]) + dot_tn(low, table_ref[0]) + dot_tn(high, table_ref[1])
            f_ref[band] = turned[:sent]
            all_ref[node, band] = turned[:sent].astype(bf16)
            piece = all_ref.at[node, band]
            cores[0, band] = start_copy(started, place, piece, piece, f_sem.at[0, band], core=1)
            for i in range(1, place.uppers):
                uppers[i, band] = start_copy(started, place, piece, piece, f_sem.at[i, band], upper=i)
        gf_ref[...] = jnp.zeros_like(gf_ref)
        for band in range(bands):
            for i in range(1, place.uppers):
                uppers[i, band].wait_recv()
                source = lax.rem(place.upper + place.uppers - i, place.uppers) * 2 + place.core
                piece = all_ref.at[source, band]
                cores[i, band] = start_copy(started, place, piece, piece, pass_sem.at[i, band], core=1)
        for key in cores:
            cores[key].wait_recv()
        loss_rows = jnp.zeros((8, 128), f32)
        loads[4].wait()
        for band in range(bands):

            def add_lat(index, total):
                return total + kern_ref[band, pl.ds(index, 1)] * all_ref[
                    index // lats, lax.rem(index, lats)
                ].astype(f32)

            total = lax.fori_loop(0, all_lats, add_lat, jnp.zeros((sent, lanes), f32), unroll=4)
            loss_rows = loss_rows + jnp.sum(total * f_ref[band])
            gf_ref[pl.ds(0, sent)] = total * (2.0 * weight)
            grad = gf_ref[...]
            high = grad.astype(bf16)
            low = (grad - high.astype(f32)).astype(bf16)
            back = dot_nt(table_ref[0], high) + dot_nt(table_ref[0], low) + dot_nt(table_ref[1], high)
            gnet_ref[band] = (back * keep_ref[band] * c_output).astype(bf16)
        loss_out[...] = loss_rows * weight

        sums_ref[...] = jnp.zeros_like(sums_ref)

        def back_feed(spot):
            grad_node = dot_nn(turned_ref[0, spot], gnet_ref[0])
            for band in range(1, bands):
                grad_node += dot_nn(turned_ref[band, spot], gnet_ref[band])
            grad_node = grad_node * third
            high = grad_node.astype(bf16)
            low = (grad_node - high.astype(f32)).astype(bf16)
            node_ref[spot, pl.ds(0, 128)] = high
            grad_out = dot_nn(high, dec_rows) + dot_nn(low, dec_rows)
            branch = grad_out.astype(bf16)
            gb_ref[spot] = branch
            grad_activ = dot_nt(branch, mlp_ref[pl.ds(hidden, hidden)])
            grad_upper = (grad_activ * slope_ref[spot].astype(f32)).astype(bf16)
            slope_ref[spot] = grad_upper
            grad_second = dot_nn(grad_upper, mlp_ref[pl.ds(0, hidden)])
            unit, inverse = norm_parts(h1_ref[spot])
            scaled = grad_second * (1.0 + mod[2])
            grad_mid = grad_out + inverse * (
                scaled
                - jnp.mean(scaled, axis=-1, keepdims=True)
                - unit * jnp.mean(scaled * unit, axis=-1, keepdims=True)
            )
            sums_ref[2:3] += jnp.sum(grad_second * unit, axis=0, keepdims=True)
            sums_ref[3:4] += jnp.sum(grad_second, axis=0, keepdims=True)
            h1_ref[spot] = grad_mid
            grad_attn = grad_mid.astype(bf16)
            gattn_ref[spot] = grad_attn
            gblend_ref[spot] = dot_nn(grad_attn, attn_ref[pl.ds(3 * width, width)]).astype(bf16)

        row_loop(tile, back_feed)

        def outer_loop(target, offset, left, right, columns):
            @pl.loop(0, columns // big)
            def _(index):
                part = pl.multiple_of(index * big, big)
                product = dot_tn(left[:, pl.ds(part, big)], right[...])
                target[pl.ds(pl.multiple_of(offset + part, big), big)] = product.astype(bf16)

        gext_ref[...] = jnp.zeros_like(gext_ref)

        def back_attend(spot):
            count = near_ref[spot].astype(f32)
            for head in range(HEAD_COUNT):
                part = pl.ds(head * head_width, head_width)
                values = pl.ds(width + head * head_width, head_width)
                prob = prob_ref[head, spot].astype(f32)
                counted_prob = prob * count
                grad_blend = gblend_ref[spot, part]
                grad_prob = dot_nt(grad_blend, ext_ref[:, values])
                mean = jnp.sum(counted_prob * grad_prob, axis=-1, keepdims=True)
                grad_logit = (counted_prob * (grad_prob - mean)).astype(bf16)
                gext_ref[:, part] += dot_tn(grad_logit, q_ref[spot, part])
                q_ref[spot, part] = (dot_nn(grad_logit, ext_ref[:, part]) * score_scale).astype(bf16)
                gext_ref[:, values] += dot_tn(counted_prob.astype(bf16), grad_blend)

        row_loop(tile, back_attend)
        gext_ref[:, pl.ds(0, width)] = gext_ref[:, pl.ds(0, width)] * score_scale
        lost_ref[0] = gext_ref[pl.ds(rows, halo)].astype(bf16)
        lost_ref[1] = gext_ref[pl.ds(rows + halo, halo)].astype(bf16)
        from_upper = to_node(nodes - 1, lost_ref.at[0], back_ref.at[pl.ds(0, halo)], back_sem.at[0])
        from_lower = to_node(1, lost_ref.at[1], back_ref.at[pl.ds(halo, halo)], back_sem.at[1])

        outer_loop(mlp_out, hidden, activ_ref, gb_ref, hidden)
        outer_loop(mlp_out, 0, slope_ref, second_ref, hidden)
        outer_loop(attn_out, 3 * width, gattn_ref, blend_ref, width)
        outer_loop(attn_out, 0, q_ref, first_ref, width)
        from_upper.wait_recv()
        from_lower.wait_recv()

        def back_encode(spot):
            grad_pairs = gext_ref[spot] + dot_nn(lendt_ref[spot], back_ref[...])
            grad_pairs = grad_pairs.astype(bf16)
            ext_ref[spot] = grad_pairs
            grad_first = dot_nn(q_ref[spot], attn_ref[pl.ds(0, width)]) + dot_nn(
                grad_pairs, attn_ref[pl.ds(width, 2 * width)]
            )
            unit, inverse = norm_parts(h0_ref[spot])
            scaled = grad_first * (1.0 + mod[0])
            grad_in = h1_ref[spot] + inverse * (
                scaled
                - jnp.mean(scaled, axis=-1, keepdims=True)
                - unit * jnp.mean(scaled * unit, axis=-1, keepdims=True)
            )
            sums_ref[0:1] += jnp.sum(grad_first * unit, axis=0, keepdims=True)
            sums_ref[1:2] += jnp.sum(grad_first, axis=0, keepdims=True)
            gb_ref[spot] = grad_in.astype(bf16)

        row_loop(big, back_encode)
        outer_loop(attn_out, width, ext_ref.at[pl.ds(0, rows)], first_ref, 2 * width)

        feats_value = feats_ref[...]
        small_rows = small_ref.shape[0]
        cond = feats_value[:, 0:1] * sums_ref[0:1]
        for j in range(1, 4):
            cond += feats_value[:, j : j + 1] * sums_ref[j : j + 1]
        for low_row in range(0, small_rows, 128):
            total = cond[low_row : low_row + 128]
            if low_row < wide:
                total += dot_tn(mixed_ref[0, :, pl.ds(low_row, 128)], gb_ref[...])
            if low_row == start:
                total += dot_tn(node_ref[:, pl.ds(0, 128)], out_ref[...])
            high = total.astype(bf16)
            high_out[pl.ds(low_row, 128)] = high
            low_out[pl.ds(low_row, 128)] = (total - high.astype(f32)).astype(bf16)
        for copy in started:
            copy.wait_send()

    vmem = pl.BlockSpec(memory_space=pltpu.VMEM)
    hbm = pl.BlockSpec(memory_space=pl.ANY)
    dma = pltpu.SemaphoreType.DMA
    struct = jax.ShapeDtypeStruct
    low = lambda *shape: pltpu.VMEM(shape, bf16)
    full = lambda *shape: pltpu.VMEM(shape, f32)
    return pl.pallas_call(
        kernel,
        out_shape=(
            struct(attn.shape, bf16),
            struct(mlp.shape, bf16),
            struct(small.shape, bf16),
            struct(small.shape, bf16),
            struct((8, 128), f32),
        ),
        in_specs=[hbm, hbm, vmem, hbm, hbm, hbm] + [vmem] * 8 + [pl.BlockSpec(memory_space=pltpu.SMEM)],
        out_specs=(vmem,) * 5,
        scratch_shapes=[
            low(*attn.shape),
            low(*mlp.shape),
            low(*near.shape),
            low(*dec.shape),
            low(*dec_turned.shape),
            full(rows, width),
            full(rows, width),
            low(rows, width),
            low(rows, width),
            low(ext_rows, 2 * width),
            low(halo, 2 * width),
            low(HEAD_COUNT, rows, ext_rows),
            low(rows, width),
            low(rows, width),
            low(rows, hidden),
            low(rows, hidden),
            low(rows, width),
            low(rows, 256),
            full(lats, sent, lanes),
            low(nodes, lats, sent, lanes),
            full(128, lanes),
            low(bands, lons, 128),
            low(rows, width),
            low(rows, width),
            low(rows, width),
            full(ext_rows, 2 * width),
            low(2 * halo, 2 * width),
            low(2, halo, 2 * width),
            full(8, width),
            dma((5,)),
            dma((2, 2)),
            dma((place.uppers, lats, 2)),
            dma((place.uppers, lats, 2)),
            dma((2, 2)),
        ],
        compiler_params=pltpu.CompilerParams(
            collective_id=collective, has_side_effects=True, vmem_limit_bytes=62 << 20
        ),
    )(attn, mlp, small, near, dec, dec_turned, mixed, lend, lendt, kern, feats, base, keep, tables, scalars)


class Scatter:
    def __init__(self, place, pieces, grads, bufs, sems):
        self.place, self.pieces, self.grads = place, pieces, grads
        count = len(grads)
        self.core_in = bufs[:count]
        (self.over_out, self.over_in, self.under_out, self.under_in, self.over_out2, self.over_in2,
         self.under_out2, self.under_in2, self.far_out, self.far_in) = bufs[count:]
        (self.core_sem, self.over_sem, self.under_sem, self.over_sem2, self.under_sem2, self.far_sem) = sems
        self.started = []
        self.order = list(range(1, place.fars)) + [0]
        self.core, self.over, self.under, self.over2, self.under2, self.far = {}, {}, {}, {}, {}, {}
        self.head_rows = sum(rows for _, _, rows in pieces.head)
        self.tail_rows = sum(rows for _, _, rows in pieces.tail)

    def send(self, source, target, sem, **steps):
        return start_copy(self.started, self.place, source, target, sem, **steps)

    def begin(self, arrays):
        place = self.place
        other = 1 - place.core
        for k in self.order:
            far = place.moved(far=k)[2]
            for upper in range(place.uppers):
                for near in range(place.nears):
                    slot = place.slot(upper, other, far, near)
                    for a in arrays:
                        self.core[k, upper, near, a] = self.send(
                            self.grads[a].at[slot], self.core_in[a].at[k, upper, near],
                            self.core_sem.at[k, upper, near, a], core=1,
                        )

    def add(self, target, k, upper, near, pieces, others):
        far = self.place.moved(far=k)[2]
        slot = self.place.slot(upper, self.place.core, far, near)
        offset = 0
        for array, start, rows in pieces:
            mine = self.grads[array].at[slot]
            theirs = self.core_in[array].at[k, upper, near]

            @pl.loop(0, rows // ROW_CHUNK)
            def _(index, start=start, offset=offset, mine=mine, theirs=theirs):
                step = index * ROW_CHUNK
                here = pl.ds(pl.multiple_of(start + step, ROW_CHUNK), ROW_CHUNK)
                there = pl.ds(pl.multiple_of(offset + step, ROW_CHUNK), ROW_CHUNK)
                total = mine[here].astype(f32) + theirs[here].astype(f32)
                for other in others:
                    total += other[there].astype(f32)
                target[there] = total.astype(target.dtype)

            offset += rows

    def one(self, k):
        place, pieces = self.place, self.pieces
        for key in self.core:
            if key[0] == k:
                self.core[key].wait_recv()
        for i in range(1, place.uppers):
            for near in range(place.nears):
                self.add(self.over_out.at[k, i - 1, near], k, place.moved(upper=i)[0], near, pieces.head, [])
            self.over[k, i] = self.send(
                self.over_out.at[k, i - 1], self.over_in.at[k, i - 1], self.over_sem.at[k, i], upper=i
            )
        for j in range(1, place.nears):
            for upper in range(place.uppers):
                self.add(self.under_out.at[k, j - 1, upper], k, upper, place.moved(near=j)[3], pieces.tail, [])
            self.under[k, j] = self.send(
                self.under_out.at[k, j - 1], self.under_in.at[k, j - 1], self.under_sem.at[k, j], near=j
            )

    def overs(self, k, near):
        return [self.over_in.at[k, i - 1, near] for i in range(1, self.place.uppers)]

    def unders(self, k, upper):
        return [self.under_in.at[k, j - 1, upper] for j in range(1, self.place.nears)]

    def two(self, k):
        place, pieces = self.place, self.pieces
        for i in range(1, place.uppers):
            self.over[k, i].wait_recv()
        for j in range(1, place.nears):
            near = place.moved(near=j)[3]
            self.add(self.over_out2.at[k, j - 1], k, place.upper, near, pieces.head, self.overs(k, near))
            self.over2[k, j] = self.send(
                self.over_out2.at[k, j - 1], self.over_in2.at[k, j - 1], self.over_sem2.at[k, j], near=j
            )
        for j in range(1, place.nears):
            self.under[k, j].wait_recv()
        for i in range(1, place.uppers):
            upper = place.moved(upper=i)[0]
            self.add(self.under_out2.at[k, i - 1], k, upper, place.near, pieces.tail, self.unders(k, upper))
            self.under2[k, i] = self.send(
                self.under_out2.at[k, i - 1], self.under_in2.at[k, i - 1], self.under_sem2.at[k, i], upper=i
            )

    def three(self, k, target, extra):
        place, pieces = self.place, self.pieces
        for j in range(1, place.nears):
            self.over2[k, j].wait_recv()
        for i in range(1, place.uppers):
            self.under2[k, i].wait_recv()
        head, tail = pl.ds(0, self.head_rows), pl.ds(self.head_rows, self.tail_rows)
        self.add(
            target.at[head], k, place.upper, place.near, pieces.head,
            self.overs(k, place.near)
            + [self.over_in2.at[k, j - 1] for j in range(1, place.nears)]
            + [item.at[head] for item in extra],
        )
        self.add(
            target.at[tail], k, place.upper, place.near, pieces.tail,
            self.unders(k, place.upper)
            + [self.under_in2.at[k, i - 1] for i in range(1, place.uppers)]
            + [item.at[tail] for item in extra],
        )

    def step(self, step):
        fars, order = self.place.fars, self.order
        if step < fars:
            self.one(order[step])
        if 1 <= step <= fars:
            self.two(order[step - 1])
        if step >= 2 and order[step - 2]:
            k = order[step - 2]
            self.three(k, self.far_out.at[k - 1], [])
            self.far[k] = self.send(self.far_out.at[k - 1], self.far_in.at[k - 1], self.far_sem.at[k], far=k)

    def steps(self):
        return self.place.fars + 2

    def finish(self, own):
        fars = self.place.fars
        for k in range(1, fars):
            self.far[k].wait_recv()
        self.three(0, own, [self.far_in.at[k - 1] for k in range(1, fars)])

    def end(self):
        for copy in self.started:
            copy.wait_send()

    @staticmethod
    def scratch(place, pieces, width):
        fars, nears, uppers = place.fars, place.nears, place.uppers
        head = sum(rows for _, _, rows in pieces.head)
        tail = sum(rows for _, _, rows in pieces.tail)
        dma = pltpu.SemaphoreType.DMA
        bufs = [(fars, uppers, nears, size) for size in pieces.sizes]
        bufs += [(fars, uppers - 1, nears, head)] * 2
        bufs += [(fars, nears - 1, uppers, tail)] * 2
        bufs += [(fars, nears - 1, head)] * 2
        bufs += [(fars, uppers - 1, tail)] * 2
        bufs += [(fars - 1, head + tail)] * 2
        if width:
            bufs = [pltpu.VMEM(shape + (width,), bf16) for shape in bufs]
        sems = [
            dma((fars, uppers, nears, len(pieces.sizes), 2)),
            dma((fars, uppers, 2)),
            dma((fars, nears, 2)),
            dma((fars, nears, 2)),
            dma((fars, uppers, 2)),
            dma((fars, 2)),
        ]
        return bufs, sems


class Strip:
    def __init__(self, ref, first, dims):
        self.ref, self.first, self.dims, self.at = ref, first, dims, self

    def __getitem__(self, index):
        index = index if isinstance(index, tuple) else (index,)
        sizes = self.dims[1:]
        flat, rows = 0, 1
        for axis, size in enumerate(sizes):
            if axis + 1 < len(index):
                flat = flat * size + index[axis + 1]
            else:
                flat, rows = flat * size, rows * size
        return self.ref.at[index[0], pl.ds(self.first + flat, rows)]


def strips(refs, shapes):
    result, at, first = [], 0, 0
    for shape in shapes:
        rows = math.prod(shape[1:])
        if first + rows > refs[at].shape[1]:
            at, first = at + 1, 0
        result.append(Strip(refs[at], first, shape))
        first += rows
    return result


class HalfGather:
    def __init__(self, place, shard, out, sems):
        self.place, self.shard, self.out = place, shard, out
        self.own_sem, self.far_sem, self.near_sem, self.mate_sem, self.core_sem = sems
        self.started, self.cores = [], []
        self.far, self.near, self.mate = {}, {}, {}

    def block(self, **steps):
        return self.out.at[self.place.slot(*self.place.moved(**steps))]

    def send(self, source, target, sem, **steps):
        return start_copy(self.started, self.place, source, target, sem, **steps)

    def begin(self):
        self.kept = pltpu.make_async_copy(self.shard, self.block(), self.own_sem)
        self.kept.start()
        for k in range(1, self.place.fars):
            self.far[k] = self.send(self.shard, self.block(), self.far_sem.at[k], far=k)

    def spread(self, k, j, source, target):
        for i in range(1, self.place.mates):
            self.mate[k, j, i] = self.send(source, target, self.mate_sem.at[k, j, i], mate=i)
        self.cores.append(self.send(source, target, self.core_sem.at[k, j, 0], core=1))

    def step(self, step):
        place = self.place
        fars, nears = place.fars, place.nears
        if step < fars:
            if step:
                self.far[step].wait_recv()
            target = self.block(far=(fars - step) % fars)
            source = target if step else self.shard
            for j in range(1, nears):
                self.near[step, j] = self.send(source, target, self.near_sem.at[step, j], near=j)
            self.spread(step, 0, source, target)
        if 1 <= step <= fars:
            k = step - 1
            for j in range(1, nears):
                self.near[k, j].wait_recv()
                item = self.block(far=(fars - k) % fars, near=nears - j)
                self.spread(k, j, item, item)
        if step >= 2:
            k = step - 2
            for j in range(nears):
                for i in range(1, place.mates):
                    self.mate[k, j, i].wait_recv()
                    item = self.block(far=(fars - k) % fars, near=(nears - j) % nears, mate=place.mates - i)
                    self.cores.append(self.send(item, item, self.core_sem.at[k, j, i], core=1))

    def end(self):
        self.kept.wait()
        wait_all(self.cores)
        for copy in self.started:
            copy.wait_send()

    @staticmethod
    def sems(place):
        dma = pltpu.SemaphoreType.DMA
        fars, nears, mates = place.fars, place.nears, place.mates
        return [
            dma,
            dma((fars, 2)),
            dma((fars, nears, 2)),
            dma((fars, nears, mates, 2)),
            dma((fars, nears, mates, 2)),
        ]


class MomentGather:
    def __init__(self, place, shards, outs, sems):
        self.place, self.shards, self.outs = place, shards, outs
        (self.own_sem, self.far_sem, self.near_sem, self.spread_sem, self.core_sem) = sems
        self.started, self.cores = [], []
        self.far, self.near, self.spread_copies = {}, {}, {}

    def block(self, **steps):
        slot = self.place.slot(*self.place.moved(**steps))
        return [out.at[slot] for out in self.outs]

    def send(self, source, target, sem, **steps):
        return start_copy(self.started, self.place, source, target, sem, **steps)

    def both(self, source, target, sems, **steps):
        return [self.send(source[a], target[a], sems.at[a], **steps) for a in range(2)]

    def spread(self, k, j, source, target):
        place = self.place
        for i in range(1, place.uppers):
            self.spread_copies[k, j, i, 0] = self.send(
                source[0], target[0], self.spread_sem.at[k, j, i, 0], upper=i
            )
        for i in range(1, place.mates):
            self.spread_copies[k, j, i, 1] = self.send(
                source[1], target[1], self.spread_sem.at[k, j, i, 1], mate=i
            )
        self.cores += self.both(source, target, self.core_sem.at[k, j, 0], core=1)

    def run(self):
        place = self.place
        fars, nears = place.fars, place.nears
        here = self.block()
        kept = [
            pltpu.make_async_copy(shard, target, self.own_sem.at[a])
            for a, (shard, target) in enumerate(zip(self.shards, here))
        ]
        for copy in kept:
            copy.start()
        for k in range(1, fars):
            self.far[k] = self.both(self.shards, here, self.far_sem.at[k], far=k)
        for step in range(fars + 2):
            if step < fars:
                k = step
                if k:
                    wait_all(self.far[k])
                target = self.block(far=(fars - k) % fars)
                source = target if k else self.shards
                for j in range(1, nears):
                    self.near[k, j] = self.both(source, target, self.near_sem.at[k, j], near=j)
                self.spread(k, 0, source, target)
            if 1 <= step <= fars:
                k = step - 1
                for j in range(1, nears):
                    wait_all(self.near[k, j])
                    item = self.block(far=(fars - k) % fars, near=nears - j)
                    self.spread(k, j, item, item)
            if step >= 2:
                k = step - 2
                for j in range(nears):
                    steps = dict(far=(fars - k) % fars, near=(nears - j) % nears)
                    for key in self.spread_copies:
                        if key[:2] != (k, j):
                            continue
                        i, a = key[2:]
                        self.spread_copies[key].wait_recv()
                        if a:
                            item = self.block(mate=place.mates - i, **steps)[1]
                        else:
                            item = self.block(upper=place.uppers - i, **steps)[0]
                        self.cores.append(self.send(item, item, self.core_sem.at[k, j, i, a], core=1))
        for copy in kept:
            copy.wait()
        wait_all(self.cores)
        for copy in self.started:
            copy.wait_send()

    @staticmethod
    def sems(place):
        dma = pltpu.SemaphoreType.DMA
        fars, nears, uppers = place.fars, place.nears, place.uppers
        return [
            dma((2,)),
            dma((fars, 2, 2)),
            dma((fars, nears, 2, 2)),
            dma((fars, nears, uppers, 2, 2)),
            dma((fars, nears, uppers, 2, 2)),
        ]


def total_body(place, tile, slots, sems):
    value = tile
    upper, core, far, near = place.moved()
    stages = (
        ("core", 2, core),
        ("near", place.nears, near),
        ("upper", place.uppers, upper),
        ("far", place.fars, far),
    )
    for stage, (name, size, mine) in enumerate(stages):
        slots[stage, mine] = value
        copies = []
        for step in range(1, size):
            piece = slots.at[stage, mine]
            start_copy(copies, place, piece, piece, sems.at[stage, step], **{name: step})
        for copy in copies:
            copy.wait()
        value = slots[stage, 0]
        for other in range(1, size):
            value = value + slots[stage, other]
    return value


def reduce_and_gather(nodes, zeros, names, grads, mlp_sum, loss_tile, mom_attn, mom_mlp, small_rows, collective):
    place = Place(nodes, zeros)
    devices, _, width = grads[0].shape
    attn_rows, mlp_rows = mom_attn.shape[0], mom_mlp.shape[0]
    lead = names.index("mlp") if "mlp" in names else 0
    pieces = Pieces([item.shape[1] for item in grads], lead)
    moment_sizes = (sixteens(attn_rows), sixteens(mlp_rows))
    bufs, sems = Scatter.scratch(place, pieces, width)
    deepest = max(place.fars, place.uppers, place.nears, 2)
    summed = [] if mlp_sum is None else [mlp_sum]
    count = len(grads)
    starts, offset = {}, 0
    for array in [lead] + [i for i in range(count) if i != lead]:
        starts[names[array]] = offset
        offset += pieces.sizes[array]

    def kernel(*refs):
        grad_refs = refs[:count]
        refs = refs[count:]
        if summed:
            sum_ref, *refs = refs
        loss_ref, attn_ref, mlp_ref = refs[:3]
        small_out, attn_out, mlp_out, total_out, attn_all, mlp_all = refs[3:9]
        own, attn_shard, mlp_shard, slots, slot_sems = refs[9:14]
        rest = refs[14:]
        place.locate()
        place.greet()
        scatter = Scatter(
            place, pieces, grad_refs, rest[: len(bufs)], rest[len(bufs) : len(bufs) + len(sems)]
        )
        scatter.begin([lead] + [i for i in range(count) if i != lead])
        for step in range(scatter.steps()):
            scatter.step(step)
        scatter.finish(own)
        g_attn = own[pl.ds(starts["attn"], attn_rows)]
        g_mlp = sum_ref[...] if summed else own[pl.ds(starts["mlp"], mlp_rows)]
        g_small = own[pl.ds(starts["high"], small_rows)] + own[pl.ds(starts["low"], small_rows)]
        small_out[...] = g_small
        squares = jnp.sum(g_attn * g_attn) + jnp.sum(g_mlp * g_mlp) + jnp.sum(g_small * g_small)
        tile = jnp.where(iota((8, 128), 0) < 4, squares, loss_ref[...])
        total = total_body(place, tile, slots, slot_sems)
        total_out[...] = total
        factor = jnp.minimum(1.0, clip_limit * lax.rsqrt(total[0:1, 0:1]))
        for ref, out, shard, grad, size in (
            (attn_ref, attn_out, attn_shard, g_attn, attn_rows),
            (mlp_ref, mlp_out, mlp_shard, g_mlp, mlp_rows),
        ):
            moment = moment_decay * ref[...] + factor * grad
            out[...] = moment
            if size < shard.shape[0]:
                shard[...] = jnp.zeros_like(shard)
            shard[pl.ds(0, size)] = moment.astype(bf16)
        moments = MomentGather(
            place, (attn_shard, mlp_shard), (attn_all, mlp_all), rest[len(bufs) + len(sems) :]
        )
        moments.run()
        scatter.end()

    vmem = pl.BlockSpec(memory_space=pltpu.VMEM)
    hbm = pl.BlockSpec(memory_space=pl.ANY)
    struct = jax.ShapeDtypeStruct
    return pl.pallas_call(
        kernel,
        out_shape=(
            struct((small_rows, width), f32),
            struct((attn_rows, width), f32),
            struct((mlp_rows, width), f32),
            struct((8, 128), f32),
            struct((devices, moment_sizes[0], width), bf16),
            struct((devices, moment_sizes[1], width), bf16),
        ),
        in_specs=[vmem] * (count + len(summed) + 3),
        out_specs=(vmem,) * 4 + (hbm,) * 2,
        scratch_shapes=[
            pltpu.VMEM((sum(pieces.sizes), width), f32),
            pltpu.VMEM((moment_sizes[0], width), bf16),
            pltpu.VMEM((moment_sizes[1], width), bf16),
            pltpu.VMEM((4, deepest, 8, 128), f32),
            pltpu.SemaphoreType.DMA((4, deepest, 2)),
        ]
        + bufs
        + sems
        + MomentGather.sems(place),
        compiler_params=pltpu.CompilerParams(
            collective_id=collective, has_side_effects=True, vmem_limit_bytes=56 << 20
        ),
    )(*grads, *summed, loss_tile, mom_attn, mom_mlp)


def basis_apply(gram, moment):
    size = gram.shape[0]
    eye = jnp.where(iota((size, size), 0) == iota((size, size), 1), 1.0, 0.0)
    trace = jnp.sum(jnp.sum(gram * eye, axis=1, keepdims=True), axis=0, keepdims=True)
    scale = lax.rsqrt(trace + trace_epsilon)
    current = gram * (scale * scale)
    result = moment * scale
    for iteration in range(NS_ITERS):
        low = current.astype(bf16)
        rest = newton_second * current + newton_third * dot_nn(low, low)
        rest_low = rest.astype(bf16)
        result = newton_first * result + dot_nn(result.astype(bf16), rest_low)
        if iteration + 1 < NS_ITERS:
            once = dot_nn(rest_low, low)
            current = (
                (newton_first * newton_first) * current
                + (2.0 * newton_first) * once
                + dot_nn(once.astype(bf16), rest_low)
            )
    return result


def update_weights(nodes, zeros, attn_sets, mlp_sets, totals, sums, moments, weights, averages, small_moments):
    width = attn_sets[0].shape[1]
    attn_rows, mlp_rows, small_rows = [w.shape[0] for w in weights]
    half = mlp_sets[0].shape[0] // 2
    block = width
    inputs = (*sums, *moments, *weights, *averages, *small_moments)
    count, sets = len(inputs), len(attn_sets)
    fresh = sets == 1

    def kernel(total_ref, *refs):
        attn_hbm, mlp_hbm, sources = refs[:sets], refs[sets : 2 * sets], refs[2 * sets : 2 * sets + count]
        refs = refs[2 * sets + count :]
        loss_out, clip_out, new_attn, new_mlp, new_small, new_m, new_v, new_e_attn, new_e_mlp, new_e_small = refs[:10]
        mom_attn_out, mom_mlp_out = refs[10:12]
        gram_attn, gram_mlp, attn_sem, mlp_sem, row_sem = refs[12:17]
        attn_refs, mlp_refs, rows = refs[17 : 17 + sets], refs[17 + sets : 17 + 2 * sets], refs[17 + 2 * sets :]
        g_refs, rows = rows[: len(sums)], rows[len(sums) :]
        mom_attn, mom_mlp, w_attn, w_mlp, w_small, e_attn, e_mlp, e_small, m_ref, v_ref = rows
        flat = lax.axis_index("node") * zeros + lax.axis_index("zero")
        attn_upper = flat * attn_rows >= 3 * width
        mlp_upper = flat * mlp_rows >= half
        mine = pl.ds(pl.multiple_of(jnp.where(mlp_upper, half, 0), half), half)
        copies_mlp = [
            pltpu.make_async_copy(mlp_hbm[i].at[mine], mlp_refs[i], mlp_sem.at[i]) for i in range(sets)
        ]
        copies_attn = [
            pltpu.make_async_copy(attn_hbm[i], attn_refs[i], attn_sem.at[i]) for i in range(sets)
        ]
        copies = [
            pltpu.make_async_copy(source, target, row_sem.at[index])
            for index, (source, target) in enumerate(zip(sources, refs[17 + 2 * sets :]))
        ]
        for copy in copies_mlp + copies_attn + copies:
            copy.start()
        total = total_ref[0]
        for index in range(1, total_ref.shape[0]):
            total = total + total_ref[index]
        loss_out[...] = total[4:5, 0:1]
        clip_out[...] = jnp.sqrt(total[0:1, 0:1])
        factor = jnp.minimum(1.0, clip_limit * lax.rsqrt(total[0:1, 0:1]))

        def momentum(refs, index):
            part = pl.ds(pl.multiple_of(index * block, block), block)
            if fresh:
                return refs[0][part]
            return (moment_decay * refs[0][part].astype(f32) + factor * refs[1][part].astype(f32)).astype(bf16)

        for copy in copies_mlp:
            copy.wait()
        gram_mlp[...] = jnp.zeros_like(gram_mlp)

        @pl.loop(0, half // block)
        def _(index):
            part = momentum(mlp_refs, index)
            gram_mlp[...] += dot_tn(part, part)

        for copy in copies_attn:
            copy.wait()
        gram_attn[...] = jnp.zeros_like(gram_attn)
        start = jnp.where(attn_upper, 3, 0)

        @pl.loop(start, jnp.where(attn_upper, 4, 3))
        def _(index):
            part = momentum(attn_refs, index)
            gram_attn[...] += dot_tn(part, part)

        for copy in copies:
            copy.wait()

        clipped = factor * g_refs[0][...]
        first = adam_first * m_ref[...] + (1.0 - adam_first) * clipped
        second = adam_second * v_ref[...] + (1.0 - adam_second) * clipped * clipped
        new_m[...] = first
        new_v[...] = second
        small = w_small[...] - adam_rate * (first / (1.0 - adam_first**STEP)) / (
            jnp.sqrt(second / (1.0 - adam_second**STEP)) + adam_epsilon
        )
        new_small[...] = small
        new_e_small[...] = average_decay * e_small[...] + (1.0 - average_decay) * small

        attn_moment, mlp_moment = mom_attn[...], mom_mlp[...]
        if not fresh:
            attn_moment = moment_decay * attn_moment + factor * g_refs[1][...]
            mlp_moment = moment_decay * mlp_moment + factor * g_refs[2][...]
        mom_attn_out[...] = attn_moment
        mom_mlp_out[...] = mlp_moment
        attn_step = basis_apply(gram_attn[...], attn_moment)
        mlp_step = basis_apply(gram_mlp[...], mlp_moment)
        attn_factor = jnp.where(attn_upper, 0.2 * math.sqrt(width), 0.2 * math.sqrt(3 * width))
        mlp_factor = 0.2 * math.sqrt(max(half, width))
        for step, rate, old, new, mean, new_mean in (
            (attn_step, orthogonal_rate * attn_factor, w_attn, new_attn, e_attn, new_e_attn),
            (mlp_step, orthogonal_rate * mlp_factor, w_mlp, new_mlp, e_mlp, new_e_mlp),
        ):
            value = old[...] - rate * step
            new[...] = value
            new_mean[...] = average_decay * mean[...] + (1.0 - average_decay) * value

    vmem = pl.BlockSpec(memory_space=pltpu.VMEM)
    hbm = pl.BlockSpec(memory_space=pl.ANY)
    one = jnp.zeros((1, 1), f32)
    outs = [one, one, weights[0], weights[1], weights[2], weights[2], weights[2], weights[0], weights[1], weights[2]]
    outs += [weights[0], weights[1]]
    dma = pltpu.SemaphoreType.DMA
    return pl.pallas_call(
        kernel,
        out_shape=tuple(jax.ShapeDtypeStruct(item.shape, f32) for item in outs),
        in_specs=[vmem] + [hbm] * (2 * sets + count),
        out_specs=(vmem,) * 12,
        scratch_shapes=[
            pltpu.VMEM((width, width), f32),
            pltpu.VMEM((width, width), f32),
            dma((sets,)),
            dma((sets,)),
            dma((count,)),
        ]
        + [pltpu.VMEM(attn_sets[0].shape, bf16)] * sets
        + [pltpu.VMEM((half, width), bf16)] * sets
        + [pltpu.VMEM(item.shape, f32) for item in inputs],
        compiler_params=pltpu.CompilerParams(vmem_limit_bytes=62 << 20),
    )(totals, *attn_sets, *mlp_sets, *inputs)


def train_step(nodes, zeros, weights, grid, target, land, near_turned, enc_turned, dec_turned, lent, legendre, vector, tables, moments, cin, collective):
    place = Place(nodes, zeros)
    devices = nodes * zeros
    attn_rows, mlp_rows, small_rows = [w.shape[0] for w in weights]
    width = weights[0].shape[1]
    hidden = devices * mlp_rows // 2
    bands, lons, channels = target.shape
    fanout, rows = near_turned.shape
    enc_edges, dec_edges = enc_turned.shape[0], dec_turned.shape[0]
    halo = lent.shape[1]
    ext_rows = rows + 2 * halo
    lats, lows, lanes = legendre.shape
    all_lats = nodes * lats
    wide = -(-cin // 128) * 128
    start = cin // 128 * 128
    shift = cin - start
    sent = sixteens(channels)
    flat_lons = -(-lons // 128) * 128
    flat_pixels = -(-bands * lons // 128) * 128
    all_small = devices * small_rows
    cond_start = cin + channels
    big, tile, chunk = 256, 128, 512
    head_width = width // HEAD_COUNT
    score_scale = head_width ** (-0.5)
    third = 1.0 / dec_edges
    first_pieces = Pieces([attn_rows, small_rows], 0)
    mlp_pieces = Pieces([mlp_rows], 0)
    last_pieces = Pieces([attn_rows, small_rows, small_rows], 0)
    attn_pieces = Pieces([attn_rows], 0)
    tile_pieces = Pieces([attn_rows, 8], 0)
    scatter_bufs, scatter_sems = Scatter.scratch(place, mlp_pieces, width)
    last_shapes, last_sems = Scatter.scratch(place, last_pieces, 0)
    groups = [
        Gather.sems(place, first_pieces),
        Gather.sems(place, mlp_pieces),
        scatter_bufs,
        scatter_sems,
        last_sems,
        Gather.sems(place, attn_pieces),
        HalfGather.sems(place),
        Gather.sems(place, tile_pieces),
        HalfGather.sems(place),
    ]

    def kernel(
        attn_in, mlp_in, small_in, grid_ref, target_ref, land_ref, near_in, enc_in, dec_in, lent_ref, leg_ref,
        vector_ref, table_ref, mom_attn_in, mom_mlp_in,
        attn_sum, mlp_sum, small_sum, tiles_out, mom_attn_all, mom_mlp_all, g_attn_all, g_mlp_all,
        high_out, low_out, own, mom_attn_shard, mom_mlp_shard, g_attn_shard, g_mlp_shard, tile_shard,
        attn_shard, mlp_shard, small_shard, legs, parts, sums, kern_ref,
        attn_ref, mlp_ref, small_ref, near_ref, dec_ref, mixed_ref, lendt_ref, h0_ref, h1_ref, first_ref, q_ref,
        ext_ref, lent_rows, prob_ref, blend_ref, second_ref, activ_ref, slope_ref, out_ref, node_ref, all_ref,
        gf_ref, gnet_ref, gnode_ref, gb_ref, gattn_ref, gblend_ref, gext_ref, back_ref, lost_ref, sums_ref,
        scale_ref, error_ref, column_ref, lists_ref, input_ref, dec_rows_ref, feats_ref,
        leg_sem, part_sem, sum_sem, lend_sem, f_sem, pass_sem, back_sem,
        *rest,
    ):
        parted = []
        for group in groups:
            parted.append(rest[: len(group)])
            rest = rest[len(group) :]
        sems_a, sems_b, bufs, sems_c, sems_d, sems_e, sems_f, sems_g, sems_h = parted
        place.locate()
        node = lax.axis_index("node")
        zero = lax.axis_index("zero")
        attn_shard[...] = attn_in[...].astype(bf16)
        small_shard[...] = small_in[...].astype(bf16)
        legs[node] = leg_ref[...]
        place.greet(nodes)
        gather = Gather(place, first_pieces, (attn_shard, small_shard), (attn_ref, small_ref), sems_a)
        gather_mlp = Gather(place, mlp_pieces, (mlp_shard,), (mlp_ref,), sems_b)
        gather.begin()
        started = []

        def to_node(step, source, target, sems):
            copy = pltpu.make_async_remote_copy(
                src_ref=source,
                dst_ref=target,
                send_sem=sems.at[0],
                recv_sem=sems.at[1],
                device_id=(lax.rem(node + step, nodes), zero),
                device_id_type=MESH,
            )
            copy.start()
            started.append(copy)
            return copy

        gather.step(0)
        leg_copies = [
            to_node(step, leg_ref, legs.at[node], leg_sem.at[step]) for step in range(1, nodes)
        ]
        mlp_shard[...] = mlp_in[...].astype(bf16)
        gather_mlp.begin()
        mom_attn_shard[...] = mom_attn_in[...].astype(bf16)
        mom_mlp_shard[...] = mom_mlp_in[...].astype(bf16)
        gather_moms = [
            Gather(place, attn_pieces, (mom_attn_shard,), (mom_attn_all,), sems_e),
            HalfGather(place, mom_mlp_shard, mom_mlp_all, sems_f),
        ]

        def mom_step(step):
            for item in gather_moms:
                item.step(step)

        def row_loop(size, body, hooks=()):
            count = rows // size
            cuts = [count * i // (len(hooks) + 1) for i in range(len(hooks) + 2)]
            for i in range(len(hooks) + 1):

                @pl.loop(cuts[i], cuts[i + 1])
                def _(index):
                    body(pl.ds(pl.multiple_of(index * size, size), size))

                if i < len(hooks):
                    hooks[i]()

        def mix():
            column_ref[pl.ds(0, enc_edges), pl.ds(0, rows)] = enc_in[...]
            lists_ref[pl.ds(0, rows), pl.ds(0, 8)] = jnp.transpose(column_ref[pl.ds(0, 8), pl.ds(0, rows)])
            lane = iota((1, cin), 1)
            scale = jnp.where(lane < channels, vector_ref[0:1, c_input_lane : c_input_lane + 1], 1.0)

            @pl.loop(0, bands)
            def _(band):
                input_ref[band] = (grid_ref[band].astype(f32) * scale).astype(bf16)

            mixed_ref[...] = jnp.zeros_like(mixed_ref)

            def mix_rows(spot):
                lists = lists_ref[spot]
                mean = jnp.zeros((tile, cin), f32)
                for band in range(bands):
                    place_of = iota((tile, lons), 1) + band * lons
                    total = jnp.zeros((tile, lons), f32)
                    for j in range(enc_edges):
                        total += jnp.where(lists[:, j : j + 1] == place_of, 1.0 / enc_edges, 0.0)
                    mean += dot_nn(total.astype(bf16), input_ref[band])
                high = mean.astype(bf16)
                mixed_ref[0, spot, pl.ds(0, cin)] = high
                mixed_ref[1, spot, pl.ds(0, cin)] = (mean - high.astype(f32)).astype(bf16)

            row_loop(tile, mix_rows)

        def count_near():
            lists_ref[pl.ds(0, rows), pl.ds(0, fanout)] = jnp.transpose(near_in[...])

            def count_rows(spot):
                lists = lists_ref[spot]
                place_of = iota((tile, ext_rows), 1)
                total = jnp.zeros((tile, ext_rows), f32)
                for j in range(fanout):
                    total += jnp.where(lists[:, j : j + 1] == place_of, 1.0, 0.0)
                near_ref[spot] = jnp.where(total > 0.0, jnp.log2(jnp.maximum(total, 1.0)), absent)

            row_loop(tile, count_rows)

        def count_dec():
            column_ref[pl.ds(0, dec_edges), pl.ds(0, bands * lons)] = dec_in[...]
            lists_ref[:, pl.ds(0, 8)] = jnp.transpose(column_ref[...])

            @pl.loop(0, bands)
            def _(band):
                lists = lists_ref[pl.ds(pl.multiple_of(band * lons, 8), lons)]
                place_of = iota((lons, rows), 1)
                total = jnp.zeros((lons, rows), f32)
                for j in range(dec_edges):
                    total += jnp.where(lists[:, j : j + 1] == place_of, 1.0, 0.0)
                dec_ref[band] = total.astype(bf16)

        near_parts, far_sums = [], []

        def gram():
            for copy in leg_copies:
                copy.wait_recv()

            @pl.loop(0, all_lats)
            def _(index):
                other = legs[index // lats, lax.rem(index, lats)]
                for t in range(lats):
                    parts[place.near, t, pl.ds(index, 1)] = jnp.sum(leg_ref[t] * other, axis=0, keepdims=True)

            for j in range(1, place.nears):
                piece = parts.at[place.near]
                near_parts.append(start_copy(started, place, piece, piece, part_sem.at[j], near=j))

        def gram_near():
            wait_all(near_parts)
            total = parts[0]
            for j in range(1, place.nears):
                total = total + parts[j]
            sums[place.far] = total
            for k in range(1, place.fars):
                piece = sums.at[place.far]
                far_sums.append(start_copy(started, place, piece, piece, sum_sem.at[k], far=k))

        def gram_far():
            wait_all(far_sums)
            total = sums[0]
            for k in range(1, place.fars):
                total = total + sums[k]
            kern_ref[...] = total

        lendt_ref[...] = jnp.where(lent_ref[...] == iota((rows, halo), 0), 1.0, 0.0).astype(bf16)
        work = [mix, gram, count_dec, gram_near]
        for k in range(1, place.fars + 2):
            gather.step(k)
            if k == 1:
                gather_mlp.step(0)
            if work:
                work.pop(0)()
        while work:
            work.pop(0)()
        gather.end()
        gather_mlp.step(1)

        def small_part(low, size):
            return small_ref[pl.ds(low // small_rows, size // small_rows)].reshape(size, width)

        row = iota((all_small, 128), 0) - cond_start
        lane = iota((all_small, 128), 1)
        feature = vector_ref[0:1]
        block = jnp.where(row >= 0, row // NOISE_FEATS, 4)
        picked = jnp.where((row - block * NOISE_FEATS == lane) & (block < 4) & (lane < NOISE_FEATS), feature, 0.0)
        column = jnp.sum(picked, axis=1, keepdims=True)
        feats_ref[...] = jnp.where(lane == block, column, 0.0)
        mods = dot_tn(feats_ref[...].astype(bf16), small_part(0, all_small))
        mod = [mods[j : j + 1] for j in range(4)]

        def attn_part(low, size):
            return attn_ref[pl.ds(low // attn_rows, size // attn_rows)].reshape(size, width)

        def mlp_part(low):
            return mlp_ref[pl.ds(low // mlp_rows, chunk // mlp_rows)].reshape(chunk, width)

        def encode(spot):
            enc = small_part(0, wide)
            h0 = dot_nn(mixed_ref[0, spot], enc) + dot_nn(mixed_ref[1, spot], enc)
            h0_ref[spot] = h0
            unit, inverse = norm_parts(h0)
            first = (unit * (1.0 + mod[0]) + mod[1]).astype(bf16)
            first_ref[spot] = first
            ext_ref[spot] = dot_nt(first, attn_part(width, 2 * width)).astype(bf16)
            q_ref[spot] = dot_nt(first, attn_part(0, width)).astype(bf16)

        row_loop(big, encode)
        lent_rows[...] = dot_tn(lendt_ref[...], ext_ref[pl.ds(0, rows)]).astype(bf16)
        up = to_node(1, lent_rows, ext_ref.at[pl.ds(rows, halo)], lend_sem.at[0])
        down = to_node(nodes - 1, lent_rows, ext_ref.at[pl.ds(rows + halo, halo)], lend_sem.at[1])
        gather_mlp.step(2)
        count_near()
        gram_far()
        gather_mlp.step(3)
        for item in gather_moms:
            item.begin()
        up.wait_recv()
        down.wait_recv()

        def attend(spot):
            often = near_ref[spot]
            for head in range(HEAD_COUNT):
                part = pl.ds(head * head_width, head_width)
                values = pl.ds(width + head * head_width, head_width)
                logits = dot_nt(q_ref[spot, part], ext_ref[:, part]) * (score_scale * log2_e) + often
                raised = jnp.exp2(logits - jnp.max(logits, axis=-1, keepdims=True))
                inverse = 1.0 / jnp.sum(raised, axis=-1, keepdims=True)
                raised = raised.astype(bf16)
                prob_ref[head, spot] = raised
                scale_ref[spot, pl.ds(head, 1)] = inverse
                blend_ref[spot, part] = (dot_nn(raised, ext_ref[:, values]) * inverse).astype(bf16)

        row_loop(tile, attend, [lambda: gather_mlp.step(4), lambda: gather_mlp.step(5)])
        for k in range(6, place.fars + 2):
            gather_mlp.step(k)
        gather_mlp.end()
        mom_step(0)
        lane = iota((1, 128), 1)
        live = jnp.where(lane < channels, 1.0, 0.0)
        dec_rows_ref[...] = pltpu.roll(small_part(start, 128).astype(f32), 128 - shift, 0).astype(bf16)

        def feed(spot):
            h1 = h0_ref[spot] + dot_nt(blend_ref[spot], attn_part(3 * width, width))
            h1_ref[spot] = h1
            unit, inverse = norm_parts(h1)
            second = (unit * (1.0 + mod[2]) + mod[3]).astype(bf16)
            second_ref[spot] = second
            h2 = h1
            for low in range(0, hidden, chunk):
                upper = dot_nt(second, mlp_part(low))
                square = upper * upper
                bend = jnp.tanh(upper * (gelu_scale + (gelu_scale * gelu_cubic) * square))
                half = 0.5 + 0.5 * bend
                activ = (upper * half).astype(bf16)
                activ_ref[low // chunk, spot] = activ
                slope = half + upper * (1.0 - bend * bend) * (
                    0.5 * gelu_scale + (1.5 * gelu_scale * gelu_cubic) * square
                )
                slope_ref[low // chunk, spot] = slope.astype(bf16)
                h2 += dot_nn(activ, mlp_part(hidden + low))
            high = h2.astype(bf16)
            out_ref[spot] = high
            low = (h2 - high.astype(f32)).astype(bf16)
            dec_rows = dec_rows_ref[...]
            projected = (dot_nt(high, dec_rows) + dot_nt(low, dec_rows)) * live
            top = projected.astype(bf16)
            node_ref[spot, pl.ds(0, 128)] = top
            node_ref[spot, pl.ds(128, 128)] = (projected - top.astype(f32)).astype(bf16)

        row_loop(big, feed, [lambda: mom_step(1)])

        c_skip = vector_ref[0:1, c_skip_lane : c_skip_lane + 1]
        c_output = vector_ref[0:1, c_output_lane : c_output_lane + 1]
        weight = vector_ref[0:1, weight_lane : weight_lane + 1]
        column_ref[pl.ds(0, bands), pl.ds(0, lons)] = land_ref[...]
        masks = jnp.transpose(column_ref[pl.ds(0, 8), pl.ds(0, flat_lons)].astype(f32))
        last = jnp.where(lane == channels - 1, 1.0, 0.0)

        def keep(band):
            return live * (1.0 - masks[:lons, band : band + 1] * last)

        error_ref[...] = jnp.zeros_like(error_ref)
        cores, uppers = {}, {}
        for band in range(bands):
            net = dot_nn(dec_ref[band], node_ref[...])
            net = (net[:, :128] + net[:, 128:]) * (c_output * third)
            noisy = grid_ref[band, :, pl.ds(0, 128)].astype(f32)
            error_ref[:, pl.ds(0, channels)] = target_ref[band]
            error = (c_skip * noisy + net - error_ref[...]) * keep(band)
            high = error.astype(bf16)
            low = (error - high.astype(f32)).astype(bf16)
            turned = dot_tn(high, table_ref[0]) + dot_tn(low, table_ref[0]) + dot_tn(high, table_ref[1])
            gext_ref[pl.ds(band * sent, sent), pl.ds(0, lanes)] = turned[:sent]
            all_ref[node, band] = turned[:sent].astype(bf16)
            piece = all_ref.at[node, band]
            for i in range(1, place.uppers):
                uppers[i, band] = start_copy(started, place, piece, piece, f_sem.at[i, band], upper=i)
            cores[0, band] = start_copy(started, place, piece, piece, f_sem.at[0, band], core=1)
        gf_ref[...] = jnp.zeros_like(gf_ref)
        mom_step(2)

        def add_nodes(base, total, band):
            def add_lat(index, value):
                source = base + index // lats
                return value + kern_ref[band, pl.ds(source * lats + lax.rem(index, lats), 1)] * all_ref[
                    source, lax.rem(index, lats)
                ].astype(f32)

            return lax.fori_loop(0, 2 * lats, add_lat, total, unroll=8)

        for band in range(bands):
            cores[0, band].wait_recv()
        for band in range(bands):
            gext_ref[pl.ds((lats + band) * sent, sent), pl.ds(0, lanes)] = add_nodes(place.upper * 2, jnp.zeros((sent, lanes), f32), band)
            for i in range(1, place.uppers):
                uppers[i, band].wait_recv()
                source = lax.rem(place.upper + place.uppers - i, place.uppers) * 2 + place.core
                piece = all_ref.at[source, band]
                cores[i, band] = start_copy(started, place, piece, piece, pass_sem.at[i, band], core=1)
        for i in range(1, place.uppers):
            for band in range(bands):
                cores[i, band].wait_recv()
        loss_rows = jnp.zeros((8, 128), f32)
        for band in range(bands):
            total = gext_ref[pl.ds((lats + band) * sent, sent), pl.ds(0, lanes)]
            for i in range(1, place.uppers):
                total = add_nodes(lax.rem(place.upper + i, place.uppers) * 2, total, band)
            loss_rows = loss_rows + jnp.sum(total * gext_ref[pl.ds(band * sent, sent), pl.ds(0, lanes)])
            gf_ref[pl.ds(0, sent)] = total * (2.0 * weight)
            grad = gf_ref[...]
            high = grad.astype(bf16)
            low = (grad - high.astype(f32)).astype(bf16)
            back = dot_nt(table_ref[0], high) + dot_nt(table_ref[0], low) + dot_nt(table_ref[1], high)
            gnet_ref[band] = (back * keep(band) * c_output).astype(bf16)
        loss_share = loss_rows * weight

        sums_ref[...] = jnp.zeros_like(sums_ref)
        grad_node = dot_tn(gnet_ref[0], dec_ref[0])
        for band in range(1, bands):
            grad_node += dot_tn(gnet_ref[band], dec_ref[band])
        gnode_ref[...] = jnp.transpose(grad_node * third)

        def back_feed(spot):
            grad_node = gnode_ref[spot]
            high = grad_node.astype(bf16)
            low = (grad_node - high.astype(f32)).astype(bf16)
            node_ref[spot, pl.ds(0, 128)] = high
            dec_rows = dec_rows_ref[...]
            grad_out = dot_nn(high, dec_rows) + dot_nn(low, dec_rows)
            branch = grad_out.astype(bf16)
            gb_ref[spot] = branch
            grad_second = jnp.zeros((big, width), f32)
            for low in range(0, hidden, chunk):
                grad_activ = dot_nt(branch, mlp_part(hidden + low))
                grad_upper = (grad_activ * slope_ref[low // chunk, spot].astype(f32)).astype(bf16)
                slope_ref[low // chunk, spot] = grad_upper
                grad_second += dot_nn(grad_upper, mlp_part(low))
            unit, inverse = norm_parts(h1_ref[spot])
            scaled = grad_second * (1.0 + mod[2])
            grad_mid = grad_out + inverse * (
                scaled
                - jnp.mean(scaled, axis=-1, keepdims=True)
                - unit * jnp.mean(scaled * unit, axis=-1, keepdims=True)
            )
            sums_ref[2:3] += jnp.sum(grad_second * unit, axis=0, keepdims=True)
            sums_ref[3:4] += jnp.sum(grad_second, axis=0, keepdims=True)
            h1_ref[spot] = grad_mid
            grad_attn = grad_mid.astype(bf16)
            gattn_ref[spot] = grad_attn
            grad_blend = dot_nn(grad_attn, attn_part(3 * width, width))
            for head in range(HEAD_COUNT):
                part = slice(head * head_width, (head + 1) * head_width)
                scaled_blend = grad_blend[:, part] * scale_ref[spot, pl.ds(head, 1)]
                gblend_ref[spot, pl.ds(head * head_width, head_width)] = scaled_blend.astype(bf16)

        mom_step(3)
        row_loop(big, back_feed, [lambda: mom_step(4)])
        for k in range(5, place.fars + 2):
            mom_step(k)

        def outer_loop(target, block, offset, left, right, columns):
            @pl.loop(0, columns // big)
            def _(index):
                part = pl.multiple_of(index * big, big)
                product = dot_tn(left[:, pl.ds(part, big)], right[...]).astype(bf16)
                target[pl.ds((offset + part) // block, big // block)] = product.reshape(
                    big // block, block, width
                )

        for low in range(0, hidden, chunk):
            outer_loop(mlp_ref, mlp_rows, hidden + low, activ_ref.at[low // chunk], gb_ref, chunk)
            outer_loop(mlp_ref, mlp_rows, low, slope_ref.at[low // chunk], second_ref, chunk)
        scatter = Scatter(place, mlp_pieces, (mlp_ref,), bufs, sems_c)
        scatter.begin([0])

        gext_ref[...] = jnp.zeros_like(gext_ref)

        def back_attend(spot):
            for head in range(HEAD_COUNT):
                part = pl.ds(head * head_width, head_width)
                values = pl.ds(width + head * head_width, head_width)
                raised = prob_ref[head, spot]
                inverse = scale_ref[spot, pl.ds(head, 1)]
                grad_blend = gblend_ref[spot, part]
                grad_prob = dot_nt(grad_blend, ext_ref[:, values])
                prob = raised.astype(f32)
                mean = jnp.sum(prob * grad_prob, axis=-1, keepdims=True) * inverse
                grad_logit = (prob * (grad_prob - mean)).astype(bf16)
                gext_ref[:, part] += dot_tn(grad_logit, q_ref[spot, part])
                q_ref[spot, part] = (dot_nn(grad_logit, ext_ref[:, part]) * score_scale).astype(bf16)
                gext_ref[:, values] += dot_tn(raised, grad_blend)

        row_loop(tile, back_attend, [lambda: scatter.step(0), lambda: scatter.step(1)])
        key_scale = jnp.where(iota((1, 2 * width), 1) < width, score_scale, 1.0)
        lost_ref[0] = (gext_ref[pl.ds(rows, halo)] * key_scale).astype(bf16)
        lost_ref[1] = (gext_ref[pl.ds(rows + halo, halo)] * key_scale).astype(bf16)
        from_upper = to_node(nodes - 1, lost_ref.at[0], back_ref.at[0], back_sem.at[0])
        from_lower = to_node(1, lost_ref.at[1], back_ref.at[1], back_sem.at[1])
        scatter.step(2)
        outer_loop(attn_ref, attn_rows, 3 * width, gattn_ref, blend_ref, width)
        scatter.step(3)
        from_upper.wait_recv()
        from_lower.wait_recv()

        def back_encode(spot):
            grad_pairs = gext_ref[spot] * key_scale + dot_nn(lendt_ref[spot], back_ref[0]) + dot_nn(
                lendt_ref[spot], back_ref[1]
            )
            grad_pairs = grad_pairs.astype(bf16)
            ext_ref[spot] = grad_pairs
            grad_first = dot_nn(q_ref[spot], attn_part(0, width)) + dot_nn(
                grad_pairs, attn_part(width, 2 * width)
            )
            unit, inverse = norm_parts(h0_ref[spot])
            scaled = grad_first * (1.0 + mod[0])
            grad_in = h1_ref[spot] + inverse * (
                scaled
                - jnp.mean(scaled, axis=-1, keepdims=True)
                - unit * jnp.mean(scaled * unit, axis=-1, keepdims=True)
            )
            sums_ref[0:1] += jnp.sum(grad_first * unit, axis=0, keepdims=True)
            sums_ref[1:2] += jnp.sum(grad_first, axis=0, keepdims=True)
            gb_ref[spot] = grad_in.astype(bf16)

        row_loop(big, back_encode)
        scatter.step(4)
        outer_loop(attn_ref, attn_rows, 0, q_ref, first_ref, width)
        outer_loop(attn_ref, attn_rows, width, ext_ref.at[pl.ds(0, rows)], first_ref, 2 * width)
        last = Scatter(
            place, last_pieces, (attn_ref, high_out, low_out), strips((activ_ref, slope_ref), last_shapes), sems_d
        )
        last.begin([0])

        @pl.loop(0, all_small // 128)
        def _(index):
            low_row = pl.multiple_of(index * 128, 128)
            part = feats_ref[pl.ds(low_row, 128)]
            total = part[:, 0:1] * sums_ref[0:1]
            for j in range(1, 4):
                total += part[:, j : j + 1] * sums_ref[j : j + 1]
            gext_ref[pl.ds(low_row, 128), pl.ds(0, width)] = total

        for low_row in range(0, wide, 128):
            gext_ref[pl.ds(low_row, 128), pl.ds(0, width)] += dot_tn(
                mixed_ref[0, :, pl.ds(low_row, 128)], gb_ref[...]
            )
        gext_ref[pl.ds(start, 128), pl.ds(0, width)] += pltpu.roll(
            dot_tn(node_ref[:, pl.ds(0, 128)], out_ref[...]), shift, 0
        )

        @pl.loop(0, all_small // 128)
        def _(index):
            total = gext_ref[pl.ds(pl.multiple_of(index * 128, 128), 128), pl.ds(0, width)]
            high = total.astype(bf16)
            blocks = pl.ds(index * (128 // small_rows), 128 // small_rows)
            shape = (128 // small_rows, small_rows, width)
            high_out[blocks] = high.reshape(shape)
            low_out[blocks] = (total - high.astype(f32)).astype(bf16).reshape(shape)

        last.begin([1, 2])
        for k in range(5, scatter.steps()):
            scatter.step(k)
        last.step(0)
        scatter.finish(mlp_sum)
        g_mlp_shard[...] = mlp_sum[...].astype(bf16)
        gather_g_mlp = HalfGather(place, g_mlp_shard, g_mlp_all, sems_h)
        gather_g_mlp.begin()
        gather_g_mlp.step(0)
        for k in range(1, last.steps()):
            last.step(k)
            gather_g_mlp.step(k)
        last.finish(own)
        g_attn, g_mlp = own[pl.ds(0, attn_rows)], mlp_sum[...]
        g_small = own[pl.ds(attn_rows, small_rows)] + own[pl.ds(attn_rows + small_rows, small_rows)]
        attn_sum[...] = g_attn
        small_sum[...] = g_small
        g_attn_shard[...] = g_attn.astype(bf16)
        squares = jnp.sum(g_attn * g_attn) + jnp.sum(g_mlp * g_mlp) + jnp.sum(g_small * g_small)
        tile_shard[...] = jnp.where(iota((8, 128), 0) < 4, squares, loss_share)
        gather_g_attn = Gather(
            place, tile_pieces, (g_attn_shard, tile_shard), (g_attn_all, tiles_out), sems_g
        )
        gather_g_attn.begin()
        for k in range(place.fars + 2):
            gather_g_attn.step(k)
        for item in (*gather_moms, gather_g_mlp, gather_g_attn):
            item.end()
        scatter.end()
        last.end()
        for copy in started:
            copy.wait_send()

    vmem = pl.BlockSpec(memory_space=pltpu.VMEM)
    dma = pltpu.SemaphoreType.DMA
    struct = jax.ShapeDtypeStruct
    low = lambda *shape: pltpu.VMEM(shape, bf16)
    full = lambda *shape: pltpu.VMEM(shape, f32)
    return pl.pallas_call(
        kernel,
        out_shape=(
            struct((attn_rows, width), f32),
            struct((mlp_rows, width), f32),
            struct((small_rows, width), f32),
            struct((devices, 8, 128), f32),
        )
        + tuple(struct((devices, size, width), bf16) for size in (attn_rows, mlp_rows) * 2),
        in_specs=[vmem] * 15,
        out_specs=(vmem,) * 3 + (pl.BlockSpec(memory_space=pl.ANY),) * 5,
        scratch_shapes=[
            low(devices, small_rows, width),
            low(devices, small_rows, width),
            full(attn_rows + 2 * small_rows, width),
            low(attn_rows, width),
            low(mlp_rows, width),
            low(attn_rows, width),
            low(mlp_rows, width),
            full(8, 128),
            low(attn_rows, width),
            low(mlp_rows, width),
            low(small_rows, width),
            full(nodes, lats, lows, lanes),
            full(place.nears, lats, all_lats, lanes),
            full(place.fars, lats, all_lats, lanes),
            full(lats, all_lats, lanes),
            low(devices, attn_rows, width),
            low(devices, mlp_rows, width),
            low(devices, small_rows, width),
            full(rows, ext_rows),
            low(bands, lons, rows),
            low(2, rows, wide),
            low(rows, halo),
            full(rows, width),
            full(rows, width),
            low(rows, width),
            low(rows, width),
            low(ext_rows, 2 * width),
            low(halo, 2 * width),
            low(HEAD_COUNT, rows, ext_rows),
            low(rows, width),
            low(rows, width),
            low(hidden // chunk, rows, chunk),
            low(hidden // chunk, rows, chunk),
            low(rows, width),
            low(rows, 256),
            low(nodes, lats, sent, lanes),
            full(128, lanes),
            low(bands, lons, 128),
            full(rows, 128),
            low(rows, width),
            low(rows, width),
            low(rows, width),
            full(ext_rows, 2 * width),
            low(2, halo, 2 * width),
            low(2, halo, 2 * width),
            full(8, width),
            full(rows, 128),
            full(lons, 128),
            pltpu.VMEM((8, flat_pixels), jnp.int32),
            pltpu.VMEM((flat_pixels, 128), jnp.int32),
            low(bands, lons, cin),
            low(128, width),
            full(all_small, 128),
            dma((nodes, 2)),
            dma((place.nears, 2)),
            dma((place.fars, 2)),
            dma((2, 2)),
            dma((place.uppers, lats, 2)),
            dma((place.uppers, lats, 2)),
            dma((2, 2)),
        ]
        + [item for group in groups for item in group],
        compiler_params=pltpu.CompilerParams(
            collective_id=collective, has_side_effects=True, vmem_limit_bytes=62 << 20
        ),
    )(*weights, grid, target, land, near_turned, enc_turned, dec_turned, lent, legendre, vector, tables, *moments)


def turn_tables(lon_count, modes):
    turns = np.arange(lon_count)[:, None] * np.arange(modes)[None, :] % lon_count
    phases = turns * (2.0 * np.pi / lon_count)
    waves = [m for m in range(modes) if (2 * m) % lon_count]
    picks = list(range(modes)) + waves
    lanes = -(-len(picks) // 128) * 128
    table = np.zeros((lon_count, lanes), np.float32)
    table[:, :modes] = np.cos(phases)
    table[:, modes : len(picks)] = -np.sin(phases[:, waves])
    high = table.astype(ml_dtypes.bfloat16)
    low = (table - high.astype(np.float32)).astype(ml_dtypes.bfloat16)
    return np.stack([high, low]), (waves[0], waves[-1] + 1, lanes - len(picks))


def to_sixteens(blocks):
    return jnp.pad(blocks, ((0, 0), (0, sixteens(blocks.shape[1]) - blocks.shape[1]), (0, 0)))


def on_device(
    grid_in,
    target,
    noise_level,
    land_mask,
    neighbours,
    halo_send,
    g2m,
    m2g,
    legendre,
    w_attn,
    w_mlp,
    w_small,
    mom_attn,
    mom_mlp,
    m_small,
    v_small,
    ema_attn,
    ema_mlp,
    ema_small,
):
    cin = grid_in.shape[-1]
    lat_rows, lon_count, channels = target.shape[1:]
    modes, degrees = legendre.shape[1:]
    halo_rows = halo_send.shape[0]
    width = w_attn.shape[1]
    nodes, zeros = lax.axis_size("node"), lax.axis_size("zero")
    devices = nodes * zeros
    attn_rows, mlp_rows, small_rows = w_attn.shape[0], w_mlp.shape[0], w_small.shape[0]

    sigma, c_input, c_skip, c_output, loss_weight = noise_scalars(noise_level[0])
    features = noise_features(sigma).astype(bf16).astype(f32)
    weight = loss_weight / (2 * modes * degrees * channels)
    tables, (wave_first, wave_end, wave_pad) = turn_tables(lon_count, modes)
    lows = -(-degrees // (8 * zeros)) * 8
    leg = jnp.pad(legendre, ((0, 0), (0, 0), (0, lows * zeros - degrees)))
    leg = lax.dynamic_slice_in_dim(leg, lax.axis_index("zero") * lows, lows, axis=2)
    leg = jnp.transpose(leg, (0, 2, 1))
    leg = jnp.concatenate(
        [leg, leg[:, :, wave_first:wave_end], jnp.zeros(leg.shape[:2] + (wave_pad,), f32)], axis=2
    )
    whole_tiles = all(size % 16 == 0 and 256 % size == 0 for size in (attn_rows, mlp_rows, small_rows))
    if whole_tiles:
        lane = jnp.arange(128)
        vector = jnp.where(lane < NOISE_FEATS, jnp.pad(features, (0, 128 - NOISE_FEATS)), 0.0)
        for spot, value in (
            (c_input_lane, c_input),
            (c_skip_lane, c_skip),
            (c_output_lane, c_output),
            (weight_lane, weight),
        ):
            vector = jnp.where(lane == spot, value, vector)
        attn_sum, mlp_sum, g_small, totals, mom_attn_all, mom_mlp_all, g_attn_all, g_mlp_all = train_step(
            nodes,
            zeros,
            (w_attn, w_mlp, w_small),
            grid_in[0],
            target[0],
            land_mask,
            neighbours.T,
            g2m.T,
            m2g.T,
            halo_send[None],
            leg,
            vector[None],
            jnp.asarray(tables),
            (mom_attn, mom_mlp),
            cin,
            1,
        )
        sums = (g_small, attn_sum, mlp_sum)
        attn_sets = [item.reshape(-1, width) for item in (mom_attn_all, g_attn_all)]
        mlp_sets = [item.reshape(-1, width) for item in (mom_mlp_all, g_mlp_all)]
        moments = (mom_attn, mom_mlp)
    else:
        scale_input = jnp.where(jnp.arange(cin) < channels, c_input, 1.0)[None]
        cond_rows = jnp.where(
            jnp.arange(128)[None, None] == jnp.arange(4)[:, None, None], features[None, :, None], 0.0
        ).reshape(-1, 128)
        feats = jnp.pad(cond_rows, ((cin + channels, 0), (0, 0)))
        shift = cin % 128
        sides = ((0, 0), (0, 0), (shift, 128 - shift - channels))
        keep_mask = 1.0 - land_mask.astype(f32)[:, :, None] * (
            jnp.arange(channels) == channels - 1
        ).astype(f32)
        base = jnp.pad(c_skip * grid_in[0, :, :, :channels].astype(f32) - target[0], sides)
        keep = jnp.pad(keep_mask, sides)
        m2g_bands = m2g.reshape(lat_rows, lon_count, -1)

        attn, mlp, small, near, dec, dec_turned, mixed, lend, lendt, kern = gather_and_count(
            nodes,
            zeros,
            (w_attn, w_mlp, w_small),
            grid_in[0].reshape(-1, cin),
            scale_input,
            g2m,
            m2g_bands,
            jnp.transpose(m2g_bands, (0, 2, 1)),
            neighbours,
            halo_send[:, None],
            jnp.concatenate([halo_send, halo_send])[None],
            leg,
            1,
        )
        full = [
            item[:, :size].reshape(-1, width)
            for item, size in ((attn, attn_rows), (mlp, mlp_rows), (small, small_rows))
        ]
        *local, loss_tile = model_step(
            nodes,
            zeros,
            full,
            (near, dec, dec_turned, mixed, lend, lendt),
            kern,
            feats,
            base,
            keep,
            jnp.asarray(tables),
            jnp.stack([c_output, weight]),
            cin,
            channels,
            m2g.shape[1],
            2,
        )
        names = ["attn", "mlp", "high", "low"]
        mlp_sum = None

        g_small, moment_attn, moment_mlp, totals, attn_all, mlp_all = reduce_and_gather(
            nodes,
            zeros,
            names,
            [to_sixteens(item.reshape(devices, -1, width)) for item in local],
            mlp_sum,
            loss_tile,
            mom_attn,
            mom_mlp,
            small_rows,
            3,
        )
        sums = (g_small,)
        attn_sets = [attn_all[:, :attn_rows].reshape(-1, width)]
        mlp_sets = [mlp_all[:, :mlp_rows].reshape(-1, width)]
        totals = totals[None]
        moments = (moment_attn, moment_mlp)

    *results, moment_attn, moment_mlp = update_weights(
        nodes,
        zeros,
        attn_sets,
        mlp_sets,
        totals,
        sums,
        moments,
        (w_attn, w_mlp, w_small),
        (ema_attn, ema_mlp, ema_small),
        (m_small, v_small),
    )
    loss, clip_norm, new_attn, new_mlp, new_small, new_m, new_v, *new_averages = results
    return (
        loss[0, 0], clip_norm[0, 0], new_attn, new_mlp, new_small, moment_attn, moment_mlp, new_m, new_v, *new_averages
    )


def solution(mesh):
    split_rows = P(("node", "zero"), None)
    return jax.shard_map(
        on_device,
        mesh=mesh,
        in_specs=(
            P("zero", "node", None, None),
            P("zero", "node", None, None),
            P("zero"),
            P("node", None),
            P("node", None),
            P("node"),
            P("node", None),
            P("node", None),
            P("node", None, None),
        )
        + (split_rows,) * 10,
        out_specs=(P(), P()) + (split_rows,) * 10,
        check_vma=False,
    )
```

```python
import math

import jax
import jax.numpy as jnp
import ml_dtypes
import numpy as np
from jax import lax
from jax.experimental import pallas as pl
from jax.experimental.pallas import tpu as pltpu
from jax.sharding import PartitionSpec as P

HEAD_COUNT = 4
NOISE_FEATS = 42
LEVELS = 16
NS_ITERS = 3
STEP = 10

top_precision = lax.Precision.HIGHEST
mid_precision = lax.Precision.HIGH
norm_epsilon = 1e-05
trace_epsilon = 1e-12
clip_limit = 1.0
moment_decay = 0.95
orthogonal_rate = 0.1
adam_first = 0.9
adam_second = 0.95
adam_rate = 0.02
adam_epsilon = 1e-08
average_decay = 0.9
newton_first = 3.4445
newton_second = -4.775
newton_third = 2.0315
sigma_lowest = 0.1
sigma_highest = 20.0
c_input_lane = 64
c_skip_lane = 65
c_output_lane = 66
weight_lane = 67
log2_e = math.log2(math.e)
absent = -1e30
gelu_scale = math.sqrt(2.0 / math.pi)
gelu_cubic = 0.044715
f32 = jnp.float32
bf16 = jnp.bfloat16


def noise_scalars(level):
    sigma = sigma_lowest * (sigma_highest / sigma_lowest) ** (level.astype(f32) / (LEVELS - 1))
    total = sigma * sigma + 1.0
    return (sigma, lax.rsqrt(total), 1.0 / total, sigma * lax.rsqrt(total), total / (sigma * sigma))


def noise_features(sigma):
    half_count = NOISE_FEATS // 2
    frequency = jnp.exp(jnp.arange(half_count).astype(f32) * (3.0 / half_count))
    phases = 0.25 * jnp.log(sigma) * frequency
    return jnp.concatenate([jnp.sin(phases), jnp.cos(phases)])


def dot(left, right, contract):
    return lax.dot_general(left, right, (contract, ((), ())), preferred_element_type=f32)


def dot_nn(left, right):
    return dot(left, right, ((1,), (0,)))


def dot_nt(left, right):
    return dot(left, right, ((1,), (1,)))


def dot_tn(left, right):
    return dot(left, right, ((0,), (0,)))


MESH = pl.DeviceIdType.MESH
ROW_CHUNK = 16


class Place:
    def __init__(self, nodes, zeros):
        self.uppers, self.cores = nodes // 2, 2
        self.nears = 2 if zeros < 16 else 4
        self.fars = zeros // self.nears
        self.mates = max(self.uppers // 2, 1)
        self.zeros = zeros

    def locate(self):
        node, zero = lax.axis_index("node"), lax.axis_index("zero")
        self.upper, self.core = node // 2, node % 2
        self.far, self.near = zero // self.nears, zero % self.nears

    def moved(self, upper=0, core=0, far=0, near=0, mate=0):
        row = lax.rem(self.upper + upper, self.uppers) if upper else self.upper
        if mate:
            group = self.upper // self.mates * self.mates
            row = group + lax.rem(self.upper - group + mate, self.mates)
        return (
            row,
            1 - self.core if core else self.core,
            lax.rem(self.far + far, self.fars) if far else self.far,
            lax.rem(self.near + near, self.nears) if near else self.near,
        )

    def device(self, **steps):
        upper, core, far, near = self.moved(**steps)
        return (upper * 2 + core, far * self.nears + near)

    def slot(self, upper, core, far, near):
        return (upper * 2 + core) * self.zeros + far * self.nears + near

    def peers(self):
        return (
            [dict(far=k) for k in range(1, self.fars)]
            + [dict(near=j) for j in range(1, self.nears)]
            + [dict(upper=i) for i in range(1, self.uppers)]
            + [dict(core=1)]
        )

    def greet(self, nodes=0):
        barrier = pltpu.get_barrier_semaphore()
        peers = [self.device(**steps) for steps in self.peers() if not nodes or set(steps) <= {"far", "near"}]
        if nodes:
            node, zero = lax.axis_index("node"), lax.axis_index("zero")
            peers += [(lax.rem(node + step, nodes), zero) for step in range(1, nodes)]
        for device in peers:
            pl.semaphore_signal(barrier, 1, device_id=device, device_id_type=MESH)
        pl.semaphore_wait(barrier, len(peers))


def half_rows(rows):
    return (rows // 2 + 15) // 16 * 16


class Pool:
    def __init__(self, ref):
        self.ref, self.used, self.at = ref, 0, self

    def __getitem__(self, index):
        return self

    def take(self):
        pair = self.ref.at[pl.ds(self.used, 2)]
        self.used += 2
        return pair

    def gather(self, own, index):
        return [own.at[pl.ds(index, 2)]] + [self] * 6

    def half(self, own, index):
        return [own.at[index]] + [self] * 4


def start_copy(started, place, source, target, sems, **steps):
    if isinstance(sems, Pool):
        sems = sems.take()
    copy = pltpu.make_async_remote_copy(
        src_ref=source,
        dst_ref=target,
        send_sem=sems.at[0],
        recv_sem=sems.at[1],
        device_id=place.device(**steps),
        device_id_type=MESH,
    )
    copy.start()
    started.append(copy)
    return copy


def sixteens(rows):
    return -(-rows // 16) * 16


class Pieces:
    def __init__(self, sizes, first, share=1 / 2):
        self.sizes = sizes
        cut = min(sixteens(int(sum(sizes) * share)), sizes[first])
        self.whole = [(i, 0, size) for i, size in enumerate(sizes)]
        self.head = [(first, 0, cut)]
        self.tail = [(first, cut, sizes[first] - cut)] if cut < sizes[first] else []
        self.tail += [(i, 0, size) for i, size in enumerate(sizes) if i != first]


def send_pieces(started, place, pieces, sources, targets, sems, **steps):
    copies = []
    for index, (array, start, rows) in enumerate(pieces):
        part = pl.ds(start, rows)
        copies.append(
            start_copy(
                started, place, sources[array].at[part], targets[array].at[part], sems.at[index], **steps
            )
        )
    return copies


def wait_all(copies):
    for copy in copies:
        copy.wait_recv()


class Gather:
    def __init__(self, place, pieces, shards, outs, sems):
        self.place, self.pieces, self.shards, self.outs = place, pieces, shards, outs
        (self.own_sem, self.far_sem, self.near_sem, self.upper_sem, self.over_sem, self.under_sem, self.core_sem) = sems
        self.started, self.cores = [], []
        self.far, self.near, self.upper, self.over, self.under = {}, {}, {}, {}, {}

    def block(self, **steps):
        slot = self.place.slot(*self.place.moved(**steps))
        return [out.at[slot] for out in self.outs]

    def send(self, pieces, source, target, sems, **steps):
        return send_pieces(self.started, self.place, pieces, source, target, sems, **steps)

    def begin(self):
        here = self.block()
        self.kept = []
        for index, (shard, target) in enumerate(zip(self.shards, here)):
            mine = target.at[pl.ds(0, shard.shape[0])]
            copy = pltpu.make_async_copy(shard, mine, self.own_sem.at[index])
            copy.start()
            self.kept.append(copy)
        for k in range(1, self.place.fars):
            self.far[k] = self.send(self.pieces.whole, self.shards, here, self.far_sem.at[k], far=k)

    def first(self, k):
        place, whole = self.place, self.pieces.whole
        if k:
            wait_all(self.far[k])
        target = self.block(far=(place.fars - k) % place.fars)
        source = target if k else self.shards
        for j in range(1, place.nears):
            self.near[k, j] = self.send(whole, source, target, self.near_sem.at[k, j], near=j)
        for i in range(1, place.uppers):
            self.upper[k, i] = self.send(whole, source, target, self.upper_sem.at[k, i], upper=i)
        self.cores += self.send(whole, source, target, self.core_sem.at[k, 0, 0], core=1)

    def second(self, k):
        place, whole = self.place, self.pieces.whole
        far = (place.fars - k) % place.fars
        for j in range(1, place.nears):
            wait_all(self.near[k, j])
            item = self.block(far=far, near=place.nears - j)
            for i in range(1, place.uppers):
                self.over[k, j, i] = self.send(
                    self.pieces.head, item, item, self.over_sem.at[k, j, i], upper=i
                )
            self.cores += self.send(whole, item, item, self.core_sem.at[k, j, 0], core=1)
        for i in range(1, place.uppers):
            wait_all(self.upper[k, i])
            item = self.block(far=far, upper=place.uppers - i)
            for j in range(1, place.nears):
                self.under[k, j, i] = self.send(
                    self.pieces.tail, item, item, self.under_sem.at[k, j, i], near=j
                )
            self.cores += self.send(whole, item, item, self.core_sem.at[k, 0, i], core=1)

    def third(self, k):
        place, whole = self.place, self.pieces.whole
        far = (place.fars - k) % place.fars
        for j in range(1, place.nears):
            for i in range(1, place.uppers):
                wait_all(self.over[k, j, i])
                wait_all(self.under[k, j, i])
                item = self.block(far=far, near=place.nears - j, upper=place.uppers - i)
                self.cores += self.send(whole, item, item, self.core_sem.at[k, j, i], core=1)

    def step(self, k):
        fars = self.place.fars
        if k < fars:
            self.first(k)
        if 1 <= k <= fars:
            self.second(k - 1)
        if k >= 2:
            self.third(k - 2)

    def end(self):
        for copy in self.kept:
            copy.wait()
        wait_all(self.cores)
        for copy in self.started:
            copy.wait_send()

    @staticmethod
    def copies(place, pieces):
        fars, nears, uppers = place.fars, place.nears, place.uppers
        whole, parts = len(pieces.whole), len(pieces.head) + len(pieces.tail)
        direct = (fars - 1) + fars * (nears - 1) + fars * (uppers - 1) + fars * nears * uppers
        return whole * direct + parts * fars * (nears - 1) * (uppers - 1)

    @staticmethod
    def sems(place, pieces):
        dma = pltpu.SemaphoreType.DMA
        fars, nears, uppers = place.fars, place.nears, place.uppers
        whole, head, tail = len(pieces.whole), len(pieces.head), len(pieces.tail)
        return [
            dma((whole,)),
            dma((fars, whole, 2)),
            dma((fars, nears, whole, 2)),
            dma((fars, uppers, whole, 2)),
            dma((fars, nears, uppers, head, 2)),
            dma((fars, nears, uppers, tail, 2)),
            dma((fars, nears, uppers, whole, 2)),
        ]


def iota(shape, axis):
    return lax.broadcasted_iota(jnp.int32, shape, axis)


def gather_and_count(nodes, zeros, weights, grid, scale, g2m, m2g, m2g_turned, neighbours, lent, lent_row, legendre, collective):
    place = Place(nodes, zeros)
    width = weights[0].shape[1]
    sizes = [sixteens(w.shape[0]) for w in weights]
    pieces = Pieces(sizes, 1)
    devices = nodes * zeros
    pixels, cin = grid.shape
    wide = -(-cin // 128) * 128
    rows, fanout = neighbours.shape
    halo = lent.shape[0]
    ext = rows + 2 * halo
    bands, lons, dec_edges = m2g.shape
    lats, lows, lanes = legendre.shape
    enc_edges = g2m.shape[1]
    tile = 128

    def kernel(
        attn_ref, mlp_ref, small_ref, grid_ref, scale_ref, g2m_ref, m2g_ref, turned_ref, near_ref, lent_ref,
        row_ref, leg_ref,
        attn_out, mlp_out, small_out, near_out, dec_out, turned_out, mixed_out, lend_out, lendt_out, kern_out,
        attn_shard, mlp_shard, small_shard, inputs, legs, parts, sums, leg_sem, part_sem, sum_sem, *sems,
    ):
        place.locate()
        node = lax.axis_index("node")
        shards = (attn_shard, mlp_shard, small_shard)
        for ref, shard, size in zip((attn_ref, mlp_ref, small_ref), shards, sizes):
            if ref.shape[0] < size:
                shard[...] = jnp.zeros_like(shard)
            shard[pl.ds(0, ref.shape[0])] = ref[...].astype(bf16)
        legs[node] = leg_ref[...]
        place.greet(nodes)
        gather = Gather(place, pieces, shards, (attn_out, mlp_out, small_out), sems)
        gather.begin()
        started = []
        leg_copies = []
        for step in range(1, nodes):
            target = (lax.rem(node + step, nodes), lax.axis_index("zero"))
            copy = pltpu.make_async_remote_copy(
                src_ref=leg_ref,
                dst_ref=legs.at[node],
                send_sem=leg_sem.at[step, 0],
                recv_sem=leg_sem.at[step, 1],
                device_id=target,
                device_id_type=MESH,
            )
            copy.start()
            leg_copies.append(copy)

        def count_near():
            @pl.loop(0, rows // tile)
            def _(index):
                spot = pl.ds(pl.multiple_of(index * tile, tile), tile)
                lists = near_ref[spot]
                place_of = iota((tile, ext), 1)
                total = jnp.zeros((tile, ext), f32)
                for j in range(fanout):
                    total += jnp.where(lists[:, j : j + 1] == place_of, 1.0, 0.0)
                near_out[spot] = total.astype(bf16)

        def count_dec():
            @pl.loop(0, bands)
            def _(band):
                lists = m2g_ref[band]
                place_of = iota((lons, rows), 1)
                total = jnp.zeros((lons, rows), f32)
                for j in range(dec_edges):
                    total += jnp.where(lists[:, j : j + 1] == place_of, 1.0, 0.0)
                dec_out[band] = total.astype(bf16)
                lists = turned_ref[band]
                place_of = iota((rows, lons), 0)
                total = jnp.zeros((rows, lons), f32)
                for j in range(dec_edges):
                    total += jnp.where(lists[j : j + 1] == place_of, 1.0, 0.0)
                turned_out[band] = total.astype(bf16)

        def mix():
            inputs[...] = (grid_ref[...].astype(f32) * scale_ref[...]).astype(bf16)
            mixed_out[...] = jnp.zeros_like(mixed_out)

            @pl.loop(0, rows // tile)
            def _(index):
                spot = pl.ds(pl.multiple_of(index * tile, tile), tile)
                lists = g2m_ref[spot]
                place_of = iota((tile, pixels), 1)
                total = jnp.zeros((tile, pixels), f32)
                for j in range(enc_edges):
                    total += jnp.where(lists[:, j : j + 1] == place_of, 1.0 / enc_edges, 0.0)
                mean = dot_nn(total.astype(bf16), inputs[...])
                high = mean.astype(bf16)
                mixed_out[0, spot, pl.ds(0, cin)] = high
                mixed_out[1, spot, pl.ds(0, cin)] = (mean - high.astype(f32)).astype(bf16)

        def lend():
            lend_out[...] = jnp.where(lent_ref[...] == iota((halo, rows), 1), 1.0, 0.0).astype(bf16)
            lendt_out[...] = jnp.where(row_ref[...] == iota((rows, 2 * halo), 0), 1.0, 0.0).astype(bf16)

        def gram():
            for copy in leg_copies:
                copy.wait()

            @pl.loop(0, nodes * lats)
            def _(index):
                other = legs[index // lats, lax.rem(index, lats)]
                for t in range(lats):
                    product = leg_ref[t] * other
                    parts[place.near, t, pl.ds(index, 1)] = jnp.sum(product, axis=0, keepdims=True)

            for j in range(1, place.nears):
                near_parts.append(
                    start_copy(
                        started, place, parts.at[place.near], parts.at[place.near], part_sem.at[j], near=j
                    )
                )

        near_parts, far_sums = [], []

        def gram_near():
            wait_all(near_parts)
            total = parts[0]
            for j in range(1, place.nears):
                total = total + parts[j]
            sums[place.far] = total
            for k in range(1, place.fars):
                far_sums.append(
                    start_copy(
                        started, place, sums.at[place.far], sums.at[place.far], sum_sem.at[k], far=k
                    )
                )

        def gram_far():
            wait_all(far_sums)
            total = sums[0]
            for k in range(1, place.fars):
                total = total + sums[k]
            kern_out[...] = total

        work = [lend, mix, gram, count_dec, gram_near, count_near, gram_far]
        steps = place.fars + 2
        for k in range(steps):
            gather.step(k)
            share = -(-len(work) // (steps - k))
            for part in work[:share]:
                part()
            work = work[share:]
        gather.end()
        for copy in started:
            copy.wait_send()

    vmem = pl.BlockSpec(memory_space=pltpu.VMEM)
    hbm = pl.BlockSpec(memory_space=pl.ANY)
    dma = pltpu.SemaphoreType.DMA
    struct = jax.ShapeDtypeStruct
    return pl.pallas_call(
        kernel,
        out_shape=tuple(struct((devices, size, width), bf16) for size in sizes)
        + (
            struct((rows, ext), bf16),
            struct((bands, lons, rows), bf16),
            struct((bands, rows, lons), bf16),
            struct((2, rows, wide), bf16),
            struct((halo, rows), bf16),
            struct((rows, 2 * halo), bf16),
            struct((lats, nodes * lats, lanes), f32),
        ),
        in_specs=[vmem] * 12,
        out_specs=(hbm,) * 3 + (vmem,) * 7,
        scratch_shapes=[pltpu.VMEM((size, width), bf16) for size in sizes]
        + [
            pltpu.VMEM((pixels, cin), bf16),
            pltpu.VMEM((nodes, lats, lows, lanes), f32),
            pltpu.VMEM((place.nears, lats, nodes * lats, lanes), f32),
            pltpu.VMEM((place.fars, lats, nodes * lats, lanes), f32),
            dma((nodes, 2)),
            dma((place.nears, 2)),
            dma((place.fars, 2)),
        ]
        + Gather.sems(place, pieces),
        compiler_params=pltpu.CompilerParams(
            collective_id=collective, has_side_effects=True, vmem_limit_bytes=56 << 20
        ),
    )(*weights, grid, scale, g2m, m2g, m2g_turned, neighbours, lent, lent_row, legendre)


def norm_parts(rows):
    centred = rows - jnp.mean(rows, axis=-1, keepdims=True)
    inverse = lax.rsqrt(jnp.mean(centred * centred, axis=-1, keepdims=True) + norm_epsilon)
    return centred * inverse, inverse


def model_step(
    nodes, zeros, weights, graph, kern, feats, base, keep, tables, scalars, first_channel, channels, dec_edges, collective
):
    place = Place(nodes, zeros)
    attn, mlp, small = weights
    near, dec, dec_turned, mixed, lend, lendt = graph
    width = attn.shape[1]
    hidden = mlp.shape[0] // 2
    rows, ext_rows = near.shape
    halo = lend.shape[0]
    bands, lons, _ = dec.shape
    wide = mixed.shape[2]
    lats, all_lats, lanes = kern.shape
    start = first_channel // 128 * 128
    shift = first_channel - start
    sent = sixteens(shift + channels)
    big, tile = 256, 128
    head_width = width // HEAD_COUNT
    score_scale = head_width ** (-0.5)
    third = 1.0 / dec_edges

    def kernel(
        attn_hbm, mlp_hbm, small_ref, near_hbm, dec_hbm, turned_hbm, mixed_ref, lend_ref, lendt_ref, kern_ref,
        feats_ref, base_ref, keep_ref, table_ref, scalar_ref,
        attn_out, mlp_out, high_out, low_out, loss_out,
        attn_ref, mlp_ref, near_ref, dec_ref, turned_ref, h0_ref, h1_ref, first_ref, q_ref, ext_ref, lent_ref,
        prob_ref, blend_ref, second_ref, activ_ref, slope_ref, out_ref, node_ref, f_ref, all_ref, gf_ref, gnet_ref,
        gb_ref, gattn_ref, gblend_ref, gext_ref, back_ref, lost_ref, sums_ref,
        load_sem, lend_sem, f_sem, pass_sem, back_sem,
    ):
        place.locate()
        node = lax.axis_index("node")
        zero = lax.axis_index("zero")
        loads = []
        for index, (source, target) in enumerate(
            (
                (attn_hbm, attn_ref),
                (near_hbm, near_ref),
                (mlp_hbm, mlp_ref),
                (dec_hbm, dec_ref),
                (turned_hbm, turned_ref),
            )
        ):
            copy = pltpu.make_async_copy(source, target, load_sem.at[index])
            copy.start()
            loads.append(copy)
        barrier = pltpu.get_barrier_semaphore()
        for step in range(1, nodes):
            pl.semaphore_signal(
                barrier, 1, device_id=(lax.rem(node + step, nodes), zero), device_id_type=MESH
            )
        started = []

        def to_node(step, source, target, sems):
            copy = pltpu.make_async_remote_copy(
                src_ref=source,
                dst_ref=target,
                send_sem=sems.at[0],
                recv_sem=sems.at[1],
                device_id=(lax.rem(node + step, nodes), zero),
                device_id_type=MESH,
            )
            copy.start()
            started.append(copy)
            return copy

        def row_loop(size, body):
            @pl.loop(0, rows // size)
            def _(index):
                body(pl.ds(pl.multiple_of(index * size, size), size))

        mods = dot_tn(feats_ref[...].astype(bf16), small_ref[...])
        mod = [mods[j : j + 1] for j in range(4)]
        enc = small_ref[pl.ds(0, wide)]
        loads[0].wait()

        def encode(spot):
            h0 = dot_nn(mixed_ref[0, spot], enc) + dot_nn(mixed_ref[1, spot], enc)
            h0_ref[spot] = h0
            unit, inverse = norm_parts(h0)
            first = (unit * (1.0 + mod[0]) + mod[1]).astype(bf16)
            first_ref[spot] = first
            ext_ref[spot] = dot_nt(first, attn_ref[pl.ds(width, 2 * width)]).astype(bf16)
            q_ref[spot] = dot_nt(first, attn_ref[pl.ds(0, width)]).astype(bf16)

        row_loop(big, encode)
        lent_ref[...] = dot_nn(lend_ref[...], ext_ref[pl.ds(0, rows)]).astype(bf16)
        pl.semaphore_wait(barrier, nodes - 1)
        up = to_node(1, lent_ref, ext_ref.at[pl.ds(rows, halo)], lend_sem.at[0])
        down = to_node(nodes - 1, lent_ref, ext_ref.at[pl.ds(rows + halo, halo)], lend_sem.at[1])
        loads[1].wait()
        up.wait_recv()
        down.wait_recv()

        def attend(spot):
            count = near_ref[spot].astype(f32)
            for head in range(HEAD_COUNT):
                part = pl.ds(head * head_width, head_width)
                values = pl.ds(width + head * head_width, head_width)
                logits = dot_nt(q_ref[spot, part], ext_ref[:, part]) * score_scale
                logits = jnp.where(count > 0.0, logits, -jnp.inf)
                raised = jnp.exp(logits - jnp.max(logits, axis=-1, keepdims=True))
                prob = raised * (1.0 / jnp.sum(raised * count, axis=-1, keepdims=True))
                prob = prob.astype(bf16)
                prob_ref[head, spot] = prob
                low = (prob.astype(f32) * count).astype(bf16)
                blend_ref[spot, part] = dot_nn(low, ext_ref[:, values]).astype(bf16)

        row_loop(tile, attend)
        loads[2].wait()
        dec_rows = small_ref[pl.ds(start, 128)]
        lane = iota((1, 128), 1)
        live = jnp.where((lane >= shift) & (lane < shift + channels), 1.0, 0.0)

        def feed(spot):
            h1 = h0_ref[spot] + dot_nt(blend_ref[spot], attn_ref[pl.ds(3 * width, width)])
            h1_ref[spot] = h1
            unit, inverse = norm_parts(h1)
            second = (unit * (1.0 + mod[2]) + mod[3]).astype(bf16)
            second_ref[spot] = second
            upper = dot_nt(second, mlp_ref[pl.ds(0, hidden)])
            square = upper * upper
            bend = jnp.tanh(gelu_scale * upper * (1.0 + gelu_cubic * square))
            half = 0.5 + 0.5 * bend
            activ = (upper * half).astype(bf16)
            activ_ref[spot] = activ
            slope = half + (0.5 * gelu_scale) * upper * (1.0 - bend * bend) * (
                1.0 + 3.0 * gelu_cubic * square
            )
            slope_ref[spot] = slope.astype(bf16)
            h2 = h1 + dot_nn(activ, mlp_ref[pl.ds(hidden, hidden)])
            high = h2.astype(bf16)
            out_ref[spot] = high
            low = (h2 - high.astype(f32)).astype(bf16)
            projected = (dot_nt(high, dec_rows) + dot_nt(low, dec_rows)) * live
            top = projected.astype(bf16)
            node_ref[spot, pl.ds(0, 128)] = top
            node_ref[spot, pl.ds(128, 128)] = (projected - top.astype(f32)).astype(bf16)

        row_loop(tile, feed)

        c_output, weight = scalar_ref[0], scalar_ref[1]
        loads[3].wait()
        cores, uppers = {}, {}
        for band in range(bands):
            net = dot_nn(dec_ref[band], node_ref[...])
            net = (net[:, :128] + net[:, 128:]) * (c_output * third)
            error = (base_ref[band] + net) * keep_ref[band]
            high = error.astype(bf16)
            low = (error - high.astype(f32)).astype(bf16)
            turned = dot_tn(high, table_ref[0]) + dot_tn(low, table_ref[0]) + dot_tn(high, table_ref[1])
            f_ref[band] = turned[:sent]
            all_ref[node, band] = turned[:sent].astype(bf16)
            piece = all_ref.at[node, band]
            cores[0, band] = start_copy(started, place, piece, piece, f_sem.at[0, band], core=1)
            for i in range(1, place.uppers):
                uppers[i, band] = start_copy(started, place, piece, piece, f_sem.at[i, band], upper=i)
        gf_ref[...] = jnp.zeros_like(gf_ref)
        for band in range(bands):
            for i in range(1, place.uppers):
                uppers[i, band].wait_recv()
                source = lax.rem(place.upper + place.uppers - i, place.uppers) * 2 + place.core
                piece = all_ref.at[source, band]
                cores[i, band] = start_copy(started, place, piece, piece, pass_sem.at[i, band], core=1)
        for key in cores:
            cores[key].wait_recv()
        loss_rows = jnp.zeros((8, 128), f32)
        loads[4].wait()
        for band in range(bands):

            def add_lat(index, total):
                return total + kern_ref[band, pl.ds(index, 1)] * all_ref[
                    index // lats, lax.rem(index, lats)
                ].astype(f32)

            total = lax.fori_loop(0, all_lats, add_lat, jnp.zeros((sent, lanes), f32), unroll=4)
            loss_rows = loss_rows + jnp.sum(total * f_ref[band])
            gf_ref[pl.ds(0, sent)] = total * (2.0 * weight)
            grad = gf_ref[...]
            high = grad.astype(bf16)
            low = (grad - high.astype(f32)).astype(bf16)
            back = dot_nt(table_ref[0], high) + dot_nt(table_ref[0], low) + dot_nt(table_ref[1], high)
            gnet_ref[band] = (back * keep_ref[band] * c_output).astype(bf16)
        loss_out[...] = loss_rows * weight

        sums_ref[...] = jnp.zeros_like(sums_ref)

        def back_feed(spot):
            grad_node = dot_nn(turned_ref[0, spot], gnet_ref[0])
            for band in range(1, bands):
                grad_node += dot_nn(turned_ref[band, spot], gnet_ref[band])
            grad_node = grad_node * third
            high = grad_node.astype(bf16)
            low = (grad_node - high.astype(f32)).astype(bf16)
            node_ref[spot, pl.ds(0, 128)] = high
            grad_out = dot_nn(high, dec_rows) + dot_nn(low, dec_rows)
            branch = grad_out.astype(bf16)
            gb_ref[spot] = branch
            grad_activ = dot_nt(branch, mlp_ref[pl.ds(hidden, hidden)])
            grad_upper = (grad_activ * slope_ref[spot].astype(f32)).astype(bf16)
            slope_ref[spot] = grad_upper
            grad_second = dot_nn(grad_upper, mlp_ref[pl.ds(0, hidden)])
            unit, inverse = norm_parts(h1_ref[spot])
            scaled = grad_second * (1.0 + mod[2])
            grad_mid = grad_out + inverse * (
                scaled
                - jnp.mean(scaled, axis=-1, keepdims=True)
                - unit * jnp.mean(scaled * unit, axis=-1, keepdims=True)
            )
            sums_ref[2:3] += jnp.sum(grad_second * unit, axis=0, keepdims=True)
            sums_ref[3:4] += jnp.sum(grad_second, axis=0, keepdims=True)
            h1_ref[spot] = grad_mid
            grad_attn = grad_mid.astype(bf16)
            gattn_ref[spot] = grad_attn
            gblend_ref[spot] = dot_nn(grad_attn, attn_ref[pl.ds(3 * width, width)]).astype(bf16)

        row_loop(tile, back_feed)

        def outer_loop(target, offset, left, right, columns):
            @pl.loop(0, columns // big)
            def _(index):
                part = pl.multiple_of(index * big, big)
                product = dot_tn(left[:, pl.ds(part, big)], right[...])
                target[pl.ds(pl.multiple_of(offset + part, big), big)] = product.astype(bf16)

        gext_ref[...] = jnp.zeros_like(gext_ref)

        def back_attend(spot):
            count = near_ref[spot].astype(f32)
            for head in range(HEAD_COUNT):
                part = pl.ds(head * head_width, head_width)
                values = pl.ds(width + head * head_width, head_width)
                prob = prob_ref[head, spot].astype(f32)
                counted_prob = prob * count
                grad_blend = gblend_ref[spot, part]
                grad_prob = dot_nt(grad_blend, ext_ref[:, values])
                mean = jnp.sum(counted_prob * grad_prob, axis=-1, keepdims=True)
                grad_logit = (counted_prob * (grad_prob - mean)).astype(bf16)
                gext_ref[:, part] += dot_tn(grad_logit, q_ref[spot, part])
                q_ref[spot, part] = (dot_nn(grad_logit, ext_ref[:, part]) * score_scale).astype(bf16)
                gext_ref[:, values] += dot_tn(counted_prob.astype(bf16), grad_blend)

        row_loop(tile, back_attend)
        gext_ref[:, pl.ds(0, width)] = gext_ref[:, pl.ds(0, width)] * score_scale
        lost_ref[0] = gext_ref[pl.ds(rows, halo)].astype(bf16)
        lost_ref[1] = gext_ref[pl.ds(rows + halo, halo)].astype(bf16)
        from_upper = to_node(nodes - 1, lost_ref.at[0], back_ref.at[pl.ds(0, halo)], back_sem.at[0])
        from_lower = to_node(1, lost_ref.at[1], back_ref.at[pl.ds(halo, halo)], back_sem.at[1])

        outer_loop(mlp_out, hidden, activ_ref, gb_ref, hidden)
        outer_loop(mlp_out, 0, slope_ref, second_ref, hidden)
        outer_loop(attn_out, 3 * width, gattn_ref, blend_ref, width)
        outer_loop(attn_out, 0, q_ref, first_ref, width)
        from_upper.wait_recv()
        from_lower.wait_recv()

        def back_encode(spot):
            grad_pairs = gext_ref[spot] + dot_nn(lendt_ref[spot], back_ref[...])
            grad_pairs = grad_pairs.astype(bf16)
            ext_ref[spot] = grad_pairs
            grad_first = dot_nn(q_ref[spot], attn_ref[pl.ds(0, width)]) + dot_nn(
                grad_pairs, attn_ref[pl.ds(width, 2 * width)]
            )
            unit, inverse = norm_parts(h0_ref[spot])
            scaled = grad_first * (1.0 + mod[0])
            grad_in = h1_ref[spot] + inverse * (
                scaled
                - jnp.mean(scaled, axis=-1, keepdims=True)
                - unit * jnp.mean(scaled * unit, axis=-1, keepdims=True)
            )
            sums_ref[0:1] += jnp.sum(grad_first * unit, axis=0, keepdims=True)
            sums_ref[1:2] += jnp.sum(grad_first, axis=0, keepdims=True)
            gb_ref[spot] = grad_in.astype(bf16)

        row_loop(big, back_encode)
        outer_loop(attn_out, width, ext_ref.at[pl.ds(0, rows)], first_ref, 2 * width)

        feats_value = feats_ref[...]
        small_rows = small_ref.shape[0]
        cond = feats_value[:, 0:1] * sums_ref[0:1]
        for j in range(1, 4):
            cond += feats_value[:, j : j + 1] * sums_ref[j : j + 1]
        for low_row in range(0, small_rows, 128):
            total = cond[low_row : low_row + 128]
            if low_row < wide:
                total += dot_tn(mixed_ref[0, :, pl.ds(low_row, 128)], gb_ref[...])
            if low_row == start:
                total += dot_tn(node_ref[:, pl.ds(0, 128)], out_ref[...])
            high = total.astype(bf16)
            high_out[pl.ds(low_row, 128)] = high
            low_out[pl.ds(low_row, 128)] = (total - high.astype(f32)).astype(bf16)
        for copy in started:
            copy.wait_send()

    vmem = pl.BlockSpec(memory_space=pltpu.VMEM)
    hbm = pl.BlockSpec(memory_space=pl.ANY)
    dma = pltpu.SemaphoreType.DMA
    struct = jax.ShapeDtypeStruct
    low = lambda *shape: pltpu.VMEM(shape, bf16)
    full = lambda *shape: pltpu.VMEM(shape, f32)
    return pl.pallas_call(
        kernel,
        out_shape=(
            struct(attn.shape, bf16),
            struct(mlp.shape, bf16),
            struct(small.shape, bf16),
            struct(small.shape, bf16),
            struct((8, 128), f32),
        ),
        in_specs=[hbm, hbm, vmem, hbm, hbm, hbm] + [vmem] * 8 + [pl.BlockSpec(memory_space=pltpu.SMEM)],
        out_specs=(vmem,) * 5,
        scratch_shapes=[
            low(*attn.shape),
            low(*mlp.shape),
            low(*near.shape),
            low(*dec.shape),
            low(*dec_turned.shape),
            full(rows, width),
            full(rows, width),
            low(rows, width),
            low(rows, width),
            low(ext_rows, 2 * width),
            low(halo, 2 * width),
            low(HEAD_COUNT, rows, ext_rows),
            low(rows, width),
            low(rows, width),
            low(rows, hidden),
            low(rows, hidden),
            low(rows, width),
            low(rows, 256),
            full(lats, sent, lanes),
            low(nodes, lats, sent, lanes),
            full(128, lanes),
            low(bands, lons, 128),
            low(rows, width),
            low(rows, width),
            low(rows, width),
            full(ext_rows, 2 * width),
            low(2 * halo, 2 * width),
            low(2, halo, 2 * width),
            full(8, width),
            dma((5,)),
            dma((2, 2)),
            dma((place.uppers, lats, 2)),
            dma((place.uppers, lats, 2)),
            dma((2, 2)),
        ],
        compiler_params=pltpu.CompilerParams(
            collective_id=collective, has_side_effects=True, vmem_limit_bytes=62 << 20
        ),
    )(attn, mlp, small, near, dec, dec_turned, mixed, lend, lendt, kern, feats, base, keep, tables, scalars)


class Scatter:
    def __init__(self, place, pieces, grads, bufs, sems):
        self.place, self.pieces, self.grads = place, pieces, grads
        count = len(grads)
        self.core_in = bufs[:count]
        (self.over_out, self.over_in, self.under_out, self.under_in, self.over_out2, self.over_in2,
         self.under_out2, self.under_in2, self.far_out, self.far_in) = bufs[count:]
        (self.core_sem, self.over_sem, self.under_sem, self.over_sem2, self.under_sem2, self.far_sem) = sems
        self.started = []
        self.order = list(range(1, place.fars)) + [0]
        self.core, self.over, self.under, self.over2, self.under2, self.far = {}, {}, {}, {}, {}, {}
        self.head_rows = sum(rows for _, _, rows in pieces.head)
        self.tail_rows = sum(rows for _, _, rows in pieces.tail)

    def send(self, source, target, sem, **steps):
        return start_copy(self.started, self.place, source, target, sem, **steps)

    def begin(self, arrays):
        place = self.place
        other = 1 - place.core
        for k in self.order:
            far = place.moved(far=k)[2]
            for upper in range(place.uppers):
                for near in range(place.nears):
                    slot = place.slot(upper, other, far, near)
                    for a in arrays:
                        self.core[k, upper, near, a] = self.send(
                            self.grads[a].at[slot], self.core_in[a].at[k, upper, near],
                            self.core_sem.at[k, upper, near, a], core=1,
                        )

    def add(self, target, k, upper, near, pieces, others):
        far = self.place.moved(far=k)[2]
        slot = self.place.slot(upper, self.place.core, far, near)
        offset = 0
        for array, start, rows in pieces:
            mine = self.grads[array].at[slot]
            theirs = self.core_in[array].at[k, upper, near]

            @pl.loop(0, rows // ROW_CHUNK)
            def _(index, start=start, offset=offset, mine=mine, theirs=theirs):
                step = index * ROW_CHUNK
                here = pl.ds(pl.multiple_of(start + step, ROW_CHUNK), ROW_CHUNK)
                there = pl.ds(pl.multiple_of(offset + step, ROW_CHUNK), ROW_CHUNK)
                total = mine[here].astype(f32) + theirs[here].astype(f32)
                for other in others:
                    total += other[there].astype(f32)
                target[there] = total.astype(target.dtype)

            offset += rows

    def one(self, k):
        place, pieces = self.place, self.pieces
        for key in self.core:
            if key[0] == k:
                self.core[key].wait_recv()
        for i in range(1, place.uppers):
            for near in range(place.nears):
                self.add(self.over_out.at[k, i - 1, near], k, place.moved(upper=i)[0], near, pieces.head, [])
            self.over[k, i] = self.send(
                self.over_out.at[k, i - 1], self.over_in.at[k, i - 1], self.over_sem.at[k, i], upper=i
            )
        for j in range(1, place.nears):
            for upper in range(place.uppers):
                self.add(self.under_out.at[k, j - 1, upper], k, upper, place.moved(near=j)[3], pieces.tail, [])
            self.under[k, j] = self.send(
                self.under_out.at[k, j - 1], self.under_in.at[k, j - 1], self.under_sem.at[k, j], near=j
            )

    def overs(self, k, near):
        return [self.over_in.at[k, i - 1, near] for i in range(1, self.place.uppers)]

    def unders(self, k, upper):
        return [self.under_in.at[k, j - 1, upper] for j in range(1, self.place.nears)]

    def two(self, k):
        place, pieces = self.place, self.pieces
        for i in range(1, place.uppers):
            self.over[k, i].wait_recv()
        for j in range(1, place.nears):
            near = place.moved(near=j)[3]
            self.add(self.over_out2.at[k, j - 1], k, place.upper, near, pieces.head, self.overs(k, near))
            self.over2[k, j] = self.send(
                self.over_out2.at[k, j - 1], self.over_in2.at[k, j - 1], self.over_sem2.at[k, j], near=j
            )
        for j in range(1, place.nears):
            self.under[k, j].wait_recv()
        for i in range(1, place.uppers):
            upper = place.moved(upper=i)[0]
            self.add(self.under_out2.at[k, i - 1], k, upper, place.near, pieces.tail, self.unders(k, upper))
            self.under2[k, i] = self.send(
                self.under_out2.at[k, i - 1], self.under_in2.at[k, i - 1], self.under_sem2.at[k, i], upper=i
            )

    def three(self, k, target, extra):
        place, pieces = self.place, self.pieces
        for j in range(1, place.nears):
            self.over2[k, j].wait_recv()
        for i in range(1, place.uppers):
            self.under2[k, i].wait_recv()
        head, tail = pl.ds(0, self.head_rows), pl.ds(self.head_rows, self.tail_rows)
        self.add(
            target.at[head], k, place.upper, place.near, pieces.head,
            self.overs(k, place.near)
            + [self.over_in2.at[k, j - 1] for j in range(1, place.nears)]
            + [item.at[head] for item in extra],
        )
        self.add(
            target.at[tail], k, place.upper, place.near, pieces.tail,
            self.unders(k, place.upper)
            + [self.under_in2.at[k, i - 1] for i in range(1, place.uppers)]
            + [item.at[tail] for item in extra],
        )

    def step(self, step):
        fars, order = self.place.fars, self.order
        if step < fars:
            self.one(order[step])
        if 1 <= step <= fars:
            self.two(order[step - 1])
        if step >= 2 and order[step - 2]:
            k = order[step - 2]
            self.three(k, self.far_out.at[k - 1], [])
            self.far[k] = self.send(self.far_out.at[k - 1], self.far_in.at[k - 1], self.far_sem.at[k], far=k)

    def steps(self):
        return self.place.fars + 2

    def finish(self, own):
        fars = self.place.fars
        for k in range(1, fars):
            self.far[k].wait_recv()
        self.three(0, own, [self.far_in.at[k - 1] for k in range(1, fars)])

    def end(self):
        for copy in self.started:
            copy.wait_send()

    @staticmethod
    def copies(place, pieces):
        fars, nears, uppers = place.fars, place.nears, place.uppers
        return fars * uppers * nears * len(pieces.sizes) + 2 * fars * (uppers + nears - 2) + fars - 1

    @staticmethod
    def scratch(place, pieces, width):
        fars, nears, uppers = place.fars, place.nears, place.uppers
        head = sum(rows for _, _, rows in pieces.head)
        tail = sum(rows for _, _, rows in pieces.tail)
        dma = pltpu.SemaphoreType.DMA
        bufs = [(fars, uppers, nears, size) for size in pieces.sizes]
        bufs += [(fars, uppers - 1, nears, head)] * 2
        bufs += [(fars, nears - 1, uppers, tail)] * 2
        bufs += [(fars, nears - 1, head)] * 2
        bufs += [(fars, uppers - 1, tail)] * 2
        bufs += [(fars - 1, head + tail)] * 2
        if width:
            bufs = [pltpu.VMEM(shape + (width,), bf16) for shape in bufs]
        sems = [
            dma((fars, uppers, nears, len(pieces.sizes), 2)),
            dma((fars, uppers, 2)),
            dma((fars, nears, 2)),
            dma((fars, nears, 2)),
            dma((fars, uppers, 2)),
            dma((fars, 2)),
        ]
        return bufs, sems


class Strip:
    def __init__(self, ref, first, dims):
        self.ref, self.first, self.dims, self.at = ref, first, dims, self

    def __getitem__(self, index):
        index = index if isinstance(index, tuple) else (index,)
        sizes = self.dims[1:]
        flat, rows = 0, 1
        for axis, size in enumerate(sizes):
            if axis + 1 < len(index):
                flat = flat * size + index[axis + 1]
            else:
                flat, rows = flat * size, rows * size
        return self.ref.at[index[0], pl.ds(self.first + flat, rows)]


def strips(refs, shapes):
    result, at, first = [], 0, 0
    for shape in shapes:
        rows = math.prod(shape[1:])
        if first + rows > refs[at].shape[1]:
            at, first = at + 1, 0
        result.append(Strip(refs[at], first, shape))
        first += rows
    return result


class HalfGather:
    def __init__(self, place, shard, out, sems):
        self.place, self.shard, self.out = place, shard, out
        self.own_sem, self.far_sem, self.near_sem, self.mate_sem, self.core_sem = sems
        self.started, self.cores = [], []
        self.far, self.near, self.mate = {}, {}, {}

    def block(self, **steps):
        return self.out.at[self.place.slot(*self.place.moved(**steps))]

    def send(self, source, target, sem, **steps):
        return start_copy(self.started, self.place, source, target, sem, **steps)

    def begin(self):
        self.kept = pltpu.make_async_copy(self.shard, self.block(), self.own_sem)
        self.kept.start()
        for k in range(1, self.place.fars):
            self.far[k] = self.send(self.shard, self.block(), self.far_sem.at[k], far=k)

    def spread(self, k, j, source, target):
        for i in range(1, self.place.mates):
            self.mate[k, j, i] = self.send(source, target, self.mate_sem.at[k, j, i], mate=i)
        self.cores.append(self.send(source, target, self.core_sem.at[k, j, 0], core=1))

    def step(self, step):
        place = self.place
        fars, nears = place.fars, place.nears
        if step < fars:
            if step:
                self.far[step].wait_recv()
            target = self.block(far=(fars - step) % fars)
            source = target if step else self.shard
            for j in range(1, nears):
                self.near[step, j] = self.send(source, target, self.near_sem.at[step, j], near=j)
            self.spread(step, 0, source, target)
        if 1 <= step <= fars:
            k = step - 1
            for j in range(1, nears):
                self.near[k, j].wait_recv()
                item = self.block(far=(fars - k) % fars, near=nears - j)
                self.spread(k, j, item, item)
        if step >= 2:
            k = step - 2
            for j in range(nears):
                for i in range(1, place.mates):
                    self.mate[k, j, i].wait_recv()
                    item = self.block(far=(fars - k) % fars, near=(nears - j) % nears, mate=place.mates - i)
                    self.cores.append(self.send(item, item, self.core_sem.at[k, j, i], core=1))

    def end(self):
        self.kept.wait()
        wait_all(self.cores)
        for copy in self.started:
            copy.wait_send()

    @staticmethod
    def copies(place):
        fars, nears, mates = place.fars, place.nears, place.mates
        return (fars - 1) + fars * (nears - 1) + fars * nears * (mates - 1) + fars * nears * mates

    @staticmethod
    def sems(place):
        dma = pltpu.SemaphoreType.DMA
        fars, nears, mates = place.fars, place.nears, place.mates
        return [
            dma,
            dma((fars, 2)),
            dma((fars, nears, 2)),
            dma((fars, nears, mates, 2)),
            dma((fars, nears, mates, 2)),
        ]


class MomentGather:
    def __init__(self, place, shards, outs, sems):
        self.place, self.shards, self.outs = place, shards, outs
        (self.own_sem, self.far_sem, self.near_sem, self.spread_sem, self.core_sem) = sems
        self.started, self.cores = [], []
        self.far, self.near, self.spread_copies = {}, {}, {}

    def block(self, **steps):
        slot = self.place.slot(*self.place.moved(**steps))
        return [out.at[slot] for out in self.outs]

    def send(self, source, target, sem, **steps):
        return start_copy(self.started, self.place, source, target, sem, **steps)

    def both(self, source, target, sems, **steps):
        return [self.send(source[a], target[a], sems.at[a], **steps) for a in range(2)]

    def spread(self, k, j, source, target):
        place = self.place
        for i in range(1, place.uppers):
            self.spread_copies[k, j, i, 0] = self.send(
                source[0], target[0], self.spread_sem.at[k, j, i, 0], upper=i
            )
        for i in range(1, place.mates):
            self.spread_copies[k, j, i, 1] = self.send(
                source[1], target[1], self.spread_sem.at[k, j, i, 1], mate=i
            )
        self.cores += self.both(source, target, self.core_sem.at[k, j, 0], core=1)

    def run(self):
        place = self.place
        fars, nears = place.fars, place.nears
        here = self.block()
        kept = [
            pltpu.make_async_copy(shard, target, self.own_sem.at[a])
            for a, (shard, target) in enumerate(zip(self.shards, here))
        ]
        for copy in kept:
            copy.start()
        for k in range(1, fars):
            self.far[k] = self.both(self.shards, here, self.far_sem.at[k], far=k)
        for step in range(fars + 2):
            if step < fars:
                k = step
                if k:
                    wait_all(self.far[k])
                target = self.block(far=(fars - k) % fars)
                source = target if k else self.shards
                for j in range(1, nears):
                    self.near[k, j] = self.both(source, target, self.near_sem.at[k, j], near=j)
                self.spread(k, 0, source, target)
            if 1 <= step <= fars:
                k = step - 1
                for j in range(1, nears):
                    wait_all(self.near[k, j])
                    item = self.block(far=(fars - k) % fars, near=nears - j)
                    self.spread(k, j, item, item)
            if step >= 2:
                k = step - 2
                for j in range(nears):
                    steps = dict(far=(fars - k) % fars, near=(nears - j) % nears)
                    for key in self.spread_copies:
                        if key[:2] != (k, j):
                            continue
                        i, a = key[2:]
                        self.spread_copies[key].wait_recv()
                        if a:
                            item = self.block(mate=place.mates - i, **steps)[1]
                        else:
                            item = self.block(upper=place.uppers - i, **steps)[0]
                        self.cores.append(self.send(item, item, self.core_sem.at[k, j, i, a], core=1))
        for copy in kept:
            copy.wait()
        wait_all(self.cores)
        for copy in self.started:
            copy.wait_send()

    @staticmethod
    def sems(place):
        dma = pltpu.SemaphoreType.DMA
        fars, nears, uppers = place.fars, place.nears, place.uppers
        return [
            dma((2,)),
            dma((fars, 2, 2)),
            dma((fars, nears, 2, 2)),
            dma((fars, nears, uppers, 2, 2)),
            dma((fars, nears, uppers, 2, 2)),
        ]


def total_body(place, tile, slots, sems):
    value = tile
    upper, core, far, near = place.moved()
    stages = (
        ("core", 2, core),
        ("near", place.nears, near),
        ("upper", place.uppers, upper),
        ("far", place.fars, far),
    )
    for stage, (name, size, mine) in enumerate(stages):
        slots[stage, mine] = value
        copies = []
        for step in range(1, size):
            piece = slots.at[stage, mine]
            start_copy(copies, place, piece, piece, sems.at[stage, step], **{name: step})
        for copy in copies:
            copy.wait()
        value = slots[stage, 0]
        for other in range(1, size):
            value = value + slots[stage, other]
    return value


def reduce_and_gather(nodes, zeros, names, grads, mlp_sum, loss_tile, mom_attn, mom_mlp, small_rows, collective):
    place = Place(nodes, zeros)
    devices, _, width = grads[0].shape
    attn_rows, mlp_rows = mom_attn.shape[0], mom_mlp.shape[0]
    lead = names.index("mlp") if "mlp" in names else 0
    pieces = Pieces([item.shape[1] for item in grads], lead)
    moment_sizes = (sixteens(attn_rows), sixteens(mlp_rows))
    bufs, sems = Scatter.scratch(place, pieces, width)
    deepest = max(place.fars, place.uppers, place.nears, 2)
    summed = [] if mlp_sum is None else [mlp_sum]
    count = len(grads)
    starts, offset = {}, 0
    for array in [lead] + [i for i in range(count) if i != lead]:
        starts[names[array]] = offset
        offset += pieces.sizes[array]

    def kernel(*refs):
        grad_refs = refs[:count]
        refs = refs[count:]
        if summed:
            sum_ref, *refs = refs
        loss_ref, attn_ref, mlp_ref = refs[:3]
        small_out, attn_out, mlp_out, total_out, attn_all, mlp_all = refs[3:9]
        own, attn_shard, mlp_shard, slots, slot_sems = refs[9:14]
        rest = refs[14:]
        place.locate()
        place.greet()
        scatter = Scatter(
            place, pieces, grad_refs, rest[: len(bufs)], rest[len(bufs) : len(bufs) + len(sems)]
        )
        scatter.begin([lead] + [i for i in range(count) if i != lead])
        for step in range(scatter.steps()):
            scatter.step(step)
        scatter.finish(own)
        g_attn = own[pl.ds(starts["attn"], attn_rows)]
        g_mlp = sum_ref[...] if summed else own[pl.ds(starts["mlp"], mlp_rows)]
        g_small = own[pl.ds(starts["high"], small_rows)] + own[pl.ds(starts["low"], small_rows)]
        small_out[...] = g_small
        squares = jnp.sum(g_attn * g_attn) + jnp.sum(g_mlp * g_mlp) + jnp.sum(g_small * g_small)
        tile = jnp.where(iota((8, 128), 0) < 4, squares, loss_ref[...])
        total = total_body(place, tile, slots, slot_sems)
        total_out[...] = total
        factor = jnp.minimum(1.0, clip_limit * lax.rsqrt(total[0:1, 0:1]))
        for ref, out, shard, grad, size in (
            (attn_ref, attn_out, attn_shard, g_attn, attn_rows),
            (mlp_ref, mlp_out, mlp_shard, g_mlp, mlp_rows),
        ):
            moment = moment_decay * ref[...] + factor * grad
            out[...] = moment
            if size < shard.shape[0]:
                shard[...] = jnp.zeros_like(shard)
            shard[pl.ds(0, size)] = moment.astype(bf16)
        moments = MomentGather(
            place, (attn_shard, mlp_shard), (attn_all, mlp_all), rest[len(bufs) + len(sems) :]
        )
        moments.run()
        scatter.end()

    vmem = pl.BlockSpec(memory_space=pltpu.VMEM)
    hbm = pl.BlockSpec(memory_space=pl.ANY)
    struct = jax.ShapeDtypeStruct
    return pl.pallas_call(
        kernel,
        out_shape=(
            struct((small_rows, width), f32),
            struct((attn_rows, width), f32),
            struct((mlp_rows, width), f32),
            struct((8, 128), f32),
            struct((devices, moment_sizes[0], width), bf16),
            struct((devices, moment_sizes[1], width), bf16),
        ),
        in_specs=[vmem] * (count + len(summed) + 3),
        out_specs=(vmem,) * 4 + (hbm,) * 2,
        scratch_shapes=[
            pltpu.VMEM((sum(pieces.sizes), width), f32),
            pltpu.VMEM((moment_sizes[0], width), bf16),
            pltpu.VMEM((moment_sizes[1], width), bf16),
            pltpu.VMEM((4, deepest, 8, 128), f32),
            pltpu.SemaphoreType.DMA((4, deepest, 2)),
        ]
        + bufs
        + sems
        + MomentGather.sems(place),
        compiler_params=pltpu.CompilerParams(
            collective_id=collective, has_side_effects=True, vmem_limit_bytes=56 << 20
        ),
    )(*grads, *summed, loss_tile, mom_attn, mom_mlp)


def basis_apply(gram, moment):
    size = gram.shape[0]
    eye = jnp.where(iota((size, size), 0) == iota((size, size), 1), 1.0, 0.0)
    trace = jnp.sum(jnp.sum(gram * eye, axis=1, keepdims=True), axis=0, keepdims=True)
    scale = lax.rsqrt(trace + trace_epsilon)
    current = gram * (scale * scale)
    result = moment * scale
    for iteration in range(NS_ITERS):
        low = current.astype(bf16)
        if iteration + 1 == NS_ITERS:
            once = dot_nn(result.astype(bf16), low)
            twice = dot_nn(once.astype(bf16), low)
            return newton_first * result + newton_second * once + newton_third * twice
        rest = newton_second * current + newton_third * dot_nn(low, low)
        rest_low = rest.astype(bf16)
        result = newton_first * result + dot_nn(result.astype(bf16), rest_low)
        once = dot_nn(rest_low, low)
        current = (
            (newton_first * newton_first) * current
            + (2.0 * newton_first) * once
            + dot_nn(once.astype(bf16), rest_low)
        )


def update_weights(nodes, zeros, attn_sets, mlp_sets, totals, sums, moments, weights, averages, small_moments):
    width = attn_sets[0].shape[1]
    attn_rows, mlp_rows, small_rows = [w.shape[0] for w in weights]
    half = mlp_sets[0].shape[0] // 2
    block = width
    inputs = (*sums, *moments, *weights, *averages, *small_moments)
    count, sets = len(inputs), len(attn_sets)
    fresh = sets == 1

    def kernel(total_ref, *refs):
        attn_hbm, mlp_hbm, sources = refs[:sets], refs[sets : 2 * sets], refs[2 * sets : 2 * sets + count]
        refs = refs[2 * sets + count :]
        loss_out, clip_out, new_attn, new_mlp, new_small, new_m, new_v, new_e_attn, new_e_mlp, new_e_small = refs[:10]
        mom_attn_out, mom_mlp_out = refs[10:12]
        gram_attn, gram_mlp, attn_sem, mlp_sem, row_sem = refs[12:17]
        attn_refs, mlp_refs, rows = refs[17 : 17 + sets], refs[17 + sets : 17 + 2 * sets], refs[17 + 2 * sets :]
        g_refs, rows = rows[: len(sums)], rows[len(sums) :]
        mom_attn, mom_mlp, w_attn, w_mlp, w_small, e_attn, e_mlp, e_small, m_ref, v_ref = rows
        flat = lax.axis_index("node") * zeros + lax.axis_index("zero")
        attn_upper = flat * attn_rows >= 3 * width
        mlp_upper = flat * mlp_rows >= half
        first_row = jnp.where(mlp_upper, half, 0)
        copies_mlp = [
            pltpu.make_async_copy(
                mlp_hbm[i].at[pl.ds(pl.multiple_of(first_row + low, block), block)],
                mlp_refs[i].at[pl.ds(low, block)],
                mlp_sem.at[low // block, i],
            )
            for low in range(0, half, block)
            for i in range(sets)
        ]
        copies_attn = [
            pltpu.make_async_copy(attn_hbm[i], attn_refs[i], attn_sem.at[i]) for i in range(sets)
        ]
        copies = [
            pltpu.make_async_copy(source, target, row_sem.at[index])
            for index, (source, target) in enumerate(zip(sources, refs[17 + 2 * sets :]))
        ]
        for copy in copies_mlp + copies_attn + copies:
            copy.start()
        total = total_ref[0]
        for index in range(1, total_ref.shape[0]):
            total = total + total_ref[index]
        loss_out[...] = total[4:5, 0:1]
        clip_out[...] = jnp.sqrt(total[0:1, 0:1])
        factor = jnp.minimum(1.0, clip_limit * lax.rsqrt(total[0:1, 0:1]))

        def momentum(refs, index):
            part = pl.ds(index * block if isinstance(index, int) else pl.multiple_of(index * block, block), block)
            if fresh:
                return refs[0][part]
            return (moment_decay * refs[0][part].astype(f32) + factor * refs[1][part].astype(f32)).astype(bf16)

        for index in range(half // block):
            for copy in copies_mlp[index * sets : (index + 1) * sets]:
                copy.wait()
            part = momentum(mlp_refs, index)
            if index:
                gram_mlp[...] += dot_tn(part, part)
            else:
                gram_mlp[...] = dot_tn(part, part)

        for copy in copies_attn:
            copy.wait()
        gram_attn[...] = jnp.zeros_like(gram_attn)
        start = jnp.where(attn_upper, 3, 0)

        @pl.loop(start, jnp.where(attn_upper, 4, 3))
        def _(index):
            part = momentum(attn_refs, index)
            gram_attn[...] += dot_tn(part, part)

        for copy in copies:
            copy.wait()

        clipped = factor * g_refs[0][...]
        first = adam_first * m_ref[...] + (1.0 - adam_first) * clipped
        second = adam_second * v_ref[...] + (1.0 - adam_second) * clipped * clipped
        new_m[...] = first
        new_v[...] = second
        small = w_small[...] - adam_rate * (first / (1.0 - adam_first**STEP)) / (
            jnp.sqrt(second / (1.0 - adam_second**STEP)) + adam_epsilon
        )
        new_small[...] = small
        new_e_small[...] = average_decay * e_small[...] + (1.0 - average_decay) * small

        attn_moment, mlp_moment = mom_attn[...], mom_mlp[...]
        if not fresh:
            attn_moment = moment_decay * attn_moment + factor * g_refs[1][...]
            mlp_moment = moment_decay * mlp_moment + factor * g_refs[2][...]
        mom_attn_out[...] = attn_moment
        mom_mlp_out[...] = mlp_moment
        attn_step = basis_apply(gram_attn[...], attn_moment)
        mlp_step = basis_apply(gram_mlp[...], mlp_moment)
        attn_factor = jnp.where(attn_upper, 0.2 * math.sqrt(width), 0.2 * math.sqrt(3 * width))
        mlp_factor = 0.2 * math.sqrt(max(half, width))
        for step, rate, old, new, mean, new_mean in (
            (attn_step, orthogonal_rate * attn_factor, w_attn, new_attn, e_attn, new_e_attn),
            (mlp_step, orthogonal_rate * mlp_factor, w_mlp, new_mlp, e_mlp, new_e_mlp),
        ):
            value = old[...] - rate * step
            new[...] = value
            new_mean[...] = average_decay * mean[...] + (1.0 - average_decay) * value

    vmem = pl.BlockSpec(memory_space=pltpu.VMEM)
    hbm = pl.BlockSpec(memory_space=pl.ANY)
    one = jnp.zeros((1, 1), f32)
    outs = [one, one, weights[0], weights[1], weights[2], weights[2], weights[2], weights[0], weights[1], weights[2]]
    outs += [weights[0], weights[1]]
    dma = pltpu.SemaphoreType.DMA
    return pl.pallas_call(
        kernel,
        out_shape=tuple(jax.ShapeDtypeStruct(item.shape, f32) for item in outs),
        in_specs=[vmem] + [hbm] * (2 * sets + count),
        out_specs=(vmem,) * 12,
        scratch_shapes=[
            pltpu.VMEM((width, width), f32),
            pltpu.VMEM((width, width), f32),
            dma((sets,)),
            dma((half // block, sets)),
            dma((count,)),
        ]
        + [pltpu.VMEM(attn_sets[0].shape, bf16)] * sets
        + [pltpu.VMEM((half, width), bf16)] * sets
        + [pltpu.VMEM(item.shape, f32) for item in inputs],
        compiler_params=pltpu.CompilerParams(vmem_limit_bytes=62 << 20),
    )(totals, *attn_sets, *mlp_sets, *inputs)


def train_step(nodes, zeros, weights, grid, target, land, near_turned, enc_turned, dec_turned, lent, legendre, vector, tables, waves, moments, cin, collective):
    place = Place(nodes, zeros)
    devices = nodes * zeros
    attn_rows, mlp_rows, small_rows = [w.shape[0] for w in weights]
    width = weights[0].shape[1]
    hidden = devices * mlp_rows // 2
    bands, lons, channels = target.shape
    fanout, rows = near_turned.shape
    enc_edges, dec_edges = enc_turned.shape[0], dec_turned.shape[0]
    halo = lent.shape[1]
    ext_rows = rows + 2 * halo
    lats, lows, flat = legendre.shape
    lanes = tables.shape[2]
    modes, wave_first, wave_end = waves
    all_lats = nodes * lats
    wide = -(-cin // 128) * 128
    start = cin // 128 * 128
    shift = cin - start
    sent = sixteens(channels)
    flat_lons = -(-lons // 128) * 128
    flat_pixels = -(-bands * lons // 128) * 128
    all_small = devices * small_rows
    cond_start = cin + channels
    big, tile, chunk = 256, 128, 512
    head_width = width // HEAD_COUNT
    score_scale = head_width ** (-0.5)
    third = 1.0 / dec_edges
    first_rows = attn_rows + small_rows
    packed_rows = first_rows + small_rows
    first_pieces = Pieces([first_rows], 0)
    mlp_pieces = Pieces([mlp_rows], 0)
    mlp_sum_pieces = Pieces([mlp_rows], 0, 5 / 8)
    last_pieces = Pieces([packed_rows], 0, 2 / 3)
    attn_pieces = Pieces([attn_rows], 0)
    tile_pieces = Pieces([attn_rows, 8], 0, 1)
    scatter_bufs, _ = Scatter.scratch(place, mlp_sum_pieces, width)
    last_shapes, _ = Scatter.scratch(place, last_pieces, 0)
    copies = (
        sum(Gather.copies(place, pieces) for pieces in (first_pieces, mlp_pieces, attn_pieces, tile_pieces))
        + 2 * HalfGather.copies(place)
        + Scatter.copies(place, mlp_sum_pieces)
        + Scatter.copies(place, last_pieces)
        + (nodes - 1) + (place.nears - 1) + (place.fars - 1) + 4 + (2 * place.uppers - 1) * lats
    )

    def kernel(
        attn_in, mlp_in, small_in, grid_ref, target_ref, land_ref, near_in, enc_in, dec_in, lent_ref, leg_ref,
        vector_ref, table_ref, mom_attn_in, mom_mlp_in,
        attn_sum, mlp_sum, small_sum, tiles_out, mom_attn_all, mom_mlp_all, g_attn_all, g_mlp_all,
        own, mom_attn_shard, mom_mlp_shard, g_attn_shard, g_mlp_shard, tile_shard,
        first_shard, mlp_shard, legs, parts, sums, kern_ref,
        packed_ref, mlp_ref, near_ref, dec_ref, mixed_ref, lendt_ref, h0_ref, h1_ref, first_ref, q_ref,
        ext_ref, lent_rows, prob_ref, blend_ref, second_ref, activ_ref, slope_ref, out_ref, node_ref, all_ref,
        gf_ref, gnet_ref, gnode_ref, gb_ref, gattn_ref, gblend_ref, gext_ref, back_ref, lost_ref, sums_ref,
        scale_ref, error_ref, column_ref, lists_ref, input_ref, dec_rows_ref, feats_ref,
        pool_ref, own_sem,
        *bufs,
    ):
        pool = Pool(pool_ref)
        place.locate()
        node = lax.axis_index("node")
        zero = lax.axis_index("zero")
        first_shard[pl.ds(0, attn_rows)] = attn_in[...].astype(bf16)
        first_shard[pl.ds(attn_rows, small_rows)] = small_in[...].astype(bf16)
        legs[node] = leg_ref[...]
        place.greet(nodes)
        gather = Gather(place, first_pieces, (first_shard,), (packed_ref,), pool.gather(own_sem, 0))
        gather_mlp = Gather(place, mlp_pieces, (mlp_shard,), (mlp_ref,), pool.gather(own_sem, 1))
        gather.begin()
        started = []

        def to_node(step, source, target):
            sems = pool.take()
            copy = pltpu.make_async_remote_copy(
                src_ref=source,
                dst_ref=target,
                send_sem=sems.at[0],
                recv_sem=sems.at[1],
                device_id=(lax.rem(node + step, nodes), zero),
                device_id_type=MESH,
            )
            copy.start()
            started.append(copy)
            return copy

        gather.step(0)
        leg_copies = [
            to_node(step, leg_ref, legs.at[node]) for step in range(1, nodes)
        ]
        mlp_shard[...] = mlp_in[...].astype(bf16)
        gather_mlp.begin()
        mom_attn_shard[...] = mom_attn_in[...].astype(bf16)
        mom_mlp_shard[...] = mom_mlp_in[...].astype(bf16)
        gather_moms = [
            Gather(place, attn_pieces, (mom_attn_shard,), (mom_attn_all,), pool.gather(own_sem, 2)),
            HalfGather(place, mom_mlp_shard, mom_mlp_all, pool.half(own_sem, 3)),
        ]

        def mom_step(step):
            for item in gather_moms:
                item.step(step)

        def row_loop(size, body, hooks=()):
            count = rows // size
            cuts = [count * i // (len(hooks) + 1) for i in range(len(hooks) + 2)]
            for i in range(len(hooks) + 1):

                @pl.loop(cuts[i], cuts[i + 1])
                def _(index):
                    body(pl.ds(pl.multiple_of(index * size, size), size))

                if i < len(hooks):
                    hooks[i]()

        def mix():
            column_ref[pl.ds(0, enc_edges), pl.ds(0, rows)] = enc_in[...]
            lists_ref[pl.ds(0, rows), pl.ds(0, 8)] = jnp.transpose(column_ref[pl.ds(0, 8), pl.ds(0, rows)])
            lane = iota((1, cin), 1)
            scale = jnp.where(lane < channels, vector_ref[0:1, c_input_lane : c_input_lane + 1], 1.0)

            @pl.loop(0, bands)
            def _(band):
                input_ref[band] = (grid_ref[band].astype(f32) * scale).astype(bf16)

            mixed_ref[...] = jnp.zeros_like(mixed_ref)

            def mix_rows(spot):
                lists = lists_ref[spot]
                mean = jnp.zeros((tile, cin), f32)
                for band in range(bands):
                    place_of = iota((tile, lons), 1) + band * lons
                    total = jnp.zeros((tile, lons), f32)
                    for j in range(enc_edges):
                        total += jnp.where(lists[:, j : j + 1] == place_of, 1.0 / enc_edges, 0.0)
                    mean += dot_nn(total.astype(bf16), input_ref[band])
                high = mean.astype(bf16)
                mixed_ref[0, spot, pl.ds(0, cin)] = high
                mixed_ref[1, spot, pl.ds(0, cin)] = (mean - high.astype(f32)).astype(bf16)

            row_loop(tile, mix_rows)

        def count_near():
            lists_ref[pl.ds(0, rows), pl.ds(0, fanout)] = jnp.transpose(near_in[...])

            def count_rows(spot):
                lists = lists_ref[spot]
                place_of = iota((tile, ext_rows), 1)
                total = jnp.zeros((tile, ext_rows), f32)
                for j in range(fanout):
                    total += jnp.where(lists[:, j : j + 1] == place_of, 1.0, 0.0)
                near_ref[spot] = jnp.where(total > 0.0, jnp.log2(jnp.maximum(total, 1.0)), absent)

            row_loop(tile, count_rows)

        def count_dec():
            column_ref[pl.ds(0, dec_edges), pl.ds(0, bands * lons)] = dec_in[...]
            lists_ref[:, pl.ds(0, 8)] = jnp.transpose(column_ref[...])

            @pl.loop(0, bands)
            def _(band):
                lists = lists_ref[pl.ds(pl.multiple_of(band * lons, 8), lons)]
                place_of = iota((lons, rows), 1)
                total = jnp.zeros((lons, rows), f32)
                for j in range(dec_edges):
                    total += jnp.where(lists[:, j : j + 1] == place_of, 1.0, 0.0)
                dec_ref[band] = total.astype(bf16)

        near_parts, far_sums = [], []

        def gram():
            for copy in leg_copies:
                copy.wait_recv()

            @pl.loop(0, all_lats)
            def _(index):
                other = legs[index // lats, lax.rem(index, lats)].astype(f32)
                for t in range(lats):
                    product = leg_ref[t].astype(f32) * other
                    parts[place.near, t, pl.ds(index, 1)] = jnp.sum(product, axis=0, keepdims=True)

            for j in range(1, place.nears):
                piece = parts.at[place.near]
                near_parts.append(start_copy(started, place, piece, piece, pool, near=j))

        def gram_near():
            wait_all(near_parts)
            total = parts[0]
            for j in range(1, place.nears):
                total = total + parts[j]
            sums[place.far] = total
            for k in range(1, place.fars):
                piece = sums.at[place.far]
                far_sums.append(start_copy(started, place, piece, piece, pool, far=k))

        def gram_far():
            wait_all(far_sums)
            total = sums[0]
            for k in range(1, place.fars):
                total = total + sums[k]
            kern_ref[...] = jnp.zeros_like(kern_ref)
            kern_ref[:, :, pl.ds(0, flat)] = total
            cosines = kern_ref[...]
            sines = pltpu.roll(cosines, modes - wave_first, 2)
            spot = iota((1, 1, lanes), 2)
            kern_ref[...] = jnp.where(
                spot < modes, cosines, jnp.where(spot < modes + wave_end - wave_first, sines, 0.0)
            )

        lendt_ref[...] = jnp.where(lent_ref[...] == iota((rows, halo), 0), 1.0, 0.0).astype(bf16)
        work = [mix, gram, count_dec, gram_near]
        for k in range(1, place.fars + 2):
            gather.step(k)
            if k == 1:
                gather_mlp.step(0)
            if work:
                work.pop(0)()
        while work:
            work.pop(0)()
        gather.end()
        gather_mlp.step(1)

        def small_part(low, size):
            blocks = pl.ds(low // small_rows, size // small_rows)
            return packed_ref[blocks, pl.ds(attn_rows, small_rows)].reshape(size, width)

        row = iota((all_small, 128), 0) - cond_start
        lane = iota((all_small, 128), 1)
        feature = vector_ref[0:1]
        block = jnp.where(row >= 0, row // NOISE_FEATS, 4)
        picked = jnp.where((row - block * NOISE_FEATS == lane) & (block < 4) & (lane < NOISE_FEATS), feature, 0.0)
        column = jnp.sum(picked, axis=1, keepdims=True)
        feats_ref[...] = jnp.where(lane == block, column, 0.0)
        mods = dot_tn(feats_ref[...].astype(bf16), small_part(0, all_small))
        mod = [mods[j : j + 1] for j in range(4)]

        def attn_part(low, size):
            return packed_ref[pl.ds(low // attn_rows, size // attn_rows), pl.ds(0, attn_rows)].reshape(size, width)

        def mlp_part(low):
            return mlp_ref[pl.ds(low // mlp_rows, chunk // mlp_rows)].reshape(chunk, width)

        def encode(spot):
            enc = small_part(0, wide)
            h0 = dot_nn(mixed_ref[0, spot], enc) + dot_nn(mixed_ref[1, spot], enc)
            h0_ref[spot] = h0
            unit, inverse = norm_parts(h0)
            first = (unit * (1.0 + mod[0]) + mod[1]).astype(bf16)
            first_ref[spot] = first
            ext_ref[spot] = dot_nt(first, attn_part(width, 2 * width)).astype(bf16)
            q_ref[spot] = dot_nt(first, attn_part(0, width)).astype(bf16)

        row_loop(big, encode)
        lent_rows[...] = dot_tn(lendt_ref[...], ext_ref[pl.ds(0, rows)]).astype(bf16)
        up = to_node(1, lent_rows, ext_ref.at[pl.ds(rows, halo)])
        down = to_node(nodes - 1, lent_rows, ext_ref.at[pl.ds(rows + halo, halo)])
        gather_mlp.step(2)
        count_near()
        gram_far()
        gather_mlp.step(3)
        for item in gather_moms:
            item.begin()
        up.wait_recv()
        down.wait_recv()

        def attend(spot):
            often = near_ref[spot]
            for head in range(HEAD_COUNT):
                part = pl.ds(head * head_width, head_width)
                values = pl.ds(width + head * head_width, head_width)
                logits = dot_nt(q_ref[spot, part], ext_ref[:, part]) * (score_scale * log2_e) + often
                raised = jnp.exp2(logits - jnp.max(logits, axis=-1, keepdims=True))
                inverse = 1.0 / jnp.sum(raised, axis=-1, keepdims=True)
                raised = raised.astype(bf16)
                prob_ref[head, spot] = raised
                scale_ref[spot, pl.ds(head, 1)] = inverse
                blend_ref[spot, part] = (dot_nn(raised, ext_ref[:, values]) * inverse).astype(bf16)

        row_loop(tile, attend, [lambda: gather_mlp.step(4), lambda: gather_mlp.step(5)])
        for k in range(6, place.fars + 2):
            gather_mlp.step(k)
        gather_mlp.end()
        mom_step(0)
        lane = iota((1, 128), 1)
        live = jnp.where(lane < channels, 1.0, 0.0)
        dec_rows_ref[...] = pltpu.roll(small_part(start, 128).astype(f32), 128 - shift, 0).astype(bf16)

        def feed(spot):
            h1 = h0_ref[spot] + dot_nt(blend_ref[spot], attn_part(3 * width, width))
            h1_ref[spot] = h1
            unit, inverse = norm_parts(h1)
            second = (unit * (1.0 + mod[2]) + mod[3]).astype(bf16)
            second_ref[spot] = second
            h2 = h1
            for low in range(0, hidden, chunk):
                upper = dot_nt(second, mlp_part(low))
                square = upper * upper
                bend = jnp.tanh(upper * (gelu_scale + (gelu_scale * gelu_cubic) * square))
                half = 0.5 + 0.5 * bend
                activ = (upper * half).astype(bf16)
                activ_ref[low // chunk, spot] = activ
                slope = half + upper * (1.0 - bend * bend) * (
                    0.5 * gelu_scale + (1.5 * gelu_scale * gelu_cubic) * square
                )
                slope_ref[low // chunk, spot] = slope.astype(bf16)
                h2 += dot_nn(activ, mlp_part(hidden + low))
            high = h2.astype(bf16)
            out_ref[spot] = high
            low = (h2 - high.astype(f32)).astype(bf16)
            dec_rows = dec_rows_ref[...]
            projected = (dot_nt(high, dec_rows) + dot_nt(low, dec_rows)) * live
            top = projected.astype(bf16)
            node_ref[spot, pl.ds(0, 128)] = top
            node_ref[spot, pl.ds(128, 128)] = (projected - top.astype(f32)).astype(bf16)

        row_loop(big, feed)
        mom_step(1)

        c_skip = vector_ref[0:1, c_skip_lane : c_skip_lane + 1]
        c_output = vector_ref[0:1, c_output_lane : c_output_lane + 1]
        weight = vector_ref[0:1, weight_lane : weight_lane + 1]
        column_ref[pl.ds(0, bands), pl.ds(0, lons)] = land_ref[...]
        masks = jnp.transpose(column_ref[pl.ds(0, 8), pl.ds(0, flat_lons)].astype(f32))
        last = jnp.where(lane == channels - 1, 1.0, 0.0)

        def keep(band):
            return live * (1.0 - masks[:lons, band : band + 1] * last)

        error_ref[...] = jnp.zeros_like(error_ref)
        cores, uppers = {}, {}
        for band in range(bands):
            net = dot_nn(dec_ref[band], node_ref[...])
            net = (net[:, :128] + net[:, 128:]) * (c_output * third)
            noisy = grid_ref[band, :, pl.ds(0, 128)].astype(f32)
            error_ref[:, pl.ds(0, channels)] = target_ref[band]
            error = (c_skip * noisy + net - error_ref[...]) * keep(band)
            high = error.astype(bf16)
            low = (error - high.astype(f32)).astype(bf16)
            turned = dot_tn(high, table_ref[0]) + dot_tn(low, table_ref[0]) + dot_tn(high, table_ref[1])
            gext_ref[pl.ds(band * sent, sent), pl.ds(0, lanes)] = turned[:sent]
            all_ref[node, band] = turned[:sent].astype(bf16)
            piece = all_ref.at[node, band]
            for i in range(1, place.uppers):
                uppers[i, band] = start_copy(started, place, piece, piece, pool, upper=i)
            cores[0, band] = start_copy(started, place, piece, piece, pool, core=1)
        gf_ref[...] = jnp.zeros_like(gf_ref)
        mom_step(2)

        def add_nodes(base, total, band):
            def add_lat(index, value):
                source = base + index // lats
                return value + kern_ref[band, pl.ds(source * lats + lax.rem(index, lats), 1)] * all_ref[
                    source, lax.rem(index, lats)
                ].astype(f32)

            return lax.fori_loop(0, 2 * lats, add_lat, total, unroll=8)

        for band in range(bands):
            cores[0, band].wait_recv()
        for band in range(bands):
            gext_ref[pl.ds((lats + band) * sent, sent), pl.ds(0, lanes)] = add_nodes(place.upper * 2, jnp.zeros((sent, lanes), f32), band)
            for i in range(1, place.uppers):
                uppers[i, band].wait_recv()
                source = lax.rem(place.upper + place.uppers - i, place.uppers) * 2 + place.core
                piece = all_ref.at[source, band]
                cores[i, band] = start_copy(started, place, piece, piece, pool, core=1)
        for i in range(1, place.uppers):
            for band in range(bands):
                cores[i, band].wait_recv()
        loss_rows = jnp.zeros((8, 128), f32)
        for band in range(bands):
            total = gext_ref[pl.ds((lats + band) * sent, sent), pl.ds(0, lanes)]
            for i in range(1, place.uppers):
                total = add_nodes(lax.rem(place.upper + i, place.uppers) * 2, total, band)
            loss_rows = loss_rows + jnp.sum(total * gext_ref[pl.ds(band * sent, sent), pl.ds(0, lanes)])
            gf_ref[pl.ds(0, sent)] = total * (2.0 * weight)
            grad = gf_ref[...]
            high = grad.astype(bf16)
            low = (grad - high.astype(f32)).astype(bf16)
            back = dot_nt(table_ref[0], high) + dot_nt(table_ref[0], low) + dot_nt(table_ref[1], high)
            gnet_ref[band] = (back * keep(band) * c_output).astype(bf16)
        loss_share = loss_rows * weight

        sums_ref[...] = jnp.zeros_like(sums_ref)
        grad_node = dot_tn(gnet_ref[0], dec_ref[0])
        for band in range(1, bands):
            grad_node += dot_tn(gnet_ref[band], dec_ref[band])
        gnode_ref[...] = jnp.transpose(grad_node * third)

        def back_feed(spot):
            grad_node = gnode_ref[spot]
            high = grad_node.astype(bf16)
            low = (grad_node - high.astype(f32)).astype(bf16)
            node_ref[spot, pl.ds(0, 128)] = high
            dec_rows = dec_rows_ref[...]
            grad_out = dot_nn(high, dec_rows) + dot_nn(low, dec_rows)
            branch = grad_out.astype(bf16)
            gb_ref[spot] = branch
            grad_second = jnp.zeros((big, width), f32)
            for low in range(0, hidden, chunk):
                grad_activ = dot_nt(branch, mlp_part(hidden + low))
                grad_upper = (grad_activ * slope_ref[low // chunk, spot].astype(f32)).astype(bf16)
                slope_ref[low // chunk, spot] = grad_upper
                grad_second += dot_nn(grad_upper, mlp_part(low))
            unit, inverse = norm_parts(h1_ref[spot])
            scaled = grad_second * (1.0 + mod[2])
            grad_mid = grad_out + inverse * (
                scaled
                - jnp.mean(scaled, axis=-1, keepdims=True)
                - unit * jnp.mean(scaled * unit, axis=-1, keepdims=True)
            )
            sums_ref[2:3] += jnp.sum(grad_second * unit, axis=0, keepdims=True)
            sums_ref[3:4] += jnp.sum(grad_second, axis=0, keepdims=True)
            h1_ref[spot] = grad_mid
            grad_attn = grad_mid.astype(bf16)
            gattn_ref[spot] = grad_attn
            grad_blend = dot_nn(grad_attn, attn_part(3 * width, width))
            for head in range(HEAD_COUNT):
                part = slice(head * head_width, (head + 1) * head_width)
                scaled_blend = grad_blend[:, part] * scale_ref[spot, pl.ds(head, 1)]
                gblend_ref[spot, pl.ds(head * head_width, head_width)] = scaled_blend.astype(bf16)

        mom_step(3)
        row_loop(big, back_feed, [lambda: mom_step(4)])
        for k in range(5, place.fars + 2):
            mom_step(k)

        def outer_loop(target, block, offset, left, right, columns):
            @pl.loop(0, columns // big)
            def _(index):
                part = pl.multiple_of(index * big, big)
                product = dot_tn(left[:, pl.ds(part, big)], right[...]).astype(bf16)
                target[pl.ds((offset + part) // block, big // block), pl.ds(0, block)] = product.reshape(
                    big // block, block, width
                )

        for low in range(0, hidden, chunk):
            outer_loop(mlp_ref, mlp_rows, hidden + low, activ_ref.at[low // chunk], gb_ref, chunk)
            outer_loop(mlp_ref, mlp_rows, low, slope_ref.at[low // chunk], second_ref, chunk)
        scatter = Scatter(place, mlp_sum_pieces, (mlp_ref,), bufs, [pool] * 6)
        scatter.begin([0])

        gext_ref[...] = jnp.zeros_like(gext_ref)

        def back_attend(spot):
            for head in range(HEAD_COUNT):
                part = pl.ds(head * head_width, head_width)
                values = pl.ds(width + head * head_width, head_width)
                raised = prob_ref[head, spot]
                grad_blend = gblend_ref[spot, part]
                grad_prob = dot_nt(grad_blend, ext_ref[:, values])
                mean = jnp.sum(
                    grad_blend.astype(f32) * blend_ref[spot, part].astype(f32), axis=-1, keepdims=True
                )
                grad_logit = (raised.astype(f32) * (grad_prob - mean)).astype(bf16)
                gext_ref[:, part] += dot_tn(grad_logit, q_ref[spot, part])
                q_ref[spot, part] = (dot_nn(grad_logit, ext_ref[:, part]) * score_scale).astype(bf16)
                gext_ref[:, values] += dot_tn(raised, grad_blend)

        row_loop(big, back_attend, [lambda: scatter.step(0), lambda: scatter.step(1)])
        key_scale = jnp.where(iota((1, 2 * width), 1) < width, score_scale, 1.0)
        lost_ref[0] = (gext_ref[pl.ds(rows, halo)] * key_scale).astype(bf16)
        lost_ref[1] = (gext_ref[pl.ds(rows + halo, halo)] * key_scale).astype(bf16)
        from_upper = to_node(nodes - 1, lost_ref.at[0], back_ref.at[0])
        from_lower = to_node(1, lost_ref.at[1], back_ref.at[1])
        scatter.step(2)
        outer_loop(packed_ref, attn_rows, 3 * width, gattn_ref, blend_ref, width)
        scatter.step(3)
        from_upper.wait_recv()
        from_lower.wait_recv()

        def back_encode(spot):
            grad_pairs = gext_ref[spot] * key_scale + dot_nn(lendt_ref[spot], back_ref[0]) + dot_nn(
                lendt_ref[spot], back_ref[1]
            )
            grad_pairs = grad_pairs.astype(bf16)
            ext_ref[spot] = grad_pairs
            grad_first = dot_nn(q_ref[spot], attn_part(0, width)) + dot_nn(
                grad_pairs, attn_part(width, 2 * width)
            )
            unit, inverse = norm_parts(h0_ref[spot])
            scaled = grad_first * (1.0 + mod[0])
            grad_in = h1_ref[spot] + inverse * (
                scaled
                - jnp.mean(scaled, axis=-1, keepdims=True)
                - unit * jnp.mean(scaled * unit, axis=-1, keepdims=True)
            )
            sums_ref[0:1] += jnp.sum(grad_first * unit, axis=0, keepdims=True)
            sums_ref[1:2] += jnp.sum(grad_first, axis=0, keepdims=True)
            gb_ref[spot] = grad_in.astype(bf16)

        row_loop(big, back_encode, [lambda: scatter.step(4)])
        for k in range(5, scatter.steps()):
            scatter.step(k)
        scatter.finish(mlp_sum)
        g_mlp_shard[...] = mlp_sum[...].astype(bf16)
        gather_g_mlp = HalfGather(place, g_mlp_shard, g_mlp_all, pool.half(own_sem, 4))
        gather_g_mlp.begin()
        gather_g_mlp.step(0)
        outer_loop(packed_ref, attn_rows, 0, q_ref, first_ref, width)
        outer_loop(packed_ref, attn_rows, width, ext_ref.at[pl.ds(0, rows)], first_ref, 2 * width)
        last = Scatter(
            place, last_pieces, (packed_ref,), strips((activ_ref, slope_ref), last_shapes), [pool] * 6
        )

        @pl.loop(0, all_small // 128)
        def _(index):
            low_row = pl.multiple_of(index * 128, 128)
            part = feats_ref[pl.ds(low_row, 128)]
            total = part[:, 0:1] * sums_ref[0:1]
            for j in range(1, 4):
                total += part[:, j : j + 1] * sums_ref[j : j + 1]
            gext_ref[pl.ds(low_row, 128), pl.ds(0, width)] = total

        for low_row in range(0, wide, 128):
            gext_ref[pl.ds(low_row, 128), pl.ds(0, width)] += dot_tn(
                mixed_ref[0, :, pl.ds(low_row, 128)], gb_ref[...]
            )
        gext_ref[pl.ds(start, 128), pl.ds(0, width)] += pltpu.roll(
            dot_tn(node_ref[:, pl.ds(0, 128)], out_ref[...]), shift, 0
        )

        @pl.loop(0, all_small // 128)
        def _(index):
            total = gext_ref[pl.ds(pl.multiple_of(index * 128, 128), 128), pl.ds(0, width)]
            high = total.astype(bf16)
            blocks = pl.ds(index * (128 // small_rows), 128 // small_rows)
            shape = (128 // small_rows, small_rows, width)
            packed_ref[blocks, pl.ds(attn_rows, small_rows)] = high.reshape(shape)
            packed_ref[blocks, pl.ds(first_rows, small_rows)] = (total - high.astype(f32)).astype(bf16).reshape(shape)

        last.begin([0])
        for k in range(last.steps()):
            last.step(k)
            if k + 1 < last.steps():
                gather_g_mlp.step(k + 1)
        last.finish(own)
        g_attn, g_mlp = own[pl.ds(0, attn_rows)], mlp_sum[...]
        g_small = own[pl.ds(attn_rows, small_rows)] + own[pl.ds(attn_rows + small_rows, small_rows)]
        attn_sum[...] = g_attn
        small_sum[...] = g_small
        g_attn_shard[...] = g_attn.astype(bf16)
        squares = jnp.sum(g_attn * g_attn) + jnp.sum(g_mlp * g_mlp) + jnp.sum(g_small * g_small)
        tile_shard[...] = jnp.where(iota((8, 128), 0) < 4, squares, loss_share)
        gather_g_attn = Gather(
            place, tile_pieces, (g_attn_shard, tile_shard), (g_attn_all, tiles_out), pool.gather(own_sem, 5)
        )
        gather_g_attn.begin()
        for k in range(place.fars + 2):
            gather_g_attn.step(k)
        for item in (*gather_moms, gather_g_mlp, gather_g_attn):
            item.end()
        scatter.end()
        last.end()
        for copy in started:
            copy.wait_send()

    vmem = pl.BlockSpec(memory_space=pltpu.VMEM)
    dma = pltpu.SemaphoreType.DMA
    struct = jax.ShapeDtypeStruct
    low = lambda *shape: pltpu.VMEM(shape, bf16)
    full = lambda *shape: pltpu.VMEM(shape, f32)
    return pl.pallas_call(
        kernel,
        out_shape=(
            struct((attn_rows, width), f32),
            struct((mlp_rows, width), f32),
            struct((small_rows, width), f32),
            struct((devices, 8, 128), f32),
        )
        + tuple(struct((devices, size, width), bf16) for size in (attn_rows, mlp_rows) * 2),
        in_specs=[vmem] * 15,
        out_specs=(vmem,) * 3 + (pl.BlockSpec(memory_space=pl.ANY),) * 5,
        scratch_shapes=[
            full(attn_rows + 2 * small_rows, width),
            low(attn_rows, width),
            low(mlp_rows, width),
            low(attn_rows, width),
            low(mlp_rows, width),
            full(8, 128),
            low(first_rows, width),
            low(mlp_rows, width),
            low(nodes, lats, lows, flat),
            full(place.nears, lats, all_lats, flat),
            full(place.fars, lats, all_lats, flat),
            full(lats, all_lats, lanes),
            low(devices, packed_rows, width),
            low(devices, mlp_rows, width),
            full(rows, ext_rows),
            low(bands, lons, rows),
            low(2, rows, wide),
            low(rows, halo),
            full(rows, width),
            full(rows, width),
            low(rows, width),
            low(rows, width),
            low(ext_rows, 2 * width),
            low(halo, 2 * width),
            low(HEAD_COUNT, rows, ext_rows),
            low(rows, width),
            low(rows, width),
            low(hidden // chunk, rows, chunk),
            low(hidden // chunk, rows, chunk),
            low(rows, width),
            low(rows, 256),
            low(nodes, lats, sent, lanes),
            full(128, lanes),
            low(bands, lons, 128),
            full(rows, 128),
            low(rows, width),
            low(rows, width),
            low(rows, width),
            full(ext_rows, 2 * width),
            low(2, halo, 2 * width),
            low(2, halo, 2 * width),
            full(8, width),
            full(rows, 128),
            full(lons, 128),
            pltpu.VMEM((8, flat_pixels), jnp.int32),
            pltpu.VMEM((flat_pixels, 128), jnp.int32),
            low(bands, lons, cin),
            low(128, width),
            full(all_small, 128),
            dma((2 * copies,)),
            dma((7,)),
        ]
        + scatter_bufs,
        compiler_params=pltpu.CompilerParams(
            collective_id=collective, has_side_effects=True, vmem_limit_bytes=62 << 20
        ),
    )(*weights, grid, target, land, near_turned, enc_turned, dec_turned, lent, legendre, vector, tables, *moments)


def turn_tables(lon_count, modes):
    turns = np.arange(lon_count)[:, None] * np.arange(modes)[None, :] % lon_count
    phases = turns * (2.0 * np.pi / lon_count)
    waves = [m for m in range(modes) if (2 * m) % lon_count]
    picks = list(range(modes)) + waves
    lanes = -(-len(picks) // 128) * 128
    table = np.zeros((lon_count, lanes), np.float32)
    table[:, :modes] = np.cos(phases)
    table[:, modes : len(picks)] = -np.sin(phases[:, waves])
    high = table.astype(ml_dtypes.bfloat16)
    low = (table - high.astype(np.float32)).astype(ml_dtypes.bfloat16)
    return np.stack([high, low]), (waves[0], waves[-1] + 1, lanes - len(picks))


def to_sixteens(blocks):
    return jnp.pad(blocks, ((0, 0), (0, sixteens(blocks.shape[1]) - blocks.shape[1]), (0, 0)))


def on_device(
    grid_in,
    target,
    noise_level,
    land_mask,
    neighbours,
    halo_send,
    g2m,
    m2g,
    legendre,
    w_attn,
    w_mlp,
    w_small,
    mom_attn,
    mom_mlp,
    m_small,
    v_small,
    ema_attn,
    ema_mlp,
    ema_small,
):
    cin = grid_in.shape[-1]
    lat_rows, lon_count, channels = target.shape[1:]
    modes, degrees = legendre.shape[1:]
    halo_rows = halo_send.shape[0]
    width = w_attn.shape[1]
    nodes, zeros = lax.axis_size("node"), lax.axis_size("zero")
    devices = nodes * zeros
    attn_rows, mlp_rows, small_rows = w_attn.shape[0], w_mlp.shape[0], w_small.shape[0]

    sigma, c_input, c_skip, c_output, loss_weight = noise_scalars(noise_level[0])
    features = noise_features(sigma).astype(bf16).astype(f32)
    weight = loss_weight / (2 * modes * degrees * channels)
    tables, (wave_first, wave_end, wave_pad) = turn_tables(lon_count, modes)
    whole_tiles = all(size % 16 == 0 and 256 % size == 0 for size in (attn_rows, mlp_rows, small_rows))
    if whole_tiles:
        lows = sixteens(-(-degrees // zeros))
        wanted = lax.axis_index("zero") * lows
        first_degree = jnp.minimum(wanted, degrees - lows)
        leg = lax.dynamic_slice_in_dim(legendre, first_degree, lows, axis=2)
        leg = jnp.where(first_degree + jnp.arange(lows) >= wanted, leg, 0.0)
        leg = jnp.pad(jnp.transpose(leg, (0, 2, 1)).astype(bf16), ((0, 0), (0, 0), (0, -modes % 128)))
        lane = jnp.arange(128)
        vector = jnp.where(lane < NOISE_FEATS, jnp.pad(features, (0, 128 - NOISE_FEATS)), 0.0)
        for spot, value in (
            (c_input_lane, c_input),
            (c_skip_lane, c_skip),
            (c_output_lane, c_output),
            (weight_lane, weight),
        ):
            vector = jnp.where(lane == spot, value, vector)
        attn_sum, mlp_sum, g_small, totals, mom_attn_all, mom_mlp_all, g_attn_all, g_mlp_all = train_step(
            nodes,
            zeros,
            (w_attn, w_mlp, w_small),
            grid_in[0],
            target[0],
            land_mask,
            neighbours.T,
            g2m.T,
            m2g.T,
            halo_send[None],
            leg,
            vector[None],
            jnp.asarray(tables),
            (modes, wave_first, wave_end),
            (mom_attn, mom_mlp),
            cin,
            1,
        )
        sums = (g_small, attn_sum, mlp_sum)
        attn_sets = [item.reshape(-1, width) for item in (mom_attn_all, g_attn_all)]
        mlp_sets = [item.reshape(-1, width) for item in (mom_mlp_all, g_mlp_all)]
        moments = (mom_attn, mom_mlp)
    else:
        scale_input = jnp.where(jnp.arange(cin) < channels, c_input, 1.0)[None]
        cond_rows = jnp.where(
            jnp.arange(128)[None, None] == jnp.arange(4)[:, None, None], features[None, :, None], 0.0
        ).reshape(-1, 128)
        feats = jnp.pad(cond_rows, ((cin + channels, 0), (0, 0)))
        shift = cin % 128
        sides = ((0, 0), (0, 0), (shift, 128 - shift - channels))
        keep_mask = 1.0 - land_mask.astype(f32)[:, :, None] * (
            jnp.arange(channels) == channels - 1
        ).astype(f32)
        base = jnp.pad(c_skip * grid_in[0, :, :, :channels].astype(f32) - target[0], sides)
        keep = jnp.pad(keep_mask, sides)
        lows = -(-degrees // (8 * zeros)) * 8
        leg = jnp.pad(legendre, ((0, 0), (0, 0), (0, lows * zeros - degrees)))
        leg = lax.dynamic_slice_in_dim(leg, lax.axis_index("zero") * lows, lows, axis=2)
        leg = jnp.transpose(leg, (0, 2, 1))
        leg = jnp.concatenate(
            [leg, leg[:, :, wave_first:wave_end], jnp.zeros(leg.shape[:2] + (wave_pad,), f32)], axis=2
        )
        m2g_bands = m2g.reshape(lat_rows, lon_count, -1)

        attn, mlp, small, near, dec, dec_turned, mixed, lend, lendt, kern = gather_and_count(
            nodes,
            zeros,
            (w_attn, w_mlp, w_small),
            grid_in[0].reshape(-1, cin),
            scale_input,
            g2m,
            m2g_bands,
            jnp.transpose(m2g_bands, (0, 2, 1)),
            neighbours,
            halo_send[:, None],
            jnp.concatenate([halo_send, halo_send])[None],
            leg,
            1,
        )
        full = [
            item[:, :size].reshape(-1, width)
            for item, size in ((attn, attn_rows), (mlp, mlp_rows), (small, small_rows))
        ]
        *local, loss_tile = model_step(
            nodes,
            zeros,
            full,
            (near, dec, dec_turned, mixed, lend, lendt),
            kern,
            feats,
            base,
            keep,
            jnp.asarray(tables),
            jnp.stack([c_output, weight]),
            cin,
            channels,
            m2g.shape[1],
            2,
        )
        names = ["attn", "mlp", "high", "low"]
        mlp_sum = None

        g_small, moment_attn, moment_mlp, totals, attn_all, mlp_all = reduce_and_gather(
            nodes,
            zeros,
            names,
            [to_sixteens(item.reshape(devices, -1, width)) for item in local],
            mlp_sum,
            loss_tile,
            mom_attn,
            mom_mlp,
            small_rows,
            3,
        )
        sums = (g_small,)
        attn_sets = [attn_all[:, :attn_rows].reshape(-1, width)]
        mlp_sets = [mlp_all[:, :mlp_rows].reshape(-1, width)]
        totals = totals[None]
        moments = (moment_attn, moment_mlp)

    *results, moment_attn, moment_mlp = update_weights(
        nodes,
        zeros,
        attn_sets,
        mlp_sets,
        totals,
        sums,
        moments,
        (w_attn, w_mlp, w_small),
        (ema_attn, ema_mlp, ema_small),
        (m_small, v_small),
    )
    loss, clip_norm, new_attn, new_mlp, new_small, new_m, new_v, *new_averages = results
    return (
        loss[0, 0], clip_norm[0, 0], new_attn, new_mlp, new_small, moment_attn, moment_mlp, new_m, new_v, *new_averages
    )


def solution(mesh):
    split_rows = P(("node", "zero"), None)
    return jax.shard_map(
        on_device,
        mesh=mesh,
        in_specs=(
            P("zero", "node", None, None),
            P("zero", "node", None, None),
            P("zero"),
            P("node", None),
            P("node", None),
            P("node"),
            P("node", None),
            P("node", None),
            P("node", None, None),
        )
        + (split_rows,) * 10,
        out_specs=(P(), P()) + (split_rows,) * 10,
        check_vma=False,
    )
```

```python
import math

import jax
import jax.numpy as jnp
import ml_dtypes
import numpy as np
from jax import lax
from jax.experimental import pallas as pl
from jax.experimental.pallas import tpu as pltpu
from jax.sharding import PartitionSpec as P

HEAD_COUNT = 4
NOISE_FEATS = 42
LEVELS = 16
NS_ITERS = 3
STEP = 10

top_precision = lax.Precision.HIGHEST
mid_precision = lax.Precision.HIGH
norm_epsilon = 1e-05
trace_epsilon = 1e-12
clip_limit = 1.0
moment_decay = 0.95
orthogonal_rate = 0.1
adam_first = 0.9
adam_second = 0.95
adam_rate = 0.02
adam_epsilon = 1e-08
average_decay = 0.9
newton_first = 3.4445
newton_second = -4.775
newton_third = 2.0315
sigma_lowest = 0.1
sigma_highest = 20.0
c_input_lane = 64
c_skip_lane = 65
c_output_lane = 66
weight_lane = 67
log2_e = math.log2(math.e)
absent = -1e30
gelu_scale = math.sqrt(2.0 / math.pi)
gelu_cubic = 0.044715
f32 = jnp.float32
bf16 = jnp.bfloat16


def noise_scalars(level):
    sigma = sigma_lowest * (sigma_highest / sigma_lowest) ** (level.astype(f32) / (LEVELS - 1))
    total = sigma * sigma + 1.0
    return (sigma, lax.rsqrt(total), 1.0 / total, sigma * lax.rsqrt(total), total / (sigma * sigma))


def noise_features(sigma):
    half_count = NOISE_FEATS // 2
    frequency = jnp.exp(jnp.arange(half_count).astype(f32) * (3.0 / half_count))
    phases = 0.25 * jnp.log(sigma) * frequency
    return jnp.concatenate([jnp.sin(phases), jnp.cos(phases)])


def dot(left, right, contract):
    return lax.dot_general(left, right, (contract, ((), ())), preferred_element_type=f32)


def dot_nn(left, right):
    return dot(left, right, ((1,), (0,)))


def dot_nt(left, right):
    return dot(left, right, ((1,), (1,)))


def dot_tn(left, right):
    return dot(left, right, ((0,), (0,)))


MESH = pl.DeviceIdType.MESH
ROW_CHUNK = 16


class Place:
    def __init__(self, nodes, zeros):
        self.uppers, self.cores = nodes // 2, 2
        self.nears = 2 if zeros < 16 else 4
        self.fars = zeros // self.nears
        self.mates = max(self.uppers // 2, 1)
        self.zeros = zeros

    def locate(self):
        node, zero = lax.axis_index("node"), lax.axis_index("zero")
        self.upper, self.core = node // 2, node % 2
        self.far, self.near = zero // self.nears, zero % self.nears

    def moved(self, upper=0, core=0, far=0, near=0, mate=0):
        row = lax.rem(self.upper + upper, self.uppers) if upper else self.upper
        if mate:
            group = self.upper // self.mates * self.mates
            row = group + lax.rem(self.upper - group + mate, self.mates)
        return (
            row,
            1 - self.core if core else self.core,
            lax.rem(self.far + far, self.fars) if far else self.far,
            lax.rem(self.near + near, self.nears) if near else self.near,
        )

    def device(self, **steps):
        upper, core, far, near = self.moved(**steps)
        return (upper * 2 + core, far * self.nears + near)

    def slot(self, upper, core, far, near):
        return (upper * 2 + core) * self.zeros + far * self.nears + near

    def peers(self):
        return (
            [dict(far=k) for k in range(1, self.fars)]
            + [dict(near=j) for j in range(1, self.nears)]
            + [dict(upper=i) for i in range(1, self.uppers)]
            + [dict(core=1)]
        )

    def greet(self, nodes=0):
        barrier = pltpu.get_barrier_semaphore()
        peers = [self.device(**steps) for steps in self.peers() if not nodes or set(steps) <= {"far", "near"}]
        if nodes:
            node, zero = lax.axis_index("node"), lax.axis_index("zero")
            peers += [(lax.rem(node + step, nodes), zero) for step in range(1, nodes)]
        for device in peers:
            pl.semaphore_signal(barrier, 1, device_id=device, device_id_type=MESH)
        pl.semaphore_wait(barrier, len(peers))


def half_rows(rows):
    return (rows // 2 + 15) // 16 * 16


class Pool:
    def __init__(self, ref):
        self.ref, self.used, self.at = ref, 0, self

    def __getitem__(self, index):
        return self

    def take(self):
        pair = self.ref.at[pl.ds(self.used, 2)]
        self.used += 2
        return pair

    def gather(self, own, index):
        return [own.at[pl.ds(index, 2)]] + [self] * 6

    def half(self, own, index):
        return [own.at[index]] + [self] * 4


def start_copy(started, place, source, target, sems, **steps):
    if isinstance(sems, Pool):
        sems = sems.take()
    copy = pltpu.make_async_remote_copy(
        src_ref=source,
        dst_ref=target,
        send_sem=sems.at[0],
        recv_sem=sems.at[1],
        device_id=place.device(**steps),
        device_id_type=MESH,
    )
    copy.start()
    started.append(copy)
    return copy


def sixteens(rows):
    return -(-rows // 16) * 16


class Pieces:
    def __init__(self, sizes, first, share=1 / 2):
        self.sizes = sizes
        cut = min(sixteens(int(sum(sizes) * share)), sizes[first])
        self.whole = [(i, 0, size) for i, size in enumerate(sizes)]
        self.head = [(first, 0, cut)]
        self.tail = [(first, cut, sizes[first] - cut)] if cut < sizes[first] else []
        self.tail += [(i, 0, size) for i, size in enumerate(sizes) if i != first]


def send_pieces(started, place, pieces, sources, targets, sems, **steps):
    copies = []
    for index, (array, start, rows) in enumerate(pieces):
        part = pl.ds(start, rows)
        copies.append(
            start_copy(
                started, place, sources[array].at[part], targets[array].at[part], sems.at[index], **steps
            )
        )
    return copies


def wait_all(copies):
    for copy in copies:
        copy.wait_recv()


class Gather:
    def __init__(self, place, pieces, shards, outs, sems):
        self.place, self.pieces, self.shards, self.outs = place, pieces, shards, outs
        (self.own_sem, self.far_sem, self.near_sem, self.upper_sem, self.over_sem, self.under_sem, self.core_sem) = sems
        self.started, self.cores = [], []
        self.far, self.near, self.upper, self.over, self.under = {}, {}, {}, {}, {}

    def block(self, **steps):
        slot = self.place.slot(*self.place.moved(**steps))
        return [out.at[slot] for out in self.outs]

    def send(self, pieces, source, target, sems, **steps):
        return send_pieces(self.started, self.place, pieces, source, target, sems, **steps)

    def begin(self):
        here = self.block()
        self.kept = []
        for index, (shard, target) in enumerate(zip(self.shards, here)):
            mine = target.at[pl.ds(0, shard.shape[0])]
            copy = pltpu.make_async_copy(shard, mine, self.own_sem.at[index])
            copy.start()
            self.kept.append(copy)
        for k in range(1, self.place.fars):
            self.far[k] = self.send(self.pieces.whole, self.shards, here, self.far_sem.at[k], far=k)

    def first(self, k):
        place, whole = self.place, self.pieces.whole
        if k:
            wait_all(self.far[k])
        target = self.block(far=(place.fars - k) % place.fars)
        source = target if k else self.shards
        for j in range(1, place.nears):
            self.near[k, j] = self.send(whole, source, target, self.near_sem.at[k, j], near=j)
        for i in range(1, place.uppers):
            self.upper[k, i] = self.send(whole, source, target, self.upper_sem.at[k, i], upper=i)
        self.cores += self.send(whole, source, target, self.core_sem.at[k, 0, 0], core=1)

    def second(self, k):
        place, whole = self.place, self.pieces.whole
        far = (place.fars - k) % place.fars
        for j in range(1, place.nears):
            wait_all(self.near[k, j])
            item = self.block(far=far, near=place.nears - j)
            for i in range(1, place.uppers):
                self.over[k, j, i] = self.send(
                    self.pieces.head, item, item, self.over_sem.at[k, j, i], upper=i
                )
            self.cores += self.send(whole, item, item, self.core_sem.at[k, j, 0], core=1)
        for i in range(1, place.uppers):
            wait_all(self.upper[k, i])
            item = self.block(far=far, upper=place.uppers - i)
            for j in range(1, place.nears):
                self.under[k, j, i] = self.send(
                    self.pieces.tail, item, item, self.under_sem.at[k, j, i], near=j
                )
            self.cores += self.send(whole, item, item, self.core_sem.at[k, 0, i], core=1)

    def third(self, k):
        place, whole = self.place, self.pieces.whole
        far = (place.fars - k) % place.fars
        for j in range(1, place.nears):
            for i in range(1, place.uppers):
                wait_all(self.over[k, j, i])
                wait_all(self.under[k, j, i])
                item = self.block(far=far, near=place.nears - j, upper=place.uppers - i)
                self.cores += self.send(whole, item, item, self.core_sem.at[k, j, i], core=1)

    def step(self, k):
        fars = self.place.fars
        if k < fars:
            self.first(k)
        if 1 <= k <= fars:
            self.second(k - 1)
        if k >= 2:
            self.third(k - 2)

    def end(self):
        for copy in self.kept:
            copy.wait()
        wait_all(self.cores)
        for copy in self.started:
            copy.wait_send()

    @staticmethod
    def copies(place, pieces):
        fars, nears, uppers = place.fars, place.nears, place.uppers
        whole, parts = len(pieces.whole), len(pieces.head) + len(pieces.tail)
        direct = (fars - 1) + fars * (nears - 1) + fars * (uppers - 1) + fars * nears * uppers
        return whole * direct + parts * fars * (nears - 1) * (uppers - 1)

    @staticmethod
    def sems(place, pieces):
        dma = pltpu.SemaphoreType.DMA
        fars, nears, uppers = place.fars, place.nears, place.uppers
        whole, head, tail = len(pieces.whole), len(pieces.head), len(pieces.tail)
        return [
            dma((whole,)),
            dma((fars, whole, 2)),
            dma((fars, nears, whole, 2)),
            dma((fars, uppers, whole, 2)),
            dma((fars, nears, uppers, head, 2)),
            dma((fars, nears, uppers, tail, 2)),
            dma((fars, nears, uppers, whole, 2)),
        ]


def iota(shape, axis):
    return lax.broadcasted_iota(jnp.int32, shape, axis)


def gather_and_count(nodes, zeros, weights, grid, scale, g2m, m2g, m2g_turned, neighbours, lent, lent_row, legendre, collective):
    place = Place(nodes, zeros)
    width = weights[0].shape[1]
    sizes = [sixteens(w.shape[0]) for w in weights]
    pieces = Pieces(sizes, 1)
    devices = nodes * zeros
    pixels, cin = grid.shape
    wide = -(-cin // 128) * 128
    rows, fanout = neighbours.shape
    halo = lent.shape[0]
    ext = rows + 2 * halo
    bands, lons, dec_edges = m2g.shape
    lats, lows, lanes = legendre.shape
    enc_edges = g2m.shape[1]
    tile = 128

    def kernel(
        attn_ref, mlp_ref, small_ref, grid_ref, scale_ref, g2m_ref, m2g_ref, turned_ref, near_ref, lent_ref,
        row_ref, leg_ref,
        attn_out, mlp_out, small_out, near_out, dec_out, turned_out, mixed_out, lend_out, lendt_out, kern_out,
        attn_shard, mlp_shard, small_shard, inputs, legs, parts, sums, leg_sem, part_sem, sum_sem, *sems,
    ):
        place.locate()
        node = lax.axis_index("node")
        shards = (attn_shard, mlp_shard, small_shard)
        for ref, shard, size in zip((attn_ref, mlp_ref, small_ref), shards, sizes):
            if ref.shape[0] < size:
                shard[...] = jnp.zeros_like(shard)
            shard[pl.ds(0, ref.shape[0])] = ref[...].astype(bf16)
        legs[node] = leg_ref[...]
        place.greet(nodes)
        gather = Gather(place, pieces, shards, (attn_out, mlp_out, small_out), sems)
        gather.begin()
        started = []
        leg_copies = []
        for step in range(1, nodes):
            target = (lax.rem(node + step, nodes), lax.axis_index("zero"))
            copy = pltpu.make_async_remote_copy(
                src_ref=leg_ref,
                dst_ref=legs.at[node],
                send_sem=leg_sem.at[step, 0],
                recv_sem=leg_sem.at[step, 1],
                device_id=target,
                device_id_type=MESH,
            )
            copy.start()
            leg_copies.append(copy)

        def count_near():
            @pl.loop(0, rows // tile)
            def _(index):
                spot = pl.ds(pl.multiple_of(index * tile, tile), tile)
                lists = near_ref[spot]
                place_of = iota((tile, ext), 1)
                total = jnp.zeros((tile, ext), f32)
                for j in range(fanout):
                    total += jnp.where(lists[:, j : j + 1] == place_of, 1.0, 0.0)
                near_out[spot] = total.astype(bf16)

        def count_dec():
            @pl.loop(0, bands)
            def _(band):
                lists = m2g_ref[band]
                place_of = iota((lons, rows), 1)
                total = jnp.zeros((lons, rows), f32)
                for j in range(dec_edges):
                    total += jnp.where(lists[:, j : j + 1] == place_of, 1.0, 0.0)
                dec_out[band] = total.astype(bf16)
                lists = turned_ref[band]
                place_of = iota((rows, lons), 0)
                total = jnp.zeros((rows, lons), f32)
                for j in range(dec_edges):
                    total += jnp.where(lists[j : j + 1] == place_of, 1.0, 0.0)
                turned_out[band] = total.astype(bf16)

        def mix():
            inputs[...] = (grid_ref[...].astype(f32) * scale_ref[...]).astype(bf16)
            mixed_out[...] = jnp.zeros_like(mixed_out)

            @pl.loop(0, rows // tile)
            def _(index):
                spot = pl.ds(pl.multiple_of(index * tile, tile), tile)
                lists = g2m_ref[spot]
                place_of = iota((tile, pixels), 1)
                total = jnp.zeros((tile, pixels), f32)
                for j in range(enc_edges):
                    total += jnp.where(lists[:, j : j + 1] == place_of, 1.0 / enc_edges, 0.0)
                mean = dot_nn(total.astype(bf16), inputs[...])
                high = mean.astype(bf16)
                mixed_out[0, spot, pl.ds(0, cin)] = high
                mixed_out[1, spot, pl.ds(0, cin)] = (mean - high.astype(f32)).astype(bf16)

        def lend():
            lend_out[...] = jnp.where(lent_ref[...] == iota((halo, rows), 1), 1.0, 0.0).astype(bf16)
            lendt_out[...] = jnp.where(row_ref[...] == iota((rows, 2 * halo), 0), 1.0, 0.0).astype(bf16)

        def gram():
            for copy in leg_copies:
                copy.wait()

            @pl.loop(0, nodes * lats)
            def _(index):
                other = legs[index // lats, lax.rem(index, lats)]
                for t in range(lats):
                    product = leg_ref[t] * other
                    parts[place.near, t, pl.ds(index, 1)] = jnp.sum(product, axis=0, keepdims=True)

            for j in range(1, place.nears):
                near_parts.append(
                    start_copy(
                        started, place, parts.at[place.near], parts.at[place.near], part_sem.at[j], near=j
                    )
                )

        near_parts, far_sums = [], []

        def gram_near():
            wait_all(near_parts)
            total = parts[0]
            for j in range(1, place.nears):
                total = total + parts[j]
            sums[place.far] = total
            for k in range(1, place.fars):
                far_sums.append(
                    start_copy(
                        started, place, sums.at[place.far], sums.at[place.far], sum_sem.at[k], far=k
                    )
                )

        def gram_far():
            wait_all(far_sums)
            total = sums[0]
            for k in range(1, place.fars):
                total = total + sums[k]
            kern_out[...] = total

        work = [lend, mix, gram, count_dec, gram_near, count_near, gram_far]
        steps = place.fars + 2
        for k in range(steps):
            gather.step(k)
            share = -(-len(work) // (steps - k))
            for part in work[:share]:
                part()
            work = work[share:]
        gather.end()
        for copy in started:
            copy.wait_send()

    vmem = pl.BlockSpec(memory_space=pltpu.VMEM)
    hbm = pl.BlockSpec(memory_space=pl.ANY)
    dma = pltpu.SemaphoreType.DMA
    struct = jax.ShapeDtypeStruct
    return pl.pallas_call(
        kernel,
        out_shape=tuple(struct((devices, size, width), bf16) for size in sizes)
        + (
            struct((rows, ext), bf16),
            struct((bands, lons, rows), bf16),
            struct((bands, rows, lons), bf16),
            struct((2, rows, wide), bf16),
            struct((halo, rows), bf16),
            struct((rows, 2 * halo), bf16),
            struct((lats, nodes * lats, lanes), f32),
        ),
        in_specs=[vmem] * 12,
        out_specs=(hbm,) * 3 + (vmem,) * 7,
        scratch_shapes=[pltpu.VMEM((size, width), bf16) for size in sizes]
        + [
            pltpu.VMEM((pixels, cin), bf16),
            pltpu.VMEM((nodes, lats, lows, lanes), f32),
            pltpu.VMEM((place.nears, lats, nodes * lats, lanes), f32),
            pltpu.VMEM((place.fars, lats, nodes * lats, lanes), f32),
            dma((nodes, 2)),
            dma((place.nears, 2)),
            dma((place.fars, 2)),
        ]
        + Gather.sems(place, pieces),
        compiler_params=pltpu.CompilerParams(
            collective_id=collective, has_side_effects=True, vmem_limit_bytes=56 << 20
        ),
    )(*weights, grid, scale, g2m, m2g, m2g_turned, neighbours, lent, lent_row, legendre)


def norm_parts(rows):
    centred = rows - jnp.mean(rows, axis=-1, keepdims=True)
    inverse = lax.rsqrt(jnp.mean(centred * centred, axis=-1, keepdims=True) + norm_epsilon)
    return centred * inverse, inverse


def model_step(
    nodes, zeros, weights, graph, kern, feats, base, keep, tables, scalars, first_channel, channels, dec_edges, collective
):
    place = Place(nodes, zeros)
    attn, mlp, small = weights
    near, dec, dec_turned, mixed, lend, lendt = graph
    width = attn.shape[1]
    hidden = mlp.shape[0] // 2
    rows, ext_rows = near.shape
    halo = lend.shape[0]
    bands, lons, _ = dec.shape
    wide = mixed.shape[2]
    lats, all_lats, lanes = kern.shape
    start = first_channel // 128 * 128
    shift = first_channel - start
    sent = sixteens(shift + channels)
    big, tile = 256, 128
    head_width = width // HEAD_COUNT
    score_scale = head_width ** (-0.5)
    third = 1.0 / dec_edges

    def kernel(
        attn_hbm, mlp_hbm, small_ref, near_hbm, dec_hbm, turned_hbm, mixed_ref, lend_ref, lendt_ref, kern_ref,
        feats_ref, base_ref, keep_ref, table_ref, scalar_ref,
        attn_out, mlp_out, high_out, low_out, loss_out,
        attn_ref, mlp_ref, near_ref, dec_ref, turned_ref, h0_ref, h1_ref, first_ref, q_ref, ext_ref, lent_ref,
        prob_ref, blend_ref, second_ref, activ_ref, slope_ref, out_ref, node_ref, f_ref, all_ref, gf_ref, gnet_ref,
        gb_ref, gattn_ref, gblend_ref, gext_ref, back_ref, lost_ref, sums_ref,
        load_sem, lend_sem, f_sem, pass_sem, back_sem,
    ):
        place.locate()
        node = lax.axis_index("node")
        zero = lax.axis_index("zero")
        loads = []
        for index, (source, target) in enumerate(
            (
                (attn_hbm, attn_ref),
                (near_hbm, near_ref),
                (mlp_hbm, mlp_ref),
                (dec_hbm, dec_ref),
                (turned_hbm, turned_ref),
            )
        ):
            copy = pltpu.make_async_copy(source, target, load_sem.at[index])
            copy.start()
            loads.append(copy)
        barrier = pltpu.get_barrier_semaphore()
        for step in range(1, nodes):
            pl.semaphore_signal(
                barrier, 1, device_id=(lax.rem(node + step, nodes), zero), device_id_type=MESH
            )
        started = []

        def to_node(step, source, target, sems):
            copy = pltpu.make_async_remote_copy(
                src_ref=source,
                dst_ref=target,
                send_sem=sems.at[0],
                recv_sem=sems.at[1],
                device_id=(lax.rem(node + step, nodes), zero),
                device_id_type=MESH,
            )
            copy.start()
            started.append(copy)
            return copy

        def row_loop(size, body):
            @pl.loop(0, rows // size)
            def _(index):
                body(pl.ds(pl.multiple_of(index * size, size), size))

        mods = dot_tn(feats_ref[...].astype(bf16), small_ref[...])
        mod = [mods[j : j + 1] for j in range(4)]
        enc = small_ref[pl.ds(0, wide)]
        loads[0].wait()

        def encode(spot):
            h0 = dot_nn(mixed_ref[0, spot], enc) + dot_nn(mixed_ref[1, spot], enc)
            h0_ref[spot] = h0
            unit, inverse = norm_parts(h0)
            first = (unit * (1.0 + mod[0]) + mod[1]).astype(bf16)
            first_ref[spot] = first
            ext_ref[spot] = dot_nt(first, attn_ref[pl.ds(width, 2 * width)]).astype(bf16)
            q_ref[spot] = dot_nt(first, attn_ref[pl.ds(0, width)]).astype(bf16)

        row_loop(big, encode)
        lent_ref[...] = dot_nn(lend_ref[...], ext_ref[pl.ds(0, rows)]).astype(bf16)
        pl.semaphore_wait(barrier, nodes - 1)
        up = to_node(1, lent_ref, ext_ref.at[pl.ds(rows, halo)], lend_sem.at[0])
        down = to_node(nodes - 1, lent_ref, ext_ref.at[pl.ds(rows + halo, halo)], lend_sem.at[1])
        loads[1].wait()
        up.wait_recv()
        down.wait_recv()

        def attend(spot):
            count = near_ref[spot].astype(f32)
            for head in range(HEAD_COUNT):
                part = pl.ds(head * head_width, head_width)
                values = pl.ds(width + head * head_width, head_width)
                logits = dot_nt(q_ref[spot, part], ext_ref[:, part]) * score_scale
                logits = jnp.where(count > 0.0, logits, -jnp.inf)
                raised = jnp.exp(logits - jnp.max(logits, axis=-1, keepdims=True))
                prob = raised * (1.0 / jnp.sum(raised * count, axis=-1, keepdims=True))
                prob = prob.astype(bf16)
                prob_ref[head, spot] = prob
                low = (prob.astype(f32) * count).astype(bf16)
                blend_ref[spot, part] = dot_nn(low, ext_ref[:, values]).astype(bf16)

        row_loop(tile, attend)
        loads[2].wait()
        dec_rows = small_ref[pl.ds(start, 128)]
        lane = iota((1, 128), 1)
        live = jnp.where((lane >= shift) & (lane < shift + channels), 1.0, 0.0)

        def feed(spot):
            h1 = h0_ref[spot] + dot_nt(blend_ref[spot], attn_ref[pl.ds(3 * width, width)])
            h1_ref[spot] = h1
            unit, inverse = norm_parts(h1)
            second = (unit * (1.0 + mod[2]) + mod[3]).astype(bf16)
            second_ref[spot] = second
            upper = dot_nt(second, mlp_ref[pl.ds(0, hidden)])
            square = upper * upper
            bend = jnp.tanh(gelu_scale * upper * (1.0 + gelu_cubic * square))
            half = 0.5 + 0.5 * bend
            activ = (upper * half).astype(bf16)
            activ_ref[spot] = activ
            slope = half + (0.5 * gelu_scale) * upper * (1.0 - bend * bend) * (
                1.0 + 3.0 * gelu_cubic * square
            )
            slope_ref[spot] = slope.astype(bf16)
            h2 = h1 + dot_nn(activ, mlp_ref[pl.ds(hidden, hidden)])
            high = h2.astype(bf16)
            out_ref[spot] = high
            low = (h2 - high.astype(f32)).astype(bf16)
            projected = (dot_nt(high, dec_rows) + dot_nt(low, dec_rows)) * live
            top = projected.astype(bf16)
            node_ref[spot, pl.ds(0, 128)] = top
            node_ref[spot, pl.ds(128, 128)] = (projected - top.astype(f32)).astype(bf16)

        row_loop(tile, feed)

        c_output, weight = scalar_ref[0], scalar_ref[1]
        loads[3].wait()
        cores, uppers = {}, {}
        for band in range(bands):
            net = dot_nn(dec_ref[band], node_ref[...])
            net = (net[:, :128] + net[:, 128:]) * (c_output * third)
            error = (base_ref[band] + net) * keep_ref[band]
            high = error.astype(bf16)
            low = (error - high.astype(f32)).astype(bf16)
            turned = dot_tn(high, table_ref[0]) + dot_tn(low, table_ref[0]) + dot_tn(high, table_ref[1])
            f_ref[band] = turned[:sent]
            all_ref[node, band] = turned[:sent].astype(bf16)
            piece = all_ref.at[node, band]
            cores[0, band] = start_copy(started, place, piece, piece, f_sem.at[0, band], core=1)
            for i in range(1, place.uppers):
                uppers[i, band] = start_copy(started, place, piece, piece, f_sem.at[i, band], upper=i)
        gf_ref[...] = jnp.zeros_like(gf_ref)
        for band in range(bands):
            for i in range(1, place.uppers):
                uppers[i, band].wait_recv()
                source = lax.rem(place.upper + place.uppers - i, place.uppers) * 2 + place.core
                piece = all_ref.at[source, band]
                cores[i, band] = start_copy(started, place, piece, piece, pass_sem.at[i, band], core=1)
        for key in cores:
            cores[key].wait_recv()
        loss_rows = jnp.zeros((8, 128), f32)
        loads[4].wait()
        for band in range(bands):

            def add_lat(index, total):
                return total + kern_ref[band, pl.ds(index, 1)] * all_ref[
                    index // lats, lax.rem(index, lats)
                ].astype(f32)

            total = lax.fori_loop(0, all_lats, add_lat, jnp.zeros((sent, lanes), f32), unroll=4)
            loss_rows = loss_rows + jnp.sum(total * f_ref[band])
            gf_ref[pl.ds(0, sent)] = total * (2.0 * weight)
            grad = gf_ref[...]
            high = grad.astype(bf16)
            low = (grad - high.astype(f32)).astype(bf16)
            back = dot_nt(table_ref[0], high) + dot_nt(table_ref[0], low) + dot_nt(table_ref[1], high)
            gnet_ref[band] = (back * keep_ref[band] * c_output).astype(bf16)
        loss_out[...] = loss_rows * weight

        sums_ref[...] = jnp.zeros_like(sums_ref)

        def back_feed(spot):
            grad_node = dot_nn(turned_ref[0, spot], gnet_ref[0])
            for band in range(1, bands):
                grad_node += dot_nn(turned_ref[band, spot], gnet_ref[band])
            grad_node = grad_node * third
            high = grad_node.astype(bf16)
            low = (grad_node - high.astype(f32)).astype(bf16)
            node_ref[spot, pl.ds(0, 128)] = high
            grad_out = dot_nn(high, dec_rows) + dot_nn(low, dec_rows)
            branch = grad_out.astype(bf16)
            gb_ref[spot] = branch
            grad_activ = dot_nt(branch, mlp_ref[pl.ds(hidden, hidden)])
            grad_upper = (grad_activ * slope_ref[spot].astype(f32)).astype(bf16)
            slope_ref[spot] = grad_upper
            grad_second = dot_nn(grad_upper, mlp_ref[pl.ds(0, hidden)])
            unit, inverse = norm_parts(h1_ref[spot])
            scaled = grad_second * (1.0 + mod[2])
            grad_mid = grad_out + inverse * (
                scaled
                - jnp.mean(scaled, axis=-1, keepdims=True)
                - unit * jnp.mean(scaled * unit, axis=-1, keepdims=True)
            )
            sums_ref[2:3] += jnp.sum(grad_second * unit, axis=0, keepdims=True)
            sums_ref[3:4] += jnp.sum(grad_second, axis=0, keepdims=True)
            h1_ref[spot] = grad_mid
            grad_attn = grad_mid.astype(bf16)
            gattn_ref[spot] = grad_attn
            gblend_ref[spot] = dot_nn(grad_attn, attn_ref[pl.ds(3 * width, width)]).astype(bf16)

        row_loop(tile, back_feed)

        def outer_loop(target, offset, left, right, columns):
            @pl.loop(0, columns // big)
            def _(index):
                part = pl.multiple_of(index * big, big)
                product = dot_tn(left[:, pl.ds(part, big)], right[...])
                target[pl.ds(pl.multiple_of(offset + part, big), big)] = product.astype(bf16)

        gext_ref[...] = jnp.zeros_like(gext_ref)

        def back_attend(spot):
            count = near_ref[spot].astype(f32)
            for head in range(HEAD_COUNT):
                part = pl.ds(head * head_width, head_width)
                values = pl.ds(width + head * head_width, head_width)
                prob = prob_ref[head, spot].astype(f32)
                counted_prob = prob * count
                grad_blend = gblend_ref[spot, part]
                grad_prob = dot_nt(grad_blend, ext_ref[:, values])
                mean = jnp.sum(counted_prob * grad_prob, axis=-1, keepdims=True)
                grad_logit = (counted_prob * (grad_prob - mean)).astype(bf16)
                gext_ref[:, part] += dot_tn(grad_logit, q_ref[spot, part])
                q_ref[spot, part] = (dot_nn(grad_logit, ext_ref[:, part]) * score_scale).astype(bf16)
                gext_ref[:, values] += dot_tn(counted_prob.astype(bf16), grad_blend)

        row_loop(tile, back_attend)
        gext_ref[:, pl.ds(0, width)] = gext_ref[:, pl.ds(0, width)] * score_scale
        lost_ref[0] = gext_ref[pl.ds(rows, halo)].astype(bf16)
        lost_ref[1] = gext_ref[pl.ds(rows + halo, halo)].astype(bf16)
        from_upper = to_node(nodes - 1, lost_ref.at[0], back_ref.at[pl.ds(0, halo)], back_sem.at[0])
        from_lower = to_node(1, lost_ref.at[1], back_ref.at[pl.ds(halo, halo)], back_sem.at[1])

        outer_loop(mlp_out, hidden, activ_ref, gb_ref, hidden)
        outer_loop(mlp_out, 0, slope_ref, second_ref, hidden)
        outer_loop(attn_out, 3 * width, gattn_ref, blend_ref, width)
        outer_loop(attn_out, 0, q_ref, first_ref, width)
        from_upper.wait_recv()
        from_lower.wait_recv()

        def back_encode(spot):
            grad_pairs = gext_ref[spot] + dot_nn(lendt_ref[spot], back_ref[...])
            grad_pairs = grad_pairs.astype(bf16)
            ext_ref[spot] = grad_pairs
            grad_first = dot_nn(q_ref[spot], attn_ref[pl.ds(0, width)]) + dot_nn(
                grad_pairs, attn_ref[pl.ds(width, 2 * width)]
            )
            unit, inverse = norm_parts(h0_ref[spot])
            scaled = grad_first * (1.0 + mod[0])
            grad_in = h1_ref[spot] + inverse * (
                scaled
                - jnp.mean(scaled, axis=-1, keepdims=True)
                - unit * jnp.mean(scaled * unit, axis=-1, keepdims=True)
            )
            sums_ref[0:1] += jnp.sum(grad_first * unit, axis=0, keepdims=True)
            sums_ref[1:2] += jnp.sum(grad_first, axis=0, keepdims=True)
            gb_ref[spot] = grad_in.astype(bf16)

        row_loop(big, back_encode)
        outer_loop(attn_out, width, ext_ref.at[pl.ds(0, rows)], first_ref, 2 * width)

        feats_value = feats_ref[...]
        small_rows = small_ref.shape[0]
        cond = feats_value[:, 0:1] * sums_ref[0:1]
        for j in range(1, 4):
            cond += feats_value[:, j : j + 1] * sums_ref[j : j + 1]
        for low_row in range(0, small_rows, 128):
            total = cond[low_row : low_row + 128]
            if low_row < wide:
                total += dot_tn(mixed_ref[0, :, pl.ds(low_row, 128)], gb_ref[...])
            if low_row == start:
                total += dot_tn(node_ref[:, pl.ds(0, 128)], out_ref[...])
            high = total.astype(bf16)
            high_out[pl.ds(low_row, 128)] = high
            low_out[pl.ds(low_row, 128)] = (total - high.astype(f32)).astype(bf16)
        for copy in started:
            copy.wait_send()

    vmem = pl.BlockSpec(memory_space=pltpu.VMEM)
    hbm = pl.BlockSpec(memory_space=pl.ANY)
    dma = pltpu.SemaphoreType.DMA
    struct = jax.ShapeDtypeStruct
    low = lambda *shape: pltpu.VMEM(shape, bf16)
    full = lambda *shape: pltpu.VMEM(shape, f32)
    return pl.pallas_call(
        kernel,
        out_shape=(
            struct(attn.shape, bf16),
            struct(mlp.shape, bf16),
            struct(small.shape, bf16),
            struct(small.shape, bf16),
            struct((8, 128), f32),
        ),
        in_specs=[hbm, hbm, vmem, hbm, hbm, hbm] + [vmem] * 8 + [pl.BlockSpec(memory_space=pltpu.SMEM)],
        out_specs=(vmem,) * 5,
        scratch_shapes=[
            low(*attn.shape),
            low(*mlp.shape),
            low(*near.shape),
            low(*dec.shape),
            low(*dec_turned.shape),
            full(rows, width),
            full(rows, width),
            low(rows, width),
            low(rows, width),
            low(ext_rows, 2 * width),
            low(halo, 2 * width),
            low(HEAD_COUNT, rows, ext_rows),
            low(rows, width),
            low(rows, width),
            low(rows, hidden),
            low(rows, hidden),
            low(rows, width),
            low(rows, 256),
            full(lats, sent, lanes),
            low(nodes, lats, sent, lanes),
            full(128, lanes),
            low(bands, lons, 128),
            low(rows, width),
            low(rows, width),
            low(rows, width),
            full(ext_rows, 2 * width),
            low(2 * halo, 2 * width),
            low(2, halo, 2 * width),
            full(8, width),
            dma((5,)),
            dma((2, 2)),
            dma((place.uppers, lats, 2)),
            dma((place.uppers, lats, 2)),
            dma((2, 2)),
        ],
        compiler_params=pltpu.CompilerParams(
            collective_id=collective, has_side_effects=True, vmem_limit_bytes=62 << 20
        ),
    )(attn, mlp, small, near, dec, dec_turned, mixed, lend, lendt, kern, feats, base, keep, tables, scalars)


class Scatter:
    def __init__(self, place, pieces, grads, bufs, sems):
        self.place, self.pieces, self.grads = place, pieces, grads
        count = len(grads)
        self.core_in = bufs[:count]
        (self.over_out, self.over_in, self.under_out, self.under_in, self.over_out2, self.over_in2,
         self.under_out2, self.under_in2, self.far_out, self.far_in) = bufs[count:]
        (self.core_sem, self.over_sem, self.under_sem, self.over_sem2, self.under_sem2, self.far_sem) = sems
        self.started = []
        self.order = list(range(1, place.fars)) + [0]
        self.core, self.over, self.under, self.over2, self.under2, self.far = {}, {}, {}, {}, {}, {}
        self.head_rows = sum(rows for _, _, rows in pieces.head)
        self.tail_rows = sum(rows for _, _, rows in pieces.tail)

    def send(self, source, target, sem, **steps):
        return start_copy(self.started, self.place, source, target, sem, **steps)

    def begin(self, arrays):
        place = self.place
        other = 1 - place.core
        for k in self.order:
            far = place.moved(far=k)[2]
            for upper in range(place.uppers):
                for near in range(place.nears):
                    slot = place.slot(upper, other, far, near)
                    for a in arrays:
                        self.core[k, upper, near, a] = self.send(
                            self.grads[a].at[slot], self.core_in[a].at[k, upper, near],
                            self.core_sem.at[k, upper, near, a], core=1,
                        )

    def add(self, target, k, upper, near, pieces, others):
        far = self.place.moved(far=k)[2]
        slot = self.place.slot(upper, self.place.core, far, near)
        offset = 0
        for array, start, rows in pieces:
            mine = self.grads[array].at[slot]
            theirs = self.core_in[array].at[k, upper, near]

            @pl.loop(0, rows // ROW_CHUNK)
            def _(index, start=start, offset=offset, mine=mine, theirs=theirs):
                step = index * ROW_CHUNK
                here = pl.ds(pl.multiple_of(start + step, ROW_CHUNK), ROW_CHUNK)
                there = pl.ds(pl.multiple_of(offset + step, ROW_CHUNK), ROW_CHUNK)
                total = mine[here].astype(f32) + theirs[here].astype(f32)
                for other in others:
                    total += other[there].astype(f32)
                target[there] = total.astype(target.dtype)

            offset += rows

    def one(self, k):
        place, pieces = self.place, self.pieces
        for key in self.core:
            if key[0] == k:
                self.core[key].wait_recv()
        for i in range(1, place.uppers):
            for near in range(place.nears):
                self.add(self.over_out.at[k, i - 1, near], k, place.moved(upper=i)[0], near, pieces.head, [])
            self.over[k, i] = self.send(
                self.over_out.at[k, i - 1], self.over_in.at[k, i - 1], self.over_sem.at[k, i], upper=i
            )
        for j in range(1, place.nears):
            for upper in range(place.uppers):
                self.add(self.under_out.at[k, j - 1, upper], k, upper, place.moved(near=j)[3], pieces.tail, [])
            self.under[k, j] = self.send(
                self.under_out.at[k, j - 1], self.under_in.at[k, j - 1], self.under_sem.at[k, j], near=j
            )

    def overs(self, k, near):
        return [self.over_in.at[k, i - 1, near] for i in range(1, self.place.uppers)]

    def unders(self, k, upper):
        return [self.under_in.at[k, j - 1, upper] for j in range(1, self.place.nears)]

    def two(self, k):
        place, pieces = self.place, self.pieces
        for i in range(1, place.uppers):
            self.over[k, i].wait_recv()
        for j in range(1, place.nears):
            near = place.moved(near=j)[3]
            self.add(self.over_out2.at[k, j - 1], k, place.upper, near, pieces.head, self.overs(k, near))
            self.over2[k, j] = self.send(
                self.over_out2.at[k, j - 1], self.over_in2.at[k, j - 1], self.over_sem2.at[k, j], near=j
            )
        for j in range(1, place.nears):
            self.under[k, j].wait_recv()
        for i in range(1, place.uppers):
            upper = place.moved(upper=i)[0]
            self.add(self.under_out2.at[k, i - 1], k, upper, place.near, pieces.tail, self.unders(k, upper))
            self.under2[k, i] = self.send(
                self.under_out2.at[k, i - 1], self.under_in2.at[k, i - 1], self.under_sem2.at[k, i], upper=i
            )

    def three(self, k, target, extra):
        place, pieces = self.place, self.pieces
        for j in range(1, place.nears):
            self.over2[k, j].wait_recv()
        for i in range(1, place.uppers):
            self.under2[k, i].wait_recv()
        head, tail = pl.ds(0, self.head_rows), pl.ds(self.head_rows, self.tail_rows)
        self.add(
            target.at[head], k, place.upper, place.near, pieces.head,
            self.overs(k, place.near)
            + [self.over_in2.at[k, j - 1] for j in range(1, place.nears)]
            + [item.at[head] for item in extra],
        )
        self.add(
            target.at[tail], k, place.upper, place.near, pieces.tail,
            self.unders(k, place.upper)
            + [self.under_in2.at[k, i - 1] for i in range(1, place.uppers)]
            + [item.at[tail] for item in extra],
        )

    def step(self, step):
        fars, order = self.place.fars, self.order
        if step < fars:
            self.one(order[step])
        if 1 <= step <= fars:
            self.two(order[step - 1])
        if step >= 2 and order[step - 2]:
            k = order[step - 2]
            self.three(k, self.far_out.at[k - 1], [])
            self.far[k] = self.send(self.far_out.at[k - 1], self.far_in.at[k - 1], self.far_sem.at[k], far=k)

    def steps(self):
        return self.place.fars + 2

    def finish(self, own):
        fars = self.place.fars
        for k in range(1, fars):
            self.far[k].wait_recv()
        self.three(0, own, [self.far_in.at[k - 1] for k in range(1, fars)])

    def end(self):
        for copy in self.started:
            copy.wait_send()

    @staticmethod
    def copies(place, pieces):
        fars, nears, uppers = place.fars, place.nears, place.uppers
        return fars * uppers * nears * len(pieces.sizes) + 2 * fars * (uppers + nears - 2) + fars - 1

    @staticmethod
    def scratch(place, pieces, width):
        fars, nears, uppers = place.fars, place.nears, place.uppers
        head = sum(rows for _, _, rows in pieces.head)
        tail = sum(rows for _, _, rows in pieces.tail)
        dma = pltpu.SemaphoreType.DMA
        bufs = [(fars, uppers, nears, size) for size in pieces.sizes]
        bufs += [(fars, uppers - 1, nears, head)] * 2
        bufs += [(fars, nears - 1, uppers, tail)] * 2
        bufs += [(fars, nears - 1, head)] * 2
        bufs += [(fars, uppers - 1, tail)] * 2
        bufs += [(fars - 1, head + tail)] * 2
        if width:
            bufs = [pltpu.VMEM(shape + (width,), bf16) for shape in bufs]
        sems = [
            dma((fars, uppers, nears, len(pieces.sizes), 2)),
            dma((fars, uppers, 2)),
            dma((fars, nears, 2)),
            dma((fars, nears, 2)),
            dma((fars, uppers, 2)),
            dma((fars, 2)),
        ]
        return bufs, sems


class Strip:
    def __init__(self, ref, first, dims):
        self.ref, self.first, self.dims, self.at = ref, first, dims, self

    def __getitem__(self, index):
        index = index if isinstance(index, tuple) else (index,)
        sizes = self.dims[1:]
        flat, rows = 0, 1
        for axis, size in enumerate(sizes):
            if axis + 1 < len(index):
                flat = flat * size + index[axis + 1]
            else:
                flat, rows = flat * size, rows * size
        return self.ref.at[index[0], pl.ds(self.first + flat, rows)]


def strips(refs, shapes):
    result, at, first = [], 0, 0
    for shape in shapes:
        rows = math.prod(shape[1:])
        if first + rows > refs[at].shape[1]:
            at, first = at + 1, 0
        result.append(Strip(refs[at], first, shape))
        first += rows
    return result


class HalfGather:
    def __init__(self, place, shard, out, sems):
        self.place, self.shard, self.out = place, shard, out
        self.own_sem, self.far_sem, self.near_sem, self.mate_sem, self.core_sem = sems
        self.started, self.cores = [], []
        self.far, self.near, self.mate = {}, {}, {}

    def block(self, **steps):
        return self.out.at[self.place.slot(*self.place.moved(**steps))]

    def send(self, source, target, sem, **steps):
        return start_copy(self.started, self.place, source, target, sem, **steps)

    def begin(self):
        self.kept = pltpu.make_async_copy(self.shard, self.block(), self.own_sem)
        self.kept.start()
        for k in range(1, self.place.fars):
            self.far[k] = self.send(self.shard, self.block(), self.far_sem.at[k], far=k)

    def spread(self, k, j, source, target):
        for i in range(1, self.place.mates):
            self.mate[k, j, i] = self.send(source, target, self.mate_sem.at[k, j, i], mate=i)
        self.cores.append(self.send(source, target, self.core_sem.at[k, j, 0], core=1))

    def step(self, step):
        place = self.place
        fars, nears = place.fars, place.nears
        if step < fars:
            if step:
                self.far[step].wait_recv()
            target = self.block(far=(fars - step) % fars)
            source = target if step else self.shard
            for j in range(1, nears):
                self.near[step, j] = self.send(source, target, self.near_sem.at[step, j], near=j)
            self.spread(step, 0, source, target)
        if 1 <= step <= fars:
            k = step - 1
            for j in range(1, nears):
                self.near[k, j].wait_recv()
                item = self.block(far=(fars - k) % fars, near=nears - j)
                self.spread(k, j, item, item)
        if step >= 2:
            k = step - 2
            for j in range(nears):
                for i in range(1, place.mates):
                    self.mate[k, j, i].wait_recv()
                    item = self.block(far=(fars - k) % fars, near=(nears - j) % nears, mate=place.mates - i)
                    self.cores.append(self.send(item, item, self.core_sem.at[k, j, i], core=1))

    def end(self):
        self.kept.wait()
        wait_all(self.cores)
        for copy in self.started:
            copy.wait_send()

    @staticmethod
    def copies(place):
        fars, nears, mates = place.fars, place.nears, place.mates
        return (fars - 1) + fars * (nears - 1) + fars * nears * (mates - 1) + fars * nears * mates

    @staticmethod
    def sems(place):
        dma = pltpu.SemaphoreType.DMA
        fars, nears, mates = place.fars, place.nears, place.mates
        return [
            dma,
            dma((fars, 2)),
            dma((fars, nears, 2)),
            dma((fars, nears, mates, 2)),
            dma((fars, nears, mates, 2)),
        ]


class MomentGather:
    def __init__(self, place, shards, outs, sems):
        self.place, self.shards, self.outs = place, shards, outs
        (self.own_sem, self.far_sem, self.near_sem, self.spread_sem, self.core_sem) = sems
        self.started, self.cores = [], []
        self.far, self.near, self.spread_copies = {}, {}, {}

    def block(self, **steps):
        slot = self.place.slot(*self.place.moved(**steps))
        return [out.at[slot] for out in self.outs]

    def send(self, source, target, sem, **steps):
        return start_copy(self.started, self.place, source, target, sem, **steps)

    def both(self, source, target, sems, **steps):
        return [self.send(source[a], target[a], sems.at[a], **steps) for a in range(2)]

    def spread(self, k, j, source, target):
        place = self.place
        for i in range(1, place.uppers):
            self.spread_copies[k, j, i, 0] = self.send(
                source[0], target[0], self.spread_sem.at[k, j, i, 0], upper=i
            )
        for i in range(1, place.mates):
            self.spread_copies[k, j, i, 1] = self.send(
                source[1], target[1], self.spread_sem.at[k, j, i, 1], mate=i
            )
        self.cores += self.both(source, target, self.core_sem.at[k, j, 0], core=1)

    def run(self):
        place = self.place
        fars, nears = place.fars, place.nears
        here = self.block()
        kept = [
            pltpu.make_async_copy(shard, target, self.own_sem.at[a])
            for a, (shard, target) in enumerate(zip(self.shards, here))
        ]
        for copy in kept:
            copy.start()
        for k in range(1, fars):
            self.far[k] = self.both(self.shards, here, self.far_sem.at[k], far=k)
        for step in range(fars + 2):
            if step < fars:
                k = step
                if k:
                    wait_all(self.far[k])
                target = self.block(far=(fars - k) % fars)
                source = target if k else self.shards
                for j in range(1, nears):
                    self.near[k, j] = self.both(source, target, self.near_sem.at[k, j], near=j)
                self.spread(k, 0, source, target)
            if 1 <= step <= fars:
                k = step - 1
                for j in range(1, nears):
                    wait_all(self.near[k, j])
                    item = self.block(far=(fars - k) % fars, near=nears - j)
                    self.spread(k, j, item, item)
            if step >= 2:
                k = step - 2
                for j in range(nears):
                    steps = dict(far=(fars - k) % fars, near=(nears - j) % nears)
                    for key in self.spread_copies:
                        if key[:2] != (k, j):
                            continue
                        i, a = key[2:]
                        self.spread_copies[key].wait_recv()
                        if a:
                            item = self.block(mate=place.mates - i, **steps)[1]
                        else:
                            item = self.block(upper=place.uppers - i, **steps)[0]
                        self.cores.append(self.send(item, item, self.core_sem.at[k, j, i, a], core=1))
        for copy in kept:
            copy.wait()
        wait_all(self.cores)
        for copy in self.started:
            copy.wait_send()

    @staticmethod
    def sems(place):
        dma = pltpu.SemaphoreType.DMA
        fars, nears, uppers = place.fars, place.nears, place.uppers
        return [
            dma((2,)),
            dma((fars, 2, 2)),
            dma((fars, nears, 2, 2)),
            dma((fars, nears, uppers, 2, 2)),
            dma((fars, nears, uppers, 2, 2)),
        ]


def total_body(place, tile, slots, sems):
    value = tile
    upper, core, far, near = place.moved()
    stages = (
        ("core", 2, core),
        ("near", place.nears, near),
        ("upper", place.uppers, upper),
        ("far", place.fars, far),
    )
    for stage, (name, size, mine) in enumerate(stages):
        slots[stage, mine] = value
        copies = []
        for step in range(1, size):
            piece = slots.at[stage, mine]
            start_copy(copies, place, piece, piece, sems.at[stage, step], **{name: step})
        for copy in copies:
            copy.wait()
        value = slots[stage, 0]
        for other in range(1, size):
            value = value + slots[stage, other]
    return value


def reduce_and_gather(nodes, zeros, names, grads, mlp_sum, loss_tile, mom_attn, mom_mlp, small_rows, collective):
    place = Place(nodes, zeros)
    devices, _, width = grads[0].shape
    attn_rows, mlp_rows = mom_attn.shape[0], mom_mlp.shape[0]
    lead = names.index("mlp") if "mlp" in names else 0
    pieces = Pieces([item.shape[1] for item in grads], lead)
    moment_sizes = (sixteens(attn_rows), sixteens(mlp_rows))
    bufs, sems = Scatter.scratch(place, pieces, width)
    deepest = max(place.fars, place.uppers, place.nears, 2)
    summed = [] if mlp_sum is None else [mlp_sum]
    count = len(grads)
    starts, offset = {}, 0
    for array in [lead] + [i for i in range(count) if i != lead]:
        starts[names[array]] = offset
        offset += pieces.sizes[array]

    def kernel(*refs):
        grad_refs = refs[:count]
        refs = refs[count:]
        if summed:
            sum_ref, *refs = refs
        loss_ref, attn_ref, mlp_ref = refs[:3]
        small_out, attn_out, mlp_out, total_out, attn_all, mlp_all = refs[3:9]
        own, attn_shard, mlp_shard, slots, slot_sems = refs[9:14]
        rest = refs[14:]
        place.locate()
        place.greet()
        scatter = Scatter(
            place, pieces, grad_refs, rest[: len(bufs)], rest[len(bufs) : len(bufs) + len(sems)]
        )
        scatter.begin([lead] + [i for i in range(count) if i != lead])
        for step in range(scatter.steps()):
            scatter.step(step)
        scatter.finish(own)
        g_attn = own[pl.ds(starts["attn"], attn_rows)]
        g_mlp = sum_ref[...] if summed else own[pl.ds(starts["mlp"], mlp_rows)]
        g_small = own[pl.ds(starts["high"], small_rows)] + own[pl.ds(starts["low"], small_rows)]
        small_out[...] = g_small
        squares = jnp.sum(g_attn * g_attn) + jnp.sum(g_mlp * g_mlp) + jnp.sum(g_small * g_small)
        tile = jnp.where(iota((8, 128), 0) < 4, squares, loss_ref[...])
        total = total_body(place, tile, slots, slot_sems)
        total_out[...] = total
        factor = jnp.minimum(1.0, clip_limit * lax.rsqrt(total[0:1, 0:1]))
        for ref, out, shard, grad, size in (
            (attn_ref, attn_out, attn_shard, g_attn, attn_rows),
            (mlp_ref, mlp_out, mlp_shard, g_mlp, mlp_rows),
        ):
            moment = moment_decay * ref[...] + factor * grad
            out[...] = moment
            if size < shard.shape[0]:
                shard[...] = jnp.zeros_like(shard)
            shard[pl.ds(0, size)] = moment.astype(bf16)
        moments = MomentGather(
            place, (attn_shard, mlp_shard), (attn_all, mlp_all), rest[len(bufs) + len(sems) :]
        )
        moments.run()
        scatter.end()

    vmem = pl.BlockSpec(memory_space=pltpu.VMEM)
    hbm = pl.BlockSpec(memory_space=pl.ANY)
    struct = jax.ShapeDtypeStruct
    return pl.pallas_call(
        kernel,
        out_shape=(
            struct((small_rows, width), f32),
            struct((attn_rows, width), f32),
            struct((mlp_rows, width), f32),
            struct((8, 128), f32),
            struct((devices, moment_sizes[0], width), bf16),
            struct((devices, moment_sizes[1], width), bf16),
        ),
        in_specs=[vmem] * (count + len(summed) + 3),
        out_specs=(vmem,) * 4 + (hbm,) * 2,
        scratch_shapes=[
            pltpu.VMEM((sum(pieces.sizes), width), f32),
            pltpu.VMEM((moment_sizes[0], width), bf16),
            pltpu.VMEM((moment_sizes[1], width), bf16),
            pltpu.VMEM((4, deepest, 8, 128), f32),
            pltpu.SemaphoreType.DMA((4, deepest, 2)),
        ]
        + bufs
        + sems
        + MomentGather.sems(place),
        compiler_params=pltpu.CompilerParams(
            collective_id=collective, has_side_effects=True, vmem_limit_bytes=56 << 20
        ),
    )(*grads, *summed, loss_tile, mom_attn, mom_mlp)


def basis_apply(grams, moments):
    size = grams[0].shape[0]
    eye = jnp.where(iota((size, size), 0) == iota((size, size), 1), 1.0, 0.0)
    both = range(len(grams))
    scales = [
        lax.rsqrt(jnp.sum(jnp.sum(gram * eye, axis=1, keepdims=True), axis=0, keepdims=True) + trace_epsilon)
        for gram in grams
    ]
    current = [grams[i] * (scales[i] * scales[i]) for i in both]
    result = [moments[i] * scales[i] for i in both]
    for iteration in range(NS_ITERS - 1):
        low = [current[i].astype(bf16) for i in both]
        rest = [newton_second * current[i] + newton_third * dot_nn(low[i], low[i]) for i in both]
        rest = [item.astype(bf16) for item in rest]
        once = [dot_nn(rest[i], low[i]) for i in both]
        result = [newton_first * result[i] + dot_nn(result[i].astype(bf16), rest[i]) for i in both]
        current = [
            (newton_first * newton_first) * current[i]
            + (2.0 * newton_first) * once[i]
            + dot_nn(once[i].astype(bf16), rest[i])
            for i in both
        ]
    low = [current[i].astype(bf16) for i in both]
    once = [dot_nn(result[i].astype(bf16), low[i]) for i in both]
    twice = [dot_nn(once[i].astype(bf16), low[i]) for i in both]
    return [newton_first * result[i] + newton_second * once[i] + newton_third * twice[i] for i in both]


def update_weights(nodes, zeros, attn_sets, mlp_sets, totals, sums, moments, weights, averages, small_moments):
    width = attn_sets[0].shape[1]
    attn_rows, mlp_rows, small_rows = [w.shape[0] for w in weights]
    half = mlp_sets[0].shape[0] // 2
    block = width
    inputs = (*sums, *moments, *weights, *averages, *small_moments)
    count, sets = len(inputs), len(attn_sets)
    fresh = sets == 1

    def kernel(total_ref, *refs):
        attn_hbm, mlp_hbm, sources = refs[:sets], refs[sets : 2 * sets], refs[2 * sets : 2 * sets + count]
        refs = refs[2 * sets + count :]
        loss_out, clip_out, new_attn, new_mlp, new_small, new_m, new_v, new_e_attn, new_e_mlp, new_e_small = refs[:10]
        mom_attn_out, mom_mlp_out = refs[10:12]
        gram_attn, gram_mlp, attn_sem, mlp_sem, row_sem = refs[12:17]
        attn_refs, mlp_refs, rows = refs[17 : 17 + sets], refs[17 + sets : 17 + 2 * sets], refs[17 + 2 * sets :]
        g_refs, rows = rows[: len(sums)], rows[len(sums) :]
        mom_attn, mom_mlp, w_attn, w_mlp, w_small, e_attn, e_mlp, e_small, m_ref, v_ref = rows
        flat = lax.axis_index("node") * zeros + lax.axis_index("zero")
        attn_upper = flat * attn_rows >= 3 * width
        mlp_upper = flat * mlp_rows >= half
        first_row = jnp.where(mlp_upper, half, 0)
        copies_mlp = [
            pltpu.make_async_copy(
                mlp_hbm[i].at[pl.ds(pl.multiple_of(first_row + low, block), block)],
                mlp_refs[i].at[pl.ds(low, block)],
                mlp_sem.at[low // block, i],
            )
            for low in range(0, half, block)
            for i in range(sets)
        ]
        copies_attn = [
            pltpu.make_async_copy(attn_hbm[i], attn_refs[i], attn_sem.at[i]) for i in range(sets)
        ]
        copies = [
            pltpu.make_async_copy(source, target, row_sem.at[index])
            for index, (source, target) in enumerate(zip(sources, refs[17 + 2 * sets :]))
        ]
        for copy in copies_mlp + copies_attn + copies:
            copy.start()
        total = total_ref[0]
        for index in range(1, total_ref.shape[0]):
            total = total + total_ref[index]
        loss_out[...] = total[4:5, 0:1]
        clip_out[...] = jnp.sqrt(total[0:1, 0:1])
        factor = jnp.minimum(1.0, clip_limit * lax.rsqrt(total[0:1, 0:1]))

        def momentum(refs, index):
            part = pl.ds(index * block if isinstance(index, int) else pl.multiple_of(index * block, block), block)
            if fresh:
                return refs[0][part]
            return (moment_decay * refs[0][part].astype(f32) + factor * refs[1][part].astype(f32)).astype(bf16)

        for index in range(half // block):
            for copy in copies_mlp[index * sets : (index + 1) * sets]:
                copy.wait()
            part = momentum(mlp_refs, index)
            if index:
                gram_mlp[...] += dot_tn(part, part)
            else:
                gram_mlp[...] = dot_tn(part, part)

        for copy in copies_attn:
            copy.wait()
        gram_attn[...] = jnp.zeros_like(gram_attn)
        start = jnp.where(attn_upper, 3, 0)

        @pl.loop(start, jnp.where(attn_upper, 4, 3))
        def _(index):
            part = momentum(attn_refs, index)
            gram_attn[...] += dot_tn(part, part)

        for copy in copies:
            copy.wait()

        clipped = factor * g_refs[0][...]
        first = adam_first * m_ref[...] + (1.0 - adam_first) * clipped
        second = adam_second * v_ref[...] + (1.0 - adam_second) * clipped * clipped
        new_m[...] = first
        new_v[...] = second
        small = w_small[...] - adam_rate * (first / (1.0 - adam_first**STEP)) / (
            jnp.sqrt(second / (1.0 - adam_second**STEP)) + adam_epsilon
        )
        new_small[...] = small
        new_e_small[...] = average_decay * e_small[...] + (1.0 - average_decay) * small

        attn_moment, mlp_moment = mom_attn[...], mom_mlp[...]
        if not fresh:
            attn_moment = moment_decay * attn_moment + factor * g_refs[1][...]
            mlp_moment = moment_decay * mlp_moment + factor * g_refs[2][...]
        mom_attn_out[...] = attn_moment
        mom_mlp_out[...] = mlp_moment
        attn_step, mlp_step = basis_apply((gram_attn[...], gram_mlp[...]), (attn_moment, mlp_moment))
        attn_factor = jnp.where(attn_upper, 0.2 * math.sqrt(width), 0.2 * math.sqrt(3 * width))
        mlp_factor = 0.2 * math.sqrt(max(half, width))
        for step, rate, old, new, mean, new_mean in (
            (attn_step, orthogonal_rate * attn_factor, w_attn, new_attn, e_attn, new_e_attn),
            (mlp_step, orthogonal_rate * mlp_factor, w_mlp, new_mlp, e_mlp, new_e_mlp),
        ):
            value = old[...] - rate * step
            new[...] = value
            new_mean[...] = average_decay * mean[...] + (1.0 - average_decay) * value

    vmem = pl.BlockSpec(memory_space=pltpu.VMEM)
    hbm = pl.BlockSpec(memory_space=pl.ANY)
    one = jnp.zeros((1, 1), f32)
    outs = [one, one, weights[0], weights[1], weights[2], weights[2], weights[2], weights[0], weights[1], weights[2]]
    outs += [weights[0], weights[1]]
    dma = pltpu.SemaphoreType.DMA
    return pl.pallas_call(
        kernel,
        out_shape=tuple(jax.ShapeDtypeStruct(item.shape, f32) for item in outs),
        in_specs=[vmem] + [hbm] * (2 * sets + count),
        out_specs=(vmem,) * 12,
        scratch_shapes=[
            pltpu.VMEM((width, width), f32),
            pltpu.VMEM((width, width), f32),
            dma((sets,)),
            dma((half // block, sets)),
            dma((count,)),
        ]
        + [pltpu.VMEM(attn_sets[0].shape, bf16)] * sets
        + [pltpu.VMEM((half, width), bf16)] * sets
        + [pltpu.VMEM(item.shape, f32) for item in inputs],
        compiler_params=pltpu.CompilerParams(vmem_limit_bytes=62 << 20),
    )(totals, *attn_sets, *mlp_sets, *inputs)


def train_step(nodes, zeros, weights, grid, target, land, near_turned, enc_turned, dec_turned, lent, legendre, vector, tables, waves, moments, cin, collective):
    place = Place(nodes, zeros)
    devices = nodes * zeros
    attn_rows, mlp_rows, small_rows = [w.shape[0] for w in weights]
    width = weights[0].shape[1]
    hidden = devices * mlp_rows // 2
    bands, lons, channels = target.shape
    fanout, rows = near_turned.shape
    enc_edges, dec_edges = enc_turned.shape[0], dec_turned.shape[0]
    halo = lent.shape[1]
    ext_rows = rows + 2 * halo
    lats, lows, flat = legendre.shape
    lanes = tables.shape[2]
    modes, wave_first, wave_end = waves
    all_lats = nodes * lats
    wide = -(-cin // 128) * 128
    start = cin // 128 * 128
    shift = cin - start
    sent = sixteens(channels)
    flat_lons = -(-lons // 128) * 128
    flat_pixels = -(-bands * lons // 128) * 128
    all_small = devices * small_rows
    cond_start = cin + channels
    big, tile, chunk = 256, 128, 512
    head_width = width // HEAD_COUNT
    score_scale = head_width ** (-0.5)
    third = 1.0 / dec_edges
    first_rows = attn_rows + small_rows
    packed_rows = first_rows + small_rows
    first_pieces = Pieces([first_rows], 0)
    mlp_pieces = Pieces([mlp_rows], 0)
    mlp_sum_pieces = Pieces([mlp_rows], 0, 5 / 8)
    last_pieces = Pieces([packed_rows], 0, 2 / 3)
    attn_pieces = Pieces([attn_rows], 0)
    tile_pieces = Pieces([attn_rows, 8], 0)
    scatter_bufs, _ = Scatter.scratch(place, mlp_sum_pieces, width)
    last_shapes, _ = Scatter.scratch(place, last_pieces, 0)
    early_copies = Gather.copies(place, first_pieces) + Gather.copies(place, mlp_pieces)
    middle_copies = Gather.copies(place, attn_pieces) + HalfGather.copies(place)
    late_copies = (
        Gather.copies(place, tile_pieces)
        + HalfGather.copies(place)
        + Scatter.copies(place, mlp_sum_pieces)
        + Scatter.copies(place, last_pieces)
    )
    others = (nodes - 1) + (place.nears - 1) + (place.fars - 1) + 4 + (2 * place.uppers - 1) * lats
    copies = early_copies + middle_copies + late_copies + others

    def kernel(
        attn_in, mlp_in, small_in, grid_ref, target_ref, land_ref, near_in, enc_in, dec_in, lent_ref, leg_ref,
        vector_ref, table_ref, mom_attn_in, mom_mlp_in,
        attn_sum, mlp_sum, small_sum, tiles_out, mom_attn_all, mom_mlp_all, g_attn_all, g_mlp_all,
        own, mom_attn_shard, mom_mlp_shard, g_attn_shard, g_mlp_shard, tile_shard,
        first_shard, mlp_shard, legs, parts, sums, kern_ref,
        packed_ref, mlp_ref, near_ref, dec_ref, mixed_ref, lendt_ref, h0_ref, h1_ref, first_ref, q_ref,
        ext_ref, lent_rows, prob_ref, blend_ref, second_ref, activ_ref, slope_ref, out_ref, node_ref, all_ref,
        gf_ref, gnet_ref, gnode_ref, gb_ref, gattn_ref, gblend_ref, gext_ref, back_ref, lost_ref, sums_ref,
        scale_ref, error_ref, column_ref, lists_ref, input_ref, dec_rows_ref, feats_ref,
        pool_ref, own_sem,
        *bufs,
    ):
        pool = Pool(pool_ref)
        place.locate()
        node = lax.axis_index("node")
        zero = lax.axis_index("zero")
        first_shard[pl.ds(0, attn_rows)] = attn_in[...].astype(bf16)
        first_shard[pl.ds(attn_rows, small_rows)] = small_in[...].astype(bf16)
        legs[node] = leg_ref[...]
        place.greet(nodes)
        gather = Gather(place, first_pieces, (first_shard,), (packed_ref,), pool.gather(own_sem, 0))
        gather_mlp = Gather(place, mlp_pieces, (mlp_shard,), (mlp_ref,), pool.gather(own_sem, 1))
        gather.begin()
        started = []

        def to_node(step, source, target):
            sems = pool.take()
            copy = pltpu.make_async_remote_copy(
                src_ref=source,
                dst_ref=target,
                send_sem=sems.at[0],
                recv_sem=sems.at[1],
                device_id=(lax.rem(node + step, nodes), zero),
                device_id_type=MESH,
            )
            copy.start()
            started.append(copy)
            return copy

        gather.step(0)
        leg_copies = [
            to_node(step, leg_ref, legs.at[node]) for step in range(1, nodes)
        ]
        mlp_shard[...] = mlp_in[...].astype(bf16)
        gather_mlp.begin()
        mom_attn_shard[...] = mom_attn_in[...].astype(bf16)
        mom_mlp_shard[...] = mom_mlp_in[...].astype(bf16)
        gather_moms = [
            Gather(place, attn_pieces, (mom_attn_shard,), (mom_attn_all,), pool.gather(own_sem, 2)),
            HalfGather(place, mom_mlp_shard, mom_mlp_all, pool.half(own_sem, 3)),
        ]

        def mom_step(step):
            for item in gather_moms:
                item.step(step)

        def row_loop(size, body, hooks=()):
            count = rows // size
            cuts = [count * i // (len(hooks) + 1) for i in range(len(hooks) + 2)]
            for i in range(len(hooks) + 1):

                @pl.loop(cuts[i], cuts[i + 1])
                def _(index):
                    body(pl.ds(pl.multiple_of(index * size, size), size))

                if i < len(hooks):
                    hooks[i]()

        def mix():
            column_ref[pl.ds(0, enc_edges), pl.ds(0, rows)] = enc_in[...]
            lists_ref[pl.ds(0, rows), pl.ds(0, 8)] = jnp.transpose(column_ref[pl.ds(0, 8), pl.ds(0, rows)])
            lane = iota((1, cin), 1)
            scale = jnp.where(lane < channels, vector_ref[0:1, c_input_lane : c_input_lane + 1], 1.0)

            @pl.loop(0, bands)
            def _(band):
                input_ref[band] = (grid_ref[band].astype(f32) * scale).astype(bf16)

            mixed_ref[...] = jnp.zeros_like(mixed_ref)

            def mix_rows(spot):
                lists = lists_ref[spot]
                mean = jnp.zeros((tile, cin), f32)
                for band in range(bands):
                    place_of = iota((tile, lons), 1) + band * lons
                    total = jnp.zeros((tile, lons), f32)
                    for j in range(enc_edges):
                        total += jnp.where(lists[:, j : j + 1] == place_of, 1.0 / enc_edges, 0.0)
                    mean += dot_nn(total.astype(bf16), input_ref[band])
                high = mean.astype(bf16)
                mixed_ref[0, spot, pl.ds(0, cin)] = high
                mixed_ref[1, spot, pl.ds(0, cin)] = (mean - high.astype(f32)).astype(bf16)

            row_loop(tile, mix_rows)

        def count_near():
            lists_ref[pl.ds(0, rows), pl.ds(0, fanout)] = jnp.transpose(near_in[...])

            def count_rows(spot):
                lists = lists_ref[spot]
                place_of = iota((tile, ext_rows), 1)
                total = jnp.zeros((tile, ext_rows), f32)
                for j in range(fanout):
                    total += jnp.where(lists[:, j : j + 1] == place_of, 1.0, 0.0)
                near_ref[spot] = jnp.where(total > 0.0, jnp.log2(jnp.maximum(total, 1.0)), absent)

            row_loop(tile, count_rows)

        def count_dec():
            column_ref[pl.ds(0, dec_edges), pl.ds(0, bands * lons)] = dec_in[...]
            lists_ref[:, pl.ds(0, 8)] = jnp.transpose(column_ref[...])

            @pl.loop(0, bands)
            def _(band):
                lists = lists_ref[pl.ds(pl.multiple_of(band * lons, 8), lons)]
                place_of = iota((lons, rows), 1)
                total = jnp.zeros((lons, rows), f32)
                for j in range(dec_edges):
                    total += jnp.where(lists[:, j : j + 1] == place_of, 1.0, 0.0)
                dec_ref[band] = total.astype(bf16)

        near_parts, far_sums = [], []

        def gram():
            for copy in leg_copies:
                copy.wait_recv()

            @pl.loop(0, all_lats)
            def _(index):
                other = legs[index // lats, lax.rem(index, lats)].astype(f32)
                for t in range(lats):
                    product = leg_ref[t].astype(f32) * other
                    parts[place.near, t, pl.ds(index, 1)] = jnp.sum(product, axis=0, keepdims=True)

            for j in range(1, place.nears):
                piece = parts.at[place.near]
                near_parts.append(start_copy(started, place, piece, piece, pool, near=j))

        def gram_near():
            wait_all(near_parts)
            total = parts[0]
            for j in range(1, place.nears):
                total = total + parts[j]
            sums[place.far] = total
            for k in range(1, place.fars):
                piece = sums.at[place.far]
                far_sums.append(start_copy(started, place, piece, piece, pool, far=k))

        def gram_far():
            wait_all(far_sums)
            total = sums[0]
            for k in range(1, place.fars):
                total = total + sums[k]
            kern_ref[...] = jnp.zeros_like(kern_ref)
            kern_ref[:, :, pl.ds(0, flat)] = total
            cosines = kern_ref[...]
            sines = pltpu.roll(cosines, modes - wave_first, 2)
            spot = iota((1, 1, lanes), 2)
            kern_ref[...] = jnp.where(
                spot < modes, cosines, jnp.where(spot < modes + wave_end - wave_first, sines, 0.0)
            )

        lendt_ref[...] = jnp.where(lent_ref[...] == iota((rows, halo), 0), 1.0, 0.0).astype(bf16)
        work = [mix, gram, count_dec, gram_near]
        for k in range(1, place.fars + 2):
            gather.step(k)
            if k == 1:
                gather_mlp.step(0)
            if work:
                work.pop(0)()
        while work:
            work.pop(0)()
        gather.end()
        gather_mlp.step(1)

        def small_part(low, size):
            blocks = pl.ds(low // small_rows, size // small_rows)
            return packed_ref[blocks, pl.ds(attn_rows, small_rows)].reshape(size, width)

        row = iota((all_small, 128), 0) - cond_start
        lane = iota((all_small, 128), 1)
        feature = vector_ref[0:1]
        block = jnp.where(row >= 0, row // NOISE_FEATS, 4)
        picked = jnp.where((row - block * NOISE_FEATS == lane) & (block < 4) & (lane < NOISE_FEATS), feature, 0.0)
        column = jnp.sum(picked, axis=1, keepdims=True)
        feats_ref[...] = jnp.where(lane == block, column, 0.0)
        mods = dot_tn(feats_ref[...].astype(bf16), small_part(0, all_small))
        mod = [mods[j : j + 1] for j in range(4)]

        def attn_part(low, size):
            return packed_ref[pl.ds(low // attn_rows, size // attn_rows), pl.ds(0, attn_rows)].reshape(size, width)

        def mlp_part(low):
            return mlp_ref[pl.ds(low // mlp_rows, chunk // mlp_rows)].reshape(chunk, width)

        def encode(spot):
            enc = small_part(0, wide)
            h0 = dot_nn(mixed_ref[0, spot], enc) + dot_nn(mixed_ref[1, spot], enc)
            h0_ref[spot] = h0
            unit, inverse = norm_parts(h0)
            first = (unit * (1.0 + mod[0]) + mod[1]).astype(bf16)
            first_ref[spot] = first
            ext_ref[spot] = dot_nt(first, attn_part(width, 2 * width)).astype(bf16)
            q_ref[spot] = dot_nt(first, attn_part(0, width)).astype(bf16)

        row_loop(big, encode)
        lent_rows[...] = dot_tn(lendt_ref[...], ext_ref[pl.ds(0, rows)]).astype(bf16)
        up = to_node(1, lent_rows, ext_ref.at[pl.ds(rows, halo)])
        down = to_node(nodes - 1, lent_rows, ext_ref.at[pl.ds(rows + halo, halo)])
        gather_mlp.step(2)
        count_near()
        gram_far()
        gather_mlp.step(3)
        for item in gather_moms:
            item.begin()
        up.wait_recv()
        down.wait_recv()

        def attend(spot):
            often = near_ref[spot]
            for head in range(HEAD_COUNT):
                part = pl.ds(head * head_width, head_width)
                values = pl.ds(width + head * head_width, head_width)
                logits = dot_nt(q_ref[spot, part], ext_ref[:, part]) * (score_scale * log2_e) + often
                raised = jnp.exp2(logits - jnp.max(logits, axis=-1, keepdims=True))
                inverse = 1.0 / jnp.sum(raised, axis=-1, keepdims=True)
                raised = raised.astype(bf16)
                prob_ref[head, spot] = raised
                scale_ref[spot, pl.ds(head, 1)] = inverse
                blend_ref[spot, part] = (dot_nn(raised, ext_ref[:, values]) * inverse).astype(bf16)

        row_loop(big, attend, [lambda: gather_mlp.step(4), lambda: gather_mlp.step(5)])
        for k in range(6, place.fars + 2):
            gather_mlp.step(k)
        gather_mlp.end()
        mom_step(0)
        lane = iota((1, 128), 1)
        live = jnp.where(lane < channels, 1.0, 0.0)
        dec_rows_ref[...] = pltpu.roll(small_part(start, 128).astype(f32), 128 - shift, 0).astype(bf16)

        def feed(spot):
            h1 = h0_ref[spot] + dot_nt(blend_ref[spot], attn_part(3 * width, width))
            h1_ref[spot] = h1
            unit, inverse = norm_parts(h1)
            second = (unit * (1.0 + mod[2]) + mod[3]).astype(bf16)
            second_ref[spot] = second
            h2 = h1
            for low in range(0, hidden, chunk):
                upper = dot_nt(second, mlp_part(low))
                square = upper * upper
                bend = jnp.tanh(upper * (gelu_scale + (gelu_scale * gelu_cubic) * square))
                half = 0.5 + 0.5 * bend
                activ = (upper * half).astype(bf16)
                activ_ref[low // chunk, spot] = activ
                slope = half + upper * (1.0 - bend * bend) * (
                    0.5 * gelu_scale + (1.5 * gelu_scale * gelu_cubic) * square
                )
                slope_ref[low // chunk, spot] = slope.astype(bf16)
                h2 += dot_nn(activ, mlp_part(hidden + low))
            high = h2.astype(bf16)
            out_ref[spot] = high
            low = (h2 - high.astype(f32)).astype(bf16)
            dec_rows = dec_rows_ref[...]
            projected = (dot_nt(high, dec_rows) + dot_nt(low, dec_rows)) * live
            top = projected.astype(bf16)
            node_ref[spot, pl.ds(0, 128)] = top
            node_ref[spot, pl.ds(128, 128)] = (projected - top.astype(f32)).astype(bf16)

        row_loop(big, feed)
        mom_step(1)

        c_skip = vector_ref[0:1, c_skip_lane : c_skip_lane + 1]
        c_output = vector_ref[0:1, c_output_lane : c_output_lane + 1]
        weight = vector_ref[0:1, weight_lane : weight_lane + 1]
        column_ref[pl.ds(0, bands), pl.ds(0, lons)] = land_ref[...]
        masks = jnp.transpose(column_ref[pl.ds(0, 8), pl.ds(0, flat_lons)].astype(f32))
        last = jnp.where(lane == channels - 1, 1.0, 0.0)

        def keep(band):
            return live * (1.0 - masks[:lons, band : band + 1] * last)

        error_ref[...] = jnp.zeros_like(error_ref)
        cores, uppers = {}, {}
        for band in range(bands):
            net = dot_nn(dec_ref[band], node_ref[...])
            net = (net[:, :128] + net[:, 128:]) * (c_output * third)
            noisy = grid_ref[band, :, pl.ds(0, 128)].astype(f32)
            error_ref[:, pl.ds(0, channels)] = target_ref[band]
            error = (c_skip * noisy + net - error_ref[...]) * keep(band)
            high = error.astype(bf16)
            low = (error - high.astype(f32)).astype(bf16)
            turned = dot_tn(high, table_ref[0]) + dot_tn(low, table_ref[0]) + dot_tn(high, table_ref[1])
            gext_ref[pl.ds(band * sent, sent), pl.ds(0, lanes)] = turned[:sent]
            all_ref[node, band] = turned[:sent].astype(bf16)
            piece = all_ref.at[node, band]
            for i in range(1, place.uppers):
                uppers[i, band] = start_copy(started, place, piece, piece, pool, upper=i)
            cores[0, band] = start_copy(started, place, piece, piece, pool, core=1)
        gf_ref[...] = jnp.zeros_like(gf_ref)
        mom_step(2)

        def add_nodes(base, total, band):
            def add_lat(index, value):
                source = base + index // lats
                return value + kern_ref[band, pl.ds(source * lats + lax.rem(index, lats), 1)] * all_ref[
                    source, lax.rem(index, lats)
                ].astype(f32)

            return lax.fori_loop(0, 2 * lats, add_lat, total, unroll=8)

        for band in range(bands):
            cores[0, band].wait_recv()
        for band in range(bands):
            gext_ref[pl.ds((lats + band) * sent, sent), pl.ds(0, lanes)] = add_nodes(place.upper * 2, jnp.zeros((sent, lanes), f32), band)
            for i in range(1, place.uppers):
                uppers[i, band].wait_recv()
                source = lax.rem(place.upper + place.uppers - i, place.uppers) * 2 + place.core
                piece = all_ref.at[source, band]
                cores[i, band] = start_copy(started, place, piece, piece, pool, core=1)
        for i in range(1, place.uppers):
            for band in range(bands):
                cores[i, band].wait_recv()
        loss_rows = jnp.zeros((8, 128), f32)
        for band in range(bands):
            total = gext_ref[pl.ds((lats + band) * sent, sent), pl.ds(0, lanes)]
            for i in range(1, place.uppers):
                total = add_nodes(lax.rem(place.upper + i, place.uppers) * 2, total, band)
            loss_rows = loss_rows + jnp.sum(total * gext_ref[pl.ds(band * sent, sent), pl.ds(0, lanes)])
            gf_ref[pl.ds(0, sent)] = total * (2.0 * weight)
            grad = gf_ref[...]
            high = grad.astype(bf16)
            low = (grad - high.astype(f32)).astype(bf16)
            back = dot_nt(table_ref[0], high) + dot_nt(table_ref[0], low) + dot_nt(table_ref[1], high)
            gnet_ref[band] = (back * keep(band) * c_output).astype(bf16)
        loss_share = loss_rows * weight

        sums_ref[...] = jnp.zeros_like(sums_ref)
        grad_node = dot_tn(gnet_ref[0], dec_ref[0])
        for band in range(1, bands):
            grad_node += dot_tn(gnet_ref[band], dec_ref[band])
        gnode_ref[...] = jnp.transpose(grad_node * third)

        def back_feed(spot):
            grad_node = gnode_ref[spot]
            high = grad_node.astype(bf16)
            low = (grad_node - high.astype(f32)).astype(bf16)
            node_ref[spot, pl.ds(0, 128)] = high
            dec_rows = dec_rows_ref[...]
            grad_out = dot_nn(high, dec_rows) + dot_nn(low, dec_rows)
            branch = grad_out.astype(bf16)
            gb_ref[spot] = branch
            grad_second = jnp.zeros((big, width), f32)
            for low in range(0, hidden, chunk):
                grad_activ = dot_nt(branch, mlp_part(hidden + low))
                grad_upper = (grad_activ * slope_ref[low // chunk, spot].astype(f32)).astype(bf16)
                slope_ref[low // chunk, spot] = grad_upper
                grad_second += dot_nn(grad_upper, mlp_part(low))
            unit, inverse = norm_parts(h1_ref[spot])
            scaled = grad_second * (1.0 + mod[2])
            grad_mid = grad_out + inverse * (
                scaled
                - jnp.mean(scaled, axis=-1, keepdims=True)
                - unit * jnp.mean(scaled * unit, axis=-1, keepdims=True)
            )
            sums_ref[2:3] += jnp.sum(grad_second * unit, axis=0, keepdims=True)
            sums_ref[3:4] += jnp.sum(grad_second, axis=0, keepdims=True)
            h1_ref[spot] = grad_mid
            grad_attn = grad_mid.astype(bf16)
            gattn_ref[spot] = grad_attn
            grad_blend = dot_nn(grad_attn, attn_part(3 * width, width))
            for head in range(HEAD_COUNT):
                part = slice(head * head_width, (head + 1) * head_width)
                scaled_blend = grad_blend[:, part] * scale_ref[spot, pl.ds(head, 1)]
                gblend_ref[spot, pl.ds(head * head_width, head_width)] = scaled_blend.astype(bf16)

        mom_step(3)
        row_loop(big, back_feed, [lambda: mom_step(4)])
        for k in range(5, place.fars + 2):
            mom_step(k)

        def outer_loop(target, block, offset, left, right, columns):
            @pl.loop(0, columns // big)
            def _(index):
                part = pl.multiple_of(index * big, big)
                product = dot_tn(left[:, pl.ds(part, big)], right[...]).astype(bf16)
                target[pl.ds((offset + part) // block, big // block), pl.ds(0, block)] = product.reshape(
                    big // block, block, width
                )

        for low in range(0, hidden, chunk):
            outer_loop(mlp_ref, mlp_rows, hidden + low, activ_ref.at[low // chunk], gb_ref, chunk)
            outer_loop(mlp_ref, mlp_rows, low, slope_ref.at[low // chunk], second_ref, chunk)
        scatter = Scatter(place, mlp_sum_pieces, (mlp_ref,), bufs, [pool] * 6)
        scatter.begin([0])

        gext_ref[...] = jnp.zeros_like(gext_ref)

        def back_attend(spot):
            for head in range(HEAD_COUNT):
                part = pl.ds(head * head_width, head_width)
                values = pl.ds(width + head * head_width, head_width)
                raised = prob_ref[head, spot]
                grad_blend = gblend_ref[spot, part]
                grad_prob = dot_nt(grad_blend, ext_ref[:, values])
                mean = jnp.sum(
                    grad_blend.astype(f32) * blend_ref[spot, part].astype(f32), axis=-1, keepdims=True
                )
                grad_logit = (raised.astype(f32) * (grad_prob - mean)).astype(bf16)
                gext_ref[:, part] += dot_tn(grad_logit, q_ref[spot, part])
                q_ref[spot, part] = (dot_nn(grad_logit, ext_ref[:, part]) * score_scale).astype(bf16)
                gext_ref[:, values] += dot_tn(raised, grad_blend)

        row_loop(big, back_attend, [lambda: scatter.step(0), lambda: scatter.step(1)])
        key_scale = jnp.where(iota((1, 2 * width), 1) < width, score_scale, 1.0)
        lost_ref[0] = (gext_ref[pl.ds(rows, halo)] * key_scale).astype(bf16)
        lost_ref[1] = (gext_ref[pl.ds(rows + halo, halo)] * key_scale).astype(bf16)
        from_upper = to_node(nodes - 1, lost_ref.at[0], back_ref.at[0])
        from_lower = to_node(1, lost_ref.at[1], back_ref.at[1])
        scatter.step(2)
        outer_loop(packed_ref, attn_rows, 3 * width, gattn_ref, blend_ref, width)
        scatter.step(3)
        from_upper.wait_recv()
        from_lower.wait_recv()

        def back_encode(spot):
            grad_pairs = gext_ref[spot] * key_scale + dot_nn(lendt_ref[spot], back_ref[0]) + dot_nn(
                lendt_ref[spot], back_ref[1]
            )
            grad_pairs = grad_pairs.astype(bf16)
            ext_ref[spot] = grad_pairs
            grad_first = dot_nn(q_ref[spot], attn_part(0, width)) + dot_nn(
                grad_pairs, attn_part(width, 2 * width)
            )
            unit, inverse = norm_parts(h0_ref[spot])
            scaled = grad_first * (1.0 + mod[0])
            grad_in = h1_ref[spot] + inverse * (
                scaled
                - jnp.mean(scaled, axis=-1, keepdims=True)
                - unit * jnp.mean(scaled * unit, axis=-1, keepdims=True)
            )
            sums_ref[0:1] += jnp.sum(grad_first * unit, axis=0, keepdims=True)
            sums_ref[1:2] += jnp.sum(grad_first, axis=0, keepdims=True)
            gb_ref[spot] = grad_in.astype(bf16)

        row_loop(big, back_encode, [lambda: scatter.step(4)])
        outer_loop(packed_ref, attn_rows, 0, q_ref, first_ref, width)
        outer_loop(packed_ref, attn_rows, width, ext_ref.at[pl.ds(0, rows)], first_ref, 2 * width)
        last = Scatter(
            place, last_pieces, (packed_ref,), strips((activ_ref, slope_ref), last_shapes), [pool] * 6
        )

        @pl.loop(0, all_small // 128)
        def _(index):
            low_row = pl.multiple_of(index * 128, 128)
            part = feats_ref[pl.ds(low_row, 128)]
            total = part[:, 0:1] * sums_ref[0:1]
            for j in range(1, 4):
                total += part[:, j : j + 1] * sums_ref[j : j + 1]
            gext_ref[pl.ds(low_row, 128), pl.ds(0, width)] = total

        for low_row in range(0, wide, 128):
            gext_ref[pl.ds(low_row, 128), pl.ds(0, width)] += dot_tn(
                mixed_ref[0, :, pl.ds(low_row, 128)], gb_ref[...]
            )
        gext_ref[pl.ds(start, 128), pl.ds(0, width)] += pltpu.roll(
            dot_tn(node_ref[:, pl.ds(0, 128)], out_ref[...]), shift, 0
        )

        @pl.loop(0, all_small // 128)
        def _(index):
            total = gext_ref[pl.ds(pl.multiple_of(index * 128, 128), 128), pl.ds(0, width)]
            high = total.astype(bf16)
            blocks = pl.ds(index * (128 // small_rows), 128 // small_rows)
            shape = (128 // small_rows, small_rows, width)
            packed_ref[blocks, pl.ds(attn_rows, small_rows)] = high.reshape(shape)
            packed_ref[blocks, pl.ds(first_rows, small_rows)] = (total - high.astype(f32)).astype(bf16).reshape(shape)

        last.begin([0])
        for k in range(5, scatter.steps()):
            scatter.step(k)
        last.step(0)
        scatter.finish(mlp_sum)
        g_mlp_shard[...] = mlp_sum[...].astype(bf16)
        gather_g_mlp = HalfGather(place, g_mlp_shard, g_mlp_all, pool.half(own_sem, 4))
        gather_g_mlp.begin()
        gather_g_mlp.step(0)
        for k in range(last.steps()):
            if k:
                last.step(k)
            if k + 1 < last.steps():
                gather_g_mlp.step(k + 1)
        last.finish(own)
        g_attn, g_mlp = own[pl.ds(0, attn_rows)], mlp_sum[...]
        g_small = own[pl.ds(attn_rows, small_rows)] + own[pl.ds(attn_rows + small_rows, small_rows)]
        attn_sum[...] = g_attn
        small_sum[...] = g_small
        g_attn_shard[...] = g_attn.astype(bf16)
        squares = jnp.sum(g_attn * g_attn) + jnp.sum(g_mlp * g_mlp) + jnp.sum(g_small * g_small)
        tile_shard[...] = jnp.where(iota((8, 128), 0) < 4, squares, loss_share)
        gather_g_attn = Gather(
            place, tile_pieces, (g_attn_shard, tile_shard), (g_attn_all, tiles_out), pool.gather(own_sem, 5)
        )
        gather_g_attn.begin()
        for k in range(place.fars + 2):
            gather_g_attn.step(k)
        for item in (*gather_moms, gather_g_mlp, gather_g_attn):
            item.end()
        scatter.end()
        last.end()
        for copy in started:
            copy.wait_send()

    vmem = pl.BlockSpec(memory_space=pltpu.VMEM)
    dma = pltpu.SemaphoreType.DMA
    struct = jax.ShapeDtypeStruct
    low = lambda *shape: pltpu.VMEM(shape, bf16)
    full = lambda *shape: pltpu.VMEM(shape, f32)
    return pl.pallas_call(
        kernel,
        out_shape=(
            struct((attn_rows, width), f32),
            struct((mlp_rows, width), f32),
            struct((small_rows, width), f32),
            struct((devices, 8, 128), f32),
        )
        + tuple(struct((devices, size, width), bf16) for size in (attn_rows, mlp_rows) * 2),
        in_specs=[vmem] * 15,
        out_specs=(vmem,) * 3 + (pl.BlockSpec(memory_space=pl.ANY),) * 5,
        scratch_shapes=[
            full(attn_rows + 2 * small_rows, width),
            low(attn_rows, width),
            low(mlp_rows, width),
            low(attn_rows, width),
            low(mlp_rows, width),
            full(8, 128),
            low(first_rows, width),
            low(mlp_rows, width),
            low(nodes, lats, lows, flat),
            full(place.nears, lats, all_lats, flat),
            full(place.fars, lats, all_lats, flat),
            full(lats, all_lats, lanes),
            low(devices, packed_rows, width),
            low(devices, mlp_rows, width),
            full(rows, ext_rows),
            low(bands, lons, rows),
            low(2, rows, wide),
            low(rows, halo),
            full(rows, width),
            full(rows, width),
            low(rows, width),
            low(rows, width),
            low(ext_rows, 2 * width),
            low(halo, 2 * width),
            low(HEAD_COUNT, rows, ext_rows),
            low(rows, width),
            low(rows, width),
            low(hidden // chunk, rows, chunk),
            low(hidden // chunk, rows, chunk),
            low(rows, width),
            low(rows, 256),
            low(nodes, lats, sent, lanes),
            full(128, lanes),
            low(bands, lons, 128),
            full(rows, 128),
            low(rows, width),
            low(rows, width),
            low(rows, width),
            full(ext_rows, 2 * width),
            low(2, halo, 2 * width),
            low(2, halo, 2 * width),
            full(8, width),
            full(rows, 128),
            full(lons, 128),
            pltpu.VMEM((8, flat_pixels), jnp.int32),
            pltpu.VMEM((flat_pixels, 128), jnp.int32),
            low(bands, lons, cin),
            low(128, width),
            full(all_small, 128),
            dma((2 * copies,)),
            dma((7,)),
        ]
        + scatter_bufs,
        compiler_params=pltpu.CompilerParams(
            collective_id=collective, has_side_effects=True, vmem_limit_bytes=62 << 20
        ),
    )(*weights, grid, target, land, near_turned, enc_turned, dec_turned, lent, legendre, vector, tables, *moments)


def turn_tables(lon_count, modes):
    turns = np.arange(lon_count)[:, None] * np.arange(modes)[None, :] % lon_count
    phases = turns * (2.0 * np.pi / lon_count)
    waves = [m for m in range(modes) if (2 * m) % lon_count]
    picks = list(range(modes)) + waves
    lanes = -(-len(picks) // 128) * 128
    table = np.zeros((lon_count, lanes), np.float32)
    table[:, :modes] = np.cos(phases)
    table[:, modes : len(picks)] = -np.sin(phases[:, waves])
    high = table.astype(ml_dtypes.bfloat16)
    low = (table - high.astype(np.float32)).astype(ml_dtypes.bfloat16)
    return np.stack([high, low]), (waves[0], waves[-1] + 1, lanes - len(picks))


def to_sixteens(blocks):
    return jnp.pad(blocks, ((0, 0), (0, sixteens(blocks.shape[1]) - blocks.shape[1]), (0, 0)))


def on_device(
    grid_in,
    target,
    noise_level,
    land_mask,
    neighbours,
    halo_send,
    g2m,
    m2g,
    legendre,
    w_attn,
    w_mlp,
    w_small,
    mom_attn,
    mom_mlp,
    m_small,
    v_small,
    ema_attn,
    ema_mlp,
    ema_small,
):
    cin = grid_in.shape[-1]
    lat_rows, lon_count, channels = target.shape[1:]
    modes, degrees = legendre.shape[1:]
    halo_rows = halo_send.shape[0]
    width = w_attn.shape[1]
    nodes, zeros = lax.axis_size("node"), lax.axis_size("zero")
    devices = nodes * zeros
    attn_rows, mlp_rows, small_rows = w_attn.shape[0], w_mlp.shape[0], w_small.shape[0]

    sigma, c_input, c_skip, c_output, loss_weight = noise_scalars(noise_level[0])
    features = noise_features(sigma).astype(bf16).astype(f32)
    weight = loss_weight / (2 * modes * degrees * channels)
    tables, (wave_first, wave_end, wave_pad) = turn_tables(lon_count, modes)
    whole_tiles = all(size % 16 == 0 and 256 % size == 0 for size in (attn_rows, mlp_rows, small_rows))
    if whole_tiles:
        lows = sixteens(-(-degrees // zeros))
        wanted = lax.axis_index("zero") * lows
        first_degree = jnp.minimum(wanted, degrees - lows)
        leg = lax.dynamic_slice_in_dim(legendre, first_degree, lows, axis=2)
        leg = jnp.where(first_degree + jnp.arange(lows) >= wanted, leg, 0.0)
        leg = jnp.pad(jnp.transpose(leg, (0, 2, 1)).astype(bf16), ((0, 0), (0, 0), (0, -modes % 128)))
        lane = jnp.arange(128)
        vector = jnp.where(lane < NOISE_FEATS, jnp.pad(features, (0, 128 - NOISE_FEATS)), 0.0)
        for spot, value in (
            (c_input_lane, c_input),
            (c_skip_lane, c_skip),
            (c_output_lane, c_output),
            (weight_lane, weight),
        ):
            vector = jnp.where(lane == spot, value, vector)
        attn_sum, mlp_sum, g_small, totals, mom_attn_all, mom_mlp_all, g_attn_all, g_mlp_all = train_step(
            nodes,
            zeros,
            (w_attn, w_mlp, w_small),
            grid_in[0],
            target[0],
            land_mask,
            neighbours.T,
            g2m.T,
            m2g.T,
            halo_send[None],
            leg,
            vector[None],
            jnp.asarray(tables),
            (modes, wave_first, wave_end),
            (mom_attn, mom_mlp),
            cin,
            1,
        )
        sums = (g_small, attn_sum, mlp_sum)
        attn_sets = [item.reshape(-1, width) for item in (mom_attn_all, g_attn_all)]
        mlp_sets = [item.reshape(-1, width) for item in (mom_mlp_all, g_mlp_all)]
        moments = (mom_attn, mom_mlp)
    else:
        scale_input = jnp.where(jnp.arange(cin) < channels, c_input, 1.0)[None]
        cond_rows = jnp.where(
            jnp.arange(128)[None, None] == jnp.arange(4)[:, None, None], features[None, :, None], 0.0
        ).reshape(-1, 128)
        feats = jnp.pad(cond_rows, ((cin + channels, 0), (0, 0)))
        shift = cin % 128
        sides = ((0, 0), (0, 0), (shift, 128 - shift - channels))
        keep_mask = 1.0 - land_mask.astype(f32)[:, :, None] * (
            jnp.arange(channels) == channels - 1
        ).astype(f32)
        base = jnp.pad(c_skip * grid_in[0, :, :, :channels].astype(f32) - target[0], sides)
        keep = jnp.pad(keep_mask, sides)
        lows = -(-degrees // (8 * zeros)) * 8
        leg = jnp.pad(legendre, ((0, 0), (0, 0), (0, lows * zeros - degrees)))
        leg = lax.dynamic_slice_in_dim(leg, lax.axis_index("zero") * lows, lows, axis=2)
        leg = jnp.transpose(leg, (0, 2, 1))
        leg = jnp.concatenate(
            [leg, leg[:, :, wave_first:wave_end], jnp.zeros(leg.shape[:2] + (wave_pad,), f32)], axis=2
        )
        m2g_bands = m2g.reshape(lat_rows, lon_count, -1)

        attn, mlp, small, near, dec, dec_turned, mixed, lend, lendt, kern = gather_and_count(
            nodes,
            zeros,
            (w_attn, w_mlp, w_small),
            grid_in[0].reshape(-1, cin),
            scale_input,
            g2m,
            m2g_bands,
            jnp.transpose(m2g_bands, (0, 2, 1)),
            neighbours,
            halo_send[:, None],
            jnp.concatenate([halo_send, halo_send])[None],
            leg,
            1,
        )
        full = [
            item[:, :size].reshape(-1, width)
            for item, size in ((attn, attn_rows), (mlp, mlp_rows), (small, small_rows))
        ]
        *local, loss_tile = model_step(
            nodes,
            zeros,
            full,
            (near, dec, dec_turned, mixed, lend, lendt),
            kern,
            feats,
            base,
            keep,
            jnp.asarray(tables),
            jnp.stack([c_output, weight]),
            cin,
            channels,
            m2g.shape[1],
            2,
        )
        names = ["attn", "mlp", "high", "low"]
        mlp_sum = None

        g_small, moment_attn, moment_mlp, totals, attn_all, mlp_all = reduce_and_gather(
            nodes,
            zeros,
            names,
            [to_sixteens(item.reshape(devices, -1, width)) for item in local],
            mlp_sum,
            loss_tile,
            mom_attn,
            mom_mlp,
            small_rows,
            3,
        )
        sums = (g_small,)
        attn_sets = [attn_all[:, :attn_rows].reshape(-1, width)]
        mlp_sets = [mlp_all[:, :mlp_rows].reshape(-1, width)]
        totals = totals[None]
        moments = (moment_attn, moment_mlp)

    *results, moment_attn, moment_mlp = update_weights(
        nodes,
        zeros,
        attn_sets,
        mlp_sets,
        totals,
        sums,
        moments,
        (w_attn, w_mlp, w_small),
        (ema_attn, ema_mlp, ema_small),
        (m_small, v_small),
    )
    loss, clip_norm, new_attn, new_mlp, new_small, new_m, new_v, *new_averages = results
    return (
        loss[0, 0], clip_norm[0, 0], new_attn, new_mlp, new_small, moment_attn, moment_mlp, new_m, new_v, *new_averages
    )


def solution(mesh):
    split_rows = P(("node", "zero"), None)
    return jax.shard_map(
        on_device,
        mesh=mesh,
        in_specs=(
            P("zero", "node", None, None),
            P("zero", "node", None, None),
            P("zero"),
            P("node", None),
            P("node", None),
            P("node"),
            P("node", None),
            P("node", None),
            P("node", None, None),
        )
        + (split_rows,) * 10,
        out_specs=(P(), P()) + (split_rows,) * 10,
        check_vma=False,
    )
```

```python
import math

import jax
import jax.numpy as jnp
import ml_dtypes
import numpy as np
from jax import lax
from jax.experimental import pallas as pl
from jax.experimental.pallas import tpu as pltpu
from jax.sharding import PartitionSpec as P

HEAD_COUNT = 4
NOISE_FEATS = 42
LEVELS = 16
NS_ITERS = 3
STEP = 10

top_precision = lax.Precision.HIGHEST
mid_precision = lax.Precision.HIGH
norm_epsilon = 1e-05
trace_epsilon = 1e-12
clip_limit = 1.0
moment_decay = 0.95
orthogonal_rate = 0.1
adam_first = 0.9
adam_second = 0.95
adam_rate = 0.02
adam_epsilon = 1e-08
average_decay = 0.9
newton_first = 3.4445
newton_second = -4.775
newton_third = 2.0315
sigma_lowest = 0.1
sigma_highest = 20.0
c_input_lane = 64
c_skip_lane = 65
c_output_lane = 66
weight_lane = 67
log2_e = math.log2(math.e)
absent = -1e30
gelu_scale = math.sqrt(2.0 / math.pi)
gelu_cubic = 0.044715
f32 = jnp.float32
bf16 = jnp.bfloat16


def noise_scalars(level):
    sigma = sigma_lowest * (sigma_highest / sigma_lowest) ** (level.astype(f32) / (LEVELS - 1))
    total = sigma * sigma + 1.0
    return (sigma, lax.rsqrt(total), 1.0 / total, sigma * lax.rsqrt(total), total / (sigma * sigma))


def noise_features(sigma):
    half_count = NOISE_FEATS // 2
    frequency = jnp.exp(jnp.arange(half_count).astype(f32) * (3.0 / half_count))
    phases = 0.25 * jnp.log(sigma) * frequency
    return jnp.concatenate([jnp.sin(phases), jnp.cos(phases)])


def dot(left, right, contract):
    return lax.dot_general(left, right, (contract, ((), ())), preferred_element_type=f32)


def dot_nn(left, right):
    return dot(left, right, ((1,), (0,)))


def dot_nt(left, right):
    return dot(left, right, ((1,), (1,)))


def dot_tn(left, right):
    return dot(left, right, ((0,), (0,)))


MESH = pl.DeviceIdType.MESH
ROW_CHUNK = 16


class Place:
    def __init__(self, nodes, zeros):
        self.uppers, self.cores = nodes // 2, 2
        self.nears = 2 if zeros < 16 else 4
        self.fars = zeros // self.nears
        self.mates = max(self.uppers // 2, 1)
        self.zeros = zeros

    def locate(self):
        node, zero = lax.axis_index("node"), lax.axis_index("zero")
        self.upper, self.core = node // 2, node % 2
        self.far, self.near = zero // self.nears, zero % self.nears

    def moved(self, upper=0, core=0, far=0, near=0, mate=0):
        row = lax.rem(self.upper + upper, self.uppers) if upper else self.upper
        if mate:
            group = self.upper // self.mates * self.mates
            row = group + lax.rem(self.upper - group + mate, self.mates)
        return (
            row,
            1 - self.core if core else self.core,
            lax.rem(self.far + far, self.fars) if far else self.far,
            lax.rem(self.near + near, self.nears) if near else self.near,
        )

    def device(self, **steps):
        upper, core, far, near = self.moved(**steps)
        return (upper * 2 + core, far * self.nears + near)

    def slot(self, upper, core, far, near):
        return (upper * 2 + core) * self.zeros + far * self.nears + near

    def peers(self):
        return (
            [dict(far=k) for k in range(1, self.fars)]
            + [dict(near=j) for j in range(1, self.nears)]
            + [dict(upper=i) for i in range(1, self.uppers)]
            + [dict(core=1)]
        )

    def greet(self, nodes=0):
        barrier = pltpu.get_barrier_semaphore()
        peers = [self.device(**steps) for steps in self.peers() if not nodes or set(steps) <= {"far", "near"}]
        if nodes:
            node, zero = lax.axis_index("node"), lax.axis_index("zero")
            peers += [(lax.rem(node + step, nodes), zero) for step in range(1, nodes)]
        for device in peers:
            pl.semaphore_signal(barrier, 1, device_id=device, device_id_type=MESH)
        pl.semaphore_wait(barrier, len(peers))


def half_rows(rows):
    return (rows // 2 + 15) // 16 * 16


class Pool:
    def __init__(self, ref):
        self.ref, self.used, self.at = ref, 0, self

    def __getitem__(self, index):
        return self

    def take(self):
        pair = self.ref.at[pl.ds(self.used, 2)]
        self.used += 2
        return pair

    def gather(self, own, index):
        return [own.at[pl.ds(index, 2)]] + [self] * 6

    def half(self, own, index):
        return [own.at[index]] + [self] * 4


def start_copy(started, place, source, target, sems, **steps):
    if isinstance(sems, Pool):
        sems = sems.take()
    copy = pltpu.make_async_remote_copy(
        src_ref=source,
        dst_ref=target,
        send_sem=sems.at[0],
        recv_sem=sems.at[1],
        device_id=place.device(**steps),
        device_id_type=MESH,
    )
    copy.start()
    started.append(copy)
    return copy


def sixteens(rows):
    return -(-rows // 16) * 16


class Pieces:
    def __init__(self, sizes, first, share=1 / 2):
        self.sizes = sizes
        cut = min(sixteens(int(sum(sizes) * share)), sizes[first])
        self.whole = [(i, 0, size) for i, size in enumerate(sizes)]
        self.head = [(first, 0, cut)]
        self.tail = [(first, cut, sizes[first] - cut)] if cut < sizes[first] else []
        self.tail += [(i, 0, size) for i, size in enumerate(sizes) if i != first]


def send_pieces(started, place, pieces, sources, targets, sems, **steps):
    copies = []
    for index, (array, start, rows) in enumerate(pieces):
        part = pl.ds(start, rows)
        copies.append(
            start_copy(
                started, place, sources[array].at[part], targets[array].at[part], sems.at[index], **steps
            )
        )
    return copies


def wait_all(copies):
    for copy in copies:
        copy.wait_recv()


class Gather:
    def __init__(self, place, pieces, shards, outs, sems):
        self.place, self.pieces, self.shards, self.outs = place, pieces, shards, outs
        (self.own_sem, self.far_sem, self.near_sem, self.upper_sem, self.over_sem, self.under_sem, self.core_sem) = sems
        self.started, self.cores = [], []
        self.far, self.near, self.upper, self.over, self.under = {}, {}, {}, {}, {}

    def block(self, **steps):
        slot = self.place.slot(*self.place.moved(**steps))
        return [out.at[slot] for out in self.outs]

    def send(self, pieces, source, target, sems, **steps):
        return send_pieces(self.started, self.place, pieces, source, target, sems, **steps)

    def begin(self):
        here = self.block()
        self.kept = []
        for index, (shard, target) in enumerate(zip(self.shards, here)):
            mine = target.at[pl.ds(0, shard.shape[0])]
            copy = pltpu.make_async_copy(shard, mine, self.own_sem.at[index])
            copy.start()
            self.kept.append(copy)
        for k in range(1, self.place.fars):
            self.far[k] = self.send(self.pieces.whole, self.shards, here, self.far_sem.at[k], far=k)

    def first(self, k):
        place, whole = self.place, self.pieces.whole
        if k:
            wait_all(self.far[k])
        target = self.block(far=(place.fars - k) % place.fars)
        source = target if k else self.shards
        for j in range(1, place.nears):
            self.near[k, j] = self.send(whole, source, target, self.near_sem.at[k, j], near=j)
        for i in range(1, place.uppers):
            self.upper[k, i] = self.send(whole, source, target, self.upper_sem.at[k, i], upper=i)

    def to_core(self, k, i):
        place = self.place
        upper, core, far, _ = place.moved(far=(place.fars - k) % place.fars, upper=(place.uppers - i) % place.uppers)
        blocks = pl.ds(place.slot(upper, core, far, 0), place.nears)
        for index, (array, start, rows) in enumerate(self.pieces.whole):
            item = self.outs[array].at[blocks, pl.ds(start, rows)]
            sems = self.core_sem.at[k, 0, i].at[index]
            self.cores.append(start_copy(self.started, place, item, item, sems, core=1))

    def second(self, k):
        place = self.place
        far = (place.fars - k) % place.fars
        for j in range(1, place.nears):
            wait_all(self.near[k, j])
            item = self.block(far=far, near=place.nears - j)
            for i in range(1, place.uppers):
                self.over[k, j, i] = self.send(
                    self.pieces.head, item, item, self.over_sem.at[k, j, i], upper=i
                )
        if not k:
            for copy in self.kept:
                copy.wait()
        self.to_core(k, 0)
        for i in range(1, place.uppers):
            wait_all(self.upper[k, i])
            item = self.block(far=far, upper=place.uppers - i)
            for j in range(1, place.nears):
                self.under[k, j, i] = self.send(
                    self.pieces.tail, item, item, self.under_sem.at[k, j, i], near=j
                )

    def third(self, k):
        place = self.place
        for i in range(1, place.uppers):
            for j in range(1, place.nears):
                wait_all(self.over[k, j, i])
                wait_all(self.under[k, j, i])
            self.to_core(k, i)

    def step(self, k):
        fars = self.place.fars
        if k < fars:
            self.first(k)
        if 1 <= k <= fars:
            self.second(k - 1)
        if k >= 2:
            self.third(k - 2)

    def end(self):
        wait_all(self.cores)
        for copy in self.started:
            copy.wait_send()

    @staticmethod
    def copies(place, pieces):
        fars, nears, uppers = place.fars, place.nears, place.uppers
        whole, parts = len(pieces.whole), len(pieces.head) + len(pieces.tail)
        direct = (fars - 1) + fars * (nears - 1) + fars * (uppers - 1) + fars * uppers
        return whole * direct + parts * fars * (nears - 1) * (uppers - 1)

    @staticmethod
    def sems(place, pieces):
        dma = pltpu.SemaphoreType.DMA
        fars, nears, uppers = place.fars, place.nears, place.uppers
        whole, head, tail = len(pieces.whole), len(pieces.head), len(pieces.tail)
        return [
            dma((whole,)),
            dma((fars, whole, 2)),
            dma((fars, nears, whole, 2)),
            dma((fars, uppers, whole, 2)),
            dma((fars, nears, uppers, head, 2)),
            dma((fars, nears, uppers, tail, 2)),
            dma((fars, nears, uppers, whole, 2)),
        ]


def iota(shape, axis):
    return lax.broadcasted_iota(jnp.int32, shape, axis)


def gather_and_count(nodes, zeros, weights, grid, scale, g2m, m2g, m2g_turned, neighbours, lent, lent_row, legendre, collective):
    place = Place(nodes, zeros)
    width = weights[0].shape[1]
    sizes = [sixteens(w.shape[0]) for w in weights]
    pieces = Pieces(sizes, 1)
    devices = nodes * zeros
    pixels, cin = grid.shape
    wide = -(-cin // 128) * 128
    rows, fanout = neighbours.shape
    halo = lent.shape[0]
    ext = rows + 2 * halo
    bands, lons, dec_edges = m2g.shape
    lats, lows, lanes = legendre.shape
    enc_edges = g2m.shape[1]
    tile = 128

    def kernel(
        attn_ref, mlp_ref, small_ref, grid_ref, scale_ref, g2m_ref, m2g_ref, turned_ref, near_ref, lent_ref,
        row_ref, leg_ref,
        attn_out, mlp_out, small_out, near_out, dec_out, turned_out, mixed_out, lend_out, lendt_out, kern_out,
        attn_shard, mlp_shard, small_shard, inputs, legs, parts, sums, leg_sem, part_sem, sum_sem, *sems,
    ):
        place.locate()
        node = lax.axis_index("node")
        shards = (attn_shard, mlp_shard, small_shard)
        for ref, shard, size in zip((attn_ref, mlp_ref, small_ref), shards, sizes):
            if ref.shape[0] < size:
                shard[...] = jnp.zeros_like(shard)
            shard[pl.ds(0, ref.shape[0])] = ref[...].astype(bf16)
        legs[node] = leg_ref[...]
        place.greet(nodes)
        gather = Gather(place, pieces, shards, (attn_out, mlp_out, small_out), sems)
        gather.begin()
        started = []
        leg_copies = []
        for step in range(1, nodes):
            target = (lax.rem(node + step, nodes), lax.axis_index("zero"))
            copy = pltpu.make_async_remote_copy(
                src_ref=leg_ref,
                dst_ref=legs.at[node],
                send_sem=leg_sem.at[step, 0],
                recv_sem=leg_sem.at[step, 1],
                device_id=target,
                device_id_type=MESH,
            )
            copy.start()
            leg_copies.append(copy)

        def count_near():
            @pl.loop(0, rows // tile)
            def _(index):
                spot = pl.ds(pl.multiple_of(index * tile, tile), tile)
                lists = near_ref[spot]
                place_of = iota((tile, ext), 1)
                total = jnp.zeros((tile, ext), f32)
                for j in range(fanout):
                    total += jnp.where(lists[:, j : j + 1] == place_of, 1.0, 0.0)
                near_out[spot] = total.astype(bf16)

        def count_dec():
            @pl.loop(0, bands)
            def _(band):
                lists = m2g_ref[band]
                place_of = iota((lons, rows), 1)
                total = jnp.zeros((lons, rows), f32)
                for j in range(dec_edges):
                    total += jnp.where(lists[:, j : j + 1] == place_of, 1.0, 0.0)
                dec_out[band] = total.astype(bf16)
                lists = turned_ref[band]
                place_of = iota((rows, lons), 0)
                total = jnp.zeros((rows, lons), f32)
                for j in range(dec_edges):
                    total += jnp.where(lists[j : j + 1] == place_of, 1.0, 0.0)
                turned_out[band] = total.astype(bf16)

        def mix():
            inputs[...] = (grid_ref[...].astype(f32) * scale_ref[...]).astype(bf16)
            mixed_out[...] = jnp.zeros_like(mixed_out)

            @pl.loop(0, rows // tile)
            def _(index):
                spot = pl.ds(pl.multiple_of(index * tile, tile), tile)
                lists = g2m_ref[spot]
                place_of = iota((tile, pixels), 1)
                total = jnp.zeros((tile, pixels), f32)
                for j in range(enc_edges):
                    total += jnp.where(lists[:, j : j + 1] == place_of, 1.0 / enc_edges, 0.0)
                mean = dot_nn(total.astype(bf16), inputs[...])
                high = mean.astype(bf16)
                mixed_out[0, spot, pl.ds(0, cin)] = high
                mixed_out[1, spot, pl.ds(0, cin)] = (mean - high.astype(f32)).astype(bf16)

        def lend():
            lend_out[...] = jnp.where(lent_ref[...] == iota((halo, rows), 1), 1.0, 0.0).astype(bf16)
            lendt_out[...] = jnp.where(row_ref[...] == iota((rows, 2 * halo), 0), 1.0, 0.0).astype(bf16)

        def gram():
            for copy in leg_copies:
                copy.wait()

            @pl.loop(0, nodes * lats)
            def _(index):
                other = legs[index // lats, lax.rem(index, lats)]
                for t in range(lats):
                    product = leg_ref[t] * other
                    parts[place.near, t, pl.ds(index, 1)] = jnp.sum(product, axis=0, keepdims=True)

            for j in range(1, place.nears):
                near_parts.append(
                    start_copy(
                        started, place, parts.at[place.near], parts.at[place.near], part_sem.at[j], near=j
                    )
                )

        near_parts, far_sums = [], []

        def gram_near():
            wait_all(near_parts)
            total = parts[0]
            for j in range(1, place.nears):
                total = total + parts[j]
            sums[place.far] = total
            for k in range(1, place.fars):
                far_sums.append(
                    start_copy(
                        started, place, sums.at[place.far], sums.at[place.far], sum_sem.at[k], far=k
                    )
                )

        def gram_far():
            wait_all(far_sums)
            total = sums[0]
            for k in range(1, place.fars):
                total = total + sums[k]
            kern_out[...] = total

        work = [lend, mix, gram, count_dec, gram_near, count_near, gram_far]
        steps = place.fars + 2
        for k in range(steps):
            gather.step(k)
            share = -(-len(work) // (steps - k))
            for part in work[:share]:
                part()
            work = work[share:]
        gather.end()
        for copy in started:
            copy.wait_send()

    vmem = pl.BlockSpec(memory_space=pltpu.VMEM)
    hbm = pl.BlockSpec(memory_space=pl.ANY)
    dma = pltpu.SemaphoreType.DMA
    struct = jax.ShapeDtypeStruct
    return pl.pallas_call(
        kernel,
        out_shape=tuple(struct((devices, size, width), bf16) for size in sizes)
        + (
            struct((rows, ext), bf16),
            struct((bands, lons, rows), bf16),
            struct((bands, rows, lons), bf16),
            struct((2, rows, wide), bf16),
            struct((halo, rows), bf16),
            struct((rows, 2 * halo), bf16),
            struct((lats, nodes * lats, lanes), f32),
        ),
        in_specs=[vmem] * 12,
        out_specs=(hbm,) * 3 + (vmem,) * 7,
        scratch_shapes=[pltpu.VMEM((size, width), bf16) for size in sizes]
        + [
            pltpu.VMEM((pixels, cin), bf16),
            pltpu.VMEM((nodes, lats, lows, lanes), f32),
            pltpu.VMEM((place.nears, lats, nodes * lats, lanes), f32),
            pltpu.VMEM((place.fars, lats, nodes * lats, lanes), f32),
            dma((nodes, 2)),
            dma((place.nears, 2)),
            dma((place.fars, 2)),
        ]
        + Gather.sems(place, pieces),
        compiler_params=pltpu.CompilerParams(
            collective_id=collective, has_side_effects=True, vmem_limit_bytes=56 << 20
        ),
    )(*weights, grid, scale, g2m, m2g, m2g_turned, neighbours, lent, lent_row, legendre)


def norm_parts(rows):
    centred = rows - jnp.mean(rows, axis=-1, keepdims=True)
    inverse = lax.rsqrt(jnp.mean(centred * centred, axis=-1, keepdims=True) + norm_epsilon)
    return centred * inverse, inverse


def model_step(
    nodes, zeros, weights, graph, kern, feats, base, keep, tables, scalars, first_channel, channels, dec_edges, collective
):
    place = Place(nodes, zeros)
    attn, mlp, small = weights
    near, dec, dec_turned, mixed, lend, lendt = graph
    width = attn.shape[1]
    hidden = mlp.shape[0] // 2
    rows, ext_rows = near.shape
    halo = lend.shape[0]
    bands, lons, _ = dec.shape
    wide = mixed.shape[2]
    lats, all_lats, lanes = kern.shape
    start = first_channel // 128 * 128
    shift = first_channel - start
    sent = sixteens(shift + channels)
    big, tile = 256, 128
    head_width = width // HEAD_COUNT
    score_scale = head_width ** (-0.5)
    third = 1.0 / dec_edges

    def kernel(
        attn_hbm, mlp_hbm, small_ref, near_hbm, dec_hbm, turned_hbm, mixed_ref, lend_ref, lendt_ref, kern_ref,
        feats_ref, base_ref, keep_ref, table_ref, scalar_ref,
        attn_out, mlp_out, high_out, low_out, loss_out,
        attn_ref, mlp_ref, near_ref, dec_ref, turned_ref, h0_ref, h1_ref, first_ref, q_ref, ext_ref, lent_ref,
        prob_ref, blend_ref, second_ref, activ_ref, slope_ref, out_ref, node_ref, f_ref, all_ref, gf_ref, gnet_ref,
        gb_ref, gattn_ref, gblend_ref, gext_ref, back_ref, lost_ref, sums_ref,
        load_sem, lend_sem, f_sem, pass_sem, back_sem,
    ):
        place.locate()
        node = lax.axis_index("node")
        zero = lax.axis_index("zero")
        loads = []
        for index, (source, target) in enumerate(
            (
                (attn_hbm, attn_ref),
                (near_hbm, near_ref),
                (mlp_hbm, mlp_ref),
                (dec_hbm, dec_ref),
                (turned_hbm, turned_ref),
            )
        ):
            copy = pltpu.make_async_copy(source, target, load_sem.at[index])
            copy.start()
            loads.append(copy)
        barrier = pltpu.get_barrier_semaphore()
        for step in range(1, nodes):
            pl.semaphore_signal(
                barrier, 1, device_id=(lax.rem(node + step, nodes), zero), device_id_type=MESH
            )
        started = []

        def to_node(step, source, target, sems):
            copy = pltpu.make_async_remote_copy(
                src_ref=source,
                dst_ref=target,
                send_sem=sems.at[0],
                recv_sem=sems.at[1],
                device_id=(lax.rem(node + step, nodes), zero),
                device_id_type=MESH,
            )
            copy.start()
            started.append(copy)
            return copy

        def row_loop(size, body):
            @pl.loop(0, rows // size)
            def _(index):
                body(pl.ds(pl.multiple_of(index * size, size), size))

        mods = dot_tn(feats_ref[...].astype(bf16), small_ref[...])
        mod = [mods[j : j + 1] for j in range(4)]
        enc = small_ref[pl.ds(0, wide)]
        loads[0].wait()

        def encode(spot):
            h0 = dot_nn(mixed_ref[0, spot], enc) + dot_nn(mixed_ref[1, spot], enc)
            h0_ref[spot] = h0
            unit, inverse = norm_parts(h0)
            first = (unit * (1.0 + mod[0]) + mod[1]).astype(bf16)
            first_ref[spot] = first
            ext_ref[spot] = dot_nt(first, attn_ref[pl.ds(width, 2 * width)]).astype(bf16)
            q_ref[spot] = dot_nt(first, attn_ref[pl.ds(0, width)]).astype(bf16)

        row_loop(big, encode)
        lent_ref[...] = dot_nn(lend_ref[...], ext_ref[pl.ds(0, rows)]).astype(bf16)
        pl.semaphore_wait(barrier, nodes - 1)
        up = to_node(1, lent_ref, ext_ref.at[pl.ds(rows, halo)], lend_sem.at[0])
        down = to_node(nodes - 1, lent_ref, ext_ref.at[pl.ds(rows + halo, halo)], lend_sem.at[1])
        loads[1].wait()
        up.wait_recv()
        down.wait_recv()

        def attend(spot):
            count = near_ref[spot].astype(f32)
            for head in range(HEAD_COUNT):
                part = pl.ds(head * head_width, head_width)
                values = pl.ds(width + head * head_width, head_width)
                logits = dot_nt(q_ref[spot, part], ext_ref[:, part]) * score_scale
                logits = jnp.where(count > 0.0, logits, -jnp.inf)
                raised = jnp.exp(logits - jnp.max(logits, axis=-1, keepdims=True))
                prob = raised * (1.0 / jnp.sum(raised * count, axis=-1, keepdims=True))
                prob = prob.astype(bf16)
                prob_ref[head, spot] = prob
                low = (prob.astype(f32) * count).astype(bf16)
                blend_ref[spot, part] = dot_nn(low, ext_ref[:, values]).astype(bf16)

        row_loop(tile, attend)
        loads[2].wait()
        dec_rows = small_ref[pl.ds(start, 128)]
        lane = iota((1, 128), 1)
        live = jnp.where((lane >= shift) & (lane < shift + channels), 1.0, 0.0)

        def feed(spot):
            h1 = h0_ref[spot] + dot_nt(blend_ref[spot], attn_ref[pl.ds(3 * width, width)])
            h1_ref[spot] = h1
            unit, inverse = norm_parts(h1)
            second = (unit * (1.0 + mod[2]) + mod[3]).astype(bf16)
            second_ref[spot] = second
            upper = dot_nt(second, mlp_ref[pl.ds(0, hidden)])
            square = upper * upper
            bend = jnp.tanh(gelu_scale * upper * (1.0 + gelu_cubic * square))
            half = 0.5 + 0.5 * bend
            activ = (upper * half).astype(bf16)
            activ_ref[spot] = activ
            slope = half + (0.5 * gelu_scale) * upper * (1.0 - bend * bend) * (
                1.0 + 3.0 * gelu_cubic * square
            )
            slope_ref[spot] = slope.astype(bf16)
            h2 = h1 + dot_nn(activ, mlp_ref[pl.ds(hidden, hidden)])
            high = h2.astype(bf16)
            out_ref[spot] = high
            low = (h2 - high.astype(f32)).astype(bf16)
            projected = (dot_nt(high, dec_rows) + dot_nt(low, dec_rows)) * live
            top = projected.astype(bf16)
            node_ref[spot, pl.ds(0, 128)] = top
            node_ref[spot, pl.ds(128, 128)] = (projected - top.astype(f32)).astype(bf16)

        row_loop(tile, feed)

        c_output, weight = scalar_ref[0], scalar_ref[1]
        loads[3].wait()
        cores, uppers = {}, {}
        for band in range(bands):
            net = dot_nn(dec_ref[band], node_ref[...])
            net = (net[:, :128] + net[:, 128:]) * (c_output * third)
            error = (base_ref[band] + net) * keep_ref[band]
            high = error.astype(bf16)
            low = (error - high.astype(f32)).astype(bf16)
            turned = dot_tn(high, table_ref[0]) + dot_tn(low, table_ref[0]) + dot_tn(high, table_ref[1])
            f_ref[band] = turned[:sent]
            all_ref[node, band] = turned[:sent].astype(bf16)
            piece = all_ref.at[node, band]
            cores[0, band] = start_copy(started, place, piece, piece, f_sem.at[0, band], core=1)
            for i in range(1, place.uppers):
                uppers[i, band] = start_copy(started, place, piece, piece, f_sem.at[i, band], upper=i)
        gf_ref[...] = jnp.zeros_like(gf_ref)
        for band in range(bands):
            for i in range(1, place.uppers):
                uppers[i, band].wait_recv()
                source = lax.rem(place.upper + place.uppers - i, place.uppers) * 2 + place.core
                piece = all_ref.at[source, band]
                cores[i, band] = start_copy(started, place, piece, piece, pass_sem.at[i, band], core=1)
        for key in cores:
            cores[key].wait_recv()
        loss_rows = jnp.zeros((8, 128), f32)
        loads[4].wait()
        for band in range(bands):

            def add_lat(index, total):
                return total + kern_ref[band, pl.ds(index, 1)] * all_ref[
                    index // lats, lax.rem(index, lats)
                ].astype(f32)

            total = lax.fori_loop(0, all_lats, add_lat, jnp.zeros((sent, lanes), f32), unroll=4)
            loss_rows = loss_rows + jnp.sum(total * f_ref[band])
            gf_ref[pl.ds(0, sent)] = total * (2.0 * weight)
            grad = gf_ref[...]
            high = grad.astype(bf16)
            low = (grad - high.astype(f32)).astype(bf16)
            back = dot_nt(table_ref[0], high) + dot_nt(table_ref[0], low) + dot_nt(table_ref[1], high)
            gnet_ref[band] = (back * keep_ref[band] * c_output).astype(bf16)
        loss_out[...] = loss_rows * weight

        sums_ref[...] = jnp.zeros_like(sums_ref)

        def back_feed(spot):
            grad_node = dot_nn(turned_ref[0, spot], gnet_ref[0])
            for band in range(1, bands):
                grad_node += dot_nn(turned_ref[band, spot], gnet_ref[band])
            grad_node = grad_node * third
            high = grad_node.astype(bf16)
            low = (grad_node - high.astype(f32)).astype(bf16)
            node_ref[spot, pl.ds(0, 128)] = high
            grad_out = dot_nn(high, dec_rows) + dot_nn(low, dec_rows)
            branch = grad_out.astype(bf16)
            gb_ref[spot] = branch
            grad_activ = dot_nt(branch, mlp_ref[pl.ds(hidden, hidden)])
            grad_upper = (grad_activ * slope_ref[spot].astype(f32)).astype(bf16)
            slope_ref[spot] = grad_upper
            grad_second = dot_nn(grad_upper, mlp_ref[pl.ds(0, hidden)])
            unit, inverse = norm_parts(h1_ref[spot])
            scaled = grad_second * (1.0 + mod[2])
            grad_mid = grad_out + inverse * (
                scaled
                - jnp.mean(scaled, axis=-1, keepdims=True)
                - unit * jnp.mean(scaled * unit, axis=-1, keepdims=True)
            )
            sums_ref[2:3] += jnp.sum(grad_second * unit, axis=0, keepdims=True)
            sums_ref[3:4] += jnp.sum(grad_second, axis=0, keepdims=True)
            h1_ref[spot] = grad_mid
            grad_attn = grad_mid.astype(bf16)
            gattn_ref[spot] = grad_attn
            gblend_ref[spot] = dot_nn(grad_attn, attn_ref[pl.ds(3 * width, width)]).astype(bf16)

        row_loop(tile, back_feed)

        def outer_loop(target, offset, left, right, columns):
            @pl.loop(0, columns // big)
            def _(index):
                part = pl.multiple_of(index * big, big)
                product = dot_tn(left[:, pl.ds(part, big)], right[...])
                target[pl.ds(pl.multiple_of(offset + part, big), big)] = product.astype(bf16)

        gext_ref[...] = jnp.zeros_like(gext_ref)

        def back_attend(spot):
            count = near_ref[spot].astype(f32)
            for head in range(HEAD_COUNT):
                part = pl.ds(head * head_width, head_width)
                values = pl.ds(width + head * head_width, head_width)
                prob = prob_ref[head, spot].astype(f32)
                counted_prob = prob * count
                grad_blend = gblend_ref[spot, part]
                grad_prob = dot_nt(grad_blend, ext_ref[:, values])
                mean = jnp.sum(counted_prob * grad_prob, axis=-1, keepdims=True)
                grad_logit = (counted_prob * (grad_prob - mean)).astype(bf16)
                gext_ref[:, part] += dot_tn(grad_logit, q_ref[spot, part])
                q_ref[spot, part] = (dot_nn(grad_logit, ext_ref[:, part]) * score_scale).astype(bf16)
                gext_ref[:, values] += dot_tn(counted_prob.astype(bf16), grad_blend)

        row_loop(tile, back_attend)
        gext_ref[:, pl.ds(0, width)] = gext_ref[:, pl.ds(0, width)] * score_scale
        lost_ref[0] = gext_ref[pl.ds(rows, halo)].astype(bf16)
        lost_ref[1] = gext_ref[pl.ds(rows + halo, halo)].astype(bf16)
        from_upper = to_node(nodes - 1, lost_ref.at[0], back_ref.at[pl.ds(0, halo)], back_sem.at[0])
        from_lower = to_node(1, lost_ref.at[1], back_ref.at[pl.ds(halo, halo)], back_sem.at[1])

        outer_loop(mlp_out, hidden, activ_ref, gb_ref, hidden)
        outer_loop(mlp_out, 0, slope_ref, second_ref, hidden)
        outer_loop(attn_out, 3 * width, gattn_ref, blend_ref, width)
        outer_loop(attn_out, 0, q_ref, first_ref, width)
        from_upper.wait_recv()
        from_lower.wait_recv()

        def back_encode(spot):
            grad_pairs = gext_ref[spot] + dot_nn(lendt_ref[spot], back_ref[...])
            grad_pairs = grad_pairs.astype(bf16)
            ext_ref[spot] = grad_pairs
            grad_first = dot_nn(q_ref[spot], attn_ref[pl.ds(0, width)]) + dot_nn(
                grad_pairs, attn_ref[pl.ds(width, 2 * width)]
            )
            unit, inverse = norm_parts(h0_ref[spot])
            scaled = grad_first * (1.0 + mod[0])
            grad_in = h1_ref[spot] + inverse * (
                scaled
                - jnp.mean(scaled, axis=-1, keepdims=True)
                - unit * jnp.mean(scaled * unit, axis=-1, keepdims=True)
            )
            sums_ref[0:1] += jnp.sum(grad_first * unit, axis=0, keepdims=True)
            sums_ref[1:2] += jnp.sum(grad_first, axis=0, keepdims=True)
            gb_ref[spot] = grad_in.astype(bf16)

        row_loop(big, back_encode)
        outer_loop(attn_out, width, ext_ref.at[pl.ds(0, rows)], first_ref, 2 * width)

        feats_value = feats_ref[...]
        small_rows = small_ref.shape[0]
        cond = feats_value[:, 0:1] * sums_ref[0:1]
        for j in range(1, 4):
            cond += feats_value[:, j : j + 1] * sums_ref[j : j + 1]
        for low_row in range(0, small_rows, 128):
            total = cond[low_row : low_row + 128]
            if low_row < wide:
                total += dot_tn(mixed_ref[0, :, pl.ds(low_row, 128)], gb_ref[...])
            if low_row == start:
                total += dot_tn(node_ref[:, pl.ds(0, 128)], out_ref[...])
            high = total.astype(bf16)
            high_out[pl.ds(low_row, 128)] = high
            low_out[pl.ds(low_row, 128)] = (total - high.astype(f32)).astype(bf16)
        for copy in started:
            copy.wait_send()

    vmem = pl.BlockSpec(memory_space=pltpu.VMEM)
    hbm = pl.BlockSpec(memory_space=pl.ANY)
    dma = pltpu.SemaphoreType.DMA
    struct = jax.ShapeDtypeStruct
    low = lambda *shape: pltpu.VMEM(shape, bf16)
    full = lambda *shape: pltpu.VMEM(shape, f32)
    return pl.pallas_call(
        kernel,
        out_shape=(
            struct(attn.shape, bf16),
            struct(mlp.shape, bf16),
            struct(small.shape, bf16),
            struct(small.shape, bf16),
            struct((8, 128), f32),
        ),
        in_specs=[hbm, hbm, vmem, hbm, hbm, hbm] + [vmem] * 8 + [pl.BlockSpec(memory_space=pltpu.SMEM)],
        out_specs=(vmem,) * 5,
        scratch_shapes=[
            low(*attn.shape),
            low(*mlp.shape),
            low(*near.shape),
            low(*dec.shape),
            low(*dec_turned.shape),
            full(rows, width),
            full(rows, width),
            low(rows, width),
            low(rows, width),
            low(ext_rows, 2 * width),
            low(halo, 2 * width),
            low(HEAD_COUNT, rows, ext_rows),
            low(rows, width),
            low(rows, width),
            low(rows, hidden),
            low(rows, hidden),
            low(rows, width),
            low(rows, 256),
            full(lats, sent, lanes),
            low(nodes, lats, sent, lanes),
            full(128, lanes),
            low(bands, lons, 128),
            low(rows, width),
            low(rows, width),
            low(rows, width),
            full(ext_rows, 2 * width),
            low(2 * halo, 2 * width),
            low(2, halo, 2 * width),
            full(8, width),
            dma((5,)),
            dma((2, 2)),
            dma((place.uppers, lats, 2)),
            dma((place.uppers, lats, 2)),
            dma((2, 2)),
        ],
        compiler_params=pltpu.CompilerParams(
            collective_id=collective, has_side_effects=True, vmem_limit_bytes=62 << 20
        ),
    )(attn, mlp, small, near, dec, dec_turned, mixed, lend, lendt, kern, feats, base, keep, tables, scalars)


class Scatter:
    def __init__(self, place, pieces, grads, bufs, sems):
        self.place, self.pieces, self.grads = place, pieces, grads
        count = len(grads)
        self.core_in = bufs[:count]
        (self.over_out, self.over_in, self.under_out, self.under_in, self.over_out2, self.over_in2,
         self.under_out2, self.under_in2, self.far_out, self.far_in) = bufs[count:]
        (self.core_sem, self.over_sem, self.under_sem, self.over_sem2, self.under_sem2, self.far_sem) = sems
        self.started = []
        self.order = list(range(1, place.fars)) + [0]
        self.core, self.over, self.under, self.over2, self.under2, self.far = {}, {}, {}, {}, {}, {}
        self.head_rows = sum(rows for _, _, rows in pieces.head)
        self.tail_rows = sum(rows for _, _, rows in pieces.tail)

    def send(self, source, target, sem, **steps):
        return start_copy(self.started, self.place, source, target, sem, **steps)

    def begin(self, arrays):
        place = self.place
        other = 1 - place.core
        for k in self.order:
            far = place.moved(far=k)[2]
            for upper in range(place.uppers):
                for near in range(place.nears):
                    slot = place.slot(upper, other, far, near)
                    for a in arrays:
                        self.core[k, upper, near, a] = self.send(
                            self.grads[a].at[slot], self.core_in[a].at[k, upper, near],
                            self.core_sem.at[k, upper, near, a], core=1,
                        )

    def add(self, target, k, upper, near, pieces, others):
        far = self.place.moved(far=k)[2]
        slot = self.place.slot(upper, self.place.core, far, near)
        offset = 0
        for array, start, rows in pieces:
            mine = self.grads[array].at[slot]
            theirs = self.core_in[array].at[k, upper, near]

            @pl.loop(0, rows // ROW_CHUNK)
            def _(index, start=start, offset=offset, mine=mine, theirs=theirs):
                step = index * ROW_CHUNK
                here = pl.ds(pl.multiple_of(start + step, ROW_CHUNK), ROW_CHUNK)
                there = pl.ds(pl.multiple_of(offset + step, ROW_CHUNK), ROW_CHUNK)
                total = mine[here].astype(f32) + theirs[here].astype(f32)
                for other in others:
                    total += other[there].astype(f32)
                target[there] = total.astype(target.dtype)

            offset += rows

    def one(self, k):
        place, pieces = self.place, self.pieces
        for key in self.core:
            if key[0] == k:
                self.core[key].wait_recv()
        for i in range(1, place.uppers):
            for near in range(place.nears):
                self.add(self.over_out.at[k, i - 1, near], k, place.moved(upper=i)[0], near, pieces.head, [])
            self.over[k, i] = self.send(
                self.over_out.at[k, i - 1], self.over_in.at[k, i - 1], self.over_sem.at[k, i], upper=i
            )
        for j in range(1, place.nears):
            for upper in range(place.uppers):
                self.add(self.under_out.at[k, j - 1, upper], k, upper, place.moved(near=j)[3], pieces.tail, [])
            self.under[k, j] = self.send(
                self.under_out.at[k, j - 1], self.under_in.at[k, j - 1], self.under_sem.at[k, j], near=j
            )

    def overs(self, k, near):
        return [self.over_in.at[k, i - 1, near] for i in range(1, self.place.uppers)]

    def unders(self, k, upper):
        return [self.under_in.at[k, j - 1, upper] for j in range(1, self.place.nears)]

    def two(self, k):
        place, pieces = self.place, self.pieces
        for i in range(1, place.uppers):
            self.over[k, i].wait_recv()
        for j in range(1, place.nears):
            near = place.moved(near=j)[3]
            self.add(self.over_out2.at[k, j - 1], k, place.upper, near, pieces.head, self.overs(k, near))
            self.over2[k, j] = self.send(
                self.over_out2.at[k, j - 1], self.over_in2.at[k, j - 1], self.over_sem2.at[k, j], near=j
            )
        for j in range(1, place.nears):
            self.under[k, j].wait_recv()
        for i in range(1, place.uppers):
            upper = place.moved(upper=i)[0]
            self.add(self.under_out2.at[k, i - 1], k, upper, place.near, pieces.tail, self.unders(k, upper))
            self.under2[k, i] = self.send(
                self.under_out2.at[k, i - 1], self.under_in2.at[k, i - 1], self.under_sem2.at[k, i], upper=i
            )

    def three(self, k, target, extra):
        place, pieces = self.place, self.pieces
        for j in range(1, place.nears):
            self.over2[k, j].wait_recv()
        for i in range(1, place.uppers):
            self.under2[k, i].wait_recv()
        head, tail = pl.ds(0, self.head_rows), pl.ds(self.head_rows, self.tail_rows)
        self.add(
            target.at[head], k, place.upper, place.near, pieces.head,
            self.overs(k, place.near)
            + [self.over_in2.at[k, j - 1] for j in range(1, place.nears)]
            + [item.at[head] for item in extra],
        )
        self.add(
            target.at[tail], k, place.upper, place.near, pieces.tail,
            self.unders(k, place.upper)
            + [self.under_in2.at[k, i - 1] for i in range(1, place.uppers)]
            + [item.at[tail] for item in extra],
        )

    def step(self, step):
        fars, order = self.place.fars, self.order
        if step < fars:
            self.one(order[step])
        if 1 <= step <= fars:
            self.two(order[step - 1])
        if step >= 2 and order[step - 2]:
            k = order[step - 2]
            self.three(k, self.far_out.at[k - 1], [])
            self.far[k] = self.send(self.far_out.at[k - 1], self.far_in.at[k - 1], self.far_sem.at[k], far=k)

    def steps(self):
        return self.place.fars + 2

    def finish(self, own):
        fars = self.place.fars
        for k in range(1, fars):
            self.far[k].wait_recv()
        self.three(0, own, [self.far_in.at[k - 1] for k in range(1, fars)])

    def end(self):
        for copy in self.started:
            copy.wait_send()

    @staticmethod
    def copies(place, pieces):
        fars, nears, uppers = place.fars, place.nears, place.uppers
        return fars * uppers * nears * len(pieces.sizes) + 2 * fars * (uppers + nears - 2) + fars - 1

    @staticmethod
    def scratch(place, pieces, width):
        fars, nears, uppers = place.fars, place.nears, place.uppers
        head = sum(rows for _, _, rows in pieces.head)
        tail = sum(rows for _, _, rows in pieces.tail)
        dma = pltpu.SemaphoreType.DMA
        bufs = [(fars, uppers, nears, size) for size in pieces.sizes]
        bufs += [(fars, uppers - 1, nears, head)] * 2
        bufs += [(fars, nears - 1, uppers, tail)] * 2
        bufs += [(fars, nears - 1, head)] * 2
        bufs += [(fars, uppers - 1, tail)] * 2
        bufs += [(fars - 1, head + tail)] * 2
        if width:
            bufs = [pltpu.VMEM(shape + (width,), bf16) for shape in bufs]
        sems = [
            dma((fars, uppers, nears, len(pieces.sizes), 2)),
            dma((fars, uppers, 2)),
            dma((fars, nears, 2)),
            dma((fars, nears, 2)),
            dma((fars, uppers, 2)),
            dma((fars, 2)),
        ]
        return bufs, sems


class Strip:
    def __init__(self, ref, first, dims):
        self.ref, self.first, self.dims, self.at = ref, first, dims, self

    def __getitem__(self, index):
        index = index if isinstance(index, tuple) else (index,)
        sizes = self.dims[1:]
        flat, rows = 0, 1
        for axis, size in enumerate(sizes):
            if axis + 1 < len(index):
                flat = flat * size + index[axis + 1]
            else:
                flat, rows = flat * size, rows * size
        return self.ref.at[index[0], pl.ds(self.first + flat, rows)]


def strips(refs, shapes):
    result, at, first = [], 0, 0
    for shape in shapes:
        rows = math.prod(shape[1:])
        if first + rows > refs[at].shape[1]:
            at, first = at + 1, 0
        result.append(Strip(refs[at], first, shape))
        first += rows
    return result


class HalfGather:
    def __init__(self, place, shard, out, sems):
        self.place, self.shard, self.out = place, shard, out
        self.own_sem, self.far_sem, self.near_sem, self.mate_sem, self.core_sem = sems
        self.started, self.cores = [], []
        self.far, self.near, self.mate = {}, {}, {}

    def block(self, **steps):
        return self.out.at[self.place.slot(*self.place.moved(**steps))]

    def send(self, source, target, sem, **steps):
        return start_copy(self.started, self.place, source, target, sem, **steps)

    def begin(self):
        self.kept = pltpu.make_async_copy(self.shard, self.block(), self.own_sem)
        self.kept.start()
        for k in range(1, self.place.fars):
            self.far[k] = self.send(self.shard, self.block(), self.far_sem.at[k], far=k)

    def spread(self, k, j, source, target):
        for i in range(1, self.place.mates):
            self.mate[k, j, i] = self.send(source, target, self.mate_sem.at[k, j, i], mate=i)

    def to_core(self, k, i):
        place = self.place
        steps = dict(far=(place.fars - k) % place.fars)
        if i:
            steps["mate"] = place.mates - i
        upper, core, far, _ = place.moved(**steps)
        item = self.out.at[pl.ds(place.slot(upper, core, far, 0), place.nears)]
        self.cores.append(self.send(item, item, self.core_sem.at[k, 0, i], core=1))

    def step(self, step):
        place = self.place
        fars, nears = place.fars, place.nears
        if step < fars:
            if step:
                self.far[step].wait_recv()
            target = self.block(far=(fars - step) % fars)
            source = target if step else self.shard
            for j in range(1, nears):
                self.near[step, j] = self.send(source, target, self.near_sem.at[step, j], near=j)
            self.spread(step, 0, source, target)
        if 1 <= step <= fars:
            k = step - 1
            if not k:
                self.kept.wait()
            for j in range(1, nears):
                self.near[k, j].wait_recv()
                item = self.block(far=(fars - k) % fars, near=nears - j)
                self.spread(k, j, item, item)
            self.to_core(k, 0)
        if step >= 2:
            k = step - 2
            for i in range(1, place.mates):
                for j in range(nears):
                    self.mate[k, j, i].wait_recv()
                self.to_core(k, i)

    def end(self):
        wait_all(self.cores)
        for copy in self.started:
            copy.wait_send()

    @staticmethod
    def copies(place):
        fars, nears, mates = place.fars, place.nears, place.mates
        return (fars - 1) + fars * (nears - 1) + fars * nears * (mates - 1) + fars * mates

    @staticmethod
    def sems(place):
        dma = pltpu.SemaphoreType.DMA
        fars, nears, mates = place.fars, place.nears, place.mates
        return [
            dma,
            dma((fars, 2)),
            dma((fars, nears, 2)),
            dma((fars, nears, mates, 2)),
            dma((fars, nears, mates, 2)),
        ]


class MomentGather:
    def __init__(self, place, shards, outs, sems):
        self.place, self.shards, self.outs = place, shards, outs
        (self.own_sem, self.far_sem, self.near_sem, self.spread_sem, self.core_sem) = sems
        self.started, self.cores = [], []
        self.far, self.near, self.spread_copies = {}, {}, {}

    def block(self, **steps):
        slot = self.place.slot(*self.place.moved(**steps))
        return [out.at[slot] for out in self.outs]

    def send(self, source, target, sem, **steps):
        return start_copy(self.started, self.place, source, target, sem, **steps)

    def both(self, source, target, sems, **steps):
        return [self.send(source[a], target[a], sems.at[a], **steps) for a in range(2)]

    def spread(self, k, j, source, target):
        place = self.place
        for i in range(1, place.uppers):
            self.spread_copies[k, j, i, 0] = self.send(
                source[0], target[0], self.spread_sem.at[k, j, i, 0], upper=i
            )
        for i in range(1, place.mates):
            self.spread_copies[k, j, i, 1] = self.send(
                source[1], target[1], self.spread_sem.at[k, j, i, 1], mate=i
            )
        self.cores += self.both(source, target, self.core_sem.at[k, j, 0], core=1)

    def run(self):
        place = self.place
        fars, nears = place.fars, place.nears
        here = self.block()
        kept = [
            pltpu.make_async_copy(shard, target, self.own_sem.at[a])
            for a, (shard, target) in enumerate(zip(self.shards, here))
        ]
        for copy in kept:
            copy.start()
        for k in range(1, fars):
            self.far[k] = self.both(self.shards, here, self.far_sem.at[k], far=k)
        for step in range(fars + 2):
            if step < fars:
                k = step
                if k:
                    wait_all(self.far[k])
                target = self.block(far=(fars - k) % fars)
                source = target if k else self.shards
                for j in range(1, nears):
                    self.near[k, j] = self.both(source, target, self.near_sem.at[k, j], near=j)
                self.spread(k, 0, source, target)
            if 1 <= step <= fars:
                k = step - 1
                for j in range(1, nears):
                    wait_all(self.near[k, j])
                    item = self.block(far=(fars - k) % fars, near=nears - j)
                    self.spread(k, j, item, item)
            if step >= 2:
                k = step - 2
                for j in range(nears):
                    steps = dict(far=(fars - k) % fars, near=(nears - j) % nears)
                    for key in self.spread_copies:
                        if key[:2] != (k, j):
                            continue
                        i, a = key[2:]
                        self.spread_copies[key].wait_recv()
                        if a:
                            item = self.block(mate=place.mates - i, **steps)[1]
                        else:
                            item = self.block(upper=place.uppers - i, **steps)[0]
                        self.cores.append(self.send(item, item, self.core_sem.at[k, j, i, a], core=1))
        for copy in kept:
            copy.wait()
        wait_all(self.cores)
        for copy in self.started:
            copy.wait_send()

    @staticmethod
    def sems(place):
        dma = pltpu.SemaphoreType.DMA
        fars, nears, uppers = place.fars, place.nears, place.uppers
        return [
            dma((2,)),
            dma((fars, 2, 2)),
            dma((fars, nears, 2, 2)),
            dma((fars, nears, uppers, 2, 2)),
            dma((fars, nears, uppers, 2, 2)),
        ]


def total_body(place, tile, slots, sems):
    value = tile
    upper, core, far, near = place.moved()
    stages = (
        ("core", 2, core),
        ("near", place.nears, near),
        ("upper", place.uppers, upper),
        ("far", place.fars, far),
    )
    for stage, (name, size, mine) in enumerate(stages):
        slots[stage, mine] = value
        copies = []
        for step in range(1, size):
            piece = slots.at[stage, mine]
            start_copy(copies, place, piece, piece, sems.at[stage, step], **{name: step})
        for copy in copies:
            copy.wait()
        value = slots[stage, 0]
        for other in range(1, size):
            value = value + slots[stage, other]
    return value


def reduce_and_gather(nodes, zeros, names, grads, mlp_sum, loss_tile, mom_attn, mom_mlp, small_rows, collective):
    place = Place(nodes, zeros)
    devices, _, width = grads[0].shape
    attn_rows, mlp_rows = mom_attn.shape[0], mom_mlp.shape[0]
    lead = names.index("mlp") if "mlp" in names else 0
    pieces = Pieces([item.shape[1] for item in grads], lead)
    moment_sizes = (sixteens(attn_rows), sixteens(mlp_rows))
    bufs, sems = Scatter.scratch(place, pieces, width)
    deepest = max(place.fars, place.uppers, place.nears, 2)
    summed = [] if mlp_sum is None else [mlp_sum]
    count = len(grads)
    starts, offset = {}, 0
    for array in [lead] + [i for i in range(count) if i != lead]:
        starts[names[array]] = offset
        offset += pieces.sizes[array]

    def kernel(*refs):
        grad_refs = refs[:count]
        refs = refs[count:]
        if summed:
            sum_ref, *refs = refs
        loss_ref, attn_ref, mlp_ref = refs[:3]
        small_out, attn_out, mlp_out, total_out, attn_all, mlp_all = refs[3:9]
        own, attn_shard, mlp_shard, slots, slot_sems = refs[9:14]
        rest = refs[14:]
        place.locate()
        place.greet()
        scatter = Scatter(
            place, pieces, grad_refs, rest[: len(bufs)], rest[len(bufs) : len(bufs) + len(sems)]
        )
        scatter.begin([lead] + [i for i in range(count) if i != lead])
        for step in range(scatter.steps()):
            scatter.step(step)
        scatter.finish(own)
        g_attn = own[pl.ds(starts["attn"], attn_rows)]
        g_mlp = sum_ref[...] if summed else own[pl.ds(starts["mlp"], mlp_rows)]
        g_small = own[pl.ds(starts["high"], small_rows)] + own[pl.ds(starts["low"], small_rows)]
        small_out[...] = g_small
        squares = jnp.sum(g_attn * g_attn) + jnp.sum(g_mlp * g_mlp) + jnp.sum(g_small * g_small)
        tile = jnp.where(iota((8, 128), 0) < 4, squares, loss_ref[...])
        total = total_body(place, tile, slots, slot_sems)
        total_out[...] = total
        factor = jnp.minimum(1.0, clip_limit * lax.rsqrt(total[0:1, 0:1]))
        for ref, out, shard, grad, size in (
            (attn_ref, attn_out, attn_shard, g_attn, attn_rows),
            (mlp_ref, mlp_out, mlp_shard, g_mlp, mlp_rows),
        ):
            moment = moment_decay * ref[...] + factor * grad
            out[...] = moment
            if size < shard.shape[0]:
                shard[...] = jnp.zeros_like(shard)
            shard[pl.ds(0, size)] = moment.astype(bf16)
        moments = MomentGather(
            place, (attn_shard, mlp_shard), (attn_all, mlp_all), rest[len(bufs) + len(sems) :]
        )
        moments.run()
        scatter.end()

    vmem = pl.BlockSpec(memory_space=pltpu.VMEM)
    hbm = pl.BlockSpec(memory_space=pl.ANY)
    struct = jax.ShapeDtypeStruct
    return pl.pallas_call(
        kernel,
        out_shape=(
            struct((small_rows, width), f32),
            struct((attn_rows, width), f32),
            struct((mlp_rows, width), f32),
            struct((8, 128), f32),
            struct((devices, moment_sizes[0], width), bf16),
            struct((devices, moment_sizes[1], width), bf16),
        ),
        in_specs=[vmem] * (count + len(summed) + 3),
        out_specs=(vmem,) * 4 + (hbm,) * 2,
        scratch_shapes=[
            pltpu.VMEM((sum(pieces.sizes), width), f32),
            pltpu.VMEM((moment_sizes[0], width), bf16),
            pltpu.VMEM((moment_sizes[1], width), bf16),
            pltpu.VMEM((4, deepest, 8, 128), f32),
            pltpu.SemaphoreType.DMA((4, deepest, 2)),
        ]
        + bufs
        + sems
        + MomentGather.sems(place),
        compiler_params=pltpu.CompilerParams(
            collective_id=collective, has_side_effects=True, vmem_limit_bytes=56 << 20
        ),
    )(*grads, *summed, loss_tile, mom_attn, mom_mlp)


def basis_apply(grams, moments):
    size = grams[0].shape[0]
    eye = jnp.where(iota((size, size), 0) == iota((size, size), 1), 1.0, 0.0)
    both = range(len(grams))
    scales = [
        lax.rsqrt(jnp.sum(jnp.sum(gram * eye, axis=1, keepdims=True), axis=0, keepdims=True) + trace_epsilon)
        for gram in grams
    ]
    current = [grams[i] * (scales[i] * scales[i]) for i in both]
    result = [moments[i] * scales[i] for i in both]
    for iteration in range(NS_ITERS - 1):
        low = [current[i].astype(bf16) for i in both]
        rest = [newton_second * current[i] + newton_third * dot_nn(low[i], low[i]) for i in both]
        rest = [item.astype(bf16) for item in rest]
        once = [dot_nn(rest[i], low[i]) for i in both]
        result = [newton_first * result[i] + dot_nn(result[i].astype(bf16), rest[i]) for i in both]
        current = [
            (newton_first * newton_first) * current[i]
            + (2.0 * newton_first) * once[i]
            + dot_nn(once[i].astype(bf16), rest[i])
            for i in both
        ]
    low = [current[i].astype(bf16) for i in both]
    once = [dot_nn(result[i].astype(bf16), low[i]) for i in both]
    twice = [dot_nn(once[i].astype(bf16), low[i]) for i in both]
    return [newton_first * result[i] + newton_second * once[i] + newton_third * twice[i] for i in both]


def update_weights(nodes, zeros, attn_sets, mlp_sets, totals, sums, moments, weights, averages, small_moments):
    width = attn_sets[0].shape[1]
    attn_rows, mlp_rows, small_rows = [w.shape[0] for w in weights]
    half = mlp_sets[0].shape[0] // 2
    block = width
    inputs = (*sums, *moments, *weights, *averages, *small_moments)
    count, sets = len(inputs), len(attn_sets)
    fresh = sets == 1

    def kernel(total_ref, *refs):
        attn_hbm, mlp_hbm, sources = refs[:sets], refs[sets : 2 * sets], refs[2 * sets : 2 * sets + count]
        refs = refs[2 * sets + count :]
        loss_out, clip_out, new_attn, new_mlp, new_small, new_m, new_v, new_e_attn, new_e_mlp, new_e_small = refs[:10]
        mom_attn_out, mom_mlp_out = refs[10:12]
        gram_attn, gram_mlp, attn_sem, mlp_sem, row_sem = refs[12:17]
        attn_refs, mlp_refs, rows = refs[17 : 17 + sets], refs[17 + sets : 17 + 2 * sets], refs[17 + 2 * sets :]
        g_refs, rows = rows[: len(sums)], rows[len(sums) :]
        mom_attn, mom_mlp, w_attn, w_mlp, w_small, e_attn, e_mlp, e_small, m_ref, v_ref = rows
        flat = lax.axis_index("node") * zeros + lax.axis_index("zero")
        attn_upper = flat * attn_rows >= 3 * width
        mlp_upper = flat * mlp_rows >= half
        first_row = jnp.where(mlp_upper, half, 0)
        copies_mlp = [
            pltpu.make_async_copy(
                mlp_hbm[i].at[pl.ds(pl.multiple_of(first_row + low, block), block)],
                mlp_refs[i].at[pl.ds(low, block)],
                mlp_sem.at[low // block, i],
            )
            for low in range(0, half, block)
            for i in range(sets)
        ]
        copies_attn = [
            pltpu.make_async_copy(attn_hbm[i], attn_refs[i], attn_sem.at[i]) for i in range(sets)
        ]
        copies = [
            pltpu.make_async_copy(source, target, row_sem.at[index])
            for index, (source, target) in enumerate(zip(sources, refs[17 + 2 * sets :]))
        ]
        for copy in copies_mlp + copies_attn + copies:
            copy.start()
        total = total_ref[0]
        for index in range(1, total_ref.shape[0]):
            total = total + total_ref[index]
        loss_out[...] = total[4:5, 0:1]
        clip_out[...] = jnp.sqrt(total[0:1, 0:1])
        factor = jnp.minimum(1.0, clip_limit * lax.rsqrt(total[0:1, 0:1]))

        def momentum(refs, index):
            part = pl.ds(index * block if isinstance(index, int) else pl.multiple_of(index * block, block), block)
            if fresh:
                return refs[0][part]
            return (moment_decay * refs[0][part].astype(f32) + factor * refs[1][part].astype(f32)).astype(bf16)

        for index in range(half // block):
            for copy in copies_mlp[index * sets : (index + 1) * sets]:
                copy.wait()
            part = momentum(mlp_refs, index)
            if index:
                gram_mlp[...] += dot_tn(part, part)
            else:
                gram_mlp[...] = dot_tn(part, part)

        for copy in copies_attn:
            copy.wait()
        gram_attn[...] = jnp.zeros_like(gram_attn)
        start = jnp.where(attn_upper, 3, 0)

        @pl.loop(start, jnp.where(attn_upper, 4, 3))
        def _(index):
            part = momentum(attn_refs, index)
            gram_attn[...] += dot_tn(part, part)

        for copy in copies:
            copy.wait()

        clipped = factor * g_refs[0][...]
        first = adam_first * m_ref[...] + (1.0 - adam_first) * clipped
        second = adam_second * v_ref[...] + (1.0 - adam_second) * clipped * clipped
        new_m[...] = first
        new_v[...] = second
        small = w_small[...] - adam_rate * (first / (1.0 - adam_first**STEP)) / (
            jnp.sqrt(second / (1.0 - adam_second**STEP)) + adam_epsilon
        )
        new_small[...] = small
        new_e_small[...] = average_decay * e_small[...] + (1.0 - average_decay) * small

        attn_moment, mlp_moment = mom_attn[...], mom_mlp[...]
        if not fresh:
            attn_moment = moment_decay * attn_moment + factor * g_refs[1][...]
            mlp_moment = moment_decay * mlp_moment + factor * g_refs[2][...]
        mom_attn_out[...] = attn_moment
        mom_mlp_out[...] = mlp_moment
        attn_step, mlp_step = basis_apply((gram_attn[...], gram_mlp[...]), (attn_moment, mlp_moment))
        attn_factor = jnp.where(attn_upper, 0.2 * math.sqrt(width), 0.2 * math.sqrt(3 * width))
        mlp_factor = 0.2 * math.sqrt(max(half, width))
        for step, rate, old, new, mean, new_mean in (
            (attn_step, orthogonal_rate * attn_factor, w_attn, new_attn, e_attn, new_e_attn),
            (mlp_step, orthogonal_rate * mlp_factor, w_mlp, new_mlp, e_mlp, new_e_mlp),
        ):
            value = old[...] - rate * step
            new[...] = value
            new_mean[...] = average_decay * mean[...] + (1.0 - average_decay) * value

    vmem = pl.BlockSpec(memory_space=pltpu.VMEM)
    hbm = pl.BlockSpec(memory_space=pl.ANY)
    one = jnp.zeros((1, 1), f32)
    outs = [one, one, weights[0], weights[1], weights[2], weights[2], weights[2], weights[0], weights[1], weights[2]]
    outs += [weights[0], weights[1]]
    dma = pltpu.SemaphoreType.DMA
    return pl.pallas_call(
        kernel,
        out_shape=tuple(jax.ShapeDtypeStruct(item.shape, f32) for item in outs),
        in_specs=[vmem] + [hbm] * (2 * sets + count),
        out_specs=(vmem,) * 12,
        scratch_shapes=[
            pltpu.VMEM((width, width), f32),
            pltpu.VMEM((width, width), f32),
            dma((sets,)),
            dma((half // block, sets)),
            dma((count,)),
        ]
        + [pltpu.VMEM(attn_sets[0].shape, bf16)] * sets
        + [pltpu.VMEM((half, width), bf16)] * sets
        + [pltpu.VMEM(item.shape, f32) for item in inputs],
        compiler_params=pltpu.CompilerParams(vmem_limit_bytes=62 << 20),
    )(totals, *attn_sets, *mlp_sets, *inputs)


def train_step(nodes, zeros, weights, grid, target, land, near_turned, enc_turned, dec_turned, lent, legendre, vector, tables, waves, moments, cin, collective):
    place = Place(nodes, zeros)
    devices = nodes * zeros
    attn_rows, mlp_rows, small_rows = [w.shape[0] for w in weights]
    width = weights[0].shape[1]
    hidden = devices * mlp_rows // 2
    bands, lons, channels = target.shape
    fanout, rows = near_turned.shape
    enc_edges, dec_edges = enc_turned.shape[0], dec_turned.shape[0]
    halo = lent.shape[1]
    ext_rows = rows + 2 * halo
    lats, lows, flat = legendre.shape
    lanes = tables.shape[2]
    modes, wave_first, wave_end = waves
    all_lats = nodes * lats
    wide = -(-cin // 128) * 128
    start = cin // 128 * 128
    shift = cin - start
    sent = sixteens(channels)
    flat_lons = -(-lons // 128) * 128
    flat_pixels = -(-bands * lons // 128) * 128
    all_small = devices * small_rows
    cond_start = cin + channels
    big, tile, chunk = 256, 128, 512
    head_width = width // HEAD_COUNT
    score_scale = head_width ** (-0.5)
    third = 1.0 / dec_edges
    first_rows = attn_rows + small_rows
    packed_rows = first_rows + small_rows
    first_pieces = Pieces([first_rows], 0)
    mlp_pieces = Pieces([mlp_rows], 0)
    mlp_sum_pieces = Pieces([mlp_rows], 0)
    last_pieces = Pieces([packed_rows], 0, 2 / 3)
    attn_pieces = Pieces([attn_rows], 0)
    tile_pieces = Pieces([attn_rows, 8], 0)
    scatter_bufs, _ = Scatter.scratch(place, mlp_sum_pieces, width)
    last_shapes, _ = Scatter.scratch(place, last_pieces, 0)
    early_copies = Gather.copies(place, first_pieces) + Gather.copies(place, mlp_pieces)
    middle_copies = Gather.copies(place, attn_pieces) + HalfGather.copies(place)
    late_copies = (
        Gather.copies(place, tile_pieces)
        + HalfGather.copies(place)
        + Scatter.copies(place, mlp_sum_pieces)
        + Scatter.copies(place, last_pieces)
    )
    others = (nodes - 1) + (place.nears - 1) + (place.fars - 1) + 4 + (2 * place.uppers - 1) * lats
    copies = early_copies + middle_copies + late_copies + others

    def kernel(
        attn_in, mlp_in, small_in, grid_ref, target_ref, land_ref, near_in, enc_in, dec_in, lent_ref, leg_ref,
        vector_ref, table_ref, mom_attn_in, mom_mlp_in,
        attn_sum, mlp_sum, small_sum, tiles_out, mom_attn_all, mom_mlp_all, g_attn_all, g_mlp_all,
        own, mom_attn_shard, mom_mlp_shard, g_attn_shard, g_mlp_shard, tile_shard,
        first_shard, mlp_shard, legs, parts, sums, kern_ref,
        packed_ref, mlp_ref, near_ref, dec_ref, mixed_ref, lendt_ref, h0_ref, h1_ref, first_ref, q_ref,
        ext_ref, lent_rows, prob_ref, blend_ref, second_ref, activ_ref, slope_ref, out_ref, node_ref, all_ref,
        gf_ref, gnet_ref, gnode_ref, gb_ref, gattn_ref, gblend_ref, gext_ref, back_ref, lost_ref, sums_ref,
        scale_ref, error_ref, column_ref, lists_ref, input_ref, dec_rows_ref, feats_ref,
        pool_ref, own_sem,
        *bufs,
    ):
        pool = Pool(pool_ref)
        place.locate()
        node = lax.axis_index("node")
        zero = lax.axis_index("zero")
        first_shard[pl.ds(0, attn_rows)] = attn_in[...].astype(bf16)
        first_shard[pl.ds(attn_rows, small_rows)] = small_in[...].astype(bf16)
        legs[node] = leg_ref[...]
        place.greet(nodes)
        gather = Gather(place, first_pieces, (first_shard,), (packed_ref,), pool.gather(own_sem, 0))
        gather_mlp = Gather(place, mlp_pieces, (mlp_shard,), (mlp_ref,), pool.gather(own_sem, 1))
        gather.begin()
        started = []

        def to_node(step, source, target):
            sems = pool.take()
            copy = pltpu.make_async_remote_copy(
                src_ref=source,
                dst_ref=target,
                send_sem=sems.at[0],
                recv_sem=sems.at[1],
                device_id=(lax.rem(node + step, nodes), zero),
                device_id_type=MESH,
            )
            copy.start()
            started.append(copy)
            return copy

        gather.step(0)
        leg_copies = [
            to_node(step, leg_ref, legs.at[node]) for step in range(1, nodes)
        ]
        mlp_shard[...] = mlp_in[...].astype(bf16)
        gather_mlp.begin()
        mom_attn_shard[...] = mom_attn_in[...].astype(bf16)
        mom_mlp_shard[...] = mom_mlp_in[...].astype(bf16)
        gather_moms = [
            Gather(place, attn_pieces, (mom_attn_shard,), (mom_attn_all,), pool.gather(own_sem, 2)),
            HalfGather(place, mom_mlp_shard, mom_mlp_all, pool.half(own_sem, 3)),
        ]

        def mom_step(step):
            for item in gather_moms:
                item.step(step)

        def row_loop(size, body, hooks=()):
            count = rows // size
            cuts = [count * i // (len(hooks) + 1) for i in range(len(hooks) + 2)]
            for i in range(len(hooks) + 1):

                @pl.loop(cuts[i], cuts[i + 1])
                def _(index):
                    body(pl.ds(pl.multiple_of(index * size, size), size))

                if i < len(hooks):
                    hooks[i]()

        def mix():
            column_ref[pl.ds(0, enc_edges), pl.ds(0, rows)] = enc_in[...]
            lists_ref[pl.ds(0, rows), pl.ds(0, 8)] = jnp.transpose(column_ref[pl.ds(0, 8), pl.ds(0, rows)])
            lane = iota((1, cin), 1)
            scale = jnp.where(lane < channels, vector_ref[0:1, c_input_lane : c_input_lane + 1], 1.0)

            @pl.loop(0, bands)
            def _(band):
                input_ref[band] = (grid_ref[band].astype(f32) * scale).astype(bf16)

            mixed_ref[...] = jnp.zeros_like(mixed_ref)

            def mix_rows(spot):
                lists = lists_ref[spot]
                mean = jnp.zeros((tile, cin), f32)
                for band in range(bands):
                    place_of = iota((tile, lons), 1) + band * lons
                    total = jnp.zeros((tile, lons), f32)
                    for j in range(enc_edges):
                        total += jnp.where(lists[:, j : j + 1] == place_of, 1.0 / enc_edges, 0.0)
                    mean += dot_nn(total.astype(bf16), input_ref[band])
                high = mean.astype(bf16)
                mixed_ref[0, spot, pl.ds(0, cin)] = high
                mixed_ref[1, spot, pl.ds(0, cin)] = (mean - high.astype(f32)).astype(bf16)

            row_loop(tile, mix_rows)

        def count_near():
            lists_ref[pl.ds(0, rows), pl.ds(0, fanout)] = jnp.transpose(near_in[...])

            def count_rows(spot):
                lists = lists_ref[spot]
                place_of = iota((tile, ext_rows), 1)
                total = jnp.zeros((tile, ext_rows), f32)
                for j in range(fanout):
                    total += jnp.where(lists[:, j : j + 1] == place_of, 1.0, 0.0)
                near_ref[spot] = jnp.where(total > 0.0, jnp.log2(jnp.maximum(total, 1.0)), absent)

            row_loop(tile, count_rows)

        def count_dec():
            column_ref[pl.ds(0, dec_edges), pl.ds(0, bands * lons)] = dec_in[...]
            lists_ref[:, pl.ds(0, 8)] = jnp.transpose(column_ref[...])

            @pl.loop(0, bands)
            def _(band):
                lists = lists_ref[pl.ds(pl.multiple_of(band * lons, 8), lons)]
                place_of = iota((lons, rows), 1)
                total = jnp.zeros((lons, rows), f32)
                for j in range(dec_edges):
                    total += jnp.where(lists[:, j : j + 1] == place_of, 1.0, 0.0)
                dec_ref[band] = total.astype(bf16)

        near_parts, far_sums = [], []

        def gram():
            for copy in leg_copies:
                copy.wait_recv()

            @pl.loop(0, all_lats)
            def _(index):
                other = legs[index // lats, lax.rem(index, lats)].astype(f32)
                for t in range(lats):
                    product = leg_ref[t].astype(f32) * other
                    parts[place.near, t, pl.ds(index, 1)] = jnp.sum(product, axis=0, keepdims=True)

            for j in range(1, place.nears):
                piece = parts.at[place.near]
                near_parts.append(start_copy(started, place, piece, piece, pool, near=j))

        def gram_near():
            wait_all(near_parts)
            total = parts[0]
            for j in range(1, place.nears):
                total = total + parts[j]
            sums[place.far] = total
            for k in range(1, place.fars):
                piece = sums.at[place.far]
                far_sums.append(start_copy(started, place, piece, piece, pool, far=k))

        def gram_far():
            wait_all(far_sums)
            total = sums[0]
            for k in range(1, place.fars):
                total = total + sums[k]
            kern_ref[...] = jnp.zeros_like(kern_ref)
            kern_ref[:, :, pl.ds(0, flat)] = total
            cosines = kern_ref[...]
            sines = pltpu.roll(cosines, modes - wave_first, 2)
            spot = iota((1, 1, lanes), 2)
            kern_ref[...] = jnp.where(
                spot < modes, cosines, jnp.where(spot < modes + wave_end - wave_first, sines, 0.0)
            )

        lendt_ref[...] = jnp.where(lent_ref[...] == iota((rows, halo), 0), 1.0, 0.0).astype(bf16)
        work = [mix, gram, count_dec, gram_near]
        for k in range(1, place.fars + 2):
            gather.step(k)
            if k == 1:
                gather_mlp.step(0)
            if work:
                work.pop(0)()
        while work:
            work.pop(0)()
        gather.end()
        gather_mlp.step(1)

        def small_part(low, size):
            blocks = pl.ds(low // small_rows, size // small_rows)
            return packed_ref[blocks, pl.ds(attn_rows, small_rows)].reshape(size, width)

        row = iota((all_small, 128), 0) - cond_start
        lane = iota((all_small, 128), 1)
        feature = vector_ref[0:1]
        block = jnp.where(row >= 0, row // NOISE_FEATS, 4)
        picked = jnp.where((row - block * NOISE_FEATS == lane) & (block < 4) & (lane < NOISE_FEATS), feature, 0.0)
        column = jnp.sum(picked, axis=1, keepdims=True)
        feats_ref[...] = jnp.where(lane == block, column, 0.0)
        mods = dot_tn(feats_ref[...].astype(bf16), small_part(0, all_small))
        mod = [mods[j : j + 1] for j in range(4)]

        def attn_part(low, size):
            return packed_ref[pl.ds(low // attn_rows, size // attn_rows), pl.ds(0, attn_rows)].reshape(size, width)

        def mlp_part(low):
            return mlp_ref[pl.ds(low // mlp_rows, chunk // mlp_rows)].reshape(chunk, width)

        def encode(spot):
            enc = small_part(0, wide)
            h0 = dot_nn(mixed_ref[0, spot], enc) + dot_nn(mixed_ref[1, spot], enc)
            h0_ref[spot] = h0
            unit, inverse = norm_parts(h0)
            first = (unit * (1.0 + mod[0]) + mod[1]).astype(bf16)
            first_ref[spot] = first
            ext_ref[spot] = dot_nt(first, attn_part(width, 2 * width)).astype(bf16)
            q_ref[spot] = dot_nt(first, attn_part(0, width)).astype(bf16)

        row_loop(big, encode)
        lent_rows[...] = dot_tn(lendt_ref[...], ext_ref[pl.ds(0, rows)]).astype(bf16)
        up = to_node(1, lent_rows, ext_ref.at[pl.ds(rows, halo)])
        down = to_node(nodes - 1, lent_rows, ext_ref.at[pl.ds(rows + halo, halo)])
        gather_mlp.step(2)
        count_near()
        gram_far()
        gather_mlp.step(3)
        for item in gather_moms:
            item.begin()
        up.wait_recv()
        down.wait_recv()

        def attend(spot):
            often = near_ref[spot]
            for head in range(HEAD_COUNT):
                part = pl.ds(head * head_width, head_width)
                values = pl.ds(width + head * head_width, head_width)
                logits = dot_nt(q_ref[spot, part], ext_ref[:, part]) * (score_scale * log2_e) + often
                raised = jnp.exp2(logits - jnp.max(logits, axis=-1, keepdims=True))
                inverse = 1.0 / jnp.sum(raised, axis=-1, keepdims=True)
                raised = raised.astype(bf16)
                prob_ref[head, spot] = raised
                scale_ref[spot, pl.ds(head, 1)] = inverse
                blend_ref[spot, part] = (dot_nn(raised, ext_ref[:, values]) * inverse).astype(bf16)

        row_loop(big, attend, [lambda: gather_mlp.step(4), lambda: gather_mlp.step(5)])
        for k in range(6, place.fars + 2):
            gather_mlp.step(k)
        gather_mlp.end()
        mom_step(0)
        lane = iota((1, 128), 1)
        live = jnp.where(lane < channels, 1.0, 0.0)
        dec_rows_ref[...] = pltpu.roll(small_part(start, 128).astype(f32), 128 - shift, 0).astype(bf16)

        def feed(spot):
            h1 = h0_ref[spot] + dot_nt(blend_ref[spot], attn_part(3 * width, width))
            h1_ref[spot] = h1
            unit, inverse = norm_parts(h1)
            second = (unit * (1.0 + mod[2]) + mod[3]).astype(bf16)
            second_ref[spot] = second
            h2 = h1
            for low in range(0, hidden, chunk):
                upper = dot_nt(second, mlp_part(low))
                square = upper * upper
                bend = jnp.tanh(upper * (gelu_scale + (gelu_scale * gelu_cubic) * square))
                half = 0.5 + 0.5 * bend
                activ = (upper * half).astype(bf16)
                activ_ref[low // chunk, spot] = activ
                slope = half + upper * (1.0 - bend * bend) * (
                    0.5 * gelu_scale + (1.5 * gelu_scale * gelu_cubic) * square
                )
                slope_ref[low // chunk, spot] = slope.astype(bf16)
                h2 += dot_nn(activ, mlp_part(hidden + low))
            high = h2.astype(bf16)
            out_ref[spot] = high
            low = (h2 - high.astype(f32)).astype(bf16)
            dec_rows = dec_rows_ref[...]
            projected = (dot_nt(high, dec_rows) + dot_nt(low, dec_rows)) * live
            top = projected.astype(bf16)
            node_ref[spot, pl.ds(0, 128)] = top
            node_ref[spot, pl.ds(128, 128)] = (projected - top.astype(f32)).astype(bf16)

        row_loop(big, feed)
        mom_step(1)

        c_skip = vector_ref[0:1, c_skip_lane : c_skip_lane + 1]
        c_output = vector_ref[0:1, c_output_lane : c_output_lane + 1]
        weight = vector_ref[0:1, weight_lane : weight_lane + 1]
        column_ref[pl.ds(0, bands), pl.ds(0, lons)] = land_ref[...]
        masks = jnp.transpose(column_ref[pl.ds(0, 8), pl.ds(0, flat_lons)].astype(f32))
        last = jnp.where(lane == channels - 1, 1.0, 0.0)

        def keep(band):
            return live * (1.0 - masks[:lons, band : band + 1] * last)

        error_ref[...] = jnp.zeros_like(error_ref)
        cores, uppers = {}, {}
        for band in range(bands):
            net = dot_nn(dec_ref[band], node_ref[...])
            net = (net[:, :128] + net[:, 128:]) * (c_output * third)
            noisy = grid_ref[band, :, pl.ds(0, 128)].astype(f32)
            error_ref[:, pl.ds(0, channels)] = target_ref[band]
            error = (c_skip * noisy + net - error_ref[...]) * keep(band)
            high = error.astype(bf16)
            low = (error - high.astype(f32)).astype(bf16)
            turned = dot_tn(high, table_ref[0]) + dot_tn(low, table_ref[0]) + dot_tn(high, table_ref[1])
            gext_ref[pl.ds(band * sent, sent), pl.ds(0, lanes)] = turned[:sent]
            all_ref[node, band] = turned[:sent].astype(bf16)
            piece = all_ref.at[node, band]
            for i in range(1, place.uppers):
                uppers[i, band] = start_copy(started, place, piece, piece, pool, upper=i)
            cores[0, band] = start_copy(started, place, piece, piece, pool, core=1)
        gf_ref[...] = jnp.zeros_like(gf_ref)
        mom_step(2)

        def add_nodes(base, total, band):
            def add_lat(index, value):
                source = base + index // lats
                return value + kern_ref[band, pl.ds(source * lats + lax.rem(index, lats), 1)] * all_ref[
                    source, lax.rem(index, lats)
                ].astype(f32)

            return lax.fori_loop(0, 2 * lats, add_lat, total, unroll=8)

        for band in range(bands):
            cores[0, band].wait_recv()
        for band in range(bands):
            gext_ref[pl.ds((lats + band) * sent, sent), pl.ds(0, lanes)] = add_nodes(place.upper * 2, jnp.zeros((sent, lanes), f32), band)
            for i in range(1, place.uppers):
                uppers[i, band].wait_recv()
                source = lax.rem(place.upper + place.uppers - i, place.uppers) * 2 + place.core
                piece = all_ref.at[source, band]
                cores[i, band] = start_copy(started, place, piece, piece, pool, core=1)
        for i in range(1, place.uppers):
            for band in range(bands):
                cores[i, band].wait_recv()
        loss_rows = jnp.zeros((8, 128), f32)
        for band in range(bands):
            total = gext_ref[pl.ds((lats + band) * sent, sent), pl.ds(0, lanes)]
            for i in range(1, place.uppers):
                total = add_nodes(lax.rem(place.upper + i, place.uppers) * 2, total, band)
            loss_rows = loss_rows + jnp.sum(total * gext_ref[pl.ds(band * sent, sent), pl.ds(0, lanes)])
            gf_ref[pl.ds(0, sent)] = total * (2.0 * weight)
            grad = gf_ref[...]
            high = grad.astype(bf16)
            low = (grad - high.astype(f32)).astype(bf16)
            back = dot_nt(table_ref[0], high) + dot_nt(table_ref[0], low) + dot_nt(table_ref[1], high)
            gnet_ref[band] = (back * keep(band) * c_output).astype(bf16)
        loss_share = loss_rows * weight

        sums_ref[...] = jnp.zeros_like(sums_ref)
        grad_node = dot_tn(gnet_ref[0], dec_ref[0])
        for band in range(1, bands):
            grad_node += dot_tn(gnet_ref[band], dec_ref[band])
        gnode_ref[...] = jnp.transpose(grad_node * third)

        def back_feed(spot):
            grad_node = gnode_ref[spot]
            high = grad_node.astype(bf16)
            low = (grad_node - high.astype(f32)).astype(bf16)
            node_ref[spot, pl.ds(0, 128)] = high
            dec_rows = dec_rows_ref[...]
            grad_out = dot_nn(high, dec_rows) + dot_nn(low, dec_rows)
            branch = grad_out.astype(bf16)
            gb_ref[spot] = branch
            grad_second = jnp.zeros((big, width), f32)
            for low in range(0, hidden, chunk):
                grad_activ = dot_nt(branch, mlp_part(hidden + low))
                grad_upper = (grad_activ * slope_ref[low // chunk, spot].astype(f32)).astype(bf16)
                slope_ref[low // chunk, spot] = grad_upper
                grad_second += dot_nn(grad_upper, mlp_part(low))
            unit, inverse = norm_parts(h1_ref[spot])
            scaled = grad_second * (1.0 + mod[2])
            grad_mid = grad_out + inverse * (
                scaled
                - jnp.mean(scaled, axis=-1, keepdims=True)
                - unit * jnp.mean(scaled * unit, axis=-1, keepdims=True)
            )
            sums_ref[2:3] += jnp.sum(grad_second * unit, axis=0, keepdims=True)
            sums_ref[3:4] += jnp.sum(grad_second, axis=0, keepdims=True)
            h1_ref[spot] = grad_mid
            grad_attn = grad_mid.astype(bf16)
            gattn_ref[spot] = grad_attn
            grad_blend = dot_nn(grad_attn, attn_part(3 * width, width))
            for head in range(HEAD_COUNT):
                part = slice(head * head_width, (head + 1) * head_width)
                scaled_blend = grad_blend[:, part] * scale_ref[spot, pl.ds(head, 1)]
                gblend_ref[spot, pl.ds(head * head_width, head_width)] = scaled_blend.astype(bf16)

        mom_step(3)
        row_loop(big, back_feed)
        for k in range(4, place.fars + 2):
            mom_step(k)

        def outer_loop(target, block, offset, left, right, columns):
            @pl.loop(0, columns // big)
            def _(index):
                part = pl.multiple_of(index * big, big)
                product = dot_tn(left[:, pl.ds(part, big)], right[...]).astype(bf16)
                target[pl.ds((offset + part) // block, big // block), pl.ds(0, block)] = product.reshape(
                    big // block, block, width
                )

        for low in range(0, hidden, chunk):
            outer_loop(mlp_ref, mlp_rows, hidden + low, activ_ref.at[low // chunk], gb_ref, chunk)
            outer_loop(mlp_ref, mlp_rows, low, slope_ref.at[low // chunk], second_ref, chunk)
        scatter = Scatter(place, mlp_sum_pieces, (mlp_ref,), bufs, [pool] * 6)
        scatter.begin([0])

        gext_ref[...] = jnp.zeros_like(gext_ref)

        def back_attend(spot):
            for head in range(HEAD_COUNT):
                part = pl.ds(head * head_width, head_width)
                values = pl.ds(width + head * head_width, head_width)
                raised = prob_ref[head, spot]
                grad_blend = gblend_ref[spot, part]
                grad_prob = dot_nt(grad_blend, ext_ref[:, values])
                mean = jnp.sum(
                    grad_blend.astype(f32) * blend_ref[spot, part].astype(f32), axis=-1, keepdims=True
                )
                grad_logit = (raised.astype(f32) * (grad_prob - mean)).astype(bf16)
                gext_ref[:, part] += dot_tn(grad_logit, q_ref[spot, part])
                q_ref[spot, part] = (dot_nn(grad_logit, ext_ref[:, part]) * score_scale).astype(bf16)
                gext_ref[:, values] += dot_tn(raised, grad_blend)

        row_loop(big, back_attend, [lambda: scatter.step(0), lambda: scatter.step(1)])
        key_scale = jnp.where(iota((1, 2 * width), 1) < width, score_scale, 1.0)
        lost_ref[0] = (gext_ref[pl.ds(rows, halo)] * key_scale).astype(bf16)
        lost_ref[1] = (gext_ref[pl.ds(rows + halo, halo)] * key_scale).astype(bf16)
        from_upper = to_node(nodes - 1, lost_ref.at[0], back_ref.at[0])
        from_lower = to_node(1, lost_ref.at[1], back_ref.at[1])
        scatter.step(2)
        outer_loop(packed_ref, attn_rows, 3 * width, gattn_ref, blend_ref, width)
        scatter.step(3)
        from_upper.wait_recv()
        from_lower.wait_recv()

        def back_encode(spot):
            grad_pairs = gext_ref[spot] * key_scale + dot_nn(lendt_ref[spot], back_ref[0]) + dot_nn(
                lendt_ref[spot], back_ref[1]
            )
            grad_pairs = grad_pairs.astype(bf16)
            ext_ref[spot] = grad_pairs
            grad_first = dot_nn(q_ref[spot], attn_part(0, width)) + dot_nn(
                grad_pairs, attn_part(width, 2 * width)
            )
            unit, inverse = norm_parts(h0_ref[spot])
            scaled = grad_first * (1.0 + mod[0])
            grad_in = h1_ref[spot] + inverse * (
                scaled
                - jnp.mean(scaled, axis=-1, keepdims=True)
                - unit * jnp.mean(scaled * unit, axis=-1, keepdims=True)
            )
            sums_ref[0:1] += jnp.sum(grad_first * unit, axis=0, keepdims=True)
            sums_ref[1:2] += jnp.sum(grad_first, axis=0, keepdims=True)
            gb_ref[spot] = grad_in.astype(bf16)

        row_loop(big, back_encode, [lambda: scatter.step(4)])
        outer_loop(packed_ref, attn_rows, 0, q_ref, first_ref, width)
        outer_loop(packed_ref, attn_rows, width, ext_ref.at[pl.ds(0, rows)], first_ref, 2 * width)
        last = Scatter(
            place, last_pieces, (packed_ref,), strips((activ_ref, slope_ref), last_shapes), [pool] * 6
        )

        @pl.loop(0, all_small // 128)
        def _(index):
            low_row = pl.multiple_of(index * 128, 128)
            part = feats_ref[pl.ds(low_row, 128)]
            total = part[:, 0:1] * sums_ref[0:1]
            for j in range(1, 4):
                total += part[:, j : j + 1] * sums_ref[j : j + 1]
            gext_ref[pl.ds(low_row, 128), pl.ds(0, width)] = total

        for low_row in range(0, wide, 128):
            gext_ref[pl.ds(low_row, 128), pl.ds(0, width)] += dot_tn(
                mixed_ref[0, :, pl.ds(low_row, 128)], gb_ref[...]
            )
        gext_ref[pl.ds(start, 128), pl.ds(0, width)] += pltpu.roll(
            dot_tn(node_ref[:, pl.ds(0, 128)], out_ref[...]), shift, 0
        )

        @pl.loop(0, all_small // 128)
        def _(index):
            total = gext_ref[pl.ds(pl.multiple_of(index * 128, 128), 128), pl.ds(0, width)]
            high = total.astype(bf16)
            blocks = pl.ds(index * (128 // small_rows), 128 // small_rows)
            shape = (128 // small_rows, small_rows, width)
            packed_ref[blocks, pl.ds(attn_rows, small_rows)] = high.reshape(shape)
            packed_ref[blocks, pl.ds(first_rows, small_rows)] = (total - high.astype(f32)).astype(bf16).reshape(shape)

        last.begin([0])
        for k in range(5, scatter.steps()):
            scatter.step(k)
        last.step(0)
        scatter.finish(mlp_sum)
        g_mlp_shard[...] = mlp_sum[...].astype(bf16)
        gather_g_mlp = HalfGather(place, g_mlp_shard, g_mlp_all, pool.half(own_sem, 4))
        gather_g_mlp.begin()
        gather_g_mlp.step(0)
        for k in range(last.steps()):
            if k:
                last.step(k)
            if k + 1 < last.steps():
                gather_g_mlp.step(k + 1)
        last.finish(own)
        g_attn, g_mlp = own[pl.ds(0, attn_rows)], mlp_sum[...]
        g_small = own[pl.ds(attn_rows, small_rows)] + own[pl.ds(attn_rows + small_rows, small_rows)]
        attn_sum[...] = g_attn
        small_sum[...] = g_small
        g_attn_shard[...] = g_attn.astype(bf16)
        squares = jnp.sum(g_attn * g_attn) + jnp.sum(g_mlp * g_mlp) + jnp.sum(g_small * g_small)
        tile_shard[...] = jnp.where(iota((8, 128), 0) < 4, squares, loss_share)
        gather_g_attn = Gather(
            place, tile_pieces, (g_attn_shard, tile_shard), (g_attn_all, tiles_out), pool.gather(own_sem, 5)
        )
        gather_g_attn.begin()
        for k in range(place.fars + 2):
            gather_g_attn.step(k)
        for item in (*gather_moms, gather_g_mlp, gather_g_attn):
            item.end()
        scatter.end()
        last.end()
        for copy in started:
            copy.wait_send()

    vmem = pl.BlockSpec(memory_space=pltpu.VMEM)
    dma = pltpu.SemaphoreType.DMA
    struct = jax.ShapeDtypeStruct
    low = lambda *shape: pltpu.VMEM(shape, bf16)
    full = lambda *shape: pltpu.VMEM(shape, f32)
    return pl.pallas_call(
        kernel,
        out_shape=(
            struct((attn_rows, width), f32),
            struct((mlp_rows, width), f32),
            struct((small_rows, width), f32),
            struct((devices, 8, 128), f32),
        )
        + tuple(struct((devices, size, width), bf16) for size in (attn_rows, mlp_rows) * 2),
        in_specs=[vmem] * 15,
        out_specs=(vmem,) * 3 + (pl.BlockSpec(memory_space=pl.ANY),) * 5,
        scratch_shapes=[
            full(attn_rows + 2 * small_rows, width),
            low(attn_rows, width),
            low(mlp_rows, width),
            low(attn_rows, width),
            low(mlp_rows, width),
            full(8, 128),
            low(first_rows, width),
            low(mlp_rows, width),
            low(nodes, lats, lows, flat),
            full(place.nears, lats, all_lats, flat),
            full(place.fars, lats, all_lats, flat),
            full(lats, all_lats, lanes),
            low(devices, packed_rows, width),
            low(devices, mlp_rows, width),
            full(rows, ext_rows),
            low(bands, lons, rows),
            low(2, rows, wide),
            low(rows, halo),
            full(rows, width),
            full(rows, width),
            low(rows, width),
            low(rows, width),
            low(ext_rows, 2 * width),
            low(halo, 2 * width),
            low(HEAD_COUNT, rows, ext_rows),
            low(rows, width),
            low(rows, width),
            low(hidden // chunk, rows, chunk),
            low(hidden // chunk, rows, chunk),
            low(rows, width),
            low(rows, 256),
            low(nodes, lats, sent, lanes),
            full(128, lanes),
            low(bands, lons, 128),
            full(rows, 128),
            low(rows, width),
            low(rows, width),
            low(rows, width),
            full(ext_rows, 2 * width),
            low(2, halo, 2 * width),
            low(2, halo, 2 * width),
            full(8, width),
            full(rows, 128),
            full(lons, 128),
            pltpu.VMEM((8, flat_pixels), jnp.int32),
            pltpu.VMEM((flat_pixels, 128), jnp.int32),
            low(bands, lons, cin),
            low(128, width),
            full(all_small, 128),
            dma((2 * copies,)),
            dma((7,)),
        ]
        + scatter_bufs,
        compiler_params=pltpu.CompilerParams(
            collective_id=collective, has_side_effects=True, vmem_limit_bytes=62 << 20
        ),
    )(*weights, grid, target, land, near_turned, enc_turned, dec_turned, lent, legendre, vector, tables, *moments)


def turn_tables(lon_count, modes):
    turns = np.arange(lon_count)[:, None] * np.arange(modes)[None, :] % lon_count
    phases = turns * (2.0 * np.pi / lon_count)
    waves = [m for m in range(modes) if (2 * m) % lon_count]
    picks = list(range(modes)) + waves
    lanes = -(-len(picks) // 128) * 128
    table = np.zeros((lon_count, lanes), np.float32)
    table[:, :modes] = np.cos(phases)
    table[:, modes : len(picks)] = -np.sin(phases[:, waves])
    high = table.astype(ml_dtypes.bfloat16)
    low = (table - high.astype(np.float32)).astype(ml_dtypes.bfloat16)
    return np.stack([high, low]), (waves[0], waves[-1] + 1, lanes - len(picks))


def to_sixteens(blocks):
    return jnp.pad(blocks, ((0, 0), (0, sixteens(blocks.shape[1]) - blocks.shape[1]), (0, 0)))


def on_device(
    grid_in,
    target,
    noise_level,
    land_mask,
    neighbours,
    halo_send,
    g2m,
    m2g,
    legendre,
    w_attn,
    w_mlp,
    w_small,
    mom_attn,
    mom_mlp,
    m_small,
    v_small,
    ema_attn,
    ema_mlp,
    ema_small,
):
    cin = grid_in.shape[-1]
    lat_rows, lon_count, channels = target.shape[1:]
    modes, degrees = legendre.shape[1:]
    halo_rows = halo_send.shape[0]
    width = w_attn.shape[1]
    nodes, zeros = lax.axis_size("node"), lax.axis_size("zero")
    devices = nodes * zeros
    attn_rows, mlp_rows, small_rows = w_attn.shape[0], w_mlp.shape[0], w_small.shape[0]

    sigma, c_input, c_skip, c_output, loss_weight = noise_scalars(noise_level[0])
    features = noise_features(sigma).astype(bf16).astype(f32)
    weight = loss_weight / (2 * modes * degrees * channels)
    tables, (wave_first, wave_end, wave_pad) = turn_tables(lon_count, modes)
    whole_tiles = all(size % 16 == 0 and 256 % size == 0 for size in (attn_rows, mlp_rows, small_rows))
    if whole_tiles:
        lows = sixteens(-(-degrees // zeros))
        wanted = lax.axis_index("zero") * lows
        first_degree = jnp.minimum(wanted, degrees - lows)
        leg = lax.dynamic_slice_in_dim(legendre, first_degree, lows, axis=2)
        leg = jnp.where(first_degree + jnp.arange(lows) >= wanted, leg, 0.0)
        leg = jnp.pad(jnp.transpose(leg, (0, 2, 1)).astype(bf16), ((0, 0), (0, 0), (0, -modes % 128)))
        lane = jnp.arange(128)
        vector = jnp.where(lane < NOISE_FEATS, jnp.pad(features, (0, 128 - NOISE_FEATS)), 0.0)
        for spot, value in (
            (c_input_lane, c_input),
            (c_skip_lane, c_skip),
            (c_output_lane, c_output),
            (weight_lane, weight),
        ):
            vector = jnp.where(lane == spot, value, vector)
        attn_sum, mlp_sum, g_small, totals, mom_attn_all, mom_mlp_all, g_attn_all, g_mlp_all = train_step(
            nodes,
            zeros,
            (w_attn, w_mlp, w_small),
            grid_in[0],
            target[0],
            land_mask,
            neighbours.T,
            g2m.T,
            m2g.T,
            halo_send[None],
            leg,
            vector[None],
            jnp.asarray(tables),
            (modes, wave_first, wave_end),
            (mom_attn, mom_mlp),
            cin,
            1,
        )
        sums = (g_small, attn_sum, mlp_sum)
        attn_sets = [item.reshape(-1, width) for item in (mom_attn_all, g_attn_all)]
        mlp_sets = [item.reshape(-1, width) for item in (mom_mlp_all, g_mlp_all)]
        moments = (mom_attn, mom_mlp)
    else:
        scale_input = jnp.where(jnp.arange(cin) < channels, c_input, 1.0)[None]
        cond_rows = jnp.where(
            jnp.arange(128)[None, None] == jnp.arange(4)[:, None, None], features[None, :, None], 0.0
        ).reshape(-1, 128)
        feats = jnp.pad(cond_rows, ((cin + channels, 0), (0, 0)))
        shift = cin % 128
        sides = ((0, 0), (0, 0), (shift, 128 - shift - channels))
        keep_mask = 1.0 - land_mask.astype(f32)[:, :, None] * (
            jnp.arange(channels) == channels - 1
        ).astype(f32)
        base = jnp.pad(c_skip * grid_in[0, :, :, :channels].astype(f32) - target[0], sides)
        keep = jnp.pad(keep_mask, sides)
        lows = -(-degrees // (8 * zeros)) * 8
        leg = jnp.pad(legendre, ((0, 0), (0, 0), (0, lows * zeros - degrees)))
        leg = lax.dynamic_slice_in_dim(leg, lax.axis_index("zero") * lows, lows, axis=2)
        leg = jnp.transpose(leg, (0, 2, 1))
        leg = jnp.concatenate(
            [leg, leg[:, :, wave_first:wave_end], jnp.zeros(leg.shape[:2] + (wave_pad,), f32)], axis=2
        )
        m2g_bands = m2g.reshape(lat_rows, lon_count, -1)

        attn, mlp, small, near, dec, dec_turned, mixed, lend, lendt, kern = gather_and_count(
            nodes,
            zeros,
            (w_attn, w_mlp, w_small),
            grid_in[0].reshape(-1, cin),
            scale_input,
            g2m,
            m2g_bands,
            jnp.transpose(m2g_bands, (0, 2, 1)),
            neighbours,
            halo_send[:, None],
            jnp.concatenate([halo_send, halo_send])[None],
            leg,
            1,
        )
        full = [
            item[:, :size].reshape(-1, width)
            for item, size in ((attn, attn_rows), (mlp, mlp_rows), (small, small_rows))
        ]
        *local, loss_tile = model_step(
            nodes,
            zeros,
            full,
            (near, dec, dec_turned, mixed, lend, lendt),
            kern,
            feats,
            base,
            keep,
            jnp.asarray(tables),
            jnp.stack([c_output, weight]),
            cin,
            channels,
            m2g.shape[1],
            2,
        )
        names = ["attn", "mlp", "high", "low"]
        mlp_sum = None

        g_small, moment_attn, moment_mlp, totals, attn_all, mlp_all = reduce_and_gather(
            nodes,
            zeros,
            names,
            [to_sixteens(item.reshape(devices, -1, width)) for item in local],
            mlp_sum,
            loss_tile,
            mom_attn,
            mom_mlp,
            small_rows,
            3,
        )
        sums = (g_small,)
        attn_sets = [attn_all[:, :attn_rows].reshape(-1, width)]
        mlp_sets = [mlp_all[:, :mlp_rows].reshape(-1, width)]
        totals = totals[None]
        moments = (moment_attn, moment_mlp)

    *results, moment_attn, moment_mlp = update_weights(
        nodes,
        zeros,
        attn_sets,
        mlp_sets,
        totals,
        sums,
        moments,
        (w_attn, w_mlp, w_small),
        (ema_attn, ema_mlp, ema_small),
        (m_small, v_small),
    )
    loss, clip_norm, new_attn, new_mlp, new_small, new_m, new_v, *new_averages = results
    return (
        loss[0, 0], clip_norm[0, 0], new_attn, new_mlp, new_small, moment_attn, moment_mlp, new_m, new_v, *new_averages
    )


def solution(mesh):
    split_rows = P(("node", "zero"), None)
    return jax.shard_map(
        on_device,
        mesh=mesh,
        in_specs=(
            P("zero", "node", None, None),
            P("zero", "node", None, None),
            P("zero"),
            P("node", None),
            P("node", None),
            P("node"),
            P("node", None),
            P("node", None),
            P("node", None, None),
        )
        + (split_rows,) * 10,
        out_specs=(P(), P()) + (split_rows,) * 10,
        check_vma=False,
    )
```
